32 devices in a mesh: solver: 16 (over z, y, core), analysis: 2 (over x).
Axes of the slice: x: 2, y: 2, z: 4, core: 2. Of those that a mesh axis runs over, the one named last changes fastest.
Arguments:
- windows: float32 [2, 5, 128, 8, 512], P(None, None, 'solver', 'analysis'), may hold values from -2.3 to 3.7, as said below
- pod_basis: bfloat16 [64, 5, 128, 8, 512], P(None, None, ('solver', 'analysis')), may hold values from -1.9 to 3.4
Outputs:
- next_windows: float32 [2, 5, 128, 8, 512], P(None, None, 'solver', 'analysis')
- coefficients: float32 [2, 64], replicated
- new_modes: float32 [2, 5, 128, 8, 512], P(None, None, ('solver', 'analysis'))
- r_factor: float32 [2, 2], replicated
The draws below stay inside these ranges and needn't reach their ends.
Inputs may be any that keep to these rules, and one draw needn't show every extreme that they name: `windows`: field 0 (density) lies between 0.4 and 1.6 everywhere.
All inputs are finite; a program needn't handle non-finite values.
Results may differ from the reference program's by a relative error of at most 0.00185.
The reference program's roundings to bfloat16 on the way (of `snapshots`) count: a program that leaves them out, or rounds other values in their place, can miss the bound.
Values may be sent and summed in bfloat16 or wider, within the bound.
No kernel may reach another device: no remote copies, remote signals or barrier semaphores. Data moves between devices by JAX's collectives and lax.ppermute only.
A program may use at most 128 MiB of HBM per device.

```python
import jax
import jax.numpy as jnp
from jax import lax

NZ = 512
RANK = 64
FIELDS = 5
WINDOWS = 2
NX = 128
NY = 8
ROWS = 2621440


def base_field(key):
    return jax.random.uniform(key, (FIELDS, NX, NY, NZ), jnp.float32, -1.0, 1.0)


def draw_windows(key, part):
    shared = base_field(key)
    key = jax.random.fold_in(key, 11)
    noise = jax.random.truncated_normal(key, -3.0, 3.0, (WINDOWS, FIELDS, NX, NY, NZ), jnp.float32)
    along_x = 0.5 + jnp.arange(NX, dtype=jnp.float32) / NX
    along_y = 0.7 + 0.6 * jnp.arange(NY, dtype=jnp.float32) / NY
    amplitude = along_x[:, None, None] * along_y[None, :, None]
    density = 1.0 + amplitude * (0.15 * shared[0] + 0.05 * noise[:, 0])
    offsets = jnp.array([0.8, 0.0, 0.0], jnp.float32)[:, None, None, None]
    momenta = amplitude * (0.4 * shared[1:4] + 0.25 * noise[:, 1:4]) + offsets
    energy = 2.5 + amplitude * (0.3 * shared[4] + 0.1 * noise[:, 4])
    return jnp.concatenate([density[:, None], momenta, energy[:, None]], axis=1)


def draw_pod_basis(key, part):
    shared = base_field(key)
    key = jax.random.fold_in(key, 23)
    key_region, key_noise, key_mode, key_cell = jax.random.split(key, 4)
    region = jax.random.randint(key_region, (NX, NY, NZ), 0, RANK)
    noise = jax.random.truncated_normal(key_noise, -3.0, 3.0, (RANK, FIELDS, NX, NY, NZ), jnp.float32)
    mode_weight = jax.random.uniform(key_mode, (RANK,), jnp.float32, 0.5, 1.5)
    cell_weight = jax.random.uniform(key_cell, (FIELDS, NX, NY, NZ), jnp.float32, 0.5, 1.5)
    chosen = (region[None] == jnp.arange(RANK)[:, None, None, None]).astype(jnp.float32)
    return (shared[None] * chosen[:, None] + 0.3 * noise + 0.5 * mode_weight[:, None, None, None, None] * cell_weight[None]).astype(jnp.bfloat16)


def setup_inputs(seed: int = 0) -> dict:
    key_list = jax.random.split(jax.random.key(seed), 3)
    windows = draw_windows(jax.random.fold_in(key_list[2], 71), 0)
    pod_basis = draw_pod_basis(jax.random.fold_in(key_list[2], 71), 0)
    return dict(windows=windows, pod_basis=pod_basis)


HEAT_RATIO = 1.4
SECTION_STEP = 0.25
CENTRAL_WEIGHTS = (0.8, -0.2, 4.0 / 105.0, -1.0 / 280.0)

def flux_parts(fields_in):
    density = fields_in[:, 0]
    moment_x = fields_in[:, 1]
    moment_y = fields_in[:, 2]
    moment_z = fields_in[:, 3]
    energy = fields_in[:, 4]
    speed_x = moment_x / density
    speed_y = moment_y / density
    speed_z = moment_z / density
    pressure = (HEAT_RATIO - 1.0) * (energy - 0.5 * (moment_x * speed_x + moment_y * speed_y + moment_z * speed_z))
    enthalpy = energy + pressure
    flux_x = jnp.stack([moment_x, moment_x * speed_x + pressure, moment_y * speed_x, moment_z * speed_x, enthalpy * speed_x], axis=1)
    flux_y = jnp.stack([moment_y, moment_x * speed_y, moment_y * speed_y + pressure, moment_z * speed_y, enthalpy * speed_y], axis=1)
    flux_z = jnp.stack([moment_z, moment_x * speed_z, moment_y * speed_z, moment_z * speed_z + pressure, enthalpy * speed_z], axis=1)
    return (flux_x, flux_y, flux_z)

def centered(extended, dimension, length):
    summed = None
    for offset, weight in enumerate(CENTRAL_WEIGHTS, start=1):
        forward_cells = lax.slice_in_dim(extended, 4 + offset, 4 + offset + length, axis=dimension)
        behind_cells = lax.slice_in_dim(extended, 4 - offset, 4 - offset + length, axis=dimension)
        term = weight * (forward_cells - behind_cells)
        summed = term if summed is None else summed + term
    return summed

def spanwise(flux_z):
    summed = None
    for offset, weight in enumerate(CENTRAL_WEIGHTS, start=1):
        term = weight * (jnp.roll(flux_z, -offset, axis=4) - jnp.roll(flux_z, offset, axis=4))
        summed = term if summed is None else summed + term
    return summed

def tendency(wide_x, wide_y, flux_z, cells_x, cells_y):
    return -(centered(wide_x, 2, cells_x) + centered(wide_y, 3, cells_y) + spanwise(flux_z))

def cholesky_lower(matrix):
    highest = lax.Precision.HIGHEST
    order = matrix.shape[0]
    index = jnp.arange(order, dtype=jnp.int32)

    def column_step(column, lower):
        picker = (index == column).astype(matrix.dtype)
        row_now = jnp.dot(picker, lower, precision=highest)
        left = jnp.dot(matrix, picker, precision=highest) - jnp.dot(lower, row_now, precision=highest)
        pivot = jnp.sqrt(jnp.dot(left, picker, precision=highest))
        fresh = jnp.where(index >= column, left / pivot, jnp.zeros_like(left))
        return lower + fresh[:, None] * picker[None, :]
    return lax.fori_loop(0, order, column_step, jnp.zeros_like(matrix))

def solve_modes(basis_gram, projected):
    highest = lax.Precision.HIGHEST
    lower = cholesky_lower(basis_gram)
    order = lower.shape[0]
    index = jnp.arange(order, dtype=jnp.int32)

    def forward_step(row, solution):
        picker = (index == row).astype(lower.dtype)
        row_now = jnp.dot(picker, lower, precision=highest)
        pivot = jnp.dot(row_now, picker, precision=highest)
        value = (jnp.dot(picker, projected, precision=highest) - jnp.dot(row_now, solution, precision=highest)) / pivot
        return solution + picker[:, None] * value[None, :]
    halfway = lax.fori_loop(0, order, forward_step, jnp.zeros_like(projected))

    def backward_step(count, solution):
        row = order - 1 - count
        picker = (index == row).astype(lower.dtype)
        column_now = jnp.dot(lower, picker, precision=highest)
        pivot = jnp.dot(column_now, picker, precision=highest)
        value = (jnp.dot(picker, halfway, precision=highest) - jnp.dot(column_now, solution, precision=highest)) / pivot
        return solution + picker[:, None] * value[None, :]
    return lax.fori_loop(0, order, backward_step, jnp.zeros_like(projected))

def small_factor(gram_small):
    first = jnp.sqrt(gram_small[0, 0])
    below = gram_small[1, 0] / first
    second = jnp.sqrt(gram_small[1, 1] - below * below)
    return (first, below, second)

def orthonormal_rows(residuals, first, below, second, scaling):
    row_zero = residuals[0] / first
    row_one = (residuals[1] - below * row_zero) / second
    return jnp.stack([row_zero, row_one], axis=0) * scaling

def upper_factor(first, below, second, scaling):
    zero = jnp.zeros_like(first)
    return jnp.stack([jnp.stack([first, below]), jnp.stack([zero, second])]) / scaling

def reference(windows, pod_basis):
    highest = lax.Precision.HIGHEST
    flux_x, flux_y, flux_z = flux_parts(windows)
    wide_x = jnp.concatenate([flux_x[:, :, -4:], flux_x, flux_x[:, :, :4]], axis=2)
    wide_y = jnp.pad(flux_y, ((0, 0), (0, 0), (0, 0), (4, 4), (0, 0)))
    next_windows = windows + SECTION_STEP * tendency(wide_x, wide_y, flux_z, NX, NY)
    snapshots = next_windows.astype(jnp.bfloat16)

    def plane_pair(plane_index):
        plane_basis = lax.dynamic_slice_in_dim(pod_basis, plane_index, 1, 2).astype(jnp.float32).reshape(RANK, -1)
        plane_snap = lax.dynamic_slice_in_dim(snapshots, plane_index, 1, 2).astype(jnp.float32).reshape(WINDOWS, -1)
        return (plane_basis, plane_snap)

    def gram_step(plane_index, running):
        basis_gram, projected = running
        plane_basis, plane_snap = plane_pair(plane_index)
        basis_gram = basis_gram + jnp.dot(plane_basis, plane_basis.T, precision=highest)
        projected = projected + jnp.dot(plane_basis, plane_snap.T, precision=highest)
        return (basis_gram, projected)
    basis_gram, projected = lax.fori_loop(0, NX, gram_step, (jnp.zeros((RANK, RANK), jnp.float32), jnp.zeros((RANK, WINDOWS), jnp.float32)))
    solved = solve_modes(basis_gram, projected)

    def residual_step(plane_index, running):
        gram_small, residuals = running
        plane_basis, plane_snap = plane_pair(plane_index)
        plane_resid = plane_snap - jnp.dot(solved.T, plane_basis, precision=highest)
        gram_small = gram_small + jnp.dot(plane_resid, plane_resid.T, precision=highest)
        residuals = lax.dynamic_update_slice_in_dim(residuals, plane_resid.reshape(WINDOWS, FIELDS, 1, NY, NZ), plane_index, 2)
        return (gram_small, residuals)
    gram_small, residuals = lax.fori_loop(0, NX, residual_step, (jnp.zeros((WINDOWS, WINDOWS), jnp.float32), jnp.zeros((WINDOWS, FIELDS, NX, NY, NZ), jnp.float32)))
    first, below, second = small_factor(gram_small)
    scaling = jnp.sqrt(jnp.float32(ROWS))
    new_modes = orthonormal_rows(residuals, first, below, second, scaling)
    return (next_windows, solved.T, new_modes, upper_factor(first, below, second, scaling))
```

```python
import functools

import jax
import jax.numpy as jnp
from jax import lax
from jax.experimental import pallas as pl
from jax.experimental.pallas import tpu as pltpu
from jax.sharding import PartitionSpec as P

PRESSURE_FACTOR = 1.4 - 1.0
SECTION_STEP = 0.25
CENTRAL_WEIGHTS = (0.8, -0.2, 4.0 / 105.0, -1.0 / 280.0)
REACH = 4
LANES = 128
HIGHEST = lax.Precision.HIGHEST
NT = (((1,), (1,)), ((), ()))


def weight(k):
    if k == 0 or abs(k) > REACH:
        return 0.0
    value = -SECTION_STEP * CENTRAL_WEIGHTS[abs(k) - 1]
    return value if k > 0 else -value


def row_weights(shape, values):
    rows = lax.broadcasted_iota(jnp.int32, shape, len(shape) - 2)
    made = jnp.full(shape, values[0], jnp.float32)
    for i, value in enumerate(values[1:], start=1):
        made = jnp.where(rows == i, jnp.float32(value), made)
    return made


def primitives(windows_ref, w, x):
    density, mx, my, mz, energy = (windows_ref[w, f, x] for f in range(5))
    inverse = 1.0 / density
    ux, uy, uz = mx * inverse, my * inverse, mz * inverse
    pressure = PRESSURE_FACTOR * (energy - 0.5 * (mx * ux + my * uy + mz * uz))
    return (mx, my, mz), (ux, uy, uz), pressure, energy + pressure


def flux(parts, direction):
    moments, speeds, pressure, enthalpy = parts
    speed = speeds[direction]
    made = [moments[direction]]
    for axis in range(3):
        term = moments[axis] * speed
        made.append(term + pressure if axis == direction else term)
    made.append(enthalpy * speed)
    return made


def face_kernel(two_sided, where_ref, windows_ref, left_ref, right_ref, *rest):
    windows, _, planes, layers, cells = windows_ref.shape
    wall_refs, scratch = rest[:-1], rest[-1]
    tile = (layers, cells)
    up = [
        row_weights(tile, [weight(j - layers - i) for i in range(layers)]) for j in range(layers)
    ]
    down = [
        row_weights(tile, [weight(layers + j - i) for i in range(layers)]) for j in range(layers)
    ]
    if two_sided:
        tables = (up, down)
    else:
        first = where_ref[0] == 0
        tables = ([jnp.where(first, u, d) for u, d in zip(up, down)],)
    for w in range(windows):
        for x in range(planes):
            parts = primitives(windows_ref, w, x)
            for f, value in enumerate(flux(parts, 0)):
                scratch[f, x] = value
            for f, value in enumerate(flux(parts, 1)):
                for ref, table in zip(wall_refs, tables):
                    total = None
                    for j in range(layers):
                        term = table[j] * value[j : j + 1, :]
                        total = term if total is None else total + term
                    ref[w, f, x] = total
        for f in range(5):
            for i in range(REACH):
                total = None
                for j in range(planes):
                    c = weight(j - planes - i)
                    if c:
                        term = c * scratch[f, j]
                        total = term if total is None else total + term
                left_ref[w, f, i] = total
                total = None
                for j in range(planes):
                    c = weight(j + REACH - i)
                    if c:
                        term = c * scratch[f, j]
                        total = term if total is None else total + term
                right_ref[w, f, i] = total


def inner_kernel(windows_ref, part_ref, scratch):
    windows, _, planes, layers, cells = windows_ref.shape
    tile = (layers, cells)
    wall = [
        row_weights(tile, [weight(j - i) for i in range(layers)]) for j in range(layers)
    ]
    for w in range(windows):
        for x in range(planes):
            parts = primitives(windows_ref, w, x)
            for f, value in enumerate(flux(parts, 0)):
                scratch[f, x] = value
            flux_y, flux_z = flux(parts, 1), flux(parts, 2)
            for f in range(5):
                total = windows_ref[w, f, x]
                for j in range(layers):
                    total = total + wall[j] * flux_y[f][j : j + 1, :]
                for k in range(1, REACH + 1):
                    total = total + weight(k) * (
                        pltpu.roll(flux_z[f], cells - k, 1) - pltpu.roll(flux_z[f], k, 1)
                    )
                part_ref[w, f, x] = total
        for f in range(5):
            for x in range(planes):
                total = part_ref[w, f, x]
                for k in range(-REACH, REACH + 1):
                    if k and 0 <= x + k < planes:
                        total = total + weight(k) * scratch[f, x + k]
                part_ref[w, f, x] = total


def join_kernel(walls, paired, where_ref, part_ref, left_ref, right_ref, *rest):
    wall_refs, next_ref = rest[:walls], rest[walls]
    windows, _, planes, layers, cells = part_ref.shape
    for w in range(windows):
        for f in range(5):
            for x in range(planes):
                total = part_ref[w, f, x]
                for ref in wall_refs:
                    total = total + ref[w, f, x]
                if x < REACH:
                    total = total + left_ref[w, f, x]
                if x >= planes - REACH:
                    total = total + right_ref[w, f, x - planes + REACH]
                next_ref[w, f, x] = total
            if paired:
                half = planes // 2
                low = jnp.concatenate([next_ref[w, f, x] for x in range(half)], axis=0)
                high = jnp.concatenate([next_ref[w, f, x] for x in range(half, planes)], axis=0)
                first = where_ref[0] == 0
                rest[walls + 1][w, f] = jnp.where(first, low, high).astype(jnp.bfloat16)
                rest[walls + 2][w, f] = jnp.where(first, high, low).astype(jnp.bfloat16)


def same_layer(shape):
    rows = lax.broadcasted_iota(jnp.int32, shape, 0)
    columns = lax.broadcasted_iota(jnp.int32, shape, 1)
    return lax.rem(rows, 8) == lax.rem(columns, 8)


def modes_of(basis_ref, t):
    modes, _, layers, cells = basis_ref.shape
    return basis_ref[:, t].reshape(modes * layers, cells)


def gram_kernel(basis_ref, gram_ref, total):
    step = pl.program_id(0)

    @pl.when(step == 0)
    def _():
        total[...] = jnp.zeros_like(total)

    for t in range(basis_ref.shape[1]):
        rows = modes_of(basis_ref, t)
        total[...] += lax.dot_general(rows, rows, NT, preferred_element_type=jnp.float32)

    @pl.when(step == pl.num_programs(0) - 1)
    def _():
        wide = total.shape[0]
        modes = wide // 8
        kept = jnp.where(same_layer(total.shape), total[...], 0.0)
        rows = jnp.sum(kept.reshape(modes, 8, wide), axis=1)
        picks = (
            lax.broadcasted_iota(jnp.int32, (wide, modes), 0) // 8
            == lax.broadcasted_iota(jnp.int32, (wide, modes), 1)
        ).astype(jnp.float32)
        gram_ref[...] = jnp.dot(
            rows, picks, precision=HIGHEST, preferred_element_type=jnp.float32
        )


def project_kernel(paired, where_ref, *rest):
    step = pl.program_id(0)
    if paired:
        own_ref, got_ref, basis_ref, sums_ref, snaps_ref, total, small, square = rest
        steps = basis_ref.shape[1]
        first = where_ref[0] == 0
        for w in range(own_ref.shape[0]):
            own = own_ref[w, 0].astype(jnp.float32)
            got = got_ref[w, 0].astype(jnp.float32)
            low = jnp.where(first, own, got)
            high = jnp.where(first, got, own)
            for t in range(steps):
                snaps_ref[t, pl.ds(8 * w, 8)] = jnp.concatenate(
                    [low[4 * t : 4 * t + 4], high[4 * t : 4 * t + 4]], axis=0
                ).astype(jnp.bfloat16)
    else:
        snaps_ref, basis_ref, sums_ref, total, small, square = rest
        steps = basis_ref.shape[1]

    @pl.when(step == 0)
    def _():
        total[...] = jnp.zeros_like(total)
        small[...] = jnp.zeros_like(small)

    for t in range(steps):
        snaps = snaps_ref[t]
        total[...] += lax.dot_general(
            modes_of(basis_ref, t), snaps, NT, preferred_element_type=jnp.float32
        )
        small[...] += lax.dot_general(snaps, snaps, NT, preferred_element_type=jnp.float32)

    @pl.when(step == pl.num_programs(0) - 1)
    def _():
        modes = total.shape[0] // 8
        columns = total.shape[1]
        kept = jnp.where(same_layer(total.shape), total[...], 0.0)
        square[...] = jnp.zeros_like(square)
        square[0:modes, 0:columns] = jnp.sum(kept.reshape(modes, 8, columns), axis=1)
        kept = jnp.where(same_layer(small.shape), small[...], 0.0)
        square[modes : modes + 1, 0:columns] = jnp.sum(kept[0:8], axis=0, keepdims=True)
        square[modes + 1 : modes + 2, 0:columns] = jnp.sum(kept[8:16], axis=0, keepdims=True)
        turned = square[...].T
        sums_ref[...] = jnp.zeros_like(sums_ref)
        sums_ref[0:1, :] = jnp.sum(turned[0:8], axis=0, keepdims=True)
        sums_ref[1:2, :] = jnp.sum(turned[8:16], axis=0, keepdims=True)


def inverse_kernel(gram_ref, inverse_ref):
    modes = gram_ref.shape[0]
    shape = (modes, 2 * modes)
    rows = lax.broadcasted_iota(jnp.int32, shape, 0)
    columns = lax.broadcasted_iota(jnp.int32, shape, 1)
    eye = (rows[:, :modes] == columns[:, :modes]).astype(jnp.float32)
    whole = jnp.concatenate([gram_ref[...], eye], axis=1)
    for k in range(modes):
        row = whole[k : k + 1, :] / whole[k : k + 1, k : k + 1]
        whole = jnp.where(rows == k, row, whole - whole[:, k : k + 1] * row)
    inverse_ref[...] = whole[:, modes:]


def finish_kernel(
    rows_total, sums_ref, gram_ref, inverse_ref, snaps_ref, basis_ref,
    modes_ref, solved_ref, factor_ref, fit, scales,
):
    step = pl.program_id(0)
    modes = gram_ref.shape[0]

    @pl.when(step == 0)
    def _():
        exact = functools.partial(
            jnp.dot, precision=HIGHEST, preferred_element_type=jnp.float32
        )
        projected = sums_ref[:, 0:modes]
        gram, inverse = gram_ref[...], inverse_ref[...]
        solved = exact(projected, inverse)
        solved = solved + exact(projected - exact(solved, gram), inverse)
        left = projected - exact(solved, gram)

        def inner(p, i, q, j):
            return jnp.sum(p[i : i + 1] * q[j : j + 1], axis=1, keepdims=True)

        def entry(i, j):
            square = sums_ref[i : i + 1, modes + j : modes + j + 1]
            return square - inner(projected, i, solved, j) - inner(solved, i, left, j)

        first = jnp.sqrt(entry(0, 0))
        below = entry(1, 0) / first
        second = jnp.sqrt(entry(1, 1) - below * below)
        scaling = jnp.sqrt(jnp.float32(rows_total))
        w00 = scaling / first
        w11 = scaling / second
        w01 = -(below / first) * w11
        solved_ref[...] = solved[0:2]
        factor_ref[0:1, 0:1] = first / scaling
        factor_ref[0:1, 1:2] = below / scaling
        factor_ref[1:2, 0:1] = jnp.zeros_like(first)
        factor_ref[1:2, 1:2] = second / scaling
        wide = fit.shape[1]
        spread = (
            lax.broadcasted_iota(jnp.int32, (modes, wide), 1) // 8
            == lax.broadcasted_iota(jnp.int32, (modes, wide), 0)
        ).astype(jnp.float32)
        scaled = jnp.concatenate(
            [solved[0:1] * w00, solved[1:2] * w11 + solved[0:1] * w01, solved[2:8]], axis=0
        )
        lines = exact(scaled, spread)
        full = jnp.concatenate(
            [jnp.broadcast_to(lines[0:1], (8, wide)), jnp.broadcast_to(lines[1:2], (8, wide))],
            axis=0,
        )
        full = jnp.where(same_layer(full.shape), full, 0.0)
        upper = full.astype(jnp.bfloat16)
        fit[0:16] = upper
        fit[16:32] = (full - upper.astype(jnp.float32)).astype(jnp.bfloat16)
        scales[0] = jnp.broadcast_to(w00, scales.shape[1:])
        scales[1] = jnp.broadcast_to(w11, scales.shape[1:])
        scales[2] = jnp.broadcast_to(w01, scales.shape[1:])

    for t in range(basis_ref.shape[1]):
        fitted = jnp.dot(fit[...], modes_of(basis_ref, t), preferred_element_type=jnp.float32)
        fitted = fitted[0:16] + fitted[16:32]
        snaps = snaps_ref[t].astype(jnp.float32)
        modes_ref[0, t] = snaps[0:8] * scales[0] - fitted[0:8]
        modes_ref[1, t] = snaps[8:16] * scales[1] + snaps[0:8] * scales[2] - fitted[8:16]


def params(mib):
    return pltpu.CompilerParams(vmem_limit_bytes=mib * 1024 * 1024)


def cost(flops, moved):
    return pl.CostEstimate(flops=flops, bytes_accessed=moved, transcendentals=0)


WHOLE = pl.BlockSpec(memory_space=pltpu.VMEM)
SCALAR = pl.BlockSpec(memory_space=pltpu.SMEM)


def summed(value, axes):
    for axis in axes:
        count = lax.axis_size(axis)
        if count & (count - 1):
            value = lax.psum(value, axis)
            continue
        bit = 1
        while bit < count:
            value = value + lax.ppermute(value, axis, [(i, i ^ bit) for i in range(count)])
            bit *= 2
    return value


def body(windows, pod_basis):
    f32, bf16 = jnp.float32, jnp.bfloat16
    shape = jax.ShapeDtypeStruct
    count, fields, planes, layers, cells = windows.shape
    ring, walls = lax.axis_size("solver"), lax.axis_size("analysis")
    paired = walls == 2 and planes == 8 and layers == 4
    place = lax.axis_index("analysis").astype(jnp.int32).reshape(1)
    modes, _, pod_planes, pod_layers, _ = pod_basis.shape
    tiles = fields * pod_planes * (pod_layers // 8)
    per_step = tiles // fields
    basis = pod_basis.reshape(modes, tiles, 8, cells)
    basis_spec = pl.BlockSpec((modes, per_step, 8, cells), lambda i: (0, i, 0, 0))
    wide = modes * 8
    basis_bytes = basis.size * 2

    sides = 1 if walls == 2 else 2
    faces = pl.pallas_call(
        functools.partial(face_kernel, sides == 2),
        out_shape=[shape((count, fields, REACH, layers, cells), f32)] * 2
        + [shape(windows.shape, f32)] * sides,
        in_specs=[SCALAR, WHOLE],
        out_specs=[WHOLE] * (2 + sides),
        scratch_shapes=[pltpu.VMEM((fields, planes, layers, cells), f32)],
        compiler_params=params(16),
        cost_estimate=cost(10_000_000, 10 * windows.size),
        name="faces",
    )(place, windows)
    to_right = [(i, (i + 1) % ring) for i in range(ring)]
    to_left = [((i + 1) % ring, i) for i in range(ring)]
    upward = [(i, i + 1) for i in range(walls - 1)]
    downward = [(i + 1, i) for i in range(walls - 1)]
    if sides == 1:
        wall_terms = [lax.ppermute(faces[2], "analysis", upward + downward)]
    else:
        wall_terms = [
            lax.ppermute(faces[2], "analysis", upward),
            lax.ppermute(faces[3], "analysis", downward),
        ]
    from_left = lax.ppermute(faces[0], "solver", to_right)
    from_right = lax.ppermute(faces[1], "solver", to_left)

    inner = pl.pallas_call(
        inner_kernel,
        out_shape=shape(windows.shape, f32),
        in_specs=[WHOLE],
        out_specs=WHOLE,
        scratch_shapes=[pltpu.VMEM((fields, planes, layers, cells), f32)],
        compiler_params=params(16),
        cost_estimate=cost(30_000_000, 8 * windows.size),
        name="inner",
    )(windows)

    gram = pl.pallas_call(
        gram_kernel,
        grid=(fields,),
        out_shape=shape((modes, modes), f32),
        in_specs=[basis_spec],
        out_specs=pl.BlockSpec((modes, modes), lambda i: (0, 0)),
        scratch_shapes=[pltpu.VMEM((wide, wide), f32)],
        compiler_params=params(32),
        cost_estimate=cost(2 * wide * wide * cells * tiles, basis_bytes),
        name="gram",
    )(basis)
    gram = summed(gram, ("analysis", "solver"))
    inverse = pl.pallas_call(
        inverse_kernel,
        out_shape=shape((modes, modes), f32),
        in_specs=[WHOLE],
        out_specs=WHOLE,
        compiler_params=params(16),
        cost_estimate=cost(20_000_000, 8 * modes * modes),
        name="inverse",
    )(gram)

    half_shape = (count, fields, planes * layers // 2, cells)
    joined = pl.pallas_call(
        functools.partial(join_kernel, sides, paired),
        out_shape=[shape(windows.shape, f32)] + ([shape(half_shape, bf16)] * 2 if paired else []),
        in_specs=[SCALAR] + [WHOLE] * (3 + sides),
        out_specs=[WHOLE] * (3 if paired else 1),
        compiler_params=params(16),
        cost_estimate=cost(1_000_000, 16 * windows.size),
        name="join",
    )(place, inner, from_left, from_right, *wall_terms)
    next_windows = joined[0]

    sums_shape = shape((8, LANES), f32)
    sums_spec = pl.BlockSpec((8, LANES), lambda i: (0, 0))
    snaps_shape = shape((tiles, 2 * 8, cells), bf16)
    snaps_spec = pl.BlockSpec((per_step, 2 * 8, cells), lambda i: (i, 0, 0))
    scratch = [
        pltpu.VMEM((wide, 2 * 8), f32),
        pltpu.VMEM((2 * 8, 2 * 8), f32),
        pltpu.VMEM((LANES, LANES), f32),
    ]
    project_cost = cost(2 * wide * 16 * cells * tiles, basis_bytes)
    if paired:
        own, given = joined[1], joined[2]
        got = lax.ppermute(given, "analysis", [(0, 1), (1, 0)])
        half_spec = pl.BlockSpec(
            (count, 1, planes * layers // 2, cells), lambda i: (0, i, 0, 0)
        )
        sums, snaps = pl.pallas_call(
            functools.partial(project_kernel, True),
            grid=(fields,),
            out_shape=[sums_shape, snaps_shape],
            in_specs=[SCALAR, half_spec, half_spec, basis_spec],
            out_specs=[sums_spec, snaps_spec],
            scratch_shapes=scratch,
            compiler_params=params(32),
            cost_estimate=project_cost,
            name="project",
        )(place, own, got, basis)
    else:
        relaid = lax.all_to_all(
            next_windows.astype(bf16), "analysis", split_axis=2, concat_axis=3, tiled=True
        )
        snaps = relaid.reshape(count, tiles, 8, cells).transpose(1, 0, 2, 3)
        snaps = snaps.reshape(tiles, count * 8, cells)
        sums = pl.pallas_call(
            functools.partial(project_kernel, False),
            grid=(fields,),
            out_shape=sums_shape,
            in_specs=[SCALAR, snaps_spec, basis_spec],
            out_specs=sums_spec,
            scratch_shapes=scratch,
            compiler_params=params(32),
            cost_estimate=project_cost,
            name="project",
        )(place, snaps, basis)
    sums = summed(sums, ("analysis", "solver"))

    rows_total = ring * walls * tiles * 8 * cells
    new_modes, solved, factor = pl.pallas_call(
        functools.partial(finish_kernel, rows_total),
        grid=(fields,),
        out_shape=[
            shape((count, tiles, 8, cells), f32),
            shape((count, modes), f32),
            shape((count, count), f32),
        ],
        in_specs=[
            sums_spec,
            pl.BlockSpec((modes, modes), lambda i: (0, 0)),
            pl.BlockSpec((modes, modes), lambda i: (0, 0)),
            snaps_spec,
            basis_spec,
        ],
        out_specs=[
            pl.BlockSpec((count, per_step, 8, cells), lambda i: (0, i, 0, 0)),
            pl.BlockSpec((count, modes), lambda i: (0, 0)),
            pl.BlockSpec((count, count), lambda i: (0, 0)),
        ],
        scratch_shapes=[pltpu.VMEM((32, wide), bf16), pltpu.VMEM((3, 8, cells), f32)],
        compiler_params=params(32),
        cost_estimate=cost(2 * wide * 32 * cells * tiles, basis_bytes + 8 * windows.size),
        name="finish",
    )(sums, gram, inverse, snaps, basis)
    new_modes = new_modes.reshape(count, fields, pod_planes, pod_layers, cells)
    return next_windows, solved, new_modes, factor


def solution(mesh):
    in_specs = (
        P(None, None, "solver", "analysis", None),
        P(None, None, ("solver", "analysis"), None, None),
    )
    out_specs = (
        P(None, None, "solver", "analysis", None),
        P(),
        P(None, None, ("solver", "analysis"), None, None),
        P(),
    )
    return jax.shard_map(body, mesh=mesh, in_specs=in_specs, out_specs=out_specs, check_vma=False)
```

```python
import functools

import jax
import jax.numpy as jnp
from jax import lax
from jax.experimental import pallas as pl
from jax.experimental.pallas import tpu as pltpu
from jax.sharding import PartitionSpec as P

PRESSURE_FACTOR = 1.4 - 1.0
SECTION_STEP = 0.25
CENTRAL_WEIGHTS = (0.8, -0.2, 4.0 / 105.0, -1.0 / 280.0)
REACH = 4
LANES = 128
HIGHEST = lax.Precision.HIGHEST
NT = (((1,), (1,)), ((), ()))


def weight(k):
    if k == 0 or abs(k) > REACH:
        return 0.0
    value = -SECTION_STEP * CENTRAL_WEIGHTS[abs(k) - 1]
    return value if k > 0 else -value


def row_weights(shape, values):
    rows = lax.broadcasted_iota(jnp.int32, shape, len(shape) - 2)
    made = jnp.full(shape, values[0], jnp.float32)
    for i, value in enumerate(values[1:], start=1):
        made = jnp.where(rows == i, jnp.float32(value), made)
    return made


def primitives(windows_ref, w, x):
    density, mx, my, mz, energy = (windows_ref[w, f, x] for f in range(5))
    inverse = 1.0 / density
    ux, uy, uz = mx * inverse, my * inverse, mz * inverse
    pressure = PRESSURE_FACTOR * (energy - 0.5 * (mx * ux + my * uy + mz * uz))
    return (mx, my, mz), (ux, uy, uz), pressure, energy + pressure


def flux(parts, direction):
    moments, speeds, pressure, enthalpy = parts
    speed = speeds[direction]
    made = [moments[direction]]
    for axis in range(3):
        term = moments[axis] * speed
        made.append(term + pressure if axis == direction else term)
    made.append(enthalpy * speed)
    return made


def face_kernel(two_sided, where_ref, source_ref, windows_ref, left_ref, right_ref, *rest):
    windows, _, planes, layers, cells = windows_ref.shape
    wall_refs, scratch, sems = rest[:-2], rest[-2], rest[-1]
    copies = [
        pltpu.make_async_copy(source_ref.at[w], windows_ref.at[w], sems.at[w])
        for w in range(windows)
    ]
    for copy in copies:
        copy.start()
    tile = (layers, cells)
    up = [
        row_weights(tile, [weight(j - layers - i) for i in range(layers)]) for j in range(layers)
    ]
    down = [
        row_weights(tile, [weight(layers + j - i) for i in range(layers)]) for j in range(layers)
    ]
    if two_sided:
        tables = (up, down)
    else:
        first = where_ref[0] == 0
        tables = ([jnp.where(first, u, d) for u, d in zip(up, down)],)
    for w in range(windows):
        copies[w].wait()
        for x in range(planes):
            parts = primitives(windows_ref, w, x)
            for f, value in enumerate(flux(parts, 0)):
                scratch[f, x] = value
            for f, value in enumerate(flux(parts, 1)):
                for ref, table in zip(wall_refs, tables):
                    total = None
                    for j in range(layers):
                        term = table[j] * value[j : j + 1, :]
                        total = term if total is None else total + term
                    ref[w, f, x] = total
        for f in range(5):
            for i in range(REACH):
                total = None
                for j in range(planes):
                    c = weight(j - planes - i)
                    if c:
                        term = c * scratch[f, j]
                        total = term if total is None else total + term
                left_ref[w, f, i] = total
                total = None
                for j in range(planes):
                    c = weight(j + REACH - i)
                    if c:
                        term = c * scratch[f, j]
                        total = term if total is None else total + term
                right_ref[w, f, i] = total


def inner_part(windows_ref, part_ref, scratch):
    windows, _, planes, layers, cells = windows_ref.shape
    tile = (layers, cells)
    wall = [
        row_weights(tile, [weight(j - i) for i in range(layers)]) for j in range(layers)
    ]
    for w in range(windows):
        for x in range(planes):
            parts = primitives(windows_ref, w, x)
            for f, value in enumerate(flux(parts, 0)):
                scratch[f, x] = value
            flux_y, flux_z = flux(parts, 1), flux(parts, 2)
            for f in range(5):
                total = windows_ref[w, f, x]
                for j in range(layers):
                    total = total + wall[j] * flux_y[f][j : j + 1, :]
                for k in range(1, REACH + 1):
                    total = total + weight(k) * (
                        pltpu.roll(flux_z[f], cells - k, 1) - pltpu.roll(flux_z[f], k, 1)
                    )
                part_ref[w, f, x] = total
        for f in range(5):
            for x in range(planes):
                total = part_ref[w, f, x]
                for k in range(-REACH, REACH + 1):
                    if k and 0 <= x + k < planes:
                        total = total + weight(k) * scratch[f, x + k]
                part_ref[w, f, x] = total


def inner_gram_kernel(windows_ref, basis_ref, part_ref, gram_ref, kept_ref, scratch, total, sems):
    chunks = sems.shape[0]
    modes, tiles, _, cells = kept_ref.shape
    per_chunk = tiles // chunks
    wide = modes * 8
    half = wide // 2
    copies = []
    for c in range(chunks):
        span = pl.ds(c * per_chunk, per_chunk)
        copies.append(
            pltpu.make_async_copy(basis_ref.at[:, span], kept_ref.at[:, span], sems.at[c])
        )
        copies[c].start()
    inner_part(windows_ref, part_ref, scratch)
    for c in range(chunks):
        copies[c].wait()
        right = jnp.zeros((wide, half), jnp.float32) if c == 0 else total[:, half:]
        left = jnp.zeros((half, half), jnp.float32) if c == 0 else total[0:half, 0:half]
        for t in range(c * per_chunk, (c + 1) * per_chunk):
            rows = modes_of(kept_ref, t)
            right = right + lax.dot_general(
                rows, rows[half:], NT, preferred_element_type=jnp.float32
            )
            left = left + lax.dot_general(
                rows[:half], rows[:half], NT, preferred_element_type=jnp.float32
            )
        total[:, half:] = right
        total[0:half, 0:half] = left
    total[half:, 0:half] = total[0:half, half:].T
    kept = jnp.where(same_layer(total.shape), total[...], 0.0)
    rows = jnp.sum(kept.reshape(modes, 8, wide), axis=1)
    lanes = gram_ref.shape[1]
    picks = (
        lax.broadcasted_iota(jnp.int32, (wide, lanes), 0) // 8
        == lax.broadcasted_iota(jnp.int32, (wide, lanes), 1)
    ).astype(jnp.float32)
    gram_ref[...] = jnp.dot(rows, picks, precision=HIGHEST, preferred_element_type=jnp.float32)


def join_kernel(walls, paired, where_ref, part_ref, left_ref, right_ref, *rest):
    wall_refs, next_ref = rest[:walls], rest[walls]
    windows, _, planes, layers, cells = part_ref.shape
    for w in range(windows):
        for f in range(5):
            for x in range(planes):
                total = part_ref[w, f, x]
                for ref in wall_refs:
                    total = total + ref[w, f, x]
                if x < REACH:
                    total = total + left_ref[w, f, x]
                if x >= planes - REACH:
                    total = total + right_ref[w, f, x - planes + REACH]
                next_ref[w, f, x] = total
            if paired:
                half = planes // 2
                low = jnp.concatenate([next_ref[w, f, x] for x in range(half)], axis=0)
                high = jnp.concatenate([next_ref[w, f, x] for x in range(half, planes)], axis=0)
                first = where_ref[0] == 0
                rest[walls + 1][w, f] = jnp.where(first, low, high).astype(jnp.bfloat16)
                rest[walls + 2][w, f] = jnp.where(first, high, low).astype(jnp.bfloat16)


def same_layer(shape):
    rows = lax.broadcasted_iota(jnp.int32, shape, 0)
    columns = lax.broadcasted_iota(jnp.int32, shape, 1)
    return lax.rem(rows, 8) == lax.rem(columns, 8)


def modes_of(basis_ref, t):
    modes, _, layers, cells = basis_ref.shape
    return basis_ref[:, t].reshape(modes * layers, cells)


def project_kernel(paired, where_ref, *rest):
    if paired:
        own_ref, got_ref, basis_ref, sums_ref, snaps_ref, square = rest
        first = where_ref[0] == 0
        for w in range(own_ref.shape[0]):
            for f in range(own_ref.shape[1]):
                own = own_ref[w, f].astype(jnp.float32)
                got = got_ref[w, f].astype(jnp.float32)
                low = jnp.where(first, own, got)
                high = jnp.where(first, got, own)
                for t in range(4):
                    snaps_ref[4 * f + t, pl.ds(8 * w, 8)] = jnp.concatenate(
                        [low[4 * t : 4 * t + 4], high[4 * t : 4 * t + 4]], axis=0
                    ).astype(jnp.bfloat16)
    else:
        snaps_ref, basis_ref, sums_ref, square = rest
    modes, tiles = basis_ref.shape[:2]
    columns = snaps_ref.shape[1]
    total = jnp.zeros((modes * 8, columns), jnp.float32)
    small = jnp.zeros((columns, columns), jnp.float32)
    for t in range(tiles):
        snaps = snaps_ref[t]
        total = total + lax.dot_general(
            modes_of(basis_ref, t), snaps, NT, preferred_element_type=jnp.float32
        )
        small = small + lax.dot_general(snaps, snaps, NT, preferred_element_type=jnp.float32)
    kept = jnp.where(same_layer(total.shape), total, 0.0)
    square[...] = jnp.zeros_like(square)
    square[0:modes, 0:columns] = jnp.sum(kept.reshape(modes, 8, columns), axis=1)
    kept = jnp.where(same_layer(small.shape), small, 0.0)
    square[modes : modes + 1, 0:columns] = jnp.sum(kept[0:8], axis=0, keepdims=True)
    square[modes + 1 : modes + 2, 0:columns] = jnp.sum(kept[8:16], axis=0, keepdims=True)
    turned = square[...].T
    sums = jnp.concatenate(
        [
            jnp.sum(turned[0:8], axis=0, keepdims=True),
            jnp.sum(turned[8:16], axis=0, keepdims=True),
        ],
        axis=0,
    )
    for device in range(sums_ref.shape[0]):
        sums_ref[device] = sums


def inverse_kernel(gram_ref, inverse_ref):
    modes = gram_ref.shape[0]
    shape = (modes, 2 * modes)
    rows = lax.broadcasted_iota(jnp.int32, shape, 0)
    columns = lax.broadcasted_iota(jnp.int32, shape, 1)
    eye = (rows[:, :modes] == columns[:, :modes]).astype(jnp.float32)
    whole = jnp.concatenate([gram_ref[:, :modes], eye], axis=1)
    for k in range(modes):
        row = whole[k : k + 1, :] / whole[k : k + 1, k : k + 1]
        whole = jnp.where(rows == k, row, whole - whole[:, k : k + 1] * row)
    inverse_ref[...] = whole[:, modes:]


def finish_kernel(
    rows_total, sums_ref, gram_ref, inverse_ref, snaps_ref, basis_ref,
    modes_ref, solved_ref, factor_ref, made, sems,
):
    modes, tiles, _, cells = basis_ref.shape
    wide = modes * 8
    exact = functools.partial(jnp.dot, precision=HIGHEST, preferred_element_type=jnp.float32)
    sums = jnp.sum(sums_ref[...], axis=0)
    sums = jnp.concatenate([sums, jnp.zeros((6, sums.shape[1]), jnp.float32)], axis=0)
    projected = sums[:, 0:modes]
    gram, inverse = gram_ref[:, :modes], inverse_ref[...]
    solved = exact(projected, inverse)
    solved = solved + exact(projected - exact(solved, gram), inverse)
    left = projected - exact(solved, gram)

    def inner(p, i, q, j):
        return jnp.sum(p[i : i + 1] * q[j : j + 1], axis=1, keepdims=True)

    def entry(i, j):
        square = sums[i : i + 1, modes + j : modes + j + 1]
        return square - inner(projected, i, solved, j) - inner(solved, i, left, j)

    first = jnp.sqrt(entry(0, 0))
    below = entry(1, 0) / first
    second = jnp.sqrt(entry(1, 1) - below * below)
    scaling = jnp.sqrt(jnp.float32(rows_total))
    w00 = scaling / first
    w11 = scaling / second
    w01 = -(below / first) * w11
    solved_ref[...] = solved[0:2]
    factor_ref[0:1, 0:1] = first / scaling
    factor_ref[0:1, 1:2] = below / scaling
    factor_ref[1:2, 0:1] = jnp.zeros_like(first)
    factor_ref[1:2, 1:2] = second / scaling
    spread = (
        lax.broadcasted_iota(jnp.int32, (modes, wide), 1) // 8
        == lax.broadcasted_iota(jnp.int32, (modes, wide), 0)
    ).astype(jnp.float32)
    scaled = jnp.concatenate(
        [solved[0:1] * w00, solved[1:2] * w11 + solved[0:1] * w01, solved[2:8]], axis=0
    )
    lines = exact(scaled, spread)
    full = jnp.concatenate(
        [jnp.broadcast_to(lines[0:1], (8, wide)), jnp.broadcast_to(lines[1:2], (8, wide))],
        axis=0,
    )
    full = jnp.where(same_layer(full.shape), full, 0.0)
    upper = full.astype(jnp.bfloat16)
    fit = jnp.concatenate([upper, (full - upper.astype(jnp.float32)).astype(jnp.bfloat16)], axis=0)

    chunks = sems.shape[0]
    per_chunk = tiles // chunks
    copies = []
    for c in range(chunks):
        for t in range(c * per_chunk, (c + 1) * per_chunk):
            fitted = jnp.dot(fit, modes_of(basis_ref, t), preferred_element_type=jnp.float32)
            fitted = fitted[0:16] + fitted[16:32]
            snaps = snaps_ref[t].astype(jnp.float32)
            made[0, t] = snaps[0:8] * w00 - fitted[0:8]
            made[1, t] = snaps[8:16] * w11 + snaps[0:8] * w01 - fitted[8:16]
        span = pl.ds(c * per_chunk, per_chunk)
        copies.append(
            pltpu.make_async_copy(made.at[:, span], modes_ref.at[:, span], sems.at[c])
        )
        copies[c].start()
    for copy in copies:
        copy.wait()


def params(mib):
    return pltpu.CompilerParams(vmem_limit_bytes=mib * 1024 * 1024)


def cost(flops, moved):
    return pl.CostEstimate(flops=flops, bytes_accessed=moved, transcendentals=0)


WHOLE = pl.BlockSpec(memory_space=pltpu.VMEM)
FAR = pl.BlockSpec(memory_space=pltpu.HBM)
SCALAR = pl.BlockSpec(memory_space=pltpu.SMEM)


BOTH = ("solver", "analysis")


def everywhere(value):
    count = lax.axis_size("solver") * lax.axis_size("analysis")
    return lax.all_to_all(
        jnp.broadcast_to(value[None], (count,) + value.shape), BOTH, 0, 0, tiled=True
    )


def summed_rows(value):
    count = lax.axis_size("solver") * lax.axis_size("analysis")
    rows, columns = value.shape
    if rows % count:
        return jnp.sum(everywhere(value), axis=0)
    shares = lax.all_to_all(
        value.reshape(count, rows // count, columns), BOTH, 0, 0, tiled=True
    )
    return everywhere(jnp.sum(shares, axis=0)).reshape(rows, columns)


def body(windows, pod_basis):
    f32, bf16 = jnp.float32, jnp.bfloat16
    shape = jax.ShapeDtypeStruct
    count, fields, planes, layers, cells = windows.shape
    ring, walls = lax.axis_size("solver"), lax.axis_size("analysis")
    paired = walls == 2 and planes == 8 and layers == 4
    place = lax.axis_index("analysis").astype(jnp.int32).reshape(1)
    modes, _, pod_planes, pod_layers, _ = pod_basis.shape
    tiles = fields * pod_planes * (pod_layers // 8)
    basis = pod_basis.reshape(modes, tiles, 8, cells)
    wide = modes * 8
    basis_bytes = basis.size * 2

    sides = 1 if walls == 2 else 2
    kept, *faces = pl.pallas_call(
        functools.partial(face_kernel, sides == 2),
        out_shape=[shape(windows.shape, f32)]
        + [shape((count, fields, REACH, layers, cells), f32)] * 2
        + [shape(windows.shape, f32)] * sides,
        in_specs=[SCALAR, FAR],
        out_specs=[WHOLE] * (3 + sides),
        scratch_shapes=[
            pltpu.VMEM((fields, planes, layers, cells), f32),
            pltpu.SemaphoreType.DMA((count,)),
        ],
        compiler_params=params(16),
        cost_estimate=cost(10_000_000, 10 * windows.size),
        name="faces",
    )(place, windows)
    to_right = [(i, (i + 1) % ring) for i in range(ring)]
    to_left = [((i + 1) % ring, i) for i in range(ring)]
    upward = [(i, i + 1) for i in range(walls - 1)]
    downward = [(i + 1, i) for i in range(walls - 1)]
    if sides == 1:
        wall_terms = [lax.ppermute(faces[2], "analysis", upward + downward)]
    else:
        wall_terms = [
            lax.ppermute(faces[2], "analysis", upward),
            lax.ppermute(faces[3], "analysis", downward),
        ]
    from_left = lax.ppermute(faces[0], "solver", to_right)
    from_right = lax.ppermute(faces[1], "solver", to_left)

    inner, gram, basis = pl.pallas_call(
        inner_gram_kernel,
        out_shape=[shape(windows.shape, f32), shape((modes, LANES), f32), shape(basis.shape, bf16)],
        in_specs=[WHOLE, FAR],
        out_specs=[WHOLE] * 3,
        scratch_shapes=[
            pltpu.VMEM((fields, planes, layers, cells), f32),
            pltpu.VMEM((wide, wide), f32),
            pltpu.SemaphoreType.DMA((fields,)),
        ],
        compiler_params=params(40),
        cost_estimate=cost(2 * wide * wide * cells * tiles, 2 * basis_bytes),
        name="inner_gram",
    )(kept, basis)
    gram = summed_rows(gram)
    inverse = pl.pallas_call(
        inverse_kernel,
        out_shape=shape((modes, modes), f32),
        in_specs=[WHOLE],
        out_specs=WHOLE,
        compiler_params=params(16),
        cost_estimate=cost(20_000_000, 8 * modes * modes),
        name="inverse",
    )(gram)

    half_shape = (count, fields, planes * layers // 2, cells)
    joined = pl.pallas_call(
        functools.partial(join_kernel, sides, paired),
        out_shape=[shape(windows.shape, f32)] + ([shape(half_shape, bf16)] * 2 if paired else []),
        in_specs=[SCALAR] + [WHOLE] * (3 + sides),
        out_specs=[WHOLE] * (3 if paired else 1),
        compiler_params=params(16),
        cost_estimate=cost(1_000_000, 16 * windows.size),
        name="join",
    )(place, inner, from_left, from_right, *wall_terms)
    next_windows = joined[0]

    sums_shape = shape((ring * walls, 2, LANES), f32)
    snaps_shape = shape((tiles, 2 * 8, cells), bf16)
    scratch = [pltpu.VMEM((LANES, LANES), f32)]
    project_cost = cost(2 * wide * 16 * cells * tiles, basis_bytes)
    if paired:
        own, given = joined[1], joined[2]
        got = lax.ppermute(given, "analysis", [(0, 1), (1, 0)])
        sums, snaps = pl.pallas_call(
            functools.partial(project_kernel, True),
            out_shape=[sums_shape, snaps_shape],
            in_specs=[SCALAR] + [WHOLE] * 3,
            out_specs=[WHOLE] * 2,
            scratch_shapes=scratch,
            compiler_params=params(16),
            cost_estimate=project_cost,
            name="project",
        )(place, own, got, basis)
    else:
        relaid = lax.all_to_all(
            next_windows.astype(bf16), "analysis", split_axis=2, concat_axis=3, tiled=True
        )
        snaps = relaid.reshape(count, tiles, 8, cells).transpose(1, 0, 2, 3)
        snaps = snaps.reshape(tiles, count * 8, cells)
        sums = pl.pallas_call(
            functools.partial(project_kernel, False),
            out_shape=sums_shape,
            in_specs=[SCALAR] + [WHOLE] * 2,
            out_specs=WHOLE,
            scratch_shapes=scratch,
            compiler_params=params(16),
            cost_estimate=project_cost,
            name="project",
        )(place, snaps, basis)
    sums = lax.all_to_all(sums, BOTH, 0, 0, tiled=True)

    rows_total = ring * walls * tiles * 8 * cells
    new_modes, solved, factor = pl.pallas_call(
        functools.partial(finish_kernel, rows_total),
        out_shape=[
            shape((count, tiles, 8, cells), f32),
            shape((count, modes), f32),
            shape((count, count), f32),
        ],
        in_specs=[WHOLE] * 5,
        out_specs=[FAR, WHOLE, WHOLE],
        scratch_shapes=[
            pltpu.VMEM((count, tiles, 8, cells), f32),
            pltpu.SemaphoreType.DMA((fields,)),
        ],
        compiler_params=params(16),
        cost_estimate=cost(2 * wide * 32 * cells * tiles, basis_bytes + 8 * windows.size),
        name="finish",
    )(sums, gram, inverse, snaps, basis)
    new_modes = new_modes.reshape(count, fields, pod_planes, pod_layers, cells)
    return next_windows, solved, new_modes, factor


def solution(mesh):
    in_specs = (
        P(None, None, "solver", "analysis", None),
        P(None, None, ("solver", "analysis"), None, None),
    )
    out_specs = (
        P(None, None, "solver", "analysis", None),
        P(),
        P(None, None, ("solver", "analysis"), None, None),
        P(),
    )
    return jax.shard_map(body, mesh=mesh, in_specs=in_specs, out_specs=out_specs, check_vma=False)
```

```python
import functools

import jax
import jax.numpy as jnp
from jax import lax
from jax.experimental import pallas as pl
from jax.experimental.pallas import tpu as pltpu
from jax.sharding import PartitionSpec as P

PRESSURE_FACTOR = 1.4 - 1.0
SECTION_STEP = 0.25
CENTRAL_WEIGHTS = (0.8, -0.2, 4.0 / 105.0, -1.0 / 280.0)
REACH = 4
LANES = 128
HIGHEST = lax.Precision.HIGHEST
NT = (((1,), (1,)), ((), ()))


def weight(k):
    if k == 0 or abs(k) > REACH:
        return 0.0
    value = -SECTION_STEP * CENTRAL_WEIGHTS[abs(k) - 1]
    return value if k > 0 else -value


def row_weights(shape, values):
    rows = lax.broadcasted_iota(jnp.int32, shape, len(shape) - 2)
    made = jnp.full(shape, values[0], jnp.float32)
    for i, value in enumerate(values[1:], start=1):
        made = jnp.where(rows == i, jnp.float32(value), made)
    return made


def primitives(windows_ref, w, x):
    density, mx, my, mz, energy = (windows_ref[w, f, x] for f in range(5))
    inverse = 1.0 / density
    ux, uy, uz = mx * inverse, my * inverse, mz * inverse
    pressure = PRESSURE_FACTOR * (energy - 0.5 * (mx * ux + my * uy + mz * uz))
    return (mx, my, mz), (ux, uy, uz), pressure, energy + pressure


def flux(parts, direction):
    moments, speeds, pressure, enthalpy = parts
    speed = speeds[direction]
    made = [moments[direction]]
    for axis in range(3):
        term = moments[axis] * speed
        made.append(term + pressure if axis == direction else term)
    made.append(enthalpy * speed)
    return made


def face_kernel(two_sided, where_ref, source_ref, windows_ref, left_ref, right_ref, *rest):
    windows, _, planes, layers, cells = windows_ref.shape
    wall_refs, scratch, sems = rest[:-2], rest[-2], rest[-1]
    copies = [
        pltpu.make_async_copy(source_ref.at[w], windows_ref.at[w], sems.at[w])
        for w in range(windows)
    ]
    for copy in copies:
        copy.start()
    tile = (layers, cells)
    up = [
        row_weights(tile, [weight(j - layers - i) for i in range(layers)]) for j in range(layers)
    ]
    down = [
        row_weights(tile, [weight(layers + j - i) for i in range(layers)]) for j in range(layers)
    ]
    if two_sided:
        tables = (up, down)
    else:
        first = where_ref[0] == 0
        tables = ([jnp.where(first, u, d) for u, d in zip(up, down)],)
    for w in range(windows):
        copies[w].wait()
        for x in range(planes):
            parts = primitives(windows_ref, w, x)
            for f, value in enumerate(flux(parts, 0)):
                scratch[f, x] = value
            for f, value in enumerate(flux(parts, 1)):
                for ref, table in zip(wall_refs, tables):
                    total = None
                    for j in range(layers):
                        term = table[j] * value[j : j + 1, :]
                        total = term if total is None else total + term
                    ref[w, f, x] = total
        for f in range(5):
            for i in range(REACH):
                total = None
                for j in range(planes):
                    c = weight(j - planes - i)
                    if c:
                        term = c * scratch[f, j]
                        total = term if total is None else total + term
                left_ref[w, f, i] = total
                total = None
                for j in range(planes):
                    c = weight(j + REACH - i)
                    if c:
                        term = c * scratch[f, j]
                        total = term if total is None else total + term
                right_ref[w, f, i] = total


def inner_part(windows_ref, part_ref, scratch):
    windows, _, planes, layers, cells = windows_ref.shape
    tile = (layers, cells)
    wall = [
        row_weights(tile, [weight(j - i) for i in range(layers)]) for j in range(layers)
    ]
    for w in range(windows):
        for x in range(planes):
            parts = primitives(windows_ref, w, x)
            for f, value in enumerate(flux(parts, 0)):
                scratch[f, x] = value
            flux_y, flux_z = flux(parts, 1), flux(parts, 2)
            for f in range(5):
                total = windows_ref[w, f, x]
                for j in range(layers):
                    total = total + wall[j] * flux_y[f][j : j + 1, :]
                for k in range(1, REACH + 1):
                    total = total + weight(k) * (
                        pltpu.roll(flux_z[f], cells - k, 1) - pltpu.roll(flux_z[f], k, 1)
                    )
                part_ref[w, f, x] = total
        for f in range(5):
            for x in range(planes):
                total = part_ref[w, f, x]
                for k in range(-REACH, REACH + 1):
                    if k and 0 <= x + k < planes:
                        total = total + weight(k) * scratch[f, x + k]
                part_ref[w, f, x] = total


def inner_gram_kernel(windows_ref, basis_ref, part_ref, gram_ref, kept_ref, scratch, total, sems):
    chunks = sems.shape[0]
    modes, tiles, _, cells = kept_ref.shape
    per_chunk = tiles // chunks
    wide = modes * 8
    half = wide // 2
    copies = []
    for c in range(chunks):
        span = pl.ds(c * per_chunk, per_chunk)
        copies.append(
            pltpu.make_async_copy(basis_ref.at[:, span], kept_ref.at[:, span], sems.at[c])
        )
        copies[c].start()
    inner_part(windows_ref, part_ref, scratch)
    right = jnp.zeros((wide, half), jnp.float32)
    left = jnp.zeros((half, half), jnp.float32)
    for c in range(chunks):
        copies[c].wait()
        rows = jnp.concatenate(
            [modes_of(kept_ref, t) for t in range(c * per_chunk, (c + 1) * per_chunk)], axis=1
        )
        right = right + lax.dot_general(
            rows, rows[half:], NT, preferred_element_type=jnp.float32
        )
        left = left + lax.dot_general(
            rows[:half], rows[:half], NT, preferred_element_type=jnp.float32
        )
    tiles_left = half // LANES
    turned = right[0:half].T
    for tile in range(tiles_left):
        span = slice(tile * LANES, (tile + 1) * LANES)
        total[tile, 0:half] = left[:, span]
        total[tile, half:] = turned[:, span]
        total[tiles_left + tile] = right[:, span]
    rows = folded(total, modes)
    lanes = gram_ref.shape[1]
    picks = (
        lax.broadcasted_iota(jnp.int32, (wide, lanes), 0) // 8
        == lax.broadcasted_iota(jnp.int32, (wide, lanes), 1)
    ).astype(jnp.float32)
    gram_ref[...] = jnp.dot(rows, picks, precision=HIGHEST, preferred_element_type=jnp.float32)


def join_kernel(walls, paired, where_ref, part_ref, left_ref, right_ref, *rest):
    wall_refs, next_ref = rest[:walls], rest[walls]
    windows, _, planes, layers, cells = part_ref.shape
    for w in range(windows):
        for f in range(5):
            for x in range(planes):
                total = part_ref[w, f, x]
                for ref in wall_refs:
                    total = total + ref[w, f, x]
                if x < REACH:
                    total = total + left_ref[w, f, x]
                if x >= planes - REACH:
                    total = total + right_ref[w, f, x - planes + REACH]
                next_ref[w, f, x] = total
            if paired:
                half = planes // 2
                low = jnp.concatenate([next_ref[w, f, x] for x in range(half)], axis=0)
                high = jnp.concatenate([next_ref[w, f, x] for x in range(half, planes)], axis=0)
                first = where_ref[0] == 0
                rest[walls + 1][w, f] = jnp.where(first, low, high).astype(jnp.bfloat16)
                rest[walls + 2][w, f] = jnp.where(first, high, low).astype(jnp.bfloat16)


def same_layer(shape):
    rows = lax.broadcasted_iota(jnp.int32, shape, 0)
    columns = lax.broadcasted_iota(jnp.int32, shape, 1)
    return lax.rem(rows, 8) == lax.rem(columns, 8)


def folded(total, modes):
    kept = lax.rem(lax.broadcasted_iota(jnp.int32, (modes, LANES), 1), 8)
    made = []
    for tile in range(total.shape[0]):
        rows = jnp.zeros((modes, LANES), jnp.float32)
        for y in range(8):
            rows = jnp.where(kept == y, total[tile, pl.ds(y, modes, 8), :], rows)
        made.append(rows)
    return made[0] if len(made) == 1 else jnp.concatenate(made, axis=1)


def modes_of(basis_ref, t):
    modes, _, layers, cells = basis_ref.shape
    return basis_ref[:, t].reshape(modes * layers, cells)


def project_kernel(paired, where_ref, *rest):
    if paired:
        own_ref, got_ref, basis_ref, sums_ref, snaps_ref, square, wide_sums = rest
        first = where_ref[0] == 0
        for w in range(own_ref.shape[0]):
            for f in range(own_ref.shape[1]):
                own = own_ref[w, f].astype(jnp.float32)
                got = got_ref[w, f].astype(jnp.float32)
                low = jnp.where(first, own, got)
                high = jnp.where(first, got, own)
                for t in range(4):
                    snaps_ref[4 * f + t, pl.ds(8 * w, 8)] = jnp.concatenate(
                        [low[4 * t : 4 * t + 4], high[4 * t : 4 * t + 4]], axis=0
                    ).astype(jnp.bfloat16)
    else:
        snaps_ref, basis_ref, sums_ref, square, wide_sums = rest
    modes, tiles = basis_ref.shape[:2]
    columns = snaps_ref.shape[1]
    total = jnp.zeros((modes * 8, columns), jnp.float32)
    small = jnp.zeros((columns, columns), jnp.float32)
    for t in range(tiles):
        snaps = snaps_ref[t]
        total = total + lax.dot_general(
            modes_of(basis_ref, t), snaps, NT, preferred_element_type=jnp.float32
        )
        small = small + lax.dot_general(snaps, snaps, NT, preferred_element_type=jnp.float32)
    wide_sums[0, :, 0:columns] = total
    square[...] = jnp.zeros_like(square)
    square[0:modes, :] = folded(wide_sums, modes)
    kept = jnp.where(same_layer(small.shape), small, 0.0)
    square[modes : modes + 1, 0:columns] = jnp.sum(kept[0:8], axis=0, keepdims=True)
    square[modes + 1 : modes + 2, 0:columns] = jnp.sum(kept[8:16], axis=0, keepdims=True)
    lanes = lax.broadcasted_iota(jnp.int32, square.shape, 1)
    turned = jnp.where(lanes < columns, square[...], 0.0).T
    sums = jnp.concatenate(
        [
            jnp.sum(turned[0:8], axis=0, keepdims=True),
            jnp.sum(turned[8:16], axis=0, keepdims=True),
        ],
        axis=0,
    )
    sums_ref[...] = jnp.concatenate([sums, jnp.zeros((6, sums.shape[1]), jnp.float32)], axis=0)


def eliminate(whole, start, stop):
    rows = lax.broadcasted_iota(jnp.int32, whole.shape, 0)
    for k in range(start, stop, 2):
        first, second = whole[k : k + 1, :], whole[k + 1 : k + 2, :]
        a, b = first[:, k : k + 1], first[:, k + 1 : k + 2]
        c, d = second[:, k : k + 1], second[:, k + 1 : k + 2]
        inverse = 1.0 / (a * d - b * c)
        upper = (d * first - b * second) * inverse
        lower = (a * second - c * first) * inverse
        rest = whole - whole[:, k : k + 1] * upper - whole[:, k + 1 : k + 2] * lower
        whole = jnp.where(rows == k, upper, jnp.where(rows == k + 1, lower, rest))
    return whole


def half_inverse_kernel(gram_ref, half_ref):
    modes = gram_ref.shape[0]
    rows = lax.broadcasted_iota(jnp.int32, (modes, modes), 0)
    columns = lax.broadcasted_iota(jnp.int32, (modes, modes), 1)
    eye = (rows == columns).astype(jnp.float32)
    whole = jnp.concatenate([gram_ref[:, :modes], eye], axis=1)
    half_ref[...] = eliminate(whole, 0, modes // 2)


def inverse_kernel(half_ref, inverse_ref):
    modes = half_ref.shape[0]
    inverse_ref[...] = eliminate(half_ref[...], modes // 2, modes)[:, modes:]


def finish_kernel(
    rows_total, sums_ref, gram_ref, inverse_ref, snaps_ref, basis_ref,
    modes_ref, solved_ref, factor_ref, made, sems,
):
    modes, tiles, _, cells = basis_ref.shape
    wide = modes * 8
    exact = functools.partial(jnp.dot, precision=HIGHEST, preferred_element_type=jnp.float32)
    sums = sums_ref[...]
    projected = sums[:, 0:modes]
    gram, inverse = gram_ref[:, :modes], inverse_ref[...]
    solved = exact(projected, inverse)
    solved = solved + exact(projected - exact(solved, gram), inverse)
    left = projected - exact(solved, gram)

    def inner(p, i, q, j):
        return jnp.sum(p[i : i + 1] * q[j : j + 1], axis=1, keepdims=True)

    def entry(i, j):
        square = sums[i : i + 1, modes + j : modes + j + 1]
        return square - inner(projected, i, solved, j) - inner(solved, i, left, j)

    first = jnp.sqrt(entry(0, 0))
    below = entry(1, 0) / first
    second = jnp.sqrt(entry(1, 1) - below * below)
    scaling = jnp.sqrt(jnp.float32(rows_total))
    w00 = scaling / first
    w11 = scaling / second
    w01 = -(below / first) * w11
    solved_ref[...] = solved[0:2]
    factor_ref[0:1, 0:1] = first / scaling
    factor_ref[0:1, 1:2] = below / scaling
    factor_ref[1:2, 0:1] = jnp.zeros_like(first)
    factor_ref[1:2, 1:2] = second / scaling
    spread = (
        lax.broadcasted_iota(jnp.int32, (modes, wide), 1) // 8
        == lax.broadcasted_iota(jnp.int32, (modes, wide), 0)
    ).astype(jnp.float32)
    scaled = jnp.concatenate(
        [solved[0:1] * w00, solved[1:2] * w11 + solved[0:1] * w01, solved[2:8]], axis=0
    )
    lines = exact(scaled, spread)
    full = jnp.concatenate(
        [jnp.broadcast_to(lines[0:1], (8, wide)), jnp.broadcast_to(lines[1:2], (8, wide))],
        axis=0,
    )
    full = jnp.where(same_layer(full.shape), full, 0.0)
    upper = full.astype(jnp.bfloat16)
    fit = jnp.concatenate([upper, (full - upper.astype(jnp.float32)).astype(jnp.bfloat16)], axis=0)

    chunks = sems.shape[0]
    per_chunk = tiles // chunks
    copies = []
    for c in range(chunks):
        for t in range(c * per_chunk, (c + 1) * per_chunk):
            fitted = jnp.dot(fit, modes_of(basis_ref, t), preferred_element_type=jnp.float32)
            fitted = fitted[0:16] + fitted[16:32]
            snaps = snaps_ref[t].astype(jnp.float32)
            made[0, t] = snaps[0:8] * w00 - fitted[0:8]
            made[1, t] = snaps[8:16] * w11 + snaps[0:8] * w01 - fitted[8:16]
        span = pl.ds(c * per_chunk, per_chunk)
        copies.append(
            pltpu.make_async_copy(made.at[:, span], modes_ref.at[:, span], sems.at[c])
        )
        copies[c].start()
    for copy in copies:
        copy.wait()


def params(mib):
    return pltpu.CompilerParams(vmem_limit_bytes=mib * 1024 * 1024)


def cost(flops, moved):
    return pl.CostEstimate(flops=flops, bytes_accessed=moved, transcendentals=0)


WHOLE = pl.BlockSpec(memory_space=pltpu.VMEM)
AXES = ("analysis", "solver")
FAR = pl.BlockSpec(memory_space=pltpu.HBM)
SCALAR = pl.BlockSpec(memory_space=pltpu.SMEM)


def summed(value, axes):
    for axis in axes:
        count = lax.axis_size(axis)
        if count & (count - 1):
            value = lax.psum(value, axis)
            continue
        bit = 1
        while bit < count:
            value = value + lax.ppermute(value, axis, [(i, i ^ bit) for i in range(count)])
            bit *= 2
    return value


def body(windows, pod_basis):
    f32, bf16 = jnp.float32, jnp.bfloat16
    shape = jax.ShapeDtypeStruct
    count, fields, planes, layers, cells = windows.shape
    ring, walls = lax.axis_size("solver"), lax.axis_size("analysis")
    paired = walls == 2 and planes == 8 and layers == 4
    place = lax.axis_index("analysis").astype(jnp.int32).reshape(1)
    modes, _, pod_planes, pod_layers, _ = pod_basis.shape
    tiles = fields * pod_planes * (pod_layers // 8)
    basis = pod_basis.reshape(modes, tiles, 8, cells)
    wide = modes * 8
    basis_bytes = basis.size * 2

    sides = 1 if walls == 2 else 2
    kept, *faces = pl.pallas_call(
        functools.partial(face_kernel, sides == 2),
        out_shape=[shape(windows.shape, f32)]
        + [shape((count, fields, REACH, layers, cells), f32)] * 2
        + [shape(windows.shape, f32)] * sides,
        in_specs=[SCALAR, FAR],
        out_specs=[WHOLE] * (3 + sides),
        scratch_shapes=[
            pltpu.VMEM((fields, planes, layers, cells), f32),
            pltpu.SemaphoreType.DMA((count,)),
        ],
        compiler_params=params(16),
        cost_estimate=cost(10_000_000, 10 * windows.size),
        name="faces",
    )(place, windows)
    to_right = [(i, (i + 1) % ring) for i in range(ring)]
    to_left = [((i + 1) % ring, i) for i in range(ring)]
    upward = [(i, i + 1) for i in range(walls - 1)]
    downward = [(i + 1, i) for i in range(walls - 1)]
    if sides == 1:
        wall_terms = [lax.ppermute(faces[2], "analysis", upward + downward)]
    else:
        wall_terms = [
            lax.ppermute(faces[2], "analysis", upward),
            lax.ppermute(faces[3], "analysis", downward),
        ]
    from_left = lax.ppermute(faces[0], "solver", to_right)
    from_right = lax.ppermute(faces[1], "solver", to_left)

    inner, gram, basis = pl.pallas_call(
        inner_gram_kernel,
        out_shape=[shape(windows.shape, f32), shape((modes, LANES), f32), shape(basis.shape, bf16)],
        in_specs=[WHOLE, FAR],
        out_specs=[WHOLE] * 3,
        scratch_shapes=[
            pltpu.VMEM((fields, planes, layers, cells), f32),
            pltpu.VMEM((wide // LANES, wide, LANES), f32),
            pltpu.SemaphoreType.DMA((fields,)),
        ],
        compiler_params=params(40),
        cost_estimate=cost(2 * wide * wide * cells * tiles, 2 * basis_bytes),
        name="inner_gram",
    )(kept, basis)
    gram = summed(gram, AXES)
    half_inverse = pl.pallas_call(
        half_inverse_kernel,
        out_shape=shape((modes, 2 * modes), f32),
        in_specs=[WHOLE],
        out_specs=WHOLE,
        compiler_params=params(16),
        cost_estimate=cost(10_000_000, 8 * modes * modes),
        name="half_inverse",
    )(gram)
    inverse = pl.pallas_call(
        inverse_kernel,
        out_shape=shape((modes, modes), f32),
        in_specs=[WHOLE],
        out_specs=WHOLE,
        compiler_params=params(16),
        cost_estimate=cost(10_000_000, 8 * modes * modes),
        name="inverse",
    )(half_inverse)

    half_shape = (count, fields, planes * layers // 2, cells)
    joined = pl.pallas_call(
        functools.partial(join_kernel, sides, paired),
        out_shape=[shape(windows.shape, f32)] + ([shape(half_shape, bf16)] * 2 if paired else []),
        in_specs=[SCALAR] + [WHOLE] * (3 + sides),
        out_specs=[WHOLE] * (3 if paired else 1),
        compiler_params=params(16),
        cost_estimate=cost(1_000_000, 16 * windows.size),
        name="join",
    )(place, inner, from_left, from_right, *wall_terms)
    next_windows = joined[0]

    sums_shape = shape((8, LANES), f32)
    snaps_shape = shape((tiles, 2 * 8, cells), bf16)
    scratch = [pltpu.VMEM((LANES, LANES), f32), pltpu.VMEM((1, wide, LANES), f32)]
    project_cost = cost(2 * wide * 16 * cells * tiles, basis_bytes)
    if paired:
        own, given = joined[1], joined[2]
        got = lax.ppermute(given, "analysis", [(0, 1), (1, 0)])
        sums, snaps = pl.pallas_call(
            functools.partial(project_kernel, True),
            out_shape=[sums_shape, snaps_shape],
            in_specs=[SCALAR] + [WHOLE] * 3,
            out_specs=[WHOLE] * 2,
            scratch_shapes=scratch,
            compiler_params=params(16),
            cost_estimate=project_cost,
            name="project",
        )(place, own, got, basis)
    else:
        relaid = lax.all_to_all(
            next_windows.astype(bf16), "analysis", split_axis=2, concat_axis=3, tiled=True
        )
        snaps = relaid.reshape(count, tiles, 8, cells).transpose(1, 0, 2, 3)
        snaps = snaps.reshape(tiles, count * 8, cells)
        sums = pl.pallas_call(
            functools.partial(project_kernel, False),
            out_shape=sums_shape,
            in_specs=[SCALAR] + [WHOLE] * 2,
            out_specs=WHOLE,
            scratch_shapes=scratch,
            compiler_params=params(16),
            cost_estimate=project_cost,
            name="project",
        )(place, snaps, basis)
    sums = summed(sums, AXES)

    rows_total = ring * walls * tiles * 8 * cells
    new_modes, solved, factor = pl.pallas_call(
        functools.partial(finish_kernel, rows_total),
        out_shape=[
            shape((count, tiles, 8, cells), f32),
            shape((count, modes), f32),
            shape((count, count), f32),
        ],
        in_specs=[WHOLE] * 5,
        out_specs=[FAR, WHOLE, WHOLE],
        scratch_shapes=[
            pltpu.VMEM((count, tiles, 8, cells), f32),
            pltpu.SemaphoreType.DMA((fields,)),
        ],
        compiler_params=params(16),
        cost_estimate=cost(2 * wide * 32 * cells * tiles, basis_bytes + 8 * windows.size),
        name="finish",
    )(sums, gram, inverse, snaps, basis)
    new_modes = new_modes.reshape(count, fields, pod_planes, pod_layers, cells)
    return next_windows, solved, new_modes, factor


def solution(mesh):
    in_specs = (
        P(None, None, "solver", "analysis", None),
        P(None, None, ("solver", "analysis"), None, None),
    )
    out_specs = (
        P(None, None, "solver", "analysis", None),
        P(),
        P(None, None, ("solver", "analysis"), None, None),
        P(),
    )
    return jax.shard_map(body, mesh=mesh, in_specs=in_specs, out_specs=out_specs, check_vma=False)
```

```python
import functools

import jax
import jax.numpy as jnp
from jax import lax
from jax.experimental import pallas as pl
from jax.experimental.pallas import tpu as pltpu
from jax.sharding import PartitionSpec as P

PRESSURE_FACTOR = 1.4 - 1.0
SECTION_STEP = 0.25
CENTRAL_WEIGHTS = (0.8, -0.2, 4.0 / 105.0, -1.0 / 280.0)
REACH = 4
LANES = 128
HIGHEST = lax.Precision.HIGHEST
NT = (((1,), (1,)), ((), ()))


def weight(k):
    if k == 0 or abs(k) > REACH:
        return 0.0
    value = -SECTION_STEP * CENTRAL_WEIGHTS[abs(k) - 1]
    return value if k > 0 else -value


def row_weights(shape, values):
    rows = lax.broadcasted_iota(jnp.int32, shape, len(shape) - 2)
    made = jnp.full(shape, values[0], jnp.float32)
    for i, value in enumerate(values[1:], start=1):
        made = jnp.where(rows == i, jnp.float32(value), made)
    return made


def primitives(windows_ref, w, x):
    density, mx, my, mz, energy = (windows_ref[w, f, x] for f in range(5))
    inverse = 1.0 / density
    ux, uy, uz = mx * inverse, my * inverse, mz * inverse
    pressure = PRESSURE_FACTOR * (energy - 0.5 * (mx * ux + my * uy + mz * uz))
    return (mx, my, mz), (ux, uy, uz), pressure, energy + pressure


def flux(parts, direction):
    moments, speeds, pressure, enthalpy = parts
    speed = speeds[direction]
    made = [moments[direction]]
    for axis in range(3):
        term = moments[axis] * speed
        made.append(term + pressure if axis == direction else term)
    made.append(enthalpy * speed)
    return made


def face_kernel(two_sided, where_ref, source_ref, windows_ref, left_ref, right_ref, *rest):
    windows, _, planes, layers, cells = windows_ref.shape
    wall_refs, scratch, sems = rest[:-2], rest[-2], rest[-1]
    copies = [
        pltpu.make_async_copy(source_ref.at[w], windows_ref.at[w], sems.at[w])
        for w in range(windows)
    ]
    for copy in copies:
        copy.start()
    tile = (layers, cells)
    up = [
        row_weights(tile, [weight(j - layers - i) for i in range(layers)]) for j in range(layers)
    ]
    down = [
        row_weights(tile, [weight(layers + j - i) for i in range(layers)]) for j in range(layers)
    ]
    if two_sided:
        tables = (up, down)
    else:
        first = where_ref[0] == 0
        tables = ([jnp.where(first, u, d) for u, d in zip(up, down)],)
    for w in range(windows):
        copies[w].wait()
        for x in range(planes):
            parts = primitives(windows_ref, w, x)
            for f, value in enumerate(flux(parts, 0)):
                scratch[f, x] = value
            for f, value in enumerate(flux(parts, 1)):
                for ref, table in zip(wall_refs, tables):
                    total = None
                    for j in range(layers):
                        term = table[j] * value[j : j + 1, :]
                        total = term if total is None else total + term
                    ref[w, f, x] = total
        for f in range(5):
            for i in range(REACH):
                total = None
                for j in range(planes):
                    c = weight(j - planes - i)
                    if c:
                        term = c * scratch[f, j]
                        total = term if total is None else total + term
                left_ref[w, f, i] = total
                total = None
                for j in range(planes):
                    c = weight(j + REACH - i)
                    if c:
                        term = c * scratch[f, j]
                        total = term if total is None else total + term
                right_ref[w, f, i] = total


def inner_part(windows_ref, part_ref, scratch):
    windows, _, planes, layers, cells = windows_ref.shape
    tile = (layers, cells)
    wall = [
        row_weights(tile, [weight(j - i) for i in range(layers)]) for j in range(layers)
    ]
    for w in range(windows):
        for x in range(planes):
            parts = primitives(windows_ref, w, x)
            for f, value in enumerate(flux(parts, 0)):
                scratch[f, x] = value
            flux_y, flux_z = flux(parts, 1), flux(parts, 2)
            for f in range(5):
                total = windows_ref[w, f, x]
                for j in range(layers):
                    total = total + wall[j] * flux_y[f][j : j + 1, :]
                for k in range(1, REACH + 1):
                    total = total + weight(k) * (
                        pltpu.roll(flux_z[f], cells - k, 1) - pltpu.roll(flux_z[f], k, 1)
                    )
                part_ref[w, f, x] = total
        for f in range(5):
            for x in range(planes):
                total = part_ref[w, f, x]
                for k in range(-REACH, REACH + 1):
                    if k and 0 <= x + k < planes:
                        total = total + weight(k) * scratch[f, x + k]
                part_ref[w, f, x] = total


def inner_gram_kernel(windows_ref, basis_ref, part_ref, gram_ref, kept_ref, scratch, total, sems):
    chunks = sems.shape[0]
    modes, tiles, _, cells = kept_ref.shape
    per_chunk = tiles // chunks
    wide = modes * 8
    half = wide // 2
    copies = []
    for c in range(chunks):
        span = pl.ds(c * per_chunk, per_chunk)
        copies.append(
            pltpu.make_async_copy(basis_ref.at[:, span], kept_ref.at[:, span], sems.at[c])
        )
        copies[c].start()
    inner_part(windows_ref, part_ref, scratch)
    right = jnp.zeros((wide, half), jnp.float32)
    left = jnp.zeros((half, half), jnp.float32)
    for c in range(chunks):
        copies[c].wait()
        rows = jnp.concatenate(
            [modes_of(kept_ref, t) for t in range(c * per_chunk, (c + 1) * per_chunk)], axis=1
        )
        right = right + lax.dot_general(
            rows, rows[half:], NT, preferred_element_type=jnp.float32
        )
        left = left + lax.dot_general(
            rows[:half], rows[:half], NT, preferred_element_type=jnp.float32
        )
    tiles_left = half // LANES
    turned = right[0:half].T
    for tile in range(tiles_left):
        span = slice(tile * LANES, (tile + 1) * LANES)
        total[tile, 0:half] = left[:, span]
        total[tile, half:] = turned[:, span]
        total[tiles_left + tile] = right[:, span]
    rows = folded(total, modes)
    lanes = gram_ref.shape[1]
    picks = (
        lax.broadcasted_iota(jnp.int32, (wide, lanes), 0) // 8
        == lax.broadcasted_iota(jnp.int32, (wide, lanes), 1)
    ).astype(jnp.float32)
    gram_ref[...] = jnp.dot(rows, picks, precision=HIGHEST, preferred_element_type=jnp.float32)


def join_kernel(walls, paired, where_ref, part_ref, left_ref, right_ref, *rest):
    wall_refs, next_ref = rest[:walls], rest[walls]
    windows, _, planes, layers, cells = part_ref.shape
    for w in range(windows):
        for f in range(5):
            for x in range(planes):
                total = part_ref[w, f, x]
                for ref in wall_refs:
                    total = total + ref[w, f, x]
                if x < REACH:
                    total = total + left_ref[w, f, x]
                if x >= planes - REACH:
                    total = total + right_ref[w, f, x - planes + REACH]
                next_ref[w, f, x] = total
            if paired:
                half = planes // 2
                low = jnp.concatenate([next_ref[w, f, x] for x in range(half)], axis=0)
                high = jnp.concatenate([next_ref[w, f, x] for x in range(half, planes)], axis=0)
                first = where_ref[0] == 0
                rest[walls + 1][w, f] = jnp.where(first, low, high).astype(jnp.bfloat16)
                rest[walls + 2][w, f] = jnp.where(first, high, low).astype(jnp.bfloat16)


def same_layer(shape):
    rows = lax.broadcasted_iota(jnp.int32, shape, 0)
    columns = lax.broadcasted_iota(jnp.int32, shape, 1)
    return lax.rem(rows, 8) == lax.rem(columns, 8)


def folded(total, modes):
    kept = lax.rem(lax.broadcasted_iota(jnp.int32, (modes, LANES), 1), 8)
    made = []
    for tile in range(total.shape[0]):
        rows = jnp.zeros((modes, LANES), jnp.float32)
        for y in range(8):
            rows = jnp.where(kept == y, total[tile, pl.ds(y, modes, 8), :], rows)
        made.append(rows)
    return made[0] if len(made) == 1 else jnp.concatenate(made, axis=1)


def modes_of(basis_ref, t):
    modes, _, layers, cells = basis_ref.shape
    return basis_ref[:, t].reshape(modes * layers, cells)


def project_kernel(paired, where_ref, gram_ref, far_ref, *rest):
    if paired:
        own_ref, got_ref, basis_ref, sums_ref, snaps_ref, square, wide_sums = rest
        first = where_ref[0] == 0
        for w in range(own_ref.shape[0]):
            for f in range(own_ref.shape[1]):
                own = own_ref[w, f].astype(jnp.float32)
                got = got_ref[w, f].astype(jnp.float32)
                low = jnp.where(first, own, got)
                high = jnp.where(first, got, own)
                for t in range(4):
                    snaps_ref[4 * f + t, pl.ds(8 * w, 8)] = jnp.concatenate(
                        [low[4 * t : 4 * t + 4], high[4 * t : 4 * t + 4]], axis=0
                    ).astype(jnp.bfloat16)
    else:
        snaps_ref, basis_ref, sums_ref, square, wide_sums = rest
    modes, tiles = basis_ref.shape[:2]
    columns = snaps_ref.shape[1]
    total = jnp.zeros((modes * 8, columns), jnp.float32)
    small = jnp.zeros((columns, columns), jnp.float32)
    for t in range(tiles):
        snaps = snaps_ref[t]
        total = total + lax.dot_general(
            modes_of(basis_ref, t), snaps, NT, preferred_element_type=jnp.float32
        )
        small = small + lax.dot_general(snaps, snaps, NT, preferred_element_type=jnp.float32)
    wide_sums[0, :, 0:columns] = total
    square[...] = jnp.zeros_like(square)
    square[0:modes, :] = folded(wide_sums, modes)
    kept = jnp.where(same_layer(small.shape), small, 0.0)
    square[modes : modes + 1, 0:columns] = jnp.sum(kept[0:8], axis=0, keepdims=True)
    square[modes + 1 : modes + 2, 0:columns] = jnp.sum(kept[8:16], axis=0, keepdims=True)
    lanes = lax.broadcasted_iota(jnp.int32, square.shape, 1)
    turned = jnp.where(lanes < columns, square[...], 0.0).T
    sums = jnp.concatenate(
        [
            jnp.sum(turned[0:8], axis=0, keepdims=True),
            jnp.sum(turned[8:16], axis=0, keepdims=True),
        ],
        axis=0,
    )
    sums_ref[0:modes] = gram_ref[...] + far_ref[...]
    sums_ref[modes : modes + 8] = jnp.concatenate(
        [sums, jnp.zeros((6, sums.shape[1]), jnp.float32)], axis=0
    )


def inverse_kernel(sums_ref, inverse_ref, plain, scaled):
    modes = inverse_ref.shape[0]
    rows = lax.broadcasted_iota(jnp.int32, (8, 2 * modes), 0)
    lanes = lax.broadcasted_iota(jnp.int32, (8, 2 * modes), 1)
    tiles = []
    for tile in range(modes // 8):
        eye = (lanes == rows + (modes + 8 * tile)).astype(jnp.float32)
        tiles.append(jnp.where(lanes < modes, sums_ref[8 * tile : 8 * tile + 8, :], eye))
    for k in range(modes):
        home, line = divmod(k, 8)
        row = tiles[home][line : line + 1, :]
        ready = row / row[:, k : k + 1]
        plain[k : k + 1, :] = row
        scaled[k : k + 1, :] = ready
        for tile in range(home, modes // 8):
            column = tiles[tile][:, k : k + 1]
            if tile == home:
                column = jnp.where(rows[:, 0:1] > line, column, 0.0)
            tiles[tile] = tiles[tile] - column * ready
    inverse_ref[...] = lax.dot_general(
        plain[:, modes:], scaled[:, modes:], (((0,), (0,)), ((), ())),
        precision=HIGHEST, preferred_element_type=jnp.float32,
    )


def finish_kernel(
    rows_total, projected_ref, sums_ref, inverse_ref, snaps_ref, basis_ref,
    modes_ref, solved_ref, factor_ref, made, sems,
):
    modes, tiles, _, cells = basis_ref.shape
    wide = modes * 8
    exact = functools.partial(jnp.dot, precision=HIGHEST, preferred_element_type=jnp.float32)
    projected = projected_ref[modes : modes + 8, 0:modes]
    gram, inverse = sums_ref[0:modes, 0:modes], inverse_ref[...]
    solved = exact(projected, inverse)
    solved = solved + exact(projected - exact(solved, gram), inverse)
    left = projected - exact(solved, gram)

    def inner(p, i, q, j):
        return jnp.sum(p[i : i + 1] * q[j : j + 1], axis=1, keepdims=True)

    def entry(i, j):
        square = projected_ref[modes + i : modes + i + 1, modes + j : modes + j + 1]
        return square - inner(projected, i, solved, j) - inner(solved, i, left, j)

    first = jnp.sqrt(entry(0, 0))
    below = entry(1, 0) / first
    second = jnp.sqrt(entry(1, 1) - below * below)
    scaling = jnp.sqrt(jnp.float32(rows_total))
    w00 = scaling / first
    w11 = scaling / second
    w01 = -(below / first) * w11
    solved_ref[...] = solved[0:2]
    factor_ref[0:1, 0:1] = first / scaling
    factor_ref[0:1, 1:2] = below / scaling
    factor_ref[1:2, 0:1] = jnp.zeros_like(first)
    factor_ref[1:2, 1:2] = second / scaling
    spread = (
        lax.broadcasted_iota(jnp.int32, (modes, wide), 1) // 8
        == lax.broadcasted_iota(jnp.int32, (modes, wide), 0)
    ).astype(jnp.float32)
    scaled = jnp.concatenate(
        [solved[0:1] * w00, solved[1:2] * w11 + solved[0:1] * w01, solved[2:8]], axis=0
    )
    lines = exact(scaled, spread)
    full = jnp.concatenate(
        [jnp.broadcast_to(lines[0:1], (8, wide)), jnp.broadcast_to(lines[1:2], (8, wide))],
        axis=0,
    )
    full = jnp.where(same_layer(full.shape), full, 0.0)
    upper = full.astype(jnp.bfloat16)
    fit = jnp.concatenate([upper, (full - upper.astype(jnp.float32)).astype(jnp.bfloat16)], axis=0)

    chunks = sems.shape[0]
    per_chunk = tiles // chunks
    copies = []
    for c in range(chunks):
        for t in range(c * per_chunk, (c + 1) * per_chunk):
            fitted = jnp.dot(fit, modes_of(basis_ref, t), preferred_element_type=jnp.float32)
            fitted = fitted[0:16] + fitted[16:32]
            snaps = snaps_ref[t].astype(jnp.float32)
            made[0, t] = snaps[0:8] * w00 - fitted[0:8]
            made[1, t] = snaps[8:16] * w11 + snaps[0:8] * w01 - fitted[8:16]
        span = pl.ds(c * per_chunk, per_chunk)
        copies.append(
            pltpu.make_async_copy(made.at[:, span], modes_ref.at[:, span], sems.at[c])
        )
        copies[c].start()
    for copy in copies:
        copy.wait()


def params(mib):
    return pltpu.CompilerParams(vmem_limit_bytes=mib * 1024 * 1024)


def cost(flops, moved):
    return pl.CostEstimate(flops=flops, bytes_accessed=moved, transcendentals=0)


WHOLE = pl.BlockSpec(memory_space=pltpu.VMEM)
FAR = pl.BlockSpec(memory_space=pltpu.HBM)
SCALAR = pl.BlockSpec(memory_space=pltpu.SMEM)


def swap_added(value, axis, bit):
    count = lax.axis_size(axis)
    return value + lax.ppermute(value, axis, [(i, i ^ bit) for i in range(count)])


def bits(count):
    made = [1 << k for k in range(count.bit_length() - 1)]
    if count != 1 << len(made):
        raise ValueError("axis size")
    return made


def body(windows, pod_basis):
    f32, bf16 = jnp.float32, jnp.bfloat16
    shape = jax.ShapeDtypeStruct
    count, fields, planes, layers, cells = windows.shape
    ring, walls = lax.axis_size("solver"), lax.axis_size("analysis")
    paired = walls == 2 and planes == 8 and layers == 4
    place = lax.axis_index("analysis").astype(jnp.int32).reshape(1)
    modes, _, pod_planes, pod_layers, _ = pod_basis.shape
    tiles = fields * pod_planes * (pod_layers // 8)
    basis = pod_basis.reshape(modes, tiles, 8, cells)
    wide = modes * 8
    basis_bytes = basis.size * 2

    sides = 1 if walls == 2 else 2
    kept, *faces = pl.pallas_call(
        functools.partial(face_kernel, sides == 2),
        out_shape=[shape(windows.shape, f32)]
        + [shape((count, fields, REACH, layers, cells), f32)] * 2
        + [shape(windows.shape, f32)] * sides,
        in_specs=[SCALAR, FAR],
        out_specs=[WHOLE] * (3 + sides),
        scratch_shapes=[
            pltpu.VMEM((fields, planes, layers, cells), f32),
            pltpu.SemaphoreType.DMA((count,)),
        ],
        compiler_params=params(16),
        cost_estimate=cost(10_000_000, 10 * windows.size),
        name="faces",
    )(place, windows)
    to_right = [(i, (i + 1) % ring) for i in range(ring)]
    to_left = [((i + 1) % ring, i) for i in range(ring)]
    upward = [(i, i + 1) for i in range(walls - 1)]
    downward = [(i + 1, i) for i in range(walls - 1)]
    if sides == 1:
        wall_terms = [lax.ppermute(faces[2], "analysis", upward + downward)]
    else:
        wall_terms = [
            lax.ppermute(faces[2], "analysis", upward),
            lax.ppermute(faces[3], "analysis", downward),
        ]
    from_left = lax.ppermute(faces[0], "solver", to_right)
    from_right = lax.ppermute(faces[1], "solver", to_left)

    inner, gram, basis = pl.pallas_call(
        inner_gram_kernel,
        out_shape=[shape(windows.shape, f32), shape((modes, LANES), f32), shape(basis.shape, bf16)],
        in_specs=[WHOLE, FAR],
        out_specs=[WHOLE] * 3,
        scratch_shapes=[
            pltpu.VMEM((fields, planes, layers, cells), f32),
            pltpu.VMEM((wide // LANES, wide, LANES), f32),
            pltpu.SemaphoreType.DMA((fields,)),
        ],
        compiler_params=params(40),
        cost_estimate=cost(2 * wide * wide * cells * tiles, 2 * basis_bytes),
        name="inner_gram",
    )(kept, basis)
    *near, far = bits(ring)
    gram_far = lax.ppermute(gram, "solver", [(i, i ^ far) for i in range(ring)])
    half_shape = (count, fields, planes * layers // 2, cells)
    joined = pl.pallas_call(
        functools.partial(join_kernel, sides, paired),
        out_shape=[shape(windows.shape, f32)] + ([shape(half_shape, bf16)] * 2 if paired else []),
        in_specs=[SCALAR] + [WHOLE] * (3 + sides),
        out_specs=[WHOLE] * (3 if paired else 1),
        compiler_params=params(16),
        cost_estimate=cost(1_000_000, 16 * windows.size),
        name="join",
    )(place, inner, from_left, from_right, *wall_terms)
    next_windows = joined[0]

    sums_shape = shape((modes + 8, LANES), f32)
    snaps_shape = shape((tiles, 2 * 8, cells), bf16)
    scratch = [pltpu.VMEM((LANES, LANES), f32), pltpu.VMEM((1, wide, LANES), f32)]
    project_cost = cost(2 * wide * 16 * cells * tiles, basis_bytes)
    if paired:
        own, given = joined[1], joined[2]
        got = lax.ppermute(given, "analysis", [(0, 1), (1, 0)])
        sums, snaps = pl.pallas_call(
            functools.partial(project_kernel, True),
            out_shape=[sums_shape, snaps_shape],
            in_specs=[SCALAR] + [WHOLE] * 5,
            out_specs=[WHOLE] * 2,
            scratch_shapes=scratch,
            compiler_params=params(16),
            cost_estimate=project_cost,
            name="project",
        )(place, gram, gram_far, own, got, basis)
    else:
        relaid = lax.all_to_all(
            next_windows.astype(bf16), "analysis", split_axis=2, concat_axis=3, tiled=True
        )
        snaps = relaid.reshape(count, tiles, 8, cells).transpose(1, 0, 2, 3)
        snaps = snaps.reshape(tiles, count * 8, cells)
        sums = pl.pallas_call(
            functools.partial(project_kernel, False),
            out_shape=sums_shape,
            in_specs=[SCALAR] + [WHOLE] * 4,
            out_specs=WHOLE,
            scratch_shapes=scratch,
            compiler_params=params(16),
            cost_estimate=project_cost,
            name="project",
        )(place, gram, gram_far, snaps, basis)
    for bit in bits(walls):
        sums = swap_added(sums, "analysis", bit)
    for bit in near:
        sums = swap_added(sums, "solver", bit)
    inverse = pl.pallas_call(
        inverse_kernel,
        out_shape=shape((modes, modes), f32),
        in_specs=[WHOLE],
        out_specs=WHOLE,
        scratch_shapes=[pltpu.VMEM((modes, 2 * modes), f32)] * 2,
        compiler_params=params(16),
        cost_estimate=cost(20_000_000, 8 * modes * modes),
        name="inverse",
    )(sums)
    projected = swap_added(sums, "solver", far)

    rows_total = ring * walls * tiles * 8 * cells
    new_modes, solved, factor = pl.pallas_call(
        functools.partial(finish_kernel, rows_total),
        out_shape=[
            shape((count, tiles, 8, cells), f32),
            shape((count, modes), f32),
            shape((count, count), f32),
        ],
        in_specs=[WHOLE] * 5,
        out_specs=[FAR, WHOLE, WHOLE],
        scratch_shapes=[
            pltpu.VMEM((count, tiles, 8, cells), f32),
            pltpu.SemaphoreType.DMA((fields,)),
        ],
        compiler_params=params(16),
        cost_estimate=cost(2 * wide * 32 * cells * tiles, basis_bytes + 8 * windows.size),
        name="finish",
    )(projected, sums, inverse, snaps, basis)
    new_modes = new_modes.reshape(count, fields, pod_planes, pod_layers, cells)
    return next_windows, solved, new_modes, factor


def solution(mesh):
    in_specs = (
        P(None, None, "solver", "analysis", None),
        P(None, None, ("solver", "analysis"), None, None),
    )
    out_specs = (
        P(None, None, "solver", "analysis", None),
        P(),
        P(None, None, ("solver", "analysis"), None, None),
        P(),
    )
    return jax.shard_map(body, mesh=mesh, in_specs=in_specs, out_specs=out_specs, check_vma=False)
```

```python
import functools

import jax
import jax.numpy as jnp
from jax import lax
from jax.experimental import pallas as pl
from jax.experimental.pallas import tpu as pltpu
from jax.sharding import PartitionSpec as P

PRESSURE_FACTOR = 1.4 - 1.0
SECTION_STEP = 0.25
CENTRAL_WEIGHTS = (0.8, -0.2, 4.0 / 105.0, -1.0 / 280.0)
REACH = 4
LANES = 128
HIGHEST = lax.Precision.HIGHEST
NT = (((1,), (1,)), ((), ()))


def weight(k):
    if k == 0 or abs(k) > REACH:
        return 0.0
    value = -SECTION_STEP * CENTRAL_WEIGHTS[abs(k) - 1]
    return value if k > 0 else -value


def row_weights(shape, values):
    rows = lax.broadcasted_iota(jnp.int32, shape, len(shape) - 2)
    made = jnp.full(shape, values[0], jnp.float32)
    for i, value in enumerate(values[1:], start=1):
        made = jnp.where(rows == i, jnp.float32(value), made)
    return made


def primitives(windows_ref, w, x):
    density, mx, my, mz, energy = (windows_ref[w, f, x] for f in range(5))
    inverse = 1.0 / density
    ux, uy, uz = mx * inverse, my * inverse, mz * inverse
    pressure = PRESSURE_FACTOR * (energy - 0.5 * (mx * ux + my * uy + mz * uz))
    return (mx, my, mz), (ux, uy, uz), pressure, energy + pressure


def flux(parts, direction):
    moments, speeds, pressure, enthalpy = parts
    speed = speeds[direction]
    made = [moments[direction]]
    for axis in range(3):
        term = moments[axis] * speed
        made.append(term + pressure if axis == direction else term)
    made.append(enthalpy * speed)
    return made


def face_kernel(two_sided, where_ref, source_ref, windows_ref, left_ref, right_ref, *rest):
    windows, _, planes, layers, cells = windows_ref.shape
    wall_refs, scratch, sems = rest[:-2], rest[-2], rest[-1]
    copies = [
        pltpu.make_async_copy(source_ref.at[w], windows_ref.at[w], sems.at[w])
        for w in range(windows)
    ]
    for copy in copies:
        copy.start()
    tile = (layers, cells)
    up = [
        row_weights(tile, [weight(j - layers - i) for i in range(layers)]) for j in range(layers)
    ]
    down = [
        row_weights(tile, [weight(layers + j - i) for i in range(layers)]) for j in range(layers)
    ]
    if two_sided:
        tables = (up, down)
    else:
        first = where_ref[0] == 0
        tables = ([jnp.where(first, u, d) for u, d in zip(up, down)],)
    for w in range(windows):
        copies[w].wait()
        for x in range(planes):
            parts = primitives(windows_ref, w, x)
            for f, value in enumerate(flux(parts, 0)):
                scratch[f, x] = value
            for f, value in enumerate(flux(parts, 1)):
                for ref, table in zip(wall_refs, tables):
                    total = None
                    for j in range(layers):
                        term = table[j] * value[j : j + 1, :]
                        total = term if total is None else total + term
                    ref[w, f, x] = total
        for f in range(5):
            for i in range(REACH):
                total = None
                for j in range(planes):
                    c = weight(j - planes - i)
                    if c:
                        term = c * scratch[f, j]
                        total = term if total is None else total + term
                left_ref[w, f, i] = total
                total = None
                for j in range(planes):
                    c = weight(j + REACH - i)
                    if c:
                        term = c * scratch[f, j]
                        total = term if total is None else total + term
                right_ref[w, f, i] = total


def paired_face_kernel(
    where_ref, source_ref, windows_ref, left_ref, right_ref, near_ref, later_ref,
    scratch, lows, sems,
):
    windows, _, planes, layers, cells = windows_ref.shape
    copies = [
        pltpu.make_async_copy(source_ref.at[w], windows_ref.at[w], sems.at[w])
        for w in range(windows)
    ]
    for copy in copies:
        copy.start()
    tile = (layers, cells)
    first = where_ref[0] == 0
    table = [
        jnp.where(
            first,
            row_weights(tile, [weight(j - layers - i) for i in range(layers)]),
            row_weights(tile, [weight(layers + j - i) for i in range(layers)]),
        )
        for j in range(layers)
    ]
    half = planes // 2
    for w in range(windows):
        copies[w].wait()
        for group, group_ref in enumerate((near_ref, later_ref)):
            base = half * (1 - where_ref[0] if group else where_ref[0])
            upper = [[] for _ in range(5)]
            lower = [[] for _ in range(5)]
            for x in range(half):
                parts = primitives(windows_ref, w, base + x)
                for f, value in enumerate(flux(parts, 0)):
                    scratch[f, base + x] = value
                for f, value in enumerate(flux(parts, 1)):
                    total = None
                    for j in range(layers):
                        term = table[j] * value[j : j + 1, :]
                        total = term if total is None else total + term
                    high = total.astype(jnp.bfloat16).astype(jnp.float32)
                    rest = total - high
                    upper[f].append(high)
                    lower[f].append(jnp.where(first, rest[0:2], rest[2:4]))
            for f in range(5):
                group_ref[f, 16 * w : 16 * w + 16] = jnp.concatenate(upper[f], axis=0).astype(
                    jnp.bfloat16
                )
                lows[group, f, 8 * w : 8 * w + 8] = jnp.concatenate(lower[f], axis=0)
        for f in range(5):
            for i in range(REACH):
                total = None
                for j in range(planes):
                    c = weight(j - planes - i)
                    if c:
                        term = c * scratch[f, j]
                        total = term if total is None else total + term
                left_ref[w, f, i] = total
                total = None
                for j in range(planes):
                    c = weight(j + REACH - i)
                    if c:
                        term = c * scratch[f, j]
                        total = term if total is None else total + term
                right_ref[w, f, i] = total
    for group, group_ref in enumerate((near_ref, later_ref)):
        for f in range(5):
            group_ref[f, 32:48] = lows[group, f].astype(jnp.bfloat16)


def inner_part(windows_ref, part_ref, scratch):
    windows, _, planes, layers, cells = windows_ref.shape
    tile = (layers, cells)
    wall = [
        row_weights(tile, [weight(j - i) for i in range(layers)]) for j in range(layers)
    ]
    for w in range(windows):
        for x in range(planes):
            parts = primitives(windows_ref, w, x)
            for f, value in enumerate(flux(parts, 0)):
                scratch[f, x] = value
            flux_y, flux_z = flux(parts, 1), flux(parts, 2)
            for f in range(5):
                total = windows_ref[w, f, x]
                for j in range(layers):
                    total = total + wall[j] * flux_y[f][j : j + 1, :]
                for k in range(1, REACH + 1):
                    total = total + weight(k) * (
                        pltpu.roll(flux_z[f], cells - k, 1) - pltpu.roll(flux_z[f], k, 1)
                    )
                part_ref[w, f, x] = total
        for f in range(5):
            for x in range(planes):
                total = part_ref[w, f, x]
                for k in range(-REACH, REACH + 1):
                    if k and 0 <= x + k < planes:
                        total = total + weight(k) * scratch[f, x + k]
                part_ref[w, f, x] = total


def gram_blocks(basis_ref, chunks, per_chunk, right, left):
    half = left.shape[0]
    for c in chunks:
        rows = jnp.concatenate(
            [modes_of(basis_ref, t) for t in range(c * per_chunk, (c + 1) * per_chunk)], axis=1
        )
        right = right + lax.dot_general(
            rows, rows[half:], NT, preferred_element_type=jnp.float32
        )
        left = left + lax.dot_general(
            rows[:half], rows[:half], NT, preferred_element_type=jnp.float32
        )
    return right, left


def inner_gram_kernel(
    early, windows_ref, basis_ref, part_ref, right_ref, left_ref, kept_ref, scratch, sems
):
    chunks = sems.shape[0]
    per_chunk = kept_ref.shape[1] // chunks
    copies = []
    for c in range(chunks):
        span = pl.ds(c * per_chunk, per_chunk)
        copies.append(
            pltpu.make_async_copy(basis_ref.at[:, span], kept_ref.at[:, span], sems.at[c])
        )
        copies[c].start()
    inner_part(windows_ref, part_ref, scratch)
    right, left = jnp.zeros(right_ref.shape, jnp.float32), jnp.zeros(left_ref.shape, jnp.float32)
    for c in range(chunks):
        copies[c].wait()
        if c < early:
            right, left = gram_blocks(kept_ref, [c], per_chunk, right, left)
    right_ref[...] = right
    left_ref[...] = left


def gram_kernel(early, chunks, _, right_ref, left_ref, basis_ref, gram_ref, total):
    modes, tiles = basis_ref.shape[:2]
    wide = modes * 8
    half = wide // 2
    right, left = gram_blocks(
        basis_ref, range(early, chunks), tiles // chunks, right_ref[...], left_ref[...]
    )
    tiles_left = half // LANES
    turned = right[0:half].T
    for tile in range(tiles_left):
        span = slice(tile * LANES, (tile + 1) * LANES)
        total[tile, 0:half] = left[:, span]
        total[tile, half:] = turned[:, span]
        total[tiles_left + tile] = right[:, span]
    rows = folded(total, modes)
    lanes = gram_ref.shape[1]
    picks = (
        lax.broadcasted_iota(jnp.int32, (wide, lanes), 0) // 8
        == lax.broadcasted_iota(jnp.int32, (wide, lanes), 1)
    ).astype(jnp.float32)
    gram_ref[...] = jnp.dot(rows, picks, precision=HIGHEST, preferred_element_type=jnp.float32)


def join_kernel(walls, part_ref, left_ref, right_ref, *rest):
    wall_refs, next_ref = rest[:walls], rest[walls]
    windows, _, planes, layers, cells = part_ref.shape
    for w in range(windows):
        for f in range(5):
            for x in range(planes):
                total = part_ref[w, f, x]
                for ref in wall_refs:
                    total = total + ref[w, f, x]
                if x < REACH:
                    total = total + left_ref[w, f, x]
                if x >= planes - REACH:
                    total = total + right_ref[w, f, x - planes + REACH]
                next_ref[w, f, x] = total


def paired_join_kernel(
    own, where_ref, _, part_ref, left_ref, right_ref, group_ref, *rest
):
    next_ref, snaps_ref, made, sem = rest[-4:]
    windows, _, planes, layers, cells = part_ref.shape
    half = planes // 2
    first = where_ref[0] == 0
    base = half * (where_ref[0] if own else 1 - where_ref[0])
    ahead = base == 0
    zero = jnp.zeros((2, cells), jnp.float32)
    for w in range(windows):
        for f in range(5):
            upper = group_ref[f, 16 * w : 16 * w + 16].astype(jnp.float32)
            lower = group_ref[f, 32:48].astype(jnp.float32)[8 * w : 8 * w + 8]
            done = []
            for x in range(half):
                rest_now = lower[2 * x : 2 * x + 2]
                total = part_ref[w, f, base + x] + (
                    upper[layers * x : layers * x + layers]
                    + jnp.where(
                        first,
                        jnp.concatenate([zero, rest_now], axis=0),
                        jnp.concatenate([rest_now, zero], axis=0),
                    )
                )
                total = total + jnp.where(ahead, left_ref[w, f, x], right_ref[w, f, x])
                made[w, f, x] = total
                done.append(total)
            snaps_ref[w, f] = jnp.concatenate(done, axis=0).astype(jnp.bfloat16)
    copy = pltpu.make_async_copy(made, next_ref.at[:, :, pl.ds(base, half)], sem)
    copy.start()
    copy.wait()


def same_layer(shape):
    rows = lax.broadcasted_iota(jnp.int32, shape, 0)
    columns = lax.broadcasted_iota(jnp.int32, shape, 1)
    return lax.rem(rows, 8) == lax.rem(columns, 8)


def folded(total, modes):
    kept = lax.rem(lax.broadcasted_iota(jnp.int32, (modes, LANES), 1), 8)
    made = []
    for tile in range(total.shape[0]):
        rows = jnp.zeros((modes, LANES), jnp.float32)
        for y in range(8):
            rows = jnp.where(kept == y, total[tile, pl.ds(y, modes, 8), :], rows)
        made.append(rows)
    return made[0] if len(made) == 1 else jnp.concatenate(made, axis=1)


def modes_of(basis_ref, t):
    modes, _, layers, cells = basis_ref.shape
    return basis_ref[:, t].reshape(modes * layers, cells)


def project_kernel(paired, where_ref, *rest):
    if paired:
        own_ref, got_ref, basis_ref, sums_ref, snaps_ref, square, wide_sums = rest
        first = where_ref[0] == 0
        for w in range(own_ref.shape[0]):
            for f in range(own_ref.shape[1]):
                own = own_ref[w, f].astype(jnp.float32)
                got = got_ref[w, f].astype(jnp.float32)
                low = jnp.where(first, own, got)
                high = jnp.where(first, got, own)
                for t in range(4):
                    snaps_ref[4 * f + t, pl.ds(8 * w, 8)] = jnp.concatenate(
                        [low[4 * t : 4 * t + 4], high[4 * t : 4 * t + 4]], axis=0
                    ).astype(jnp.bfloat16)
    else:
        snaps_ref, basis_ref, sums_ref, square, wide_sums = rest
    modes, tiles = basis_ref.shape[:2]
    columns = snaps_ref.shape[1]
    total = jnp.zeros((modes * 8, columns), jnp.float32)
    small = jnp.zeros((columns, columns), jnp.float32)
    for t in range(tiles):
        snaps = snaps_ref[t]
        total = total + lax.dot_general(
            modes_of(basis_ref, t), snaps, NT, preferred_element_type=jnp.float32
        )
        small = small + lax.dot_general(snaps, snaps, NT, preferred_element_type=jnp.float32)
    wide_sums[0, :, 0:columns] = total
    square[...] = jnp.zeros_like(square)
    square[0:modes, :] = folded(wide_sums, modes)
    kept = jnp.where(same_layer(small.shape), small, 0.0)
    square[modes : modes + 1, 0:columns] = jnp.sum(kept[0:8], axis=0, keepdims=True)
    square[modes + 1 : modes + 2, 0:columns] = jnp.sum(kept[8:16], axis=0, keepdims=True)
    lanes = lax.broadcasted_iota(jnp.int32, square.shape, 1)
    turned = jnp.where(lanes < columns, square[...], 0.0).T
    sums = jnp.concatenate(
        [
            jnp.sum(turned[0:8], axis=0, keepdims=True),
            jnp.sum(turned[8:16], axis=0, keepdims=True),
        ],
        axis=0,
    )
    sums_ref[...] = jnp.concatenate(
        [sums, jnp.zeros((6, sums.shape[1]), jnp.float32)], axis=0
    )


def merge_kernel(gram_ref, far_ref, sums_ref, merged_ref):
    modes = gram_ref.shape[0]
    merged_ref[0:modes] = gram_ref[...] + far_ref[...]
    merged_ref[modes:] = sums_ref[...]


def inverse_kernel(sums_ref, inverse_ref, plain, scaled):
    modes = inverse_ref.shape[0]
    rows = lax.broadcasted_iota(jnp.int32, (8, 2 * modes), 0)
    lanes = lax.broadcasted_iota(jnp.int32, (8, 2 * modes), 1)
    tiles = []
    for tile in range(modes // 8):
        eye = (lanes == rows + (modes + 8 * tile)).astype(jnp.float32)
        tiles.append(jnp.where(lanes < modes, sums_ref[8 * tile : 8 * tile + 8, :], eye))
    count = modes // 8
    for home in range(count):
        columns = [
            [
                jnp.broadcast_to(
                    tiles[tile][:, 8 * home + j : 8 * home + j + 1], (8, 2 * modes)
                )
                for tile in range(home, count)
            ]
            for j in range(8)
        ]
        for j in range(8):
            k = 8 * home + j
            inverse = 1.0 / columns[j][0]
            inverse = inverse[j : j + 1, :]
            row = tiles[home][j : j + 1, :]
            ready = row * inverse
            plain[k : k + 1, :] = row
            scaled[k : k + 1, :] = ready
            factors = [jnp.where(rows > j, columns[j][0], 0.0)] + columns[j][1:]
            for later in range(j + 1, 8):
                share = columns[j][0][later : later + 1, :] * inverse
                columns[later] = [c - f * share for c, f in zip(columns[later], factors)]
            for tile in range(home, count):
                tiles[tile] = tiles[tile] - factors[tile - home] * ready
    inverse_ref[...] = lax.dot_general(
        plain[:, modes:], scaled[:, modes:], (((0,), (0,)), ((), ())),
        precision=HIGHEST, preferred_element_type=jnp.float32,
    )


def finish_kernel(
    rows_total, projected_ref, sums_ref, inverse_ref, snaps_ref, basis_ref,
    modes_ref, solved_ref, factor_ref, made, sems,
):
    modes, tiles, _, cells = basis_ref.shape
    wide = modes * 8
    exact = functools.partial(jnp.dot, precision=HIGHEST, preferred_element_type=jnp.float32)
    projected = projected_ref[modes : modes + 8, 0:modes]
    gram, inverse = sums_ref[0:modes, 0:modes], inverse_ref[...]
    solved = exact(projected, inverse)
    solved = solved + exact(projected - exact(solved, gram), inverse)
    left = projected - exact(solved, gram)

    def inner(p, i, q, j):
        return jnp.sum(p[i : i + 1] * q[j : j + 1], axis=1, keepdims=True)

    def entry(i, j):
        square = projected_ref[modes + i : modes + i + 1, modes + j : modes + j + 1]
        return square - inner(projected, i, solved, j) - inner(solved, i, left, j)

    first = jnp.sqrt(entry(0, 0))
    below = entry(1, 0) / first
    second = jnp.sqrt(entry(1, 1) - below * below)
    scaling = jnp.sqrt(jnp.float32(rows_total))
    w00 = scaling / first
    w11 = scaling / second
    w01 = -(below / first) * w11
    solved_ref[...] = solved[0:2]
    factor_ref[0:1, 0:1] = first / scaling
    factor_ref[0:1, 1:2] = below / scaling
    factor_ref[1:2, 0:1] = jnp.zeros_like(first)
    factor_ref[1:2, 1:2] = second / scaling
    spread = (
        lax.broadcasted_iota(jnp.int32, (modes, wide), 1) // 8
        == lax.broadcasted_iota(jnp.int32, (modes, wide), 0)
    ).astype(jnp.float32)
    scaled = jnp.concatenate(
        [solved[0:1] * w00, solved[1:2] * w11 + solved[0:1] * w01, solved[2:8]], axis=0
    )
    lines = exact(scaled, spread)
    full = jnp.concatenate(
        [jnp.broadcast_to(lines[0:1], (8, wide)), jnp.broadcast_to(lines[1:2], (8, wide))],
        axis=0,
    )
    full = jnp.where(same_layer(full.shape), full, 0.0)
    upper = full.astype(jnp.bfloat16)
    fit = jnp.concatenate([upper, (full - upper.astype(jnp.float32)).astype(jnp.bfloat16)], axis=0)

    chunks = sems.shape[0]
    per_chunk = tiles // chunks
    copies = []
    for c in range(chunks):
        for t in range(c * per_chunk, (c + 1) * per_chunk):
            fitted = jnp.dot(fit, modes_of(basis_ref, t), preferred_element_type=jnp.float32)
            fitted = fitted[0:16] + fitted[16:32]
            snaps = snaps_ref[t].astype(jnp.float32)
            made[0, t] = snaps[0:8] * w00 - fitted[0:8]
            made[1, t] = snaps[8:16] * w11 + snaps[0:8] * w01 - fitted[8:16]
        span = pl.ds(c * per_chunk, per_chunk)
        copies.append(
            pltpu.make_async_copy(made.at[:, span], modes_ref.at[:, span], sems.at[c])
        )
        copies[c].start()
    for copy in copies:
        copy.wait()


def params(mib):
    return pltpu.CompilerParams(vmem_limit_bytes=mib * 1024 * 1024)


def cost(flops, moved):
    return pl.CostEstimate(flops=flops, bytes_accessed=moved, transcendentals=0)


WHOLE = pl.BlockSpec(memory_space=pltpu.VMEM)
FAR = pl.BlockSpec(memory_space=pltpu.HBM)
LOOSE = pl.BlockSpec(memory_space=pl.ANY)
SCALAR = pl.BlockSpec(memory_space=pltpu.SMEM)


def swap_added(value, axis, bit):
    count = lax.axis_size(axis)
    return value + lax.ppermute(value, axis, [(i, i ^ bit) for i in range(count)])


def bits(count):
    made = [1 << k for k in range(count.bit_length() - 1)]
    if count != 1 << len(made):
        raise ValueError("axis size")
    return made


def body(windows, pod_basis):
    f32, bf16 = jnp.float32, jnp.bfloat16
    shape = jax.ShapeDtypeStruct
    count, fields, planes, layers, cells = windows.shape
    ring, walls = lax.axis_size("solver"), lax.axis_size("analysis")
    paired = walls == 2 and planes == 8 and layers == 4
    place = lax.axis_index("analysis").astype(jnp.int32).reshape(1)
    modes, _, pod_planes, pod_layers, _ = pod_basis.shape
    tiles = fields * pod_planes * (pod_layers // 8)
    basis = pod_basis.reshape(modes, tiles, 8, cells)
    wide = modes * 8
    basis_bytes = basis.size * 2

    to_right = [(i, (i + 1) % ring) for i in range(ring)]
    to_left = [((i + 1) % ring, i) for i in range(ring)]
    edge_shape = shape((count, fields, REACH, layers, cells), f32)
    face_scratch = [pltpu.VMEM((fields, planes, layers, cells), f32)]
    face_cost = cost(10_000_000, 10 * windows.size)
    if paired:
        swap = [(0, 1), (1, 0)]
        group_shape = shape((fields, 48, cells), bf16)
        kept, to_next, to_last, near_group, later_group = pl.pallas_call(
            paired_face_kernel,
            out_shape=[shape(windows.shape, f32)] + [edge_shape] * 2 + [group_shape] * 2,
            in_specs=[SCALAR, FAR],
            out_specs=[WHOLE] * 5,
            scratch_shapes=face_scratch
            + [pltpu.VMEM((2, fields, 16, cells), f32), pltpu.SemaphoreType.DMA((count,))],
            compiler_params=params(16),
            cost_estimate=face_cost,
            name="faces",
        )(place, windows)
        near_group = lax.ppermute(near_group, "analysis", swap)
        from_left = lax.ppermute(to_next, "solver", to_right)
        from_right = lax.ppermute(to_last, "solver", to_left)
        later_group = lax.ppermute(later_group, "analysis", swap)
    else:
        kept, to_next, to_last, up, down = pl.pallas_call(
            functools.partial(face_kernel, True),
            out_shape=[shape(windows.shape, f32)]
            + [edge_shape] * 2
            + [shape(windows.shape, f32)] * 2,
            in_specs=[SCALAR, FAR],
            out_specs=[WHOLE] * 5,
            scratch_shapes=face_scratch + [pltpu.SemaphoreType.DMA((count,))],
            compiler_params=params(16),
            cost_estimate=face_cost,
            name="faces",
        )(place, windows)
        wall_terms = [
            lax.ppermute(up, "analysis", [(i, i + 1) for i in range(walls - 1)]),
            lax.ppermute(down, "analysis", [(i + 1, i) for i in range(walls - 1)]),
        ]
        from_left = lax.ppermute(to_next, "solver", to_right)
        from_right = lax.ppermute(to_last, "solver", to_left)

    early = 2
    gram_flops = 2 * wide * wide * cells * tiles
    inner, right, left, basis = pl.pallas_call(
        functools.partial(inner_gram_kernel, early),
        out_shape=[
            shape(windows.shape, f32),
            shape((wide, wide // 2), f32),
            shape((wide // 2, wide // 2), f32),
            shape(basis.shape, bf16),
        ],
        in_specs=[WHOLE, FAR],
        out_specs=[WHOLE] * 4,
        scratch_shapes=[
            pltpu.VMEM((fields, planes, layers, cells), f32),
            pltpu.SemaphoreType.DMA((fields,)),
        ],
        compiler_params=params(40),
        cost_estimate=cost(gram_flops // 2, 2 * basis_bytes),
        name="inner_gram",
    )(kept, basis)

    def rest_of_gram(after):
        return pl.pallas_call(
            functools.partial(gram_kernel, early, fields),
            out_shape=shape((modes, LANES), f32),
            in_specs=[LOOSE] + [WHOLE] * 3,
            out_specs=WHOLE,
            scratch_shapes=[pltpu.VMEM((wide // LANES, wide, LANES), f32)],
            compiler_params=params(24),
            cost_estimate=cost(gram_flops // 2, basis_bytes),
            name="gram",
        )(after, right, left, basis)

    join_cost = cost(1_000_000, 16 * windows.size)
    if paired:
        half_shape = (count, fields, planes * layers // 2, cells)

        def join(own, after, group, *base):
            return pl.pallas_call(
                functools.partial(paired_join_kernel, own),
                out_shape=[shape(windows.shape, f32), shape(half_shape, bf16)],
                in_specs=[SCALAR, LOOSE] + [WHOLE] * 4 + [FAR] * len(base),
                out_specs=[FAR, WHOLE],
                scratch_shapes=[
                    pltpu.VMEM((count, fields, planes // 2, layers, cells), f32),
                    pltpu.SemaphoreType.DMA,
                ],
                input_output_aliases={6: 0} if base else {},
                compiler_params=params(16),
                cost_estimate=join_cost,
                name="join_own" if own else "join_given",
            )(place, after, inner, from_left, from_right, group, *base)

        next_windows, given = join(False, place, near_group)
        got = lax.ppermute(given, "analysis", swap)
        gram = rest_of_gram(given)
    else:
        next_windows = pl.pallas_call(
            functools.partial(join_kernel, 2),
            out_shape=shape(windows.shape, f32),
            in_specs=[WHOLE] * 5,
            out_specs=WHOLE,
            compiler_params=params(16),
            cost_estimate=join_cost,
            name="join",
        )(inner, from_left, from_right, *wall_terms)
        gram = rest_of_gram(place)
    *near, far = bits(ring)
    gram_far = lax.ppermute(gram, "solver", [(i, i ^ far) for i in range(ring)])
    if paired:
        next_windows, own = join(True, gram, later_group, next_windows)

    sums_shape = shape((8, LANES), f32)
    snaps_shape = shape((tiles, 2 * 8, cells), bf16)
    scratch = [pltpu.VMEM((LANES, LANES), f32), pltpu.VMEM((1, wide, LANES), f32)]
    project_cost = cost(2 * wide * 16 * cells * tiles, basis_bytes)
    if paired:
        sums, snaps = pl.pallas_call(
            functools.partial(project_kernel, True),
            out_shape=[sums_shape, snaps_shape],
            in_specs=[SCALAR] + [WHOLE] * 3,
            out_specs=[WHOLE] * 2,
            scratch_shapes=scratch,
            compiler_params=params(16),
            cost_estimate=project_cost,
            name="project",
        )(place, own, got, basis)
    else:
        relaid = lax.all_to_all(
            next_windows.astype(bf16), "analysis", split_axis=2, concat_axis=3, tiled=True
        )
        snaps = relaid.reshape(count, tiles, 8, cells).transpose(1, 0, 2, 3)
        snaps = snaps.reshape(tiles, count * 8, cells)
        sums = pl.pallas_call(
            functools.partial(project_kernel, False),
            out_shape=sums_shape,
            in_specs=[SCALAR] + [WHOLE] * 2,
            out_specs=WHOLE,
            scratch_shapes=scratch,
            compiler_params=params(16),
            cost_estimate=project_cost,
            name="project",
        )(place, snaps, basis)
    sums = pl.pallas_call(
        merge_kernel,
        out_shape=shape((modes + 8, LANES), f32),
        in_specs=[WHOLE] * 3,
        out_specs=WHOLE,
        compiler_params=params(16),
        cost_estimate=cost(10_000, 8 * modes * LANES),
        name="merge",
    )(gram, gram_far, sums)
    for bit in bits(walls):
        sums = swap_added(sums, "analysis", bit)
    for bit in near:
        sums = swap_added(sums, "solver", bit)
    inverse = pl.pallas_call(
        inverse_kernel,
        out_shape=shape((modes, modes), f32),
        in_specs=[WHOLE],
        out_specs=WHOLE,
        scratch_shapes=[pltpu.VMEM((modes, 2 * modes), f32)] * 2,
        compiler_params=params(16),
        cost_estimate=cost(20_000_000, 8 * modes * modes),
        name="inverse",
    )(sums)
    projected = swap_added(sums, "solver", far)

    rows_total = ring * walls * tiles * 8 * cells
    new_modes, solved, factor = pl.pallas_call(
        functools.partial(finish_kernel, rows_total),
        out_shape=[
            shape((count, tiles, 8, cells), f32),
            shape((count, modes), f32),
            shape((count, count), f32),
        ],
        in_specs=[WHOLE] * 5,
        out_specs=[FAR, WHOLE, WHOLE],
        scratch_shapes=[
            pltpu.VMEM((count, tiles, 8, cells), f32),
            pltpu.SemaphoreType.DMA((fields,)),
        ],
        compiler_params=params(16),
        cost_estimate=cost(2 * wide * 32 * cells * tiles, basis_bytes + 8 * windows.size),
        name="finish",
    )(projected, sums, inverse, snaps, basis)
    new_modes = new_modes.reshape(count, fields, pod_planes, pod_layers, cells)
    return next_windows, solved, new_modes, factor


def solution(mesh):
    in_specs = (
        P(None, None, "solver", "analysis", None),
        P(None, None, ("solver", "analysis"), None, None),
    )
    out_specs = (
        P(None, None, "solver", "analysis", None),
        P(),
        P(None, None, ("solver", "analysis"), None, None),
        P(),
    )
    return jax.shard_map(body, mesh=mesh, in_specs=in_specs, out_specs=out_specs, check_vma=False)
```

```python
import functools

import jax
import jax.numpy as jnp
from jax import lax
from jax.experimental import pallas as pl
from jax.experimental.pallas import tpu as pltpu
from jax.sharding import PartitionSpec as P

PRESSURE_FACTOR = 1.4 - 1.0
SECTION_STEP = 0.25
CENTRAL_WEIGHTS = (0.8, -0.2, 4.0 / 105.0, -1.0 / 280.0)
REACH = 4
LANES = 128
HIGHEST = lax.Precision.HIGHEST
NT = (((1,), (1,)), ((), ()))


def weight(k):
    if k == 0 or abs(k) > REACH:
        return 0.0
    value = -SECTION_STEP * CENTRAL_WEIGHTS[abs(k) - 1]
    return value if k > 0 else -value


def row_weights(shape, values):
    rows = lax.broadcasted_iota(jnp.int32, shape, len(shape) - 2)
    made = jnp.full(shape, values[0], jnp.float32)
    for i, value in enumerate(values[1:], start=1):
        made = jnp.where(rows == i, jnp.float32(value), made)
    return made


def primitives(fields):
    density, mx, my, mz, energy = fields
    inverse = 1.0 / density
    ux, uy, uz = mx * inverse, my * inverse, mz * inverse
    pressure = PRESSURE_FACTOR * (energy - 0.5 * (mx * ux + my * uy + mz * uz))
    return (mx, my, mz), (ux, uy, uz), pressure, energy + pressure


def flux(parts, direction):
    moments, speeds, pressure, enthalpy = parts
    speed = speeds[direction]
    made = [moments[direction]]
    for axis in range(3):
        term = moments[axis] * speed
        made.append(term + pressure if axis == direction else term)
    made.append(enthalpy * speed)
    return made


def face_kernel(two_sided, where_ref, source_ref, windows_ref, left_ref, right_ref, *rest):
    windows, _, planes, layers, cells = windows_ref.shape
    wall_refs, scratch, sems = rest[:-2], rest[-2], rest[-1]
    copies = [
        pltpu.make_async_copy(source_ref.at[w], windows_ref.at[w], sems.at[w])
        for w in range(windows)
    ]
    for copy in copies:
        copy.start()
    tile = (layers, cells)
    up = [
        row_weights(tile, [weight(j - layers - i) for i in range(layers)]) for j in range(layers)
    ]
    down = [
        row_weights(tile, [weight(layers + j - i) for i in range(layers)]) for j in range(layers)
    ]
    if two_sided:
        tables = (up, down)
    else:
        first = where_ref[0] == 0
        tables = ([jnp.where(first, u, d) for u, d in zip(up, down)],)
    for w in range(windows):
        copies[w].wait()
        for x in range(planes):
            parts = primitives([windows_ref[w, f, x] for f in range(5)])
            for f, value in enumerate(flux(parts, 0)):
                scratch[f, x] = value
            for f, value in enumerate(flux(parts, 1)):
                for ref, table in zip(wall_refs, tables):
                    total = None
                    for j in range(layers):
                        term = table[j] * value[j : j + 1, :]
                        total = term if total is None else total + term
                    ref[w, f, x] = total
        for f in range(5):
            for i in range(REACH):
                total = None
                for j in range(planes):
                    c = weight(j - planes - i)
                    if c:
                        term = c * scratch[f, j]
                        total = term if total is None else total + term
                left_ref[w, f, i] = total
                total = None
                for j in range(planes):
                    c = weight(j + REACH - i)
                    if c:
                        term = c * scratch[f, j]
                        total = term if total is None else total + term
                right_ref[w, f, i] = total


def paired_face_kernel(
    where_ref, source_ref, windows_ref, left_ref, right_ref, near_ref, later_ref,
    scratch, lows, sems,
):
    windows, _, planes, layers, cells = windows_ref.shape
    copies = [
        pltpu.make_async_copy(source_ref.at[w], windows_ref.at[w], sems.at[w])
        for w in range(windows)
    ]
    for copy in copies:
        copy.start()
    tile = (layers, cells)
    first = where_ref[0] == 0
    table = [
        jnp.where(
            first,
            row_weights(tile, [weight(j - layers - i) for i in range(layers)]),
            row_weights(tile, [weight(layers + j - i) for i in range(layers)]),
        )
        for j in range(layers)
    ]
    half = planes // 2
    for w in range(windows):
        copies[w].wait()
        for group, group_ref in enumerate((near_ref, later_ref)):
            base = half * (1 - where_ref[0] if group else where_ref[0])
            upper = [[] for _ in range(5)]
            lower = [[] for _ in range(5)]
            for x in range(half):
                parts = primitives([windows_ref[w, f, base + x] for f in range(5)])
                for f, value in enumerate(flux(parts, 0)):
                    scratch[f, base + x] = value
                for f, value in enumerate(flux(parts, 1)):
                    total = None
                    for j in range(layers):
                        term = table[j] * value[j : j + 1, :]
                        total = term if total is None else total + term
                    high = total.astype(jnp.bfloat16).astype(jnp.float32)
                    rest = total - high
                    upper[f].append(high)
                    lower[f].append(jnp.where(first, rest[0:2], rest[2:4]))
            for f in range(5):
                group_ref[f, 16 * w : 16 * w + 16] = jnp.concatenate(upper[f], axis=0).astype(
                    jnp.bfloat16
                )
                lows[group, f, 8 * w : 8 * w + 8] = jnp.concatenate(lower[f], axis=0)
        for f in range(5):
            for i in range(REACH):
                total = None
                for j in range(planes):
                    c = weight(j - planes - i)
                    if c:
                        term = c * scratch[f, j]
                        total = term if total is None else total + term
                left_ref[w, f, i] = total
                total = None
                for j in range(planes):
                    c = weight(j + REACH - i)
                    if c:
                        term = c * scratch[f, j]
                        total = term if total is None else total + term
                right_ref[w, f, i] = total
    for group, group_ref in enumerate((near_ref, later_ref)):
        for f in range(5):
            group_ref[f, 32:48] = lows[group, f].astype(jnp.bfloat16)


def inner_part(windows_ref, part_ref, scratch):
    windows, _, planes, layers, cells = windows_ref.shape
    tile = (windows * layers, cells)
    walls = {
        k: row_weights(
            tile, [weight(k) if 0 <= i + k < layers else 0.0 for i in range(layers)] * windows
        )
        for k in range(-REACH, REACH + 1)
        if 0 < abs(k) < layers
    }
    for x in range(planes):
        fields = [
            jnp.concatenate([windows_ref[w, f, x] for w in range(windows)], axis=0)
            for f in range(5)
        ]
        parts = primitives(fields)
        for f, value in enumerate(flux(parts, 0)):
            scratch[f, x] = value
        flux_y, flux_z = flux(parts, 1), flux(parts, 2)
        for f in range(5):
            total = fields[f]
            for k, line in walls.items():
                total = total + line * pltpu.roll(flux_y[f], -k % tile[0], 0)
            for k in range(1, REACH + 1):
                total = total + weight(k) * (
                    pltpu.roll(flux_z[f], cells - k, 1) - pltpu.roll(flux_z[f], k, 1)
                )
            scratch[5 + f, x] = total
    for f in range(5):
        for x in range(planes):
            total = scratch[5 + f, x]
            for k in range(-REACH, REACH + 1):
                if k and 0 <= x + k < planes:
                    total = total + weight(k) * scratch[f, x + k]
            for w in range(windows):
                part_ref[w, f, x] = total[layers * w : layers * (w + 1)]


def gram_blocks(basis_ref, chunks, per_chunk, right, left):
    half = left.shape[0]
    for c in chunks:
        rows = jnp.concatenate(
            [modes_of(basis_ref, t) for t in range(c * per_chunk, (c + 1) * per_chunk)], axis=1
        )
        right = right + lax.dot_general(
            rows, rows[half:], NT, preferred_element_type=jnp.float32
        )
        left = left + lax.dot_general(
            rows[:half], rows[:half], NT, preferred_element_type=jnp.float32
        )
    return right, left


def inner_gram_kernel(
    early, windows_ref, basis_ref, part_ref, right_ref, left_ref, kept_ref, scratch, sems
):
    chunks = sems.shape[0]
    per_chunk = kept_ref.shape[1] // chunks
    copies = []
    for c in range(chunks):
        span = pl.ds(c * per_chunk, per_chunk)
        copies.append(
            pltpu.make_async_copy(basis_ref.at[:, span], kept_ref.at[:, span], sems.at[c])
        )
        copies[c].start()
    inner_part(windows_ref, part_ref, scratch)
    right, left = jnp.zeros(right_ref.shape, jnp.float32), jnp.zeros(left_ref.shape, jnp.float32)
    for c in range(chunks):
        copies[c].wait()
        if c < early:
            right, left = gram_blocks(kept_ref, [c], per_chunk, right, left)
    right_ref[...] = right
    left_ref[...] = left


def gram_kernel(early, chunks, _, right_ref, left_ref, basis_ref, gram_ref, total):
    modes, tiles = basis_ref.shape[:2]
    wide = modes * 8
    half = wide // 2
    right, left = gram_blocks(
        basis_ref, range(early, chunks), tiles // chunks, right_ref[...], left_ref[...]
    )
    tiles_left = half // LANES
    turned = right[0:half].T
    for tile in range(tiles_left):
        span = slice(tile * LANES, (tile + 1) * LANES)
        total[tile, 0:half] = left[:, span]
        total[tile, half:] = turned[:, span]
        total[tiles_left + tile] = right[:, span]
    rows = folded(total, modes)
    lanes = gram_ref.shape[1]
    picks = (
        lax.broadcasted_iota(jnp.int32, (wide, lanes), 0) // 8
        == lax.broadcasted_iota(jnp.int32, (wide, lanes), 1)
    ).astype(jnp.float32)
    gram_ref[...] = jnp.dot(rows, picks, precision=HIGHEST, preferred_element_type=jnp.float32)


def join_kernel(walls, part_ref, left_ref, right_ref, *rest):
    wall_refs, next_ref = rest[:walls], rest[walls]
    windows, _, planes, layers, cells = part_ref.shape
    for w in range(windows):
        for f in range(5):
            for x in range(planes):
                total = part_ref[w, f, x]
                for ref in wall_refs:
                    total = total + ref[w, f, x]
                if x < REACH:
                    total = total + left_ref[w, f, x]
                if x >= planes - REACH:
                    total = total + right_ref[w, f, x - planes + REACH]
                next_ref[w, f, x] = total


def paired_join_kernel(
    own, where_ref, _, part_ref, left_ref, right_ref, group_ref, made, snaps_ref
):
    windows, _, planes, layers, cells = part_ref.shape
    half = planes // 2
    first = where_ref[0] == 0
    base = half * (where_ref[0] if own else 1 - where_ref[0])
    ahead = base == 0
    zero = jnp.zeros((2, cells), jnp.float32)
    for w in range(windows):
        for f in range(5):
            upper = group_ref[f, 16 * w : 16 * w + 16].astype(jnp.float32)
            lower = group_ref[f, 32:48].astype(jnp.float32)[8 * w : 8 * w + 8]
            done = []
            for x in range(half):
                rest_now = lower[2 * x : 2 * x + 2]
                total = part_ref[w, f, base + x] + (
                    upper[layers * x : layers * x + layers]
                    + jnp.where(
                        first,
                        jnp.concatenate([zero, rest_now], axis=0),
                        jnp.concatenate([rest_now, zero], axis=0),
                    )
                )
                total = total + jnp.where(ahead, left_ref[w, f, x], right_ref[w, f, x])
                made[w, f, x] = total
                done.append(total)
            snaps_ref[w, f] = jnp.concatenate(done, axis=0).astype(jnp.bfloat16)


def same_layer(shape):
    rows = lax.broadcasted_iota(jnp.int32, shape, 0)
    columns = lax.broadcasted_iota(jnp.int32, shape, 1)
    return lax.rem(rows, 8) == lax.rem(columns, 8)


def folded(total, modes):
    kept = lax.rem(lax.broadcasted_iota(jnp.int32, (modes, LANES), 1), 8)
    made = []
    for tile in range(total.shape[0]):
        rows = jnp.zeros((modes, LANES), jnp.float32)
        for y in range(8):
            rows = jnp.where(kept == y, total[tile, pl.ds(y, modes, 8), :], rows)
        made.append(rows)
    return made[0] if len(made) == 1 else jnp.concatenate(made, axis=1)


def modes_of(basis_ref, t):
    modes, _, layers, cells = basis_ref.shape
    return basis_ref[:, t].reshape(modes * layers, cells)


def project_kernel(paired, where_ref, *rest):
    if paired:
        (
            own_ref, got_ref, next_own_ref, next_given_ref, basis_ref,
            sums_ref, snaps_ref, next_ref, square, wide_sums, sems,
        ) = rest
        first = where_ref[0] == 0
        half = next_own_ref.shape[2]
        copies = []
        for i, (source, base) in enumerate(
            ((next_own_ref, half * where_ref[0]), (next_given_ref, half * (1 - where_ref[0])))
        ):
            copies.append(
                pltpu.make_async_copy(source, next_ref.at[:, :, pl.ds(base, half)], sems.at[i])
            )
            copies[i].start()
        for w in range(own_ref.shape[0]):
            for f in range(own_ref.shape[1]):
                own = own_ref[w, f].astype(jnp.float32)
                got = got_ref[w, f].astype(jnp.float32)
                low = jnp.where(first, own, got)
                high = jnp.where(first, got, own)
                for t in range(4):
                    snaps_ref[4 * f + t, pl.ds(8 * w, 8)] = jnp.concatenate(
                        [low[4 * t : 4 * t + 4], high[4 * t : 4 * t + 4]], axis=0
                    ).astype(jnp.bfloat16)
    else:
        snaps_ref, basis_ref, sums_ref, square, wide_sums = rest
        copies = []
    modes, tiles = basis_ref.shape[:2]
    columns = snaps_ref.shape[1]
    total = jnp.zeros((modes * 8, columns), jnp.float32)
    small = jnp.zeros((columns, columns), jnp.float32)
    for t in range(tiles):
        snaps = snaps_ref[t]
        total = total + lax.dot_general(
            modes_of(basis_ref, t), snaps, NT, preferred_element_type=jnp.float32
        )
        small = small + lax.dot_general(snaps, snaps, NT, preferred_element_type=jnp.float32)
    wide_sums[0, :, 0:columns] = total
    square[...] = jnp.zeros_like(square)
    square[0:modes, :] = folded(wide_sums, modes)
    kept = jnp.where(same_layer(small.shape), small, 0.0)
    square[modes : modes + 1, 0:columns] = jnp.sum(kept[0:8], axis=0, keepdims=True)
    square[modes + 1 : modes + 2, 0:columns] = jnp.sum(kept[8:16], axis=0, keepdims=True)
    lanes = lax.broadcasted_iota(jnp.int32, square.shape, 1)
    turned = jnp.where(lanes < columns, square[...], 0.0).T
    sums = jnp.concatenate(
        [
            jnp.sum(turned[0:8], axis=0, keepdims=True),
            jnp.sum(turned[8:16], axis=0, keepdims=True),
        ],
        axis=0,
    )
    sums_ref[...] = jnp.concatenate(
        [sums, jnp.zeros((6, sums.shape[1]), jnp.float32)], axis=0
    )
    for copy in copies:
        copy.wait()


def merge_kernel(gram_ref, far_ref, sums_ref, merged_ref):
    modes = gram_ref.shape[0]
    merged_ref[0:modes] = gram_ref[...] + far_ref[...]
    merged_ref[modes:] = sums_ref[...]


def inverse_kernel(sums_ref, inverse_ref, spread_ref, plain, scaled):
    modes = inverse_ref.shape[0]
    rows = lax.broadcasted_iota(jnp.int32, (8, 2 * modes), 0)
    lanes = lax.broadcasted_iota(jnp.int32, (8, 2 * modes), 1)
    tiles = []
    for tile in range(modes // 8):
        eye = (lanes == rows + (modes + 8 * tile)).astype(jnp.float32)
        tiles.append(jnp.where(lanes < modes, sums_ref[8 * tile : 8 * tile + 8, :], eye))
    count = modes // 8
    for home in range(count):
        columns = [
            [
                jnp.broadcast_to(
                    tiles[tile][:, 8 * home + j : 8 * home + j + 1], (8, 2 * modes)
                )
                for tile in range(home, count)
            ]
            for j in range(8)
        ]
        for j in range(8):
            k = 8 * home + j
            inverse = 1.0 / columns[j][0]
            inverse = inverse[j : j + 1, :]
            row = tiles[home][j : j + 1, :]
            ready = row * inverse
            plain[k : k + 1, :] = row
            scaled[k : k + 1, :] = ready
            factors = [jnp.where(rows > j, columns[j][0], 0.0)] + columns[j][1:]
            for later in range(j + 1, 8):
                share = columns[j][0][later : later + 1, :] * inverse
                columns[later] = [c - f * share for c, f in zip(columns[later], factors)]
            for tile in range(home, count):
                tiles[tile] = tiles[tile] - factors[tile - home] * ready
    exact = functools.partial(
        lax.dot_general, precision=HIGHEST, preferred_element_type=jnp.float32
    )
    plainly = (((1,), (0,)), ((), ()))
    inverse = exact(plain[:, modes:], scaled[:, modes:], (((0,), (0,)), ((), ())))
    square = (modes, modes)
    eye = lax.broadcasted_iota(jnp.int32, square, 0) == lax.broadcasted_iota(jnp.int32, square, 1)
    off = eye.astype(jnp.float32) - exact(sums_ref[0:modes, 0:modes], inverse, plainly)
    inverse = inverse + exact(inverse, off, plainly)
    inverse_ref[...] = inverse
    wide = spread_ref.shape[1]
    spread = (
        lax.broadcasted_iota(jnp.int32, (modes, wide), 1) // 8
        == lax.broadcasted_iota(jnp.int32, (modes, wide), 0)
    ).astype(jnp.float32)
    spread_ref[...] = exact(inverse, spread, plainly)


def finish_kernel(
    rows_total, projected_ref, sums_ref, inverse_ref, spread_ref, snaps_ref, basis_ref,
    modes_ref, solved_ref, factor_ref, made, sems,
):
    modes, tiles, _, cells = basis_ref.shape
    wide = modes * 8
    exact = functools.partial(jnp.dot, precision=HIGHEST, preferred_element_type=jnp.float32)
    projected = projected_ref[modes : modes + 8, 0:modes]
    lines = exact(projected, spread_ref[...])
    full = jnp.concatenate(
        [jnp.broadcast_to(lines[0:1], (8, wide)), jnp.broadcast_to(lines[1:2], (8, wide))],
        axis=0,
    )
    full = jnp.where(same_layer(full.shape), full, 0.0)
    upper = full.astype(jnp.bfloat16)
    fit = jnp.concatenate([upper, (full - upper.astype(jnp.float32)).astype(jnp.bfloat16)], axis=0)
    solved = exact(projected, inverse_ref[...])
    left = projected - exact(solved, sums_ref[0:modes, 0:modes])

    def inner(p, i, q, j):
        return jnp.sum(p[i : i + 1] * q[j : j + 1], axis=1, keepdims=True)

    def entry(i, j):
        square = projected_ref[modes + i : modes + i + 1, modes + j : modes + j + 1]
        return square - inner(projected, i, solved, j) - inner(solved, i, left, j)

    first = jnp.sqrt(entry(0, 0))
    below = entry(1, 0) / first
    second = jnp.sqrt(entry(1, 1) - below * below)
    scaling = jnp.sqrt(jnp.float32(rows_total))
    w00 = scaling / first
    w11 = scaling / second
    w01 = -(below / first) * w11
    solved_ref[...] = solved[0:2]
    factor_ref[0:1, 0:1] = first / scaling
    factor_ref[0:1, 1:2] = below / scaling
    factor_ref[1:2, 0:1] = jnp.zeros_like(first)
    factor_ref[1:2, 1:2] = second / scaling
    chunks = sems.shape[0]
    per_chunk = tiles // chunks
    copies = []
    for c in range(chunks):
        for t in range(c * per_chunk, (c + 1) * per_chunk):
            fitted = jnp.dot(fit, modes_of(basis_ref, t), preferred_element_type=jnp.float32)
            fitted = fitted[0:16] + fitted[16:32]
            snaps = snaps_ref[t].astype(jnp.float32)
            left_over = snaps - fitted
            made[0, t] = left_over[0:8] * w00
            made[1, t] = left_over[8:16] * w11 + left_over[0:8] * w01
        span = pl.ds(c * per_chunk, per_chunk)
        copies.append(
            pltpu.make_async_copy(made.at[:, span], modes_ref.at[:, span], sems.at[c])
        )
        copies[c].start()
    for copy in copies:
        copy.wait()


def params(mib):
    return pltpu.CompilerParams(vmem_limit_bytes=mib * 1024 * 1024)


def cost(flops, moved):
    return pl.CostEstimate(flops=flops, bytes_accessed=moved, transcendentals=0)


WHOLE = pl.BlockSpec(memory_space=pltpu.VMEM)
FAR = pl.BlockSpec(memory_space=pltpu.HBM)
LOOSE = pl.BlockSpec(memory_space=pl.ANY)
SCALAR = pl.BlockSpec(memory_space=pltpu.SMEM)


def swap_added(value, axis, bit):
    count = lax.axis_size(axis)
    return value + lax.ppermute(value, axis, [(i, i ^ bit) for i in range(count)])


def bits(count):
    made = [1 << k for k in range(count.bit_length() - 1)]
    if count != 1 << len(made):
        raise ValueError("axis size")
    return made


def body(windows, pod_basis):
    f32, bf16 = jnp.float32, jnp.bfloat16
    shape = jax.ShapeDtypeStruct
    count, fields, planes, layers, cells = windows.shape
    ring, walls = lax.axis_size("solver"), lax.axis_size("analysis")
    paired = walls == 2 and planes == 8 and layers == 4
    place = lax.axis_index("analysis").astype(jnp.int32).reshape(1)
    modes, _, pod_planes, pod_layers, _ = pod_basis.shape
    tiles = fields * pod_planes * (pod_layers // 8)
    basis = pod_basis.reshape(modes, tiles, 8, cells)
    wide = modes * 8
    basis_bytes = basis.size * 2

    to_right = [(i, (i + 1) % ring) for i in range(ring)]
    to_left = [((i + 1) % ring, i) for i in range(ring)]
    edge_shape = shape((count, fields, REACH, layers, cells), f32)
    face_scratch = [pltpu.VMEM((fields, planes, layers, cells), f32)]
    face_cost = cost(10_000_000, 10 * windows.size)
    if paired:
        swap = [(0, 1), (1, 0)]
        group_shape = shape((fields, 48, cells), bf16)
        kept, to_next, to_last, near_group, later_group = pl.pallas_call(
            paired_face_kernel,
            out_shape=[shape(windows.shape, f32)] + [edge_shape] * 2 + [group_shape] * 2,
            in_specs=[SCALAR, FAR],
            out_specs=[WHOLE] * 5,
            scratch_shapes=face_scratch
            + [pltpu.VMEM((2, fields, 16, cells), f32), pltpu.SemaphoreType.DMA((count,))],
            compiler_params=params(16),
            cost_estimate=face_cost,
            name="faces",
        )(place, windows)
        near_group = lax.ppermute(near_group, "analysis", swap)
        from_left = lax.ppermute(to_next, "solver", to_right)
        from_right = lax.ppermute(to_last, "solver", to_left)
        later_group = lax.ppermute(later_group, "analysis", swap)
    else:
        kept, to_next, to_last, up, down = pl.pallas_call(
            functools.partial(face_kernel, True),
            out_shape=[shape(windows.shape, f32)]
            + [edge_shape] * 2
            + [shape(windows.shape, f32)] * 2,
            in_specs=[SCALAR, FAR],
            out_specs=[WHOLE] * 5,
            scratch_shapes=face_scratch + [pltpu.SemaphoreType.DMA((count,))],
            compiler_params=params(16),
            cost_estimate=face_cost,
            name="faces",
        )(place, windows)
        wall_terms = [
            lax.ppermute(up, "analysis", [(i, i + 1) for i in range(walls - 1)]),
            lax.ppermute(down, "analysis", [(i + 1, i) for i in range(walls - 1)]),
        ]
        from_left = lax.ppermute(to_next, "solver", to_right)
        from_right = lax.ppermute(to_last, "solver", to_left)

    early = 2
    gram_flops = 2 * wide * wide * cells * tiles
    inner, right, left, basis = pl.pallas_call(
        functools.partial(inner_gram_kernel, early),
        out_shape=[
            shape(windows.shape, f32),
            shape((wide, wide // 2), f32),
            shape((wide // 2, wide // 2), f32),
            shape(basis.shape, bf16),
        ],
        in_specs=[WHOLE, FAR],
        out_specs=[WHOLE] * 4,
        scratch_shapes=[
            pltpu.VMEM((2 * fields, planes, count * layers, cells), f32),
            pltpu.SemaphoreType.DMA((fields,)),
        ],
        compiler_params=params(40),
        cost_estimate=cost(gram_flops // 2, 2 * basis_bytes),
        name="inner_gram",
    )(kept, basis)

    def rest_of_gram(after):
        return pl.pallas_call(
            functools.partial(gram_kernel, early, fields),
            out_shape=shape((modes, LANES), f32),
            in_specs=[LOOSE] + [WHOLE] * 3,
            out_specs=WHOLE,
            scratch_shapes=[pltpu.VMEM((wide // LANES, wide, LANES), f32)],
            compiler_params=params(24),
            cost_estimate=cost(gram_flops // 2, basis_bytes),
            name="gram",
        )(after, right, left, basis)

    join_cost = cost(1_000_000, 16 * windows.size)
    if paired:
        half_shape = (count, fields, planes * layers // 2, cells)

        half_next = shape((count, fields, planes // 2, layers, cells), f32)

        def join(own, after, group):
            return pl.pallas_call(
                functools.partial(paired_join_kernel, own),
                out_shape=[half_next, shape(half_shape, bf16)],
                in_specs=[SCALAR, LOOSE] + [WHOLE] * 4,
                out_specs=[WHOLE] * 2,
                compiler_params=params(16),
                cost_estimate=join_cost,
                name="join_own" if own else "join_given",
            )(place, after, inner, from_left, from_right, group)

        next_given, given = join(False, place, near_group)
        got = lax.ppermute(given, "analysis", swap)
        gram = rest_of_gram(given)
    else:
        next_windows = pl.pallas_call(
            functools.partial(join_kernel, 2),
            out_shape=shape(windows.shape, f32),
            in_specs=[WHOLE] * 5,
            out_specs=WHOLE,
            compiler_params=params(16),
            cost_estimate=join_cost,
            name="join",
        )(inner, from_left, from_right, *wall_terms)
        gram = rest_of_gram(place)
    ring_bits = bits(ring)
    lone = ring_bits.pop(1 if len(ring_bits) > 1 else 0)
    gram_far = lax.ppermute(gram, "solver", [(i, i ^ lone) for i in range(ring)])
    if paired:
        next_own, own = join(True, gram, later_group)

    sums_shape = shape((8, LANES), f32)
    snaps_shape = shape((tiles, 2 * 8, cells), bf16)
    scratch = [pltpu.VMEM((LANES, LANES), f32), pltpu.VMEM((1, wide, LANES), f32)]
    project_cost = cost(2 * wide * 16 * cells * tiles, basis_bytes)
    if paired:
        sums, snaps, next_windows = pl.pallas_call(
            functools.partial(project_kernel, True),
            out_shape=[sums_shape, snaps_shape, shape(windows.shape, f32)],
            in_specs=[SCALAR] + [WHOLE] * 5,
            out_specs=[WHOLE, WHOLE, FAR],
            scratch_shapes=scratch + [pltpu.SemaphoreType.DMA((2,))],
            compiler_params=params(16),
            cost_estimate=project_cost,
            name="project",
        )(place, own, got, next_own, next_given, basis)
    else:
        relaid = lax.all_to_all(
            next_windows.astype(bf16), "analysis", split_axis=2, concat_axis=3, tiled=True
        )
        snaps = relaid.reshape(count, tiles, 8, cells).transpose(1, 0, 2, 3)
        snaps = snaps.reshape(tiles, count * 8, cells)
        sums = pl.pallas_call(
            functools.partial(project_kernel, False),
            out_shape=sums_shape,
            in_specs=[SCALAR] + [WHOLE] * 2,
            out_specs=WHOLE,
            scratch_shapes=scratch,
            compiler_params=params(16),
            cost_estimate=project_cost,
            name="project",
        )(place, snaps, basis)
    sums = pl.pallas_call(
        merge_kernel,
        out_shape=shape((modes + 8, LANES), f32),
        in_specs=[WHOLE] * 3,
        out_specs=WHOLE,
        compiler_params=params(16),
        cost_estimate=cost(10_000, 8 * modes * LANES),
        name="merge",
    )(gram, gram_far, sums)
    for bit in bits(walls):
        sums = swap_added(sums, "analysis", bit)
    for bit in ring_bits:
        sums = swap_added(sums, "solver", bit)
    inverse, spread = pl.pallas_call(
        inverse_kernel,
        out_shape=[shape((modes, modes), f32), shape((modes, wide), f32)],
        in_specs=[WHOLE],
        out_specs=[WHOLE] * 2,
        scratch_shapes=[pltpu.VMEM((modes, 2 * modes), f32)] * 2,
        compiler_params=params(16),
        cost_estimate=cost(20_000_000, 8 * modes * modes),
        name="inverse",
    )(sums)
    projected = swap_added(sums, "solver", lone)

    rows_total = ring * walls * tiles * 8 * cells
    new_modes, solved, factor = pl.pallas_call(
        functools.partial(finish_kernel, rows_total),
        out_shape=[
            shape((count, tiles, 8, cells), f32),
            shape((count, modes), f32),
            shape((count, count), f32),
        ],
        in_specs=[WHOLE] * 6,
        out_specs=[FAR, WHOLE, WHOLE],
        scratch_shapes=[
            pltpu.VMEM((count, tiles, 8, cells), f32),
            pltpu.SemaphoreType.DMA((fields,)),
        ],
        compiler_params=params(16),
        cost_estimate=cost(2 * wide * 32 * cells * tiles, basis_bytes + 8 * windows.size),
        name="finish",
    )(projected, sums, inverse, spread, snaps, basis)
    new_modes = new_modes.reshape(count, fields, pod_planes, pod_layers, cells)
    return next_windows, solved, new_modes, factor


def solution(mesh):
    in_specs = (
        P(None, None, "solver", "analysis", None),
        P(None, None, ("solver", "analysis"), None, None),
    )
    out_specs = (
        P(None, None, "solver", "analysis", None),
        P(),
        P(None, None, ("solver", "analysis"), None, None),
        P(),
    )
    return jax.shard_map(body, mesh=mesh, in_specs=in_specs, out_specs=out_specs, check_vma=False)
```

```python
import functools

import jax
import jax.numpy as jnp
from jax import lax
from jax.experimental import pallas as pl
from jax.experimental.pallas import tpu as pltpu
from jax.sharding import PartitionSpec as P

PRESSURE_FACTOR = 1.4 - 1.0
SECTION_STEP = 0.25
CENTRAL_WEIGHTS = (0.8, -0.2, 4.0 / 105.0, -1.0 / 280.0)
REACH = 4
LANES = 128
HIGHEST = lax.Precision.HIGHEST
NT = (((1,), (1,)), ((), ()))


def weight(k):
    if k == 0 or abs(k) > REACH:
        return 0.0
    value = -SECTION_STEP * CENTRAL_WEIGHTS[abs(k) - 1]
    return value if k > 0 else -value


def row_weights(shape, values):
    rows = lax.broadcasted_iota(jnp.int32, shape, len(shape) - 2)
    made = jnp.full(shape, values[0], jnp.float32)
    for i, value in enumerate(values[1:], start=1):
        made = jnp.where(rows == i, jnp.float32(value), made)
    return made


def primitives(fields):
    density, mx, my, mz, energy = fields
    inverse = 1.0 / density
    ux, uy, uz = mx * inverse, my * inverse, mz * inverse
    pressure = PRESSURE_FACTOR * (energy - 0.5 * (mx * ux + my * uy + mz * uz))
    return (mx, my, mz), (ux, uy, uz), pressure, energy + pressure


def flux(parts, direction):
    moments, speeds, pressure, enthalpy = parts
    speed = speeds[direction]
    made = [moments[direction]]
    for axis in range(3):
        term = moments[axis] * speed
        made.append(term + pressure if axis == direction else term)
    made.append(enthalpy * speed)
    return made


def face_kernel(two_sided, where_ref, source_ref, windows_ref, left_ref, right_ref, *rest):
    windows, _, planes, layers, cells = windows_ref.shape
    wall_refs, scratch, sems = rest[:-2], rest[-2], rest[-1]
    copies = [
        pltpu.make_async_copy(source_ref.at[w], windows_ref.at[w], sems.at[w])
        for w in range(windows)
    ]
    for copy in copies:
        copy.start()
    tile = (layers, cells)
    up = [
        row_weights(tile, [weight(j - layers - i) for i in range(layers)]) for j in range(layers)
    ]
    down = [
        row_weights(tile, [weight(layers + j - i) for i in range(layers)]) for j in range(layers)
    ]
    if two_sided:
        tables = (up, down)
    else:
        first = where_ref[0] == 0
        tables = ([jnp.where(first, u, d) for u, d in zip(up, down)],)
    for w in range(windows):
        copies[w].wait()
        for x in range(planes):
            parts = primitives([windows_ref[w, f, x] for f in range(5)])
            for f, value in enumerate(flux(parts, 0)):
                scratch[f, x] = value
            for f, value in enumerate(flux(parts, 1)):
                for ref, table in zip(wall_refs, tables):
                    total = None
                    for j in range(layers):
                        term = table[j] * value[j : j + 1, :]
                        total = term if total is None else total + term
                    ref[w, f, x] = total
        for f in range(5):
            for i in range(REACH):
                total = None
                for j in range(planes):
                    c = weight(j - planes - i)
                    if c:
                        term = c * scratch[f, j]
                        total = term if total is None else total + term
                left_ref[w, f, i] = total
                total = None
                for j in range(planes):
                    c = weight(j + REACH - i)
                    if c:
                        term = c * scratch[f, j]
                        total = term if total is None else total + term
                right_ref[w, f, i] = total


def wall_group(where_ref, windows_ref, group_ref, lows, base, keep_x):
    windows, _, planes, layers, cells = windows_ref.shape
    tile = (layers, cells)
    first = where_ref[0] == 0
    table = [
        jnp.where(
            first,
            row_weights(tile, [weight(j - layers - i) for i in range(layers)]),
            row_weights(tile, [weight(layers + j - i) for i in range(layers)]),
        )
        for j in range(layers)
    ]
    for w in range(windows):
        upper = [[] for _ in range(5)]
        lower = [[] for _ in range(5)]
        for x in range(planes // 2):
            parts = primitives([windows_ref[w, f, base + x] for f in range(5)])
            keep_x(w, base + x, parts)
            for f, value in enumerate(flux(parts, 1)):
                total = None
                for j in range(layers):
                    term = table[j] * value[j : j + 1, :]
                    total = term if total is None else total + term
                high = total.astype(jnp.bfloat16).astype(jnp.float32)
                rest = total - high
                upper[f].append(high)
                lower[f].append(jnp.where(first, rest[0:2], rest[2:4]))
        for f in range(5):
            group_ref[f, 16 * w : 16 * w + 16] = jnp.concatenate(upper[f], axis=0).astype(
                jnp.bfloat16
            )
            lows[f, 8 * w : 8 * w + 8] = jnp.concatenate(lower[f], axis=0)
    for f in range(5):
        group_ref[f, 32:48] = lows[f].astype(jnp.bfloat16)


def near_kernel(where_ref, source_ref, group_ref, kept_ref, lows, sem):
    copy = pltpu.make_async_copy(source_ref, kept_ref, sem)
    copy.start()
    base = source_ref.shape[2] // 2 * where_ref[0]
    wall_group(where_ref, source_ref, group_ref, lows, base, lambda w, x, parts: None)
    copy.wait()


def later_kernel(where_ref, _, windows_ref, group_ref, left_ref, right_ref, scratch, lows):
    windows, _, planes, layers, cells = windows_ref.shape
    half = planes // 2

    def keep_x(w, x, parts):
        for f, value in enumerate(flux(parts, 0)):
            scratch[w, f, x] = value

    base = half * (1 - where_ref[0])
    wall_group(where_ref, windows_ref, group_ref, lows, base, keep_x)
    for w in range(windows):
        for x in range(half):
            plane = half * where_ref[0] + x
            keep_x(w, plane, primitives([windows_ref[w, f, plane] for f in range(5)]))
        for f in range(5):
            for i in range(REACH):
                for ref, offset in ((left_ref, -planes), (right_ref, REACH)):
                    total = None
                    for j in range(planes):
                        c = weight(j + offset - i)
                        if c:
                            term = c * scratch[w, f, j]
                            total = term if total is None else total + term
                    ref[w, f, i] = total


def inner_part(windows_ref, part_ref, scratch):
    windows, _, planes, layers, cells = windows_ref.shape
    tile = (windows * layers, cells)
    walls = {
        k: row_weights(
            tile, [weight(k) if 0 <= i + k < layers else 0.0 for i in range(layers)] * windows
        )
        for k in range(-REACH, REACH + 1)
        if 0 < abs(k) < layers
    }
    for x in range(planes):
        fields = [
            jnp.concatenate([windows_ref[w, f, x] for w in range(windows)], axis=0)
            for f in range(5)
        ]
        parts = primitives(fields)
        for f, value in enumerate(flux(parts, 0)):
            scratch[f, x] = value
        flux_y, flux_z = flux(parts, 1), flux(parts, 2)
        for f in range(5):
            total = fields[f]
            for k, line in walls.items():
                total = total + line * pltpu.roll(flux_y[f], -k % tile[0], 0)
            for k in range(1, REACH + 1):
                total = total + weight(k) * (
                    pltpu.roll(flux_z[f], cells - k, 1) - pltpu.roll(flux_z[f], k, 1)
                )
            scratch[5 + f, x] = total
    for f in range(5):
        for x in range(planes):
            total = scratch[5 + f, x]
            for k in range(-REACH, REACH + 1):
                if k and 0 <= x + k < planes:
                    total = total + weight(k) * scratch[f, x + k]
            for w in range(windows):
                part_ref[w, f, x] = total[layers * w : layers * (w + 1)]


def gram_blocks(basis_ref, chunks, per_chunk, right, left):
    half = left.shape[0]
    for c in chunks:
        rows = jnp.concatenate(
            [modes_of(basis_ref, t) for t in range(c * per_chunk, (c + 1) * per_chunk)], axis=1
        )
        right = right + lax.dot_general(
            rows, rows[half:], NT, preferred_element_type=jnp.float32
        )
        left = left + lax.dot_general(
            rows[:half], rows[:half], NT, preferred_element_type=jnp.float32
        )
    return right, left


def inner_kernel(windows_ref, basis_ref, part_ref, kept_ref, scratch, sems):
    chunks = sems.shape[0]
    per_chunk = kept_ref.shape[1] // chunks
    copies = []
    for c in range(chunks):
        span = pl.ds(c * per_chunk, per_chunk)
        copies.append(
            pltpu.make_async_copy(basis_ref.at[:, span], kept_ref.at[:, span], sems.at[c])
        )
        copies[c].start()
    inner_part(windows_ref, part_ref, scratch)
    for copy in copies:
        copy.wait()


def early_gram_kernel(early, chunks, _, basis_ref, right_ref, left_ref):
    right, left = gram_blocks(
        basis_ref,
        range(early),
        basis_ref.shape[1] // chunks,
        jnp.zeros(right_ref.shape, jnp.float32),
        jnp.zeros(left_ref.shape, jnp.float32),
    )
    right_ref[...] = right
    left_ref[...] = left


def gram_kernel(early, chunks, _, right_ref, left_ref, basis_ref, gram_ref, total):
    modes, tiles = basis_ref.shape[:2]
    wide = modes * 8
    half = wide // 2
    right, left = gram_blocks(
        basis_ref, range(early, chunks), tiles // chunks, right_ref[...], left_ref[...]
    )
    tiles_left = half // LANES
    turned = right[0:half].T
    for tile in range(tiles_left):
        span = slice(tile * LANES, (tile + 1) * LANES)
        total[tile, 0:half] = left[:, span]
        total[tile, half:] = turned[:, span]
        total[tiles_left + tile] = right[:, span]
    rows = folded(total, modes)
    picks = (
        lax.broadcasted_iota(jnp.int32, (wide, modes), 0) // 8
        == lax.broadcasted_iota(jnp.int32, (wide, modes), 1)
    ).astype(jnp.float32)
    gram = jnp.dot(rows, picks, precision=HIGHEST, preferred_element_type=jnp.float32)
    gram_ref[:, 0:modes] = gram[0 : modes // 2]
    gram_ref[:, modes:] = gram[modes // 2 :]


def join_kernel(walls, part_ref, left_ref, right_ref, *rest):
    wall_refs, next_ref = rest[:walls], rest[walls]
    windows, _, planes, layers, cells = part_ref.shape
    for w in range(windows):
        for f in range(5):
            for x in range(planes):
                total = part_ref[w, f, x]
                for ref in wall_refs:
                    total = total + ref[w, f, x]
                if x < REACH:
                    total = total + left_ref[w, f, x]
                if x >= planes - REACH:
                    total = total + right_ref[w, f, x - planes + REACH]
                next_ref[w, f, x] = total


def paired_join_kernel(
    own, where_ref, _, part_ref, left_ref, right_ref, group_ref, made, snaps_ref
):
    windows, _, planes, layers, cells = part_ref.shape
    half = planes // 2
    first = where_ref[0] == 0
    base = half * (where_ref[0] if own else 1 - where_ref[0])
    ahead = base == 0
    zero = jnp.zeros((2, cells), jnp.float32)
    for w in range(windows):
        for f in range(5):
            upper = group_ref[f, 16 * w : 16 * w + 16].astype(jnp.float32)
            lower = group_ref[f, 32:48].astype(jnp.float32)[8 * w : 8 * w + 8]
            done = []
            for x in range(half):
                rest_now = lower[2 * x : 2 * x + 2]
                total = part_ref[w, f, base + x] + (
                    upper[layers * x : layers * x + layers]
                    + jnp.where(
                        first,
                        jnp.concatenate([zero, rest_now], axis=0),
                        jnp.concatenate([rest_now, zero], axis=0),
                    )
                )
                total = total + jnp.where(ahead, left_ref[w, f, x], right_ref[w, f, x])
                made[w, f, x] = total
                done.append(total)
            snaps_ref[w, f] = jnp.concatenate(done, axis=0).astype(jnp.bfloat16)


def same_layer(shape):
    rows = lax.broadcasted_iota(jnp.int32, shape, 0)
    columns = lax.broadcasted_iota(jnp.int32, shape, 1)
    return lax.rem(rows, 8) == lax.rem(columns, 8)


def folded(total, modes):
    kept = lax.rem(lax.broadcasted_iota(jnp.int32, (modes, LANES), 1), 8)
    made = []
    for tile in range(total.shape[0]):
        rows = jnp.zeros((modes, LANES), jnp.float32)
        for y in range(8):
            rows = jnp.where(kept == y, total[tile, pl.ds(y, modes, 8), :], rows)
        made.append(rows)
    return made[0] if len(made) == 1 else jnp.concatenate(made, axis=1)


def modes_of(basis_ref, t):
    modes, _, layers, cells = basis_ref.shape
    return basis_ref[:, t].reshape(modes * layers, cells)


def project_kernel(paired, where_ref, *rest):
    if paired:
        (
            own_ref, got_ref, next_own_ref, next_given_ref, basis_ref,
            sums_ref, snaps_ref, next_ref, square, wide_sums, sems,
        ) = rest
        first = where_ref[0] == 0
        half = next_own_ref.shape[2]
        copies = []
        for i, (source, base) in enumerate(
            ((next_own_ref, half * where_ref[0]), (next_given_ref, half * (1 - where_ref[0])))
        ):
            copies.append(
                pltpu.make_async_copy(source, next_ref.at[:, :, pl.ds(base, half)], sems.at[i])
            )
            copies[i].start()
        for w in range(own_ref.shape[0]):
            for f in range(own_ref.shape[1]):
                own = own_ref[w, f].astype(jnp.float32)
                got = got_ref[w, f].astype(jnp.float32)
                low = jnp.where(first, own, got)
                high = jnp.where(first, got, own)
                for t in range(4):
                    snaps_ref[4 * f + t, pl.ds(8 * w, 8)] = jnp.concatenate(
                        [low[4 * t : 4 * t + 4], high[4 * t : 4 * t + 4]], axis=0
                    ).astype(jnp.bfloat16)
    else:
        snaps_ref, basis_ref, sums_ref, square, wide_sums = rest
        copies = []
    modes, tiles = basis_ref.shape[:2]
    columns = snaps_ref.shape[1]
    total = jnp.zeros((modes * 8, columns), jnp.float32)
    small = jnp.zeros((columns, columns), jnp.float32)
    for t in range(tiles):
        snaps = snaps_ref[t]
        total = total + lax.dot_general(
            modes_of(basis_ref, t), snaps, NT, preferred_element_type=jnp.float32
        )
        small = small + lax.dot_general(snaps, snaps, NT, preferred_element_type=jnp.float32)
    wide_sums[0, :, 0:columns] = total
    square[...] = jnp.zeros_like(square)
    square[0:modes, :] = folded(wide_sums, modes)
    kept = jnp.where(same_layer(small.shape), small, 0.0)
    square[modes : modes + 1, 0:columns] = jnp.sum(kept[0:8], axis=0, keepdims=True)
    square[modes + 1 : modes + 2, 0:columns] = jnp.sum(kept[8:16], axis=0, keepdims=True)
    lanes = lax.broadcasted_iota(jnp.int32, square.shape, 1)
    turned = jnp.where(lanes < columns, square[...], 0.0).T
    sums = jnp.concatenate(
        [
            jnp.sum(turned[0:8], axis=0, keepdims=True),
            jnp.sum(turned[8:16], axis=0, keepdims=True),
        ],
        axis=0,
    )
    sums_ref[...] = jnp.concatenate(
        [sums, jnp.zeros((6, sums.shape[1]), jnp.float32)], axis=0
    )
    for copy in copies:
        copy.wait()


def merge_kernel(gram_ref, far_ref, sums_ref, merged_ref):
    rows = gram_ref.shape[0]
    merged_ref[0:rows] = gram_ref[...] + far_ref[...]
    merged_ref[rows:] = sums_ref[...]


def unpacked(sums_ref, modes):
    half = modes // 2
    return jnp.concatenate([sums_ref[0:half, 0:modes], sums_ref[0:half, modes:]], axis=0)


def inverse_kernel(sums_ref, inverse_ref, spread_ref, plain, scaled):
    modes = inverse_ref.shape[0]
    rows = lax.broadcasted_iota(jnp.int32, (8, 2 * modes), 0)
    lanes = lax.broadcasted_iota(jnp.int32, (8, 2 * modes), 1)
    tiles = []
    gram = unpacked(sums_ref, modes)
    for tile in range(modes // 8):
        eye = (lanes == rows + (modes + 8 * tile)).astype(jnp.float32)
        start = 8 * tile % (modes // 2)
        line = sums_ref[start : start + 8, :]
        if 8 * tile >= modes // 2:
            line = pltpu.roll(line, modes, 1)
        tiles.append(jnp.where(lanes < modes, line, eye))
    count = modes // 8
    for home in range(count):
        columns = [
            [
                jnp.broadcast_to(
                    tiles[tile][:, 8 * home + j : 8 * home + j + 1], (8, 2 * modes)
                )
                for tile in range(home, count)
            ]
            for j in range(8)
        ]
        for j in range(8):
            k = 8 * home + j
            inverse = 1.0 / columns[j][0]
            inverse = inverse[j : j + 1, :]
            row = tiles[home][j : j + 1, :]
            ready = row * inverse
            plain[k : k + 1, :] = row
            scaled[k : k + 1, :] = ready
            factors = [jnp.where(rows > j, columns[j][0], 0.0)] + columns[j][1:]
            for later in range(j + 1, 8):
                share = columns[j][0][later : later + 1, :] * inverse
                columns[later] = [c - f * share for c, f in zip(columns[later], factors)]
            for tile in range(home, count):
                tiles[tile] = tiles[tile] - factors[tile - home] * ready
    exact = functools.partial(
        lax.dot_general, precision=HIGHEST, preferred_element_type=jnp.float32
    )
    plainly = (((1,), (0,)), ((), ()))
    inverse = exact(plain[:, modes:], scaled[:, modes:], (((0,), (0,)), ((), ())))
    square = (modes, modes)
    eye = lax.broadcasted_iota(jnp.int32, square, 0) == lax.broadcasted_iota(jnp.int32, square, 1)
    off = eye.astype(jnp.float32) - exact(gram, inverse, plainly)
    inverse = inverse + exact(inverse, off, plainly)
    inverse_ref[...] = inverse
    wide = spread_ref.shape[1]
    spread = (
        lax.broadcasted_iota(jnp.int32, (modes, wide), 1) // 8
        == lax.broadcasted_iota(jnp.int32, (modes, wide), 0)
    ).astype(jnp.float32)
    spread_ref[...] = exact(inverse, spread, plainly)


def finish_kernel(
    rows_total, projected_ref, sums_ref, inverse_ref, spread_ref, snaps_ref, basis_ref,
    modes_ref, solved_ref, factor_ref, made, sems,
):
    modes, tiles, _, cells = basis_ref.shape
    wide = modes * 8
    exact = functools.partial(jnp.dot, precision=HIGHEST, preferred_element_type=jnp.float32)
    base = modes // 2
    projected = projected_ref[base : base + 8, 0:modes]
    lines = exact(projected, spread_ref[...])
    full = jnp.concatenate(
        [jnp.broadcast_to(lines[0:1], (8, wide)), jnp.broadcast_to(lines[1:2], (8, wide))],
        axis=0,
    )
    full = jnp.where(same_layer(full.shape), full, 0.0)
    upper = full.astype(jnp.bfloat16)
    fit = jnp.concatenate([upper, (full - upper.astype(jnp.float32)).astype(jnp.bfloat16)], axis=0)
    solved = exact(projected, inverse_ref[...])
    left = projected - exact(solved, unpacked(sums_ref, modes))

    def inner(p, i, q, j):
        return jnp.sum(p[i : i + 1] * q[j : j + 1], axis=1, keepdims=True)

    def entry(i, j):
        square = projected_ref[base + i : base + i + 1, modes + j : modes + j + 1]
        return square - inner(projected, i, solved, j) - inner(solved, i, left, j)

    first = jnp.sqrt(entry(0, 0))
    below = entry(1, 0) / first
    second = jnp.sqrt(entry(1, 1) - below * below)
    scaling = jnp.sqrt(jnp.float32(rows_total))
    w00 = scaling / first
    w11 = scaling / second
    w01 = -(below / first) * w11
    solved_ref[...] = solved[0:2]
    factor_ref[0:1, 0:1] = first / scaling
    factor_ref[0:1, 1:2] = below / scaling
    factor_ref[1:2, 0:1] = jnp.zeros_like(first)
    factor_ref[1:2, 1:2] = second / scaling
    chunks = sems.shape[0]
    per_chunk = tiles // chunks
    copies = []
    for c in range(chunks):
        for t in range(c * per_chunk, (c + 1) * per_chunk):
            fitted = jnp.dot(fit, modes_of(basis_ref, t), preferred_element_type=jnp.float32)
            fitted = fitted[0:16] + fitted[16:32]
            snaps = snaps_ref[t].astype(jnp.float32)
            left_over = snaps - fitted
            made[0, t] = left_over[0:8] * w00
            made[1, t] = left_over[8:16] * w11 + left_over[0:8] * w01
        span = pl.ds(c * per_chunk, per_chunk)
        copies.append(
            pltpu.make_async_copy(made.at[:, span], modes_ref.at[:, span], sems.at[c])
        )
        copies[c].start()
    for copy in copies:
        copy.wait()


def params(mib):
    return pltpu.CompilerParams(vmem_limit_bytes=mib * 1024 * 1024)


def cost(flops, moved):
    return pl.CostEstimate(flops=flops, bytes_accessed=moved, transcendentals=0)


WHOLE = pl.BlockSpec(memory_space=pltpu.VMEM)
FAR = pl.BlockSpec(memory_space=pltpu.HBM)
LOOSE = pl.BlockSpec(memory_space=pl.ANY)
SCALAR = pl.BlockSpec(memory_space=pltpu.SMEM)


def swap_added(value, axis, bit):
    count = lax.axis_size(axis)
    return value + lax.ppermute(value, axis, [(i, i ^ bit) for i in range(count)])


def bits(count):
    made = [1 << k for k in range(count.bit_length() - 1)]
    if count != 1 << len(made):
        raise ValueError("axis size")
    return made


def body(windows, pod_basis):
    f32, bf16 = jnp.float32, jnp.bfloat16
    shape = jax.ShapeDtypeStruct
    count, fields, planes, layers, cells = windows.shape
    ring, walls = lax.axis_size("solver"), lax.axis_size("analysis")
    paired = walls == 2 and planes == 8 and layers == 4
    place = lax.axis_index("analysis").astype(jnp.int32).reshape(1)
    modes, _, pod_planes, pod_layers, _ = pod_basis.shape
    tiles = fields * pod_planes * (pod_layers // 8)
    basis = pod_basis.reshape(modes, tiles, 8, cells)
    wide = modes * 8
    basis_bytes = basis.size * 2

    to_right = [(i, (i + 1) % ring) for i in range(ring)]
    to_left = [((i + 1) % ring, i) for i in range(ring)]
    edge_shape = shape((count, fields, REACH, layers, cells), f32)
    face_scratch = [pltpu.VMEM((fields, planes, layers, cells), f32)]
    face_cost = cost(10_000_000, 10 * windows.size)
    if paired:
        swap = [(0, 1), (1, 0)]
        group_shape = shape((fields, 48, cells), bf16)
        lows = pltpu.VMEM((fields, 16, cells), f32)
        near_group, kept = pl.pallas_call(
            near_kernel,
            out_shape=[group_shape, shape(windows.shape, f32)],
            in_specs=[SCALAR, WHOLE],
            out_specs=[WHOLE] * 2,
            scratch_shapes=[lows, pltpu.SemaphoreType.DMA],
            compiler_params=params(16),
            cost_estimate=face_cost,
            name="near_faces",
        )(place, windows)
        later_group, to_next, to_last = pl.pallas_call(
            later_kernel,
            out_shape=[group_shape] + [edge_shape] * 2,
            in_specs=[SCALAR, LOOSE, WHOLE],
            out_specs=[WHOLE] * 3,
            scratch_shapes=[pltpu.VMEM((count, fields, planes, layers, cells), f32), lows],
            compiler_params=params(16),
            cost_estimate=face_cost,
            name="later_faces",
        )(place, near_group, kept)
        near_group = lax.ppermute(near_group, "analysis", swap)
        from_left = lax.ppermute(to_next, "solver", to_right)
        from_right = lax.ppermute(to_last, "solver", to_left)
        later_group = lax.ppermute(later_group, "analysis", swap)
    else:
        kept, to_next, to_last, up, down = pl.pallas_call(
            functools.partial(face_kernel, True),
            out_shape=[shape(windows.shape, f32)]
            + [edge_shape] * 2
            + [shape(windows.shape, f32)] * 2,
            in_specs=[SCALAR, FAR],
            out_specs=[WHOLE] * 5,
            scratch_shapes=face_scratch + [pltpu.SemaphoreType.DMA((count,))],
            compiler_params=params(16),
            cost_estimate=face_cost,
            name="faces",
        )(place, windows)
        wall_terms = [
            lax.ppermute(up, "analysis", [(i, i + 1) for i in range(walls - 1)]),
            lax.ppermute(down, "analysis", [(i + 1, i) for i in range(walls - 1)]),
        ]
        from_left = lax.ppermute(to_next, "solver", to_right)
        from_right = lax.ppermute(to_last, "solver", to_left)

    early = 2
    gram_flops = 2 * wide * wide * cells * tiles
    inner, basis = pl.pallas_call(
        inner_kernel,
        out_shape=[shape(windows.shape, f32), shape(basis.shape, bf16)],
        in_specs=[WHOLE, FAR],
        out_specs=[WHOLE] * 2,
        scratch_shapes=[
            pltpu.VMEM((2 * fields, planes, count * layers, cells), f32),
            pltpu.SemaphoreType.DMA((fields,)),
        ],
        compiler_params=params(40),
        cost_estimate=cost(1_000_000, windows.size),
        name="inner",
    )(kept, basis)
    right, left = pl.pallas_call(
        functools.partial(early_gram_kernel, early, fields),
        out_shape=[shape((wide, wide // 2), f32), shape((wide // 2, wide // 2), f32)],
        in_specs=[LOOSE, WHOLE],
        out_specs=[WHOLE] * 2,
        compiler_params=params(24),
        cost_estimate=cost(gram_flops // 2, basis_bytes),
        name="early_gram",
    )(near_group if paired else place, basis)

    def rest_of_gram(after):
        return pl.pallas_call(
            functools.partial(gram_kernel, early, fields),
            out_shape=shape((modes // 2, 2 * modes), f32),
            in_specs=[LOOSE] + [WHOLE] * 3,
            out_specs=WHOLE,
            scratch_shapes=[pltpu.VMEM((wide // LANES, wide, LANES), f32)],
            compiler_params=params(24),
            cost_estimate=cost(gram_flops // 2, basis_bytes),
            name="gram",
        )(after, right, left, basis)

    join_cost = cost(1_000_000, 16 * windows.size)
    if paired:
        half_shape = (count, fields, planes * layers // 2, cells)

        half_next = shape((count, fields, planes // 2, layers, cells), f32)

        def join(own, after, group):
            return pl.pallas_call(
                functools.partial(paired_join_kernel, own),
                out_shape=[half_next, shape(half_shape, bf16)],
                in_specs=[SCALAR, LOOSE] + [WHOLE] * 4,
                out_specs=[WHOLE] * 2,
                compiler_params=params(16),
                cost_estimate=join_cost,
                name="join_own" if own else "join_given",
            )(place, after, inner, from_left, from_right, group)

        next_given, given = join(False, place, near_group)
        got = lax.ppermute(given, "analysis", swap)
        gram = rest_of_gram(given)
    else:
        next_windows = pl.pallas_call(
            functools.partial(join_kernel, 2),
            out_shape=shape(windows.shape, f32),
            in_specs=[WHOLE] * 5,
            out_specs=WHOLE,
            compiler_params=params(16),
            cost_estimate=join_cost,
            name="join",
        )(inner, from_left, from_right, *wall_terms)
        gram = rest_of_gram(place)
    ring_bits = bits(ring)
    lone = ring_bits.pop(1 if len(ring_bits) > 1 else 0)
    gram_far = lax.ppermute(gram, "solver", [(i, i ^ lone) for i in range(ring)])
    if paired:
        next_own, own = join(True, gram, later_group)

    sums_shape = shape((8, LANES), f32)
    snaps_shape = shape((tiles, 2 * 8, cells), bf16)
    scratch = [pltpu.VMEM((LANES, LANES), f32), pltpu.VMEM((1, wide, LANES), f32)]
    project_cost = cost(2 * wide * 16 * cells * tiles, basis_bytes)
    if paired:
        sums, snaps, next_windows = pl.pallas_call(
            functools.partial(project_kernel, True),
            out_shape=[sums_shape, snaps_shape, shape(windows.shape, f32)],
            in_specs=[SCALAR] + [WHOLE] * 5,
            out_specs=[WHOLE, WHOLE, FAR],
            scratch_shapes=scratch + [pltpu.SemaphoreType.DMA((2,))],
            compiler_params=params(16),
            cost_estimate=project_cost,
            name="project",
        )(place, own, got, next_own, next_given, basis)
    else:
        relaid = lax.all_to_all(
            next_windows.astype(bf16), "analysis", split_axis=2, concat_axis=3, tiled=True
        )
        snaps = relaid.reshape(count, tiles, 8, cells).transpose(1, 0, 2, 3)
        snaps = snaps.reshape(tiles, count * 8, cells)
        sums = pl.pallas_call(
            functools.partial(project_kernel, False),
            out_shape=sums_shape,
            in_specs=[SCALAR] + [WHOLE] * 2,
            out_specs=WHOLE,
            scratch_shapes=scratch,
            compiler_params=params(16),
            cost_estimate=project_cost,
            name="project",
        )(place, snaps, basis)
    sums = pl.pallas_call(
        merge_kernel,
        out_shape=shape((modes // 2 + 8, LANES), f32),
        in_specs=[WHOLE] * 3,
        out_specs=WHOLE,
        compiler_params=params(16),
        cost_estimate=cost(10_000, 8 * modes * LANES),
        name="merge",
    )(gram, gram_far, sums)
    for bit in bits(walls):
        sums = swap_added(sums, "analysis", bit)
    for bit in ring_bits:
        sums = swap_added(sums, "solver", bit)
    inverse, spread = pl.pallas_call(
        inverse_kernel,
        out_shape=[shape((modes, modes), f32), shape((modes, wide), f32)],
        in_specs=[WHOLE],
        out_specs=[WHOLE] * 2,
        scratch_shapes=[pltpu.VMEM((modes, 2 * modes), f32)] * 2,
        compiler_params=params(16),
        cost_estimate=cost(20_000_000, 8 * modes * modes),
        name="inverse",
    )(sums)
    projected = swap_added(sums, "solver", lone)

    rows_total = ring * walls * tiles * 8 * cells
    new_modes, solved, factor = pl.pallas_call(
        functools.partial(finish_kernel, rows_total),
        out_shape=[
            shape((count, tiles, 8, cells), f32),
            shape((count, modes), f32),
            shape((count, count), f32),
        ],
        in_specs=[WHOLE] * 6,
        out_specs=[FAR, WHOLE, WHOLE],
        scratch_shapes=[
            pltpu.VMEM((count, tiles, 8, cells), f32),
            pltpu.SemaphoreType.DMA((fields,)),
        ],
        compiler_params=params(16),
        cost_estimate=cost(2 * wide * 32 * cells * tiles, basis_bytes + 8 * windows.size),
        name="finish",
    )(projected, sums, inverse, spread, snaps, basis)
    new_modes = new_modes.reshape(count, fields, pod_planes, pod_layers, cells)
    return next_windows, solved, new_modes, factor


def solution(mesh):
    in_specs = (
        P(None, None, "solver", "analysis", None),
        P(None, None, ("solver", "analysis"), None, None),
    )
    out_specs = (
        P(None, None, "solver", "analysis", None),
        P(),
        P(None, None, ("solver", "analysis"), None, None),
        P(),
    )
    return jax.shard_map(body, mesh=mesh, in_specs=in_specs, out_specs=out_specs, check_vma=False)
```

```python
import functools

import jax
import jax.numpy as jnp
from jax import lax
from jax.experimental import pallas as pl
from jax.experimental.pallas import tpu as pltpu
from jax.sharding import PartitionSpec as P

PRESSURE_FACTOR = 1.4 - 1.0
SECTION_STEP = 0.25
CENTRAL_WEIGHTS = (0.8, -0.2, 4.0 / 105.0, -1.0 / 280.0)
REACH = 4
LANES = 128
HIGHEST = lax.Precision.HIGHEST
NT = (((1,), (1,)), ((), ()))


def weight(k):
    if k == 0 or abs(k) > REACH:
        return 0.0
    value = -SECTION_STEP * CENTRAL_WEIGHTS[abs(k) - 1]
    return value if k > 0 else -value


def row_weights(shape, values):
    rows = lax.broadcasted_iota(jnp.int32, shape, len(shape) - 2)
    made = jnp.full(shape, values[0], jnp.float32)
    for i, value in enumerate(values[1:], start=1):
        made = jnp.where(rows == i, jnp.float32(value), made)
    return made


def primitives(fields):
    density, mx, my, mz, energy = fields
    inverse = 1.0 / density
    ux, uy, uz = mx * inverse, my * inverse, mz * inverse
    pressure = PRESSURE_FACTOR * (energy - 0.5 * (mx * ux + my * uy + mz * uz))
    return (mx, my, mz), (ux, uy, uz), pressure, energy + pressure


def flux(parts, direction):
    moments, speeds, pressure, enthalpy = parts
    speed = speeds[direction]
    made = [moments[direction]]
    for axis in range(3):
        term = moments[axis] * speed
        made.append(term + pressure if axis == direction else term)
    made.append(enthalpy * speed)
    return made


def face_kernel(two_sided, where_ref, source_ref, windows_ref, left_ref, right_ref, *rest):
    windows, _, planes, layers, cells = windows_ref.shape
    wall_refs, scratch, sems = rest[:-2], rest[-2], rest[-1]
    copies = [
        pltpu.make_async_copy(source_ref.at[w], windows_ref.at[w], sems.at[w])
        for w in range(windows)
    ]
    for copy in copies:
        copy.start()
    tile = (layers, cells)
    up = [
        row_weights(tile, [weight(j - layers - i) for i in range(layers)]) for j in range(layers)
    ]
    down = [
        row_weights(tile, [weight(layers + j - i) for i in range(layers)]) for j in range(layers)
    ]
    if two_sided:
        tables = (up, down)
    else:
        first = where_ref[0] == 0
        tables = ([jnp.where(first, u, d) for u, d in zip(up, down)],)
    for w in range(windows):
        copies[w].wait()
        for x in range(planes):
            parts = primitives([windows_ref[w, f, x] for f in range(5)])
            for f, value in enumerate(flux(parts, 0)):
                scratch[f, x] = value
            for f, value in enumerate(flux(parts, 1)):
                for ref, table in zip(wall_refs, tables):
                    total = None
                    for j in range(layers):
                        term = table[j] * value[j : j + 1, :]
                        total = term if total is None else total + term
                    ref[w, f, x] = total
        for f in range(5):
            for i in range(REACH):
                total = None
                for j in range(planes):
                    c = weight(j - planes - i)
                    if c:
                        term = c * scratch[f, j]
                        total = term if total is None else total + term
                left_ref[w, f, i] = total
                total = None
                for j in range(planes):
                    c = weight(j + REACH - i)
                    if c:
                        term = c * scratch[f, j]
                        total = term if total is None else total + term
                right_ref[w, f, i] = total


def wall_group(where_ref, windows_ref, group_ref, lows, base, keep_x):
    windows, _, planes, layers, cells = windows_ref.shape
    tile = (layers, cells)
    first = where_ref[0] == 0
    table = [
        jnp.where(
            first,
            row_weights(tile, [weight(j - layers - i) for i in range(layers)]),
            row_weights(tile, [weight(layers + j - i) for i in range(layers)]),
        )
        for j in range(layers)
    ]
    for w in range(windows):
        upper = [[] for _ in range(5)]
        lower = [[] for _ in range(5)]
        for x in range(planes // 2):
            parts = primitives([windows_ref[w, f, base + x] for f in range(5)])
            keep_x(w, base + x, parts)
            for f, value in enumerate(flux(parts, 1)):
                total = None
                for j in range(layers):
                    term = table[j] * value[j : j + 1, :]
                    total = term if total is None else total + term
                high = total.astype(jnp.bfloat16).astype(jnp.float32)
                rest = total - high
                upper[f].append(high)
                lower[f].append(jnp.where(first, rest[0:2], rest[2:4]))
        for f in range(5):
            group_ref[f, 16 * w : 16 * w + 16] = jnp.concatenate(upper[f], axis=0).astype(
                jnp.bfloat16
            )
            lows[f, 8 * w : 8 * w + 8] = jnp.concatenate(lower[f], axis=0)
    for f in range(5):
        group_ref[f, 32:48] = lows[f].astype(jnp.bfloat16)


def near_kernel(where_ref, source_ref, group_ref, kept_ref, lows, sem):
    copy = pltpu.make_async_copy(source_ref, kept_ref, sem)
    copy.start()
    base = source_ref.shape[2] // 2 * where_ref[0]
    wall_group(where_ref, source_ref, group_ref, lows, base, lambda w, x, parts: None)
    copy.wait()


def later_kernel(where_ref, _, windows_ref, group_ref, left_ref, right_ref, scratch, lows):
    windows, _, planes, layers, cells = windows_ref.shape
    half = planes // 2

    def keep_x(w, x, parts):
        for f, value in enumerate(flux(parts, 0)):
            scratch[w, f, x] = value

    base = half * (1 - where_ref[0])
    wall_group(where_ref, windows_ref, group_ref, lows, base, keep_x)
    for w in range(windows):
        for x in range(half):
            plane = half * where_ref[0] + x
            keep_x(w, plane, primitives([windows_ref[w, f, plane] for f in range(5)]))
        for f in range(5):
            for i in range(REACH):
                for ref, offset in ((left_ref, -planes), (right_ref, REACH)):
                    total = None
                    for j in range(planes):
                        c = weight(j + offset - i)
                        if c:
                            term = c * scratch[w, f, j]
                            total = term if total is None else total + term
                    ref[w, f, i] = total


def inner_part(windows_ref, part_ref, scratch):
    windows, _, planes, layers, cells = windows_ref.shape
    tile = (windows * layers, cells)
    walls = {
        k: row_weights(
            tile, [weight(k) if 0 <= i + k < layers else 0.0 for i in range(layers)] * windows
        )
        for k in range(-REACH, REACH + 1)
        if 0 < abs(k) < layers
    }
    for x in range(planes):
        fields = [
            jnp.concatenate([windows_ref[w, f, x] for w in range(windows)], axis=0)
            for f in range(5)
        ]
        parts = primitives(fields)
        for f, value in enumerate(flux(parts, 0)):
            scratch[f, x] = value
        flux_y, flux_z = flux(parts, 1), flux(parts, 2)
        for f in range(5):
            total = fields[f]
            for k, line in walls.items():
                total = total + line * pltpu.roll(flux_y[f], -k % tile[0], 0)
            for k in range(1, REACH + 1):
                total = total + weight(k) * (
                    pltpu.roll(flux_z[f], cells - k, 1) - pltpu.roll(flux_z[f], k, 1)
                )
            scratch[5 + f, x] = total
    for f in range(5):
        for x in range(planes):
            total = scratch[5 + f, x]
            for k in range(-REACH, REACH + 1):
                if k and 0 <= x + k < planes:
                    total = total + weight(k) * scratch[f, x + k]
            for w in range(windows):
                part_ref[w, f, x] = total[layers * w : layers * (w + 1)]


def gram_blocks(basis_ref, chunks, per_chunk, right, left):
    half = left.shape[0]
    for c in chunks:
        rows = jnp.concatenate(
            [modes_of(basis_ref, t) for t in range(c * per_chunk, (c + 1) * per_chunk)], axis=1
        )
        right = right + lax.dot_general(
            rows, rows[half:], NT, preferred_element_type=jnp.float32
        )
        left = left + lax.dot_general(
            rows[:half], rows[:half], NT, preferred_element_type=jnp.float32
        )
    return right, left


def inner_gram_kernel(
    early, windows_ref, basis_ref, part_ref, right_ref, left_ref, kept_ref, scratch, sems
):
    chunks = sems.shape[0]
    per_chunk = kept_ref.shape[1] // chunks
    copies = []
    for c in range(chunks):
        span = pl.ds(c * per_chunk, per_chunk)
        copies.append(
            pltpu.make_async_copy(basis_ref.at[:, span], kept_ref.at[:, span], sems.at[c])
        )
        copies[c].start()
    inner_part(windows_ref, part_ref, scratch)
    right, left = jnp.zeros(right_ref.shape, jnp.float32), jnp.zeros(left_ref.shape, jnp.float32)
    for c in range(chunks):
        copies[c].wait()
        if c < early:
            right, left = gram_blocks(kept_ref, [c], per_chunk, right, left)
    right_ref[...] = right
    left_ref[...] = left


def gram_kernel(early, chunks, _, right_ref, left_ref, basis_ref, gram_ref, total):
    modes, tiles = basis_ref.shape[:2]
    wide = modes * 8
    half = wide // 2
    right, left = gram_blocks(
        basis_ref, range(early, chunks), tiles // chunks, right_ref[...], left_ref[...]
    )
    tiles_left = half // LANES
    turned = right[0:half].T
    for tile in range(tiles_left):
        span = slice(tile * LANES, (tile + 1) * LANES)
        total[tile, 0:half] = left[:, span]
        total[tile, half:] = turned[:, span]
        total[tiles_left + tile] = right[:, span]
    rows = folded(total, modes)
    picks = (
        lax.broadcasted_iota(jnp.int32, (wide, modes), 0) // 8
        == lax.broadcasted_iota(jnp.int32, (wide, modes), 1)
    ).astype(jnp.float32)
    gram = jnp.dot(rows, picks, precision=HIGHEST, preferred_element_type=jnp.float32)
    gram_ref[:, 0:modes] = gram[0 : modes // 2]
    gram_ref[:, modes:] = gram[modes // 2 :]


def join_kernel(walls, part_ref, left_ref, right_ref, *rest):
    wall_refs, next_ref = rest[:walls], rest[walls]
    windows, _, planes, layers, cells = part_ref.shape
    for w in range(windows):
        for f in range(5):
            for x in range(planes):
                total = part_ref[w, f, x]
                for ref in wall_refs:
                    total = total + ref[w, f, x]
                if x < REACH:
                    total = total + left_ref[w, f, x]
                if x >= planes - REACH:
                    total = total + right_ref[w, f, x - planes + REACH]
                next_ref[w, f, x] = total


def wall_terms_of(first, group_ref, w, f):
    upper = group_ref[f, 16 * w : 16 * w + 16].astype(jnp.float32)
    lower = group_ref[f, 32:48].astype(jnp.float32)[8 * w : 8 * w + 8]
    zero = jnp.zeros((2, upper.shape[1]), jnp.float32)
    made = []
    for x in range(4):
        rest = lower[2 * x : 2 * x + 2]
        rest = jnp.where(
            first, jnp.concatenate([zero, rest], axis=0), jnp.concatenate([rest, zero], axis=0)
        )
        made.append(upper[4 * x : 4 * x + 4] + rest)
    return made


def wall_join_kernel(where_ref, part_ref, group_ref, given_ref):
    windows, _, planes = part_ref.shape[:3]
    base = planes // 2 * (1 - where_ref[0])
    for w in range(windows):
        for f in range(5):
            for x, term in enumerate(wall_terms_of(where_ref[0] == 0, group_ref, w, f)):
                given_ref[w, f, x] = part_ref[w, f, base + x] + term


def edge_join_kernel(where_ref, part_ref, left_ref, right_ref, made, snaps_ref):
    windows, _, half = part_ref.shape[:3]
    ahead = where_ref[0] == 1
    for w in range(windows):
        for f in range(5):
            done = []
            for x in range(half):
                total = part_ref[w, f, x] + jnp.where(ahead, left_ref[w, f, x], right_ref[w, f, x])
                made[w, f, x] = total
                done.append(total)
            snaps_ref[w, f] = jnp.concatenate(done, axis=0).astype(jnp.bfloat16)


def own_join_kernel(where_ref, _, part_ref, left_ref, right_ref, group_ref, made, snaps_ref):
    windows, _, planes = part_ref.shape[:3]
    half = planes // 2
    ahead = where_ref[0] == 0
    base = half * where_ref[0]
    for w in range(windows):
        for f in range(5):
            done = []
            for x, term in enumerate(wall_terms_of(ahead, group_ref, w, f)):
                total = part_ref[w, f, base + x] + term
                total = total + jnp.where(ahead, left_ref[w, f, x], right_ref[w, f, x])
                made[w, f, x] = total
                done.append(total)
            snaps_ref[w, f] = jnp.concatenate(done, axis=0).astype(jnp.bfloat16)


def same_layer(shape):
    rows = lax.broadcasted_iota(jnp.int32, shape, 0)
    columns = lax.broadcasted_iota(jnp.int32, shape, 1)
    return lax.rem(rows, 8) == lax.rem(columns, 8)


def folded(total, modes):
    kept = lax.rem(lax.broadcasted_iota(jnp.int32, (modes, LANES), 1), 8)
    made = []
    for tile in range(total.shape[0]):
        rows = jnp.zeros((modes, LANES), jnp.float32)
        for y in range(8):
            rows = jnp.where(kept == y, total[tile, pl.ds(y, modes, 8), :], rows)
        made.append(rows)
    return made[0] if len(made) == 1 else jnp.concatenate(made, axis=1)


def modes_of(basis_ref, t):
    modes, _, layers, cells = basis_ref.shape
    return basis_ref[:, t].reshape(modes * layers, cells)


def project_kernel(paired, where_ref, *rest):
    if paired:
        (
            own_ref, got_ref, next_own_ref, next_given_ref, basis_ref,
            sums_ref, snaps_ref, next_ref, square, wide_sums, sems,
        ) = rest
        first = where_ref[0] == 0
        half = next_own_ref.shape[2]
        copies = []
        for i, (source, base) in enumerate(
            ((next_own_ref, half * where_ref[0]), (next_given_ref, half * (1 - where_ref[0])))
        ):
            copies.append(
                pltpu.make_async_copy(source, next_ref.at[:, :, pl.ds(base, half)], sems.at[i])
            )
            copies[i].start()
        for w in range(own_ref.shape[0]):
            for f in range(own_ref.shape[1]):
                own = own_ref[w, f].astype(jnp.float32)
                got = got_ref[w, f].astype(jnp.float32)
                low = jnp.where(first, own, got)
                high = jnp.where(first, got, own)
                for t in range(4):
                    snaps_ref[4 * f + t, pl.ds(8 * w, 8)] = jnp.concatenate(
                        [low[4 * t : 4 * t + 4], high[4 * t : 4 * t + 4]], axis=0
                    ).astype(jnp.bfloat16)
    else:
        snaps_ref, basis_ref, sums_ref, square, wide_sums = rest
        copies = []
    modes, tiles = basis_ref.shape[:2]
    columns = snaps_ref.shape[1]
    total = jnp.zeros((modes * 8, columns), jnp.float32)
    small = jnp.zeros((columns, columns), jnp.float32)
    for t in range(tiles):
        snaps = snaps_ref[t]
        total = total + lax.dot_general(
            modes_of(basis_ref, t), snaps, NT, preferred_element_type=jnp.float32
        )
        small = small + lax.dot_general(snaps, snaps, NT, preferred_element_type=jnp.float32)
    wide_sums[0, :, 0:columns] = total
    square[...] = jnp.zeros_like(square)
    square[0:modes, :] = folded(wide_sums, modes)
    kept = jnp.where(same_layer(small.shape), small, 0.0)
    square[modes : modes + 1, 0:columns] = jnp.sum(kept[0:8], axis=0, keepdims=True)
    square[modes + 1 : modes + 2, 0:columns] = jnp.sum(kept[8:16], axis=0, keepdims=True)
    lanes = lax.broadcasted_iota(jnp.int32, square.shape, 1)
    turned = jnp.where(lanes < columns, square[...], 0.0).T
    sums = jnp.concatenate(
        [
            jnp.sum(turned[0:8], axis=0, keepdims=True),
            jnp.sum(turned[8:16], axis=0, keepdims=True),
        ],
        axis=0,
    )
    sums_ref[...] = jnp.concatenate(
        [sums, jnp.zeros((6, sums.shape[1]), jnp.float32)], axis=0
    )
    for copy in copies:
        copy.wait()


def merge_kernel(gram_ref, far_ref, sums_ref, merged_ref):
    rows = gram_ref.shape[0]
    merged_ref[0:rows] = gram_ref[...] + far_ref[...]
    merged_ref[rows:] = sums_ref[...]


def unpacked(sums_ref, modes):
    half = modes // 2
    return jnp.concatenate([sums_ref[0:half, 0:modes], sums_ref[0:half, modes:]], axis=0)


def inverse_kernel(sums_ref, inverse_ref, spread_ref, plain, scaled):
    modes = inverse_ref.shape[0]
    rows = lax.broadcasted_iota(jnp.int32, (8, 2 * modes), 0)
    lanes = lax.broadcasted_iota(jnp.int32, (8, 2 * modes), 1)
    tiles = []
    gram = unpacked(sums_ref, modes)
    for tile in range(modes // 8):
        eye = (lanes == rows + (modes + 8 * tile)).astype(jnp.float32)
        start = 8 * tile % (modes // 2)
        line = sums_ref[start : start + 8, :]
        if 8 * tile >= modes // 2:
            line = pltpu.roll(line, modes, 1)
        tiles.append(jnp.where(lanes < modes, line, eye))
    count = modes // 8
    for home in range(count):
        columns = [
            [
                jnp.broadcast_to(
                    tiles[tile][:, 8 * home + j : 8 * home + j + 1], (8, 2 * modes)
                )
                for tile in range(home, count)
            ]
            for j in range(8)
        ]
        for j in range(8):
            k = 8 * home + j
            inverse = 1.0 / columns[j][0]
            inverse = inverse[j : j + 1, :]
            row = tiles[home][j : j + 1, :]
            ready = row * inverse
            plain[k : k + 1, :] = row
            scaled[k : k + 1, :] = ready
            factors = [jnp.where(rows > j, columns[j][0], 0.0)] + columns[j][1:]
            for later in range(j + 1, 8):
                share = columns[j][0][later : later + 1, :] * inverse
                columns[later] = [c - f * share for c, f in zip(columns[later], factors)]
            for tile in range(home, count):
                tiles[tile] = tiles[tile] - factors[tile - home] * ready
    exact = functools.partial(
        lax.dot_general, precision=HIGHEST, preferred_element_type=jnp.float32
    )
    plainly = (((1,), (0,)), ((), ()))
    inverse = exact(plain[:, modes:], scaled[:, modes:], (((0,), (0,)), ((), ())))
    square = (modes, modes)
    eye = lax.broadcasted_iota(jnp.int32, square, 0) == lax.broadcasted_iota(jnp.int32, square, 1)
    off = eye.astype(jnp.float32) - exact(gram, inverse, plainly)
    inverse = inverse + exact(inverse, off, plainly)
    inverse_ref[...] = inverse
    wide = spread_ref.shape[1]
    spread = (
        lax.broadcasted_iota(jnp.int32, (modes, wide), 1) // 8
        == lax.broadcasted_iota(jnp.int32, (modes, wide), 0)
    ).astype(jnp.float32)
    spread_ref[...] = exact(inverse, spread, plainly)


def finish_kernel(
    rows_total, projected_ref, sums_ref, inverse_ref, spread_ref, snaps_ref, basis_ref,
    modes_ref, solved_ref, factor_ref, made, sems,
):
    modes, tiles, _, cells = basis_ref.shape
    wide = modes * 8
    exact = functools.partial(jnp.dot, precision=HIGHEST, preferred_element_type=jnp.float32)
    base = modes // 2
    projected = projected_ref[base : base + 8, 0:modes]
    lines = exact(projected, spread_ref[...])
    full = jnp.concatenate(
        [jnp.broadcast_to(lines[0:1], (8, wide)), jnp.broadcast_to(lines[1:2], (8, wide))],
        axis=0,
    )
    full = jnp.where(same_layer(full.shape), full, 0.0)
    upper = full.astype(jnp.bfloat16)
    fit = jnp.concatenate([upper, (full - upper.astype(jnp.float32)).astype(jnp.bfloat16)], axis=0)
    solved = exact(projected, inverse_ref[...])
    left = projected - exact(solved, unpacked(sums_ref, modes))

    def inner(p, i, q, j):
        return jnp.sum(p[i : i + 1] * q[j : j + 1], axis=1, keepdims=True)

    def entry(i, j):
        square = projected_ref[base + i : base + i + 1, modes + j : modes + j + 1]
        return square - inner(projected, i, solved, j) - inner(solved, i, left, j)

    first = jnp.sqrt(entry(0, 0))
    below = entry(1, 0) / first
    second = jnp.sqrt(entry(1, 1) - below * below)
    scaling = jnp.sqrt(jnp.float32(rows_total))
    w00 = scaling / first
    w11 = scaling / second
    w01 = -(below / first) * w11
    solved_ref[...] = solved[0:2]
    factor_ref[0:1, 0:1] = first / scaling
    factor_ref[0:1, 1:2] = below / scaling
    factor_ref[1:2, 0:1] = jnp.zeros_like(first)
    factor_ref[1:2, 1:2] = second / scaling
    chunks = sems.shape[0]
    per_chunk = tiles // chunks
    copies = []
    for c in range(chunks):
        for t in range(c * per_chunk, (c + 1) * per_chunk):
            fitted = jnp.dot(fit, modes_of(basis_ref, t), preferred_element_type=jnp.float32)
            fitted = fitted[0:16] + fitted[16:32]
            snaps = snaps_ref[t].astype(jnp.float32)
            left_over = snaps - fitted
            made[0, t] = left_over[0:8] * w00
            made[1, t] = left_over[8:16] * w11 + left_over[0:8] * w01
        span = pl.ds(c * per_chunk, per_chunk)
        copies.append(
            pltpu.make_async_copy(made.at[:, span], modes_ref.at[:, span], sems.at[c])
        )
        copies[c].start()
    for copy in copies:
        copy.wait()


def params(mib):
    return pltpu.CompilerParams(vmem_limit_bytes=mib * 1024 * 1024)


def cost(flops, moved):
    return pl.CostEstimate(flops=flops, bytes_accessed=moved, transcendentals=0)


WHOLE = pl.BlockSpec(memory_space=pltpu.VMEM)
FAR = pl.BlockSpec(memory_space=pltpu.HBM)
LOOSE = pl.BlockSpec(memory_space=pl.ANY)
SCALAR = pl.BlockSpec(memory_space=pltpu.SMEM)


def swap_added(value, axis, bit):
    count = lax.axis_size(axis)
    return value + lax.ppermute(value, axis, [(i, i ^ bit) for i in range(count)])


def bits(count):
    made = [1 << k for k in range(count.bit_length() - 1)]
    if count != 1 << len(made):
        raise ValueError("axis size")
    return made


def body(windows, pod_basis):
    f32, bf16 = jnp.float32, jnp.bfloat16
    shape = jax.ShapeDtypeStruct
    count, fields, planes, layers, cells = windows.shape
    ring, walls = lax.axis_size("solver"), lax.axis_size("analysis")
    paired = walls == 2 and planes == 8 and layers == 4
    place = lax.axis_index("analysis").astype(jnp.int32).reshape(1)
    modes, _, pod_planes, pod_layers, _ = pod_basis.shape
    tiles = fields * pod_planes * (pod_layers // 8)
    basis = pod_basis.reshape(modes, tiles, 8, cells)
    wide = modes * 8
    basis_bytes = basis.size * 2

    to_right = [(i, (i + 1) % ring) for i in range(ring)]
    to_left = [((i + 1) % ring, i) for i in range(ring)]
    edge_shape = shape((count, fields, REACH, layers, cells), f32)
    face_scratch = [pltpu.VMEM((fields, planes, layers, cells), f32)]
    face_cost = cost(10_000_000, 10 * windows.size)
    if paired:
        swap = [(0, 1), (1, 0)]
        group_shape = shape((fields, 48, cells), bf16)
        lows = pltpu.VMEM((fields, 16, cells), f32)
        near_group, kept = pl.pallas_call(
            near_kernel,
            out_shape=[group_shape, shape(windows.shape, f32)],
            in_specs=[SCALAR, WHOLE],
            out_specs=[WHOLE] * 2,
            scratch_shapes=[lows, pltpu.SemaphoreType.DMA],
            compiler_params=params(16),
            cost_estimate=face_cost,
            name="near_faces",
        )(place, windows)
        later_group, to_next, to_last = pl.pallas_call(
            later_kernel,
            out_shape=[group_shape] + [edge_shape] * 2,
            in_specs=[SCALAR, LOOSE, WHOLE],
            out_specs=[WHOLE] * 3,
            scratch_shapes=[pltpu.VMEM((count, fields, planes, layers, cells), f32), lows],
            compiler_params=params(16),
            cost_estimate=face_cost,
            name="later_faces",
        )(place, near_group, kept)
        near_group = lax.ppermute(near_group, "analysis", swap)
        from_left = lax.ppermute(to_next, "solver", to_right)
        from_right = lax.ppermute(to_last, "solver", to_left)
        later_group = lax.ppermute(later_group, "analysis", swap)
    else:
        kept, to_next, to_last, up, down = pl.pallas_call(
            functools.partial(face_kernel, True),
            out_shape=[shape(windows.shape, f32)]
            + [edge_shape] * 2
            + [shape(windows.shape, f32)] * 2,
            in_specs=[SCALAR, FAR],
            out_specs=[WHOLE] * 5,
            scratch_shapes=face_scratch + [pltpu.SemaphoreType.DMA((count,))],
            compiler_params=params(16),
            cost_estimate=face_cost,
            name="faces",
        )(place, windows)
        wall_terms = [
            lax.ppermute(up, "analysis", [(i, i + 1) for i in range(walls - 1)]),
            lax.ppermute(down, "analysis", [(i + 1, i) for i in range(walls - 1)]),
        ]
        from_left = lax.ppermute(to_next, "solver", to_right)
        from_right = lax.ppermute(to_last, "solver", to_left)

    early = 3
    gram_flops = 2 * wide * wide * cells * tiles
    inner, right, left, basis = pl.pallas_call(
        functools.partial(inner_gram_kernel, early),
        out_shape=[
            shape(windows.shape, f32),
            shape((wide, wide // 2), f32),
            shape((wide // 2, wide // 2), f32),
            shape(basis.shape, bf16),
        ],
        in_specs=[WHOLE, FAR],
        out_specs=[WHOLE] * 4,
        scratch_shapes=[
            pltpu.VMEM((2 * fields, planes, count * layers, cells), f32),
            pltpu.SemaphoreType.DMA((fields,)),
        ],
        compiler_params=params(40),
        cost_estimate=cost(1_000_000, windows.size),
        name="inner_gram",
    )(kept, basis)

    def rest_of_gram(after):
        return pl.pallas_call(
            functools.partial(gram_kernel, early, fields),
            out_shape=shape((modes // 2, 2 * modes), f32),
            in_specs=[LOOSE] + [WHOLE] * 3,
            out_specs=WHOLE,
            scratch_shapes=[pltpu.VMEM((wide // LANES, wide, LANES), f32)],
            compiler_params=params(24),
            cost_estimate=cost(gram_flops // 2, basis_bytes),
            name="gram",
        )(after, right, left, basis)

    join_cost = cost(1_000_000, 16 * windows.size)
    if paired:
        half_shape = (count, fields, planes * layers // 2, cells)

        half_next = shape((count, fields, planes // 2, layers, cells), f32)

        inner_given = pl.pallas_call(
            wall_join_kernel,
            out_shape=half_next,
            in_specs=[SCALAR] + [WHOLE] * 2,
            out_specs=WHOLE,
            compiler_params=params(16),
            cost_estimate=cost(gram_flops, 2 * basis_bytes),
            name="wall_join",
        )(place, inner, near_group)
        next_given, given = pl.pallas_call(
            edge_join_kernel,
            out_shape=[half_next, shape(half_shape, bf16)],
            in_specs=[SCALAR] + [WHOLE] * 3,
            out_specs=[WHOLE] * 2,
            compiler_params=params(16),
            cost_estimate=join_cost,
            name="edge_join",
        )(place, inner_given, from_left, from_right)
        got = lax.ppermute(given, "analysis", swap)
        gram = rest_of_gram(given)
    else:
        next_windows = pl.pallas_call(
            functools.partial(join_kernel, 2),
            out_shape=shape(windows.shape, f32),
            in_specs=[WHOLE] * 5,
            out_specs=WHOLE,
            compiler_params=params(16),
            cost_estimate=join_cost,
            name="join",
        )(inner, from_left, from_right, *wall_terms)
        gram = rest_of_gram(place)
    ring_bits = bits(ring)
    lone = ring_bits.pop(1 if len(ring_bits) > 1 else 0)
    gram_far = lax.ppermute(gram, "solver", [(i, i ^ lone) for i in range(ring)])
    if paired:
        next_own, own = pl.pallas_call(
            own_join_kernel,
            out_shape=[half_next, shape(half_shape, bf16)],
            in_specs=[SCALAR, LOOSE] + [WHOLE] * 4,
            out_specs=[WHOLE] * 2,
            compiler_params=params(16),
            cost_estimate=join_cost,
            name="own_join",
        )(place, gram, inner, from_left, from_right, later_group)

    sums_shape = shape((8, LANES), f32)
    snaps_shape = shape((tiles, 2 * 8, cells), bf16)
    scratch = [pltpu.VMEM((LANES, LANES), f32), pltpu.VMEM((1, wide, LANES), f32)]
    project_cost = cost(2 * wide * 16 * cells * tiles, basis_bytes)
    if paired:
        sums, snaps, next_windows = pl.pallas_call(
            functools.partial(project_kernel, True),
            out_shape=[sums_shape, snaps_shape, shape(windows.shape, f32)],
            in_specs=[SCALAR] + [WHOLE] * 5,
            out_specs=[WHOLE, WHOLE, FAR],
            scratch_shapes=scratch + [pltpu.SemaphoreType.DMA((2,))],
            compiler_params=params(16),
            cost_estimate=project_cost,
            name="project",
        )(place, own, got, next_own, next_given, basis)
    else:
        relaid = lax.all_to_all(
            next_windows.astype(bf16), "analysis", split_axis=2, concat_axis=3, tiled=True
        )
        snaps = relaid.reshape(count, tiles, 8, cells).transpose(1, 0, 2, 3)
        snaps = snaps.reshape(tiles, count * 8, cells)
        sums = pl.pallas_call(
            functools.partial(project_kernel, False),
            out_shape=sums_shape,
            in_specs=[SCALAR] + [WHOLE] * 2,
            out_specs=WHOLE,
            scratch_shapes=scratch,
            compiler_params=params(16),
            cost_estimate=project_cost,
            name="project",
        )(place, snaps, basis)
    sums = pl.pallas_call(
        merge_kernel,
        out_shape=shape((modes // 2 + 8, LANES), f32),
        in_specs=[WHOLE] * 3,
        out_specs=WHOLE,
        compiler_params=params(16),
        cost_estimate=cost(10_000, 8 * modes * LANES),
        name="merge",
    )(gram, gram_far, sums)
    for bit in bits(walls):
        sums = swap_added(sums, "analysis", bit)
    for bit in ring_bits:
        sums = swap_added(sums, "solver", bit)
    inverse, spread = pl.pallas_call(
        inverse_kernel,
        out_shape=[shape((modes, modes), f32), shape((modes, wide), f32)],
        in_specs=[WHOLE],
        out_specs=[WHOLE] * 2,
        scratch_shapes=[pltpu.VMEM((modes, 2 * modes), f32)] * 2,
        compiler_params=params(16),
        cost_estimate=cost(20_000_000, 8 * modes * modes),
        name="inverse",
    )(sums)
    projected = swap_added(sums, "solver", lone)

    rows_total = ring * walls * tiles * 8 * cells
    new_modes, solved, factor = pl.pallas_call(
        functools.partial(finish_kernel, rows_total),
        out_shape=[
            shape((count, tiles, 8, cells), f32),
            shape((count, modes), f32),
            shape((count, count), f32),
        ],
        in_specs=[WHOLE] * 6,
        out_specs=[FAR, WHOLE, WHOLE],
        scratch_shapes=[
            pltpu.VMEM((count, tiles, 8, cells), f32),
            pltpu.SemaphoreType.DMA((fields,)),
        ],
        compiler_params=params(16),
        cost_estimate=cost(2 * wide * 32 * cells * tiles, basis_bytes + 8 * windows.size),
        name="finish",
    )(projected, sums, inverse, spread, snaps, basis)
    new_modes = new_modes.reshape(count, fields, pod_planes, pod_layers, cells)
    return next_windows, solved, new_modes, factor


def solution(mesh):
    in_specs = (
        P(None, None, "solver", "analysis", None),
        P(None, None, ("solver", "analysis"), None, None),
    )
    out_specs = (
        P(None, None, "solver", "analysis", None),
        P(),
        P(None, None, ("solver", "analysis"), None, None),
        P(),
    )
    return jax.shard_map(body, mesh=mesh, in_specs=in_specs, out_specs=out_specs, check_vma=False)
```

```python
import functools

import jax
import jax.numpy as jnp
from jax import lax
from jax.experimental import pallas as pl
from jax.experimental.pallas import tpu as pltpu
from jax.sharding import PartitionSpec as P

PRESSURE_FACTOR = 1.4 - 1.0
SECTION_STEP = 0.25
CENTRAL_WEIGHTS = (0.8, -0.2, 4.0 / 105.0, -1.0 / 280.0)
REACH = 4
LANES = 128
HIGHEST = lax.Precision.HIGHEST
NT = (((1,), (1,)), ((), ()))


def weight(k):
    if k == 0 or abs(k) > REACH:
        return 0.0
    value = -SECTION_STEP * CENTRAL_WEIGHTS[abs(k) - 1]
    return value if k > 0 else -value


def row_weights(shape, values):
    rows = lax.broadcasted_iota(jnp.int32, shape, len(shape) - 2)
    made = jnp.full(shape, values[0], jnp.float32)
    for i, value in enumerate(values[1:], start=1):
        made = jnp.where(rows == i, jnp.float32(value), made)
    return made


def primitives(fields):
    density, mx, my, mz, energy = fields
    inverse = 1.0 / density
    ux, uy, uz = mx * inverse, my * inverse, mz * inverse
    pressure = PRESSURE_FACTOR * (energy - 0.5 * (mx * ux + my * uy + mz * uz))
    return (mx, my, mz), (ux, uy, uz), pressure, energy + pressure


def flux(parts, direction):
    moments, speeds, pressure, enthalpy = parts
    speed = speeds[direction]
    made = [moments[direction]]
    for axis in range(3):
        term = moments[axis] * speed
        made.append(term + pressure if axis == direction else term)
    made.append(enthalpy * speed)
    return made


def face_kernel(two_sided, where_ref, source_ref, windows_ref, left_ref, right_ref, *rest):
    windows, _, planes, layers, cells = windows_ref.shape
    wall_refs, scratch, sems = rest[:-2], rest[-2], rest[-1]
    copies = [
        pltpu.make_async_copy(source_ref.at[w], windows_ref.at[w], sems.at[w])
        for w in range(windows)
    ]
    for copy in copies:
        copy.start()
    tile = (layers, cells)
    up = [
        row_weights(tile, [weight(j - layers - i) for i in range(layers)]) for j in range(layers)
    ]
    down = [
        row_weights(tile, [weight(layers + j - i) for i in range(layers)]) for j in range(layers)
    ]
    if two_sided:
        tables = (up, down)
    else:
        first = where_ref[0] == 0
        tables = ([jnp.where(first, u, d) for u, d in zip(up, down)],)
    for w in range(windows):
        copies[w].wait()
        for x in range(planes):
            parts = primitives([windows_ref[w, f, x] for f in range(5)])
            for f, value in enumerate(flux(parts, 0)):
                scratch[f, x] = value
            for f, value in enumerate(flux(parts, 1)):
                for ref, table in zip(wall_refs, tables):
                    total = None
                    for j in range(layers):
                        term = table[j] * value[j : j + 1, :]
                        total = term if total is None else total + term
                    ref[w, f, x] = total
        for f in range(5):
            for i in range(REACH):
                total = None
                for j in range(planes):
                    c = weight(j - planes - i)
                    if c:
                        term = c * scratch[f, j]
                        total = term if total is None else total + term
                left_ref[w, f, i] = total
                total = None
                for j in range(planes):
                    c = weight(j + REACH - i)
                    if c:
                        term = c * scratch[f, j]
                        total = term if total is None else total + term
                right_ref[w, f, i] = total


def wall_group(where_ref, windows_ref, group_ref, lows, base, keep_x):
    windows, _, planes, layers, cells = windows_ref.shape
    tile = (layers, cells)
    first = where_ref[0] == 0
    table = [
        jnp.where(
            first,
            row_weights(tile, [weight(j - layers - i) for i in range(layers)]),
            row_weights(tile, [weight(layers + j - i) for i in range(layers)]),
        )
        for j in range(layers)
    ]
    for w in range(windows):
        upper = [[] for _ in range(5)]
        lower = [[] for _ in range(5)]
        for x in range(planes // 2):
            parts = primitives([windows_ref[w, f, base + x] for f in range(5)])
            keep_x(w, base + x, parts)
            for f, value in enumerate(flux(parts, 1)):
                total = None
                for j in range(layers):
                    term = table[j] * value[j : j + 1, :]
                    total = term if total is None else total + term
                high = total.astype(jnp.bfloat16).astype(jnp.float32)
                rest = total - high
                upper[f].append(high)
                lower[f].append(jnp.where(first, rest[0:2], rest[2:4]))
        for f in range(5):
            group_ref[f, 16 * w : 16 * w + 16] = jnp.concatenate(upper[f], axis=0).astype(
                jnp.bfloat16
            )
            lows[f, 8 * w : 8 * w + 8] = jnp.concatenate(lower[f], axis=0)
    for f in range(5):
        group_ref[f, 32:48] = lows[f].astype(jnp.bfloat16)


def near_kernel(where_ref, source_ref, group_ref, kept_ref, lows, sem):
    copy = pltpu.make_async_copy(source_ref, kept_ref, sem)
    copy.start()
    base = source_ref.shape[2] // 2 * where_ref[0]
    wall_group(where_ref, source_ref, group_ref, lows, base, lambda w, x, parts: None)
    copy.wait()


def later_kernel(where_ref, _, windows_ref, group_ref, left_ref, right_ref, scratch, lows):
    windows, _, planes, layers, cells = windows_ref.shape
    half = planes // 2

    def keep_x(w, x, parts):
        for f, value in enumerate(flux(parts, 0)):
            scratch[w, f, x] = value

    base = half * (1 - where_ref[0])
    wall_group(where_ref, windows_ref, group_ref, lows, base, keep_x)
    for w in range(windows):
        for x in range(half):
            plane = half * where_ref[0] + x
            keep_x(w, plane, primitives([windows_ref[w, f, plane] for f in range(5)]))
        for f in range(5):
            for i in range(REACH):
                for ref, offset in ((left_ref, -planes), (right_ref, REACH)):
                    total = None
                    for j in range(planes):
                        c = weight(j + offset - i)
                        if c:
                            term = c * scratch[w, f, j]
                            total = term if total is None else total + term
                    ref[w, f, i] = total


def inner_part(windows_ref, part_ref, scratch):
    windows, _, planes, layers, cells = windows_ref.shape
    tile = (windows * layers, cells)
    walls = {
        k: row_weights(
            tile, [weight(k) if 0 <= i + k < layers else 0.0 for i in range(layers)] * windows
        )
        for k in range(-REACH, REACH + 1)
        if 0 < abs(k) < layers
    }
    for x in range(planes):
        fields = [
            jnp.concatenate([windows_ref[w, f, x] for w in range(windows)], axis=0)
            for f in range(5)
        ]
        parts = primitives(fields)
        for f, value in enumerate(flux(parts, 0)):
            scratch[f, x] = value
        flux_y, flux_z = flux(parts, 1), flux(parts, 2)
        for f in range(5):
            total = fields[f]
            for k, line in walls.items():
                total = total + line * pltpu.roll(flux_y[f], -k % tile[0], 0)
            for k in range(1, REACH + 1):
                total = total + weight(k) * (
                    pltpu.roll(flux_z[f], cells - k, 1) - pltpu.roll(flux_z[f], k, 1)
                )
            scratch[5 + f, x] = total
    for f in range(5):
        for x in range(planes):
            total = scratch[5 + f, x]
            for k in range(-REACH, REACH + 1):
                if k and 0 <= x + k < planes:
                    total = total + weight(k) * scratch[f, x + k]
            for w in range(windows):
                part_ref[w, f, x] = total[layers * w : layers * (w + 1)]


def gram_blocks(basis_ref, chunks, per_chunk, right, left):
    half = left.shape[0]
    for c in chunks:
        rows = jnp.concatenate(
            [modes_of(basis_ref, t) for t in range(c * per_chunk, (c + 1) * per_chunk)], axis=1
        )
        right = right + lax.dot_general(
            rows, rows[half:], NT, preferred_element_type=jnp.float32
        )
        left = left + lax.dot_general(
            rows[:half], rows[:half], NT, preferred_element_type=jnp.float32
        )
    return right, left


def inner_gram_kernel(
    early, windows_ref, basis_ref, part_ref, right_ref, left_ref, kept_ref, scratch, sems
):
    chunks = sems.shape[0]
    per_chunk = kept_ref.shape[1] // chunks
    copies = []
    for c in range(chunks):
        span = pl.ds(c * per_chunk, per_chunk)
        copies.append(
            pltpu.make_async_copy(basis_ref.at[:, span], kept_ref.at[:, span], sems.at[c])
        )
        copies[c].start()
    inner_part(windows_ref, part_ref, scratch)
    right, left = jnp.zeros(right_ref.shape, jnp.float32), jnp.zeros(left_ref.shape, jnp.float32)
    for c in range(chunks):
        copies[c].wait()
        if c < early:
            right, left = gram_blocks(kept_ref, [c], per_chunk, right, left)
    right_ref[...] = right
    left_ref[...] = left


def gram_kernel(early, chunks, _, right_ref, left_ref, basis_ref, gram_ref, total):
    modes, tiles = basis_ref.shape[:2]
    wide = modes * 8
    half = wide // 2
    right, left = gram_blocks(
        basis_ref, range(early, chunks), tiles // chunks, right_ref[...], left_ref[...]
    )
    tiles_left = half // LANES
    turned = right[0:half].T
    for tile in range(tiles_left):
        span = slice(tile * LANES, (tile + 1) * LANES)
        total[tile, 0:half] = left[:, span]
        total[tile, half:] = turned[:, span]
        total[tiles_left + tile] = right[:, span]
    rows = folded(total, modes)
    picks = (
        lax.broadcasted_iota(jnp.int32, (wide, modes), 0) // 8
        == lax.broadcasted_iota(jnp.int32, (wide, modes), 1)
    ).astype(jnp.float32)
    gram = jnp.dot(rows, picks, precision=HIGHEST, preferred_element_type=jnp.float32)
    gram_ref[:, 0:modes] = gram[0 : modes // 2]
    gram_ref[:, modes:] = gram[modes // 2 :]


def join_kernel(walls, part_ref, left_ref, right_ref, *rest):
    wall_refs, next_ref = rest[:walls], rest[walls]
    windows, _, planes, layers, cells = part_ref.shape
    for w in range(windows):
        for f in range(5):
            for x in range(planes):
                total = part_ref[w, f, x]
                for ref in wall_refs:
                    total = total + ref[w, f, x]
                if x < REACH:
                    total = total + left_ref[w, f, x]
                if x >= planes - REACH:
                    total = total + right_ref[w, f, x - planes + REACH]
                next_ref[w, f, x] = total


def wall_terms_of(first, group_ref, w, f):
    upper = group_ref[f, 16 * w : 16 * w + 16].astype(jnp.float32)
    lower = group_ref[f, 32:48].astype(jnp.float32)[8 * w : 8 * w + 8]
    zero = jnp.zeros((2, upper.shape[1]), jnp.float32)
    made = []
    for x in range(4):
        rest = lower[2 * x : 2 * x + 2]
        rest = jnp.where(
            first, jnp.concatenate([zero, rest], axis=0), jnp.concatenate([rest, zero], axis=0)
        )
        made.append(upper[4 * x : 4 * x + 4] + rest)
    return made


def wall_join_kernel(where_ref, part_ref, group_ref, given_ref):
    windows, _, planes = part_ref.shape[:3]
    base = planes // 2 * (1 - where_ref[0])
    for w in range(windows):
        for f in range(5):
            for x, term in enumerate(wall_terms_of(where_ref[0] == 0, group_ref, w, f)):
                given_ref[w, f, x] = part_ref[w, f, base + x] + term


def edge_join_kernel(where_ref, part_ref, left_ref, right_ref, made, snaps_ref):
    windows, _, half = part_ref.shape[:3]
    ahead = where_ref[0] == 1
    for w in range(windows):
        for f in range(5):
            done = []
            for x in range(half):
                total = part_ref[w, f, x] + jnp.where(ahead, left_ref[w, f, x], right_ref[w, f, x])
                made[w, f, x] = total
                done.append(total)
            snaps_ref[w, f] = jnp.concatenate(done, axis=0).astype(jnp.bfloat16)


def own_join_kernel(where_ref, _, part_ref, left_ref, right_ref, group_ref, made, snaps_ref):
    windows, _, planes = part_ref.shape[:3]
    half = planes // 2
    ahead = where_ref[0] == 0
    base = half * where_ref[0]
    for w in range(windows):
        for f in range(5):
            done = []
            for x, term in enumerate(wall_terms_of(ahead, group_ref, w, f)):
                total = part_ref[w, f, base + x] + term
                total = total + jnp.where(ahead, left_ref[w, f, x], right_ref[w, f, x])
                made[w, f, x] = total
                done.append(total)
            snaps_ref[w, f] = jnp.concatenate(done, axis=0).astype(jnp.bfloat16)


def same_layer(shape):
    rows = lax.broadcasted_iota(jnp.int32, shape, 0)
    columns = lax.broadcasted_iota(jnp.int32, shape, 1)
    return lax.rem(rows, 8) == lax.rem(columns, 8)


def folded(total, modes):
    kept = lax.rem(lax.broadcasted_iota(jnp.int32, (modes, LANES), 1), 8)
    made = []
    for tile in range(total.shape[0]):
        rows = jnp.zeros((modes, LANES), jnp.float32)
        for y in range(8):
            rows = jnp.where(kept == y, total[tile, pl.ds(y, modes, 8), :], rows)
        made.append(rows)
    return made[0] if len(made) == 1 else jnp.concatenate(made, axis=1)


def modes_of(basis_ref, t):
    modes, _, layers, cells = basis_ref.shape
    return basis_ref[:, t].reshape(modes * layers, cells)


def project_kernel(paired, where_ref, *rest):
    if paired:
        (
            own_ref, got_ref, next_own_ref, next_given_ref, basis_ref,
            sums_ref, snaps_ref, next_ref, square, wide_sums, sems,
        ) = rest
        first = where_ref[0] == 0
        half = next_own_ref.shape[2]
        copies = []
        for i, (source, base) in enumerate(
            ((next_own_ref, half * where_ref[0]), (next_given_ref, half * (1 - where_ref[0])))
        ):
            copies.append(
                pltpu.make_async_copy(source, next_ref.at[:, :, pl.ds(base, half)], sems.at[i])
            )
            copies[i].start()
        for w in range(own_ref.shape[0]):
            for f in range(own_ref.shape[1]):
                own = own_ref[w, f].astype(jnp.float32)
                got = got_ref[w, f].astype(jnp.float32)
                low = jnp.where(first, own, got)
                high = jnp.where(first, got, own)
                for t in range(4):
                    snaps_ref[4 * f + t, pl.ds(8 * w, 8)] = jnp.concatenate(
                        [low[4 * t : 4 * t + 4], high[4 * t : 4 * t + 4]], axis=0
                    ).astype(jnp.bfloat16)
    else:
        snaps_ref, basis_ref, sums_ref, square, wide_sums = rest
        copies = []
    modes, tiles = basis_ref.shape[:2]
    columns = snaps_ref.shape[1]
    total = jnp.zeros((modes * 8, columns), jnp.float32)
    small = jnp.zeros((columns, columns), jnp.float32)
    for t in range(tiles):
        snaps = snaps_ref[t]
        total = total + lax.dot_general(
            modes_of(basis_ref, t), snaps, NT, preferred_element_type=jnp.float32
        )
        small = small + lax.dot_general(snaps, snaps, NT, preferred_element_type=jnp.float32)
    wide_sums[0, :, 0:columns] = total
    square[...] = jnp.zeros_like(square)
    square[0:modes, :] = folded(wide_sums, modes)
    kept = jnp.where(same_layer(small.shape), small, 0.0)
    square[modes : modes + 1, 0:columns] = jnp.sum(kept[0:8], axis=0, keepdims=True)
    square[modes + 1 : modes + 2, 0:columns] = jnp.sum(kept[8:16], axis=0, keepdims=True)
    lanes = lax.broadcasted_iota(jnp.int32, square.shape, 1)
    turned = jnp.where(lanes < columns, square[...], 0.0).T
    sums = jnp.concatenate(
        [
            jnp.sum(turned[0:8], axis=0, keepdims=True),
            jnp.sum(turned[8:16], axis=0, keepdims=True),
        ],
        axis=0,
    )
    sums_ref[...] = jnp.concatenate(
        [sums, jnp.zeros((6, sums.shape[1]), jnp.float32)], axis=0
    )
    for copy in copies:
        copy.wait()


def merge_kernel(gram_ref, far_ref, sums_ref, merged_ref):
    rows = gram_ref.shape[0]
    merged_ref[0:rows] = gram_ref[...] + far_ref[...]
    merged_ref[rows:] = sums_ref[...]


def unpacked(sums_ref, modes):
    half = modes // 2
    return jnp.concatenate([sums_ref[0:half, 0:modes], sums_ref[0:half, modes:]], axis=0)


def inverse_kernel(sums_ref, inverse_ref, spread_ref, plain, scaled):
    modes = inverse_ref.shape[0]
    rows = lax.broadcasted_iota(jnp.int32, (8, 2 * modes), 0)
    lanes = lax.broadcasted_iota(jnp.int32, (8, 2 * modes), 1)
    tiles = []
    gram = unpacked(sums_ref, modes)
    for tile in range(modes // 8):
        eye = (lanes == rows + (modes + 8 * tile)).astype(jnp.float32)
        start = 8 * tile % (modes // 2)
        line = sums_ref[start : start + 8, :]
        if 8 * tile >= modes // 2:
            line = pltpu.roll(line, modes, 1)
        tiles.append(jnp.where(lanes < modes, line, eye))
    count = modes // 8
    for home in range(count):
        columns = [
            [
                jnp.broadcast_to(
                    tiles[tile][:, 8 * home + j : 8 * home + j + 1], (8, 2 * modes)
                )
                for tile in range(home, count)
            ]
            for j in range(8)
        ]
        for j in range(8):
            k = 8 * home + j
            inverse = 1.0 / columns[j][0]
            inverse = inverse[j : j + 1, :]
            row = tiles[home][j : j + 1, :]
            ready = row * inverse
            plain[k : k + 1, :] = row
            scaled[k : k + 1, :] = ready
            factors = [jnp.where(rows > j, columns[j][0], 0.0)] + columns[j][1:]
            for later in range(j + 1, 8):
                share = columns[j][0][later : later + 1, :] * inverse
                columns[later] = [c - f * share for c, f in zip(columns[later], factors)]
            for tile in range(home, count):
                tiles[tile] = tiles[tile] - factors[tile - home] * ready
    exact = functools.partial(
        lax.dot_general, precision=HIGHEST, preferred_element_type=jnp.float32
    )
    plainly = (((1,), (0,)), ((), ()))
    inverse = exact(plain[:, modes:], scaled[:, modes:], (((0,), (0,)), ((), ())))
    square = (modes, modes)
    eye = lax.broadcasted_iota(jnp.int32, square, 0) == lax.broadcasted_iota(jnp.int32, square, 1)
    off = eye.astype(jnp.float32) - exact(gram, inverse, plainly)
    inverse = inverse + exact(inverse, off, plainly)
    inverse_ref[...] = inverse
    wide = spread_ref.shape[1]
    spread = (
        lax.broadcasted_iota(jnp.int32, (modes, wide), 1) // 8
        == lax.broadcasted_iota(jnp.int32, (modes, wide), 0)
    ).astype(jnp.float32)
    spread_ref[...] = exact(inverse, spread, plainly)


def finish_kernel(
    rows_total, projected_ref, sums_ref, inverse_ref, spread_ref, snaps_ref, basis_ref,
    modes_ref, solved_ref, factor_ref, made, sems,
):
    modes, tiles, _, cells = basis_ref.shape
    wide = modes * 8
    exact = functools.partial(jnp.dot, precision=HIGHEST, preferred_element_type=jnp.float32)
    base = modes // 2
    projected = projected_ref[base : base + 8, 0:modes]
    lines = exact(projected, spread_ref[...])
    full = jnp.concatenate(
        [jnp.broadcast_to(lines[0:1], (8, wide)), jnp.broadcast_to(lines[1:2], (8, wide))],
        axis=0,
    )
    full = jnp.where(same_layer(full.shape), full, 0.0)
    upper = full.astype(jnp.bfloat16)
    fit = jnp.concatenate([upper, (full - upper.astype(jnp.float32)).astype(jnp.bfloat16)], axis=0)
    solved = exact(projected, inverse_ref[...])
    left = projected - exact(solved, unpacked(sums_ref, modes))

    def inner(p, i, q, j):
        return jnp.sum(p[i : i + 1] * q[j : j + 1], axis=1, keepdims=True)

    def entry(i, j):
        square = projected_ref[base + i : base + i + 1, modes + j : modes + j + 1]
        return square - inner(projected, i, solved, j) - inner(solved, i, left, j)

    first = jnp.sqrt(entry(0, 0))
    below = entry(1, 0) / first
    second = jnp.sqrt(entry(1, 1) - below * below)
    scaling = jnp.sqrt(jnp.float32(rows_total))
    w00 = scaling / first
    w11 = scaling / second
    w01 = -(below / first) * w11
    solved_ref[...] = solved[0:2]
    factor_ref[0:1, 0:1] = first / scaling
    factor_ref[0:1, 1:2] = below / scaling
    factor_ref[1:2, 0:1] = jnp.zeros_like(first)
    factor_ref[1:2, 1:2] = second / scaling
    chunks = sems.shape[0]
    per_chunk = tiles // chunks
    copies = []
    for c in range(chunks):
        for t in range(c * per_chunk, (c + 1) * per_chunk):
            fitted = jnp.dot(fit, modes_of(basis_ref, t), preferred_element_type=jnp.float32)
            fitted = fitted[0:16] + fitted[16:32]
            snaps = snaps_ref[t].astype(jnp.float32)
            left_over = snaps - fitted
            made[0, t] = left_over[0:8] * w00
            made[1, t] = left_over[8:16] * w11 + left_over[0:8] * w01
        span = pl.ds(c * per_chunk, per_chunk)
        copies.append(
            pltpu.make_async_copy(made.at[:, span], modes_ref.at[:, span], sems.at[c])
        )
        copies[c].start()
    for copy in copies:
        copy.wait()


def params(mib):
    return pltpu.CompilerParams(vmem_limit_bytes=mib * 1024 * 1024)


def cost(flops, moved):
    return pl.CostEstimate(flops=flops, bytes_accessed=moved, transcendentals=0)


WHOLE = pl.BlockSpec(memory_space=pltpu.VMEM)
FAR = pl.BlockSpec(memory_space=pltpu.HBM)
LOOSE = pl.BlockSpec(memory_space=pl.ANY)
SCALAR = pl.BlockSpec(memory_space=pltpu.SMEM)


def swap_added(value, axis, bit):
    count = lax.axis_size(axis)
    return value + lax.ppermute(value, axis, [(i, i ^ bit) for i in range(count)])


def bits(count):
    made = [1 << k for k in range(count.bit_length() - 1)]
    if count != 1 << len(made):
        raise ValueError("axis size")
    return made


def body(windows, pod_basis):
    f32, bf16 = jnp.float32, jnp.bfloat16
    shape = jax.ShapeDtypeStruct
    count, fields, planes, layers, cells = windows.shape
    ring, walls = lax.axis_size("solver"), lax.axis_size("analysis")
    paired = walls == 2 and planes == 8 and layers == 4
    place = lax.axis_index("analysis").astype(jnp.int32).reshape(1)
    modes, _, pod_planes, pod_layers, _ = pod_basis.shape
    tiles = fields * pod_planes * (pod_layers // 8)
    basis = pod_basis.reshape(modes, tiles, 8, cells)
    wide = modes * 8
    basis_bytes = basis.size * 2

    to_right = [(i, (i + 1) % ring) for i in range(ring)]
    to_left = [((i + 1) % ring, i) for i in range(ring)]
    edge_shape = shape((count, fields, REACH, layers, cells), f32)
    face_scratch = [pltpu.VMEM((fields, planes, layers, cells), f32)]
    face_cost = cost(10_000_000, 10 * windows.size)
    if paired:
        swap = [(0, 1), (1, 0)]
        group_shape = shape((fields, 48, cells), bf16)
        lows = pltpu.VMEM((fields, 16, cells), f32)
        near_group, kept = pl.pallas_call(
            near_kernel,
            out_shape=[group_shape, shape(windows.shape, f32)],
            in_specs=[SCALAR, WHOLE],
            out_specs=[WHOLE] * 2,
            scratch_shapes=[lows, pltpu.SemaphoreType.DMA],
            compiler_params=params(16),
            cost_estimate=face_cost,
            name="near_faces",
        )(place, windows)
        later_group, to_next, to_last = pl.pallas_call(
            later_kernel,
            out_shape=[group_shape] + [edge_shape] * 2,
            in_specs=[SCALAR, LOOSE, WHOLE],
            out_specs=[WHOLE] * 3,
            scratch_shapes=[pltpu.VMEM((count, fields, planes, layers, cells), f32), lows],
            compiler_params=params(16),
            cost_estimate=face_cost,
            name="later_faces",
        )(place, near_group, kept)
        near_group = lax.ppermute(near_group, "analysis", swap)
        from_left = lax.ppermute(to_next, "solver", to_right)
        from_right = lax.ppermute(to_last, "solver", to_left)
        later_group = lax.ppermute(later_group, "analysis", swap)
    else:
        kept, to_next, to_last, up, down = pl.pallas_call(
            functools.partial(face_kernel, True),
            out_shape=[shape(windows.shape, f32)]
            + [edge_shape] * 2
            + [shape(windows.shape, f32)] * 2,
            in_specs=[SCALAR, FAR],
            out_specs=[WHOLE] * 5,
            scratch_shapes=face_scratch + [pltpu.SemaphoreType.DMA((count,))],
            compiler_params=params(16),
            cost_estimate=face_cost,
            name="faces",
        )(place, windows)
        wall_terms = [
            lax.ppermute(up, "analysis", [(i, i + 1) for i in range(walls - 1)]),
            lax.ppermute(down, "analysis", [(i + 1, i) for i in range(walls - 1)]),
        ]
        from_left = lax.ppermute(to_next, "solver", to_right)
        from_right = lax.ppermute(to_last, "solver", to_left)

    early = 2
    gram_flops = 2 * wide * wide * cells * tiles
    inner, right, left, basis = pl.pallas_call(
        functools.partial(inner_gram_kernel, early),
        out_shape=[
            shape(windows.shape, f32),
            shape((wide, wide // 2), f32),
            shape((wide // 2, wide // 2), f32),
            shape(basis.shape, bf16),
        ],
        in_specs=[WHOLE, FAR],
        out_specs=[WHOLE] * 4,
        scratch_shapes=[
            pltpu.VMEM((2 * fields, planes, count * layers, cells), f32),
            pltpu.SemaphoreType.DMA((fields,)),
        ],
        compiler_params=params(40),
        cost_estimate=cost(1_000_000, windows.size),
        name="inner_gram",
    )(kept, basis)

    def rest_of_gram(after):
        return pl.pallas_call(
            functools.partial(gram_kernel, early, fields),
            out_shape=shape((modes // 2, 2 * modes), f32),
            in_specs=[LOOSE] + [WHOLE] * 3,
            out_specs=WHOLE,
            scratch_shapes=[pltpu.VMEM((wide // LANES, wide, LANES), f32)],
            compiler_params=params(24),
            cost_estimate=cost(gram_flops // 2, basis_bytes),
            name="gram",
        )(after, right, left, basis)

    join_cost = cost(1_000_000, 16 * windows.size)
    if paired:
        half_shape = (count, fields, planes * layers // 2, cells)

        half_next = shape((count, fields, planes // 2, layers, cells), f32)

        inner_given = pl.pallas_call(
            wall_join_kernel,
            out_shape=half_next,
            in_specs=[SCALAR] + [WHOLE] * 2,
            out_specs=WHOLE,
            compiler_params=params(16),
            cost_estimate=cost(gram_flops // 2, basis_bytes),
            name="wall_join",
        )(place, inner, near_group)
        next_given, given = pl.pallas_call(
            edge_join_kernel,
            out_shape=[half_next, shape(half_shape, bf16)],
            in_specs=[SCALAR] + [WHOLE] * 3,
            out_specs=[WHOLE] * 2,
            compiler_params=params(16),
            cost_estimate=join_cost,
            name="edge_join",
        )(place, inner_given, from_left, from_right)
        got = lax.ppermute(given, "analysis", swap)
        gram = rest_of_gram(given)
    else:
        next_windows = pl.pallas_call(
            functools.partial(join_kernel, 2),
            out_shape=shape(windows.shape, f32),
            in_specs=[WHOLE] * 5,
            out_specs=WHOLE,
            compiler_params=params(16),
            cost_estimate=join_cost,
            name="join",
        )(inner, from_left, from_right, *wall_terms)
        gram = rest_of_gram(place)
    ring_bits = bits(ring)
    lone = ring_bits.pop(1 if len(ring_bits) > 1 else 0)
    gram_far = lax.ppermute(gram, "solver", [(i, i ^ lone) for i in range(ring)])
    if paired:
        next_own, own = pl.pallas_call(
            own_join_kernel,
            out_shape=[half_next, shape(half_shape, bf16)],
            in_specs=[SCALAR, LOOSE] + [WHOLE] * 4,
            out_specs=[WHOLE] * 2,
            compiler_params=params(16),
            cost_estimate=join_cost,
            name="own_join",
        )(place, gram, inner, from_left, from_right, later_group)

    sums_shape = shape((8, LANES), f32)
    snaps_shape = shape((tiles, 2 * 8, cells), bf16)
    scratch = [pltpu.VMEM((LANES, LANES), f32), pltpu.VMEM((1, wide, LANES), f32)]
    project_cost = cost(2 * wide * 16 * cells * tiles, basis_bytes)
    if paired:
        sums, snaps, next_windows = pl.pallas_call(
            functools.partial(project_kernel, True),
            out_shape=[sums_shape, snaps_shape, shape(windows.shape, f32)],
            in_specs=[SCALAR] + [WHOLE] * 5,
            out_specs=[WHOLE, WHOLE, FAR],
            scratch_shapes=scratch + [pltpu.SemaphoreType.DMA((2,))],
            compiler_params=params(16),
            cost_estimate=project_cost,
            name="project",
        )(place, own, got, next_own, next_given, basis)
    else:
        relaid = lax.all_to_all(
            next_windows.astype(bf16), "analysis", split_axis=2, concat_axis=3, tiled=True
        )
        snaps = relaid.reshape(count, tiles, 8, cells).transpose(1, 0, 2, 3)
        snaps = snaps.reshape(tiles, count * 8, cells)
        sums = pl.pallas_call(
            functools.partial(project_kernel, False),
            out_shape=sums_shape,
            in_specs=[SCALAR] + [WHOLE] * 2,
            out_specs=WHOLE,
            scratch_shapes=scratch,
            compiler_params=params(16),
            cost_estimate=project_cost,
            name="project",
        )(place, snaps, basis)
    sums = pl.pallas_call(
        merge_kernel,
        out_shape=shape((modes // 2 + 8, LANES), f32),
        in_specs=[WHOLE] * 3,
        out_specs=WHOLE,
        compiler_params=params(16),
        cost_estimate=cost(10_000, 8 * modes * LANES),
        name="merge",
    )(gram, gram_far, sums)
    for bit in bits(walls):
        sums = swap_added(sums, "analysis", bit)
    for bit in ring_bits:
        sums = swap_added(sums, "solver", bit)
    inverse, spread = pl.pallas_call(
        inverse_kernel,
        out_shape=[shape((modes, modes), f32), shape((modes, wide), f32)],
        in_specs=[WHOLE],
        out_specs=[WHOLE] * 2,
        scratch_shapes=[pltpu.VMEM((modes, 2 * modes), f32)] * 2,
        compiler_params=params(16),
        cost_estimate=cost(20_000_000, 8 * modes * modes),
        name="inverse",
    )(sums)
    projected = swap_added(sums, "solver", lone)

    rows_total = ring * walls * tiles * 8 * cells
    new_modes, solved, factor = pl.pallas_call(
        functools.partial(finish_kernel, rows_total),
        out_shape=[
            shape((count, tiles, 8, cells), f32),
            shape((count, modes), f32),
            shape((count, count), f32),
        ],
        in_specs=[WHOLE] * 6,
        out_specs=[FAR, WHOLE, WHOLE],
        scratch_shapes=[
            pltpu.VMEM((count, tiles, 8, cells), f32),
            pltpu.SemaphoreType.DMA((fields,)),
        ],
        compiler_params=params(16),
        cost_estimate=cost(2 * wide * 32 * cells * tiles, basis_bytes + 8 * windows.size),
        name="finish",
    )(projected, sums, inverse, spread, snaps, basis)
    new_modes = new_modes.reshape(count, fields, pod_planes, pod_layers, cells)
    return next_windows, solved, new_modes, factor


def solution(mesh):
    in_specs = (
        P(None, None, "solver", "analysis", None),
        P(None, None, ("solver", "analysis"), None, None),
    )
    out_specs = (
        P(None, None, "solver", "analysis", None),
        P(),
        P(None, None, ("solver", "analysis"), None, None),
        P(),
    )
    return jax.shard_map(body, mesh=mesh, in_specs=in_specs, out_specs=out_specs, check_vma=False)
```

```python
import functools

import jax
import jax.numpy as jnp
from jax import lax
from jax.experimental import pallas as pl
from jax.experimental.pallas import tpu as pltpu
from jax.sharding import PartitionSpec as P

PRESSURE_FACTOR = 1.4 - 1.0
SECTION_STEP = 0.25
CENTRAL_WEIGHTS = (0.8, -0.2, 4.0 / 105.0, -1.0 / 280.0)
REACH = 4
LANES = 128
HIGHEST = lax.Precision.HIGHEST
NT = (((1,), (1,)), ((), ()))


def weight(k):
    if k == 0 or abs(k) > REACH:
        return 0.0
    value = -SECTION_STEP * CENTRAL_WEIGHTS[abs(k) - 1]
    return value if k > 0 else -value


def row_weights(shape, values):
    rows = lax.broadcasted_iota(jnp.int32, shape, len(shape) - 2)
    made = jnp.full(shape, values[0], jnp.float32)
    for i, value in enumerate(values[1:], start=1):
        made = jnp.where(rows == i, jnp.float32(value), made)
    return made


def primitives(fields):
    density, mx, my, mz, energy = fields
    inverse = 1.0 / density
    ux, uy, uz = mx * inverse, my * inverse, mz * inverse
    pressure = PRESSURE_FACTOR * (energy - 0.5 * (mx * ux + my * uy + mz * uz))
    return (mx, my, mz), (ux, uy, uz), pressure, energy + pressure


def flux(parts, direction):
    moments, speeds, pressure, enthalpy = parts
    speed = speeds[direction]
    made = [moments[direction]]
    for axis in range(3):
        term = moments[axis] * speed
        made.append(term + pressure if axis == direction else term)
    made.append(enthalpy * speed)
    return made


def face_kernel(two_sided, where_ref, source_ref, windows_ref, left_ref, right_ref, *rest):
    windows, _, planes, layers, cells = windows_ref.shape
    wall_refs, scratch, sems = rest[:-2], rest[-2], rest[-1]
    copies = [
        pltpu.make_async_copy(source_ref.at[w], windows_ref.at[w], sems.at[w])
        for w in range(windows)
    ]
    for copy in copies:
        copy.start()
    tile = (layers, cells)
    up = [
        row_weights(tile, [weight(j - layers - i) for i in range(layers)]) for j in range(layers)
    ]
    down = [
        row_weights(tile, [weight(layers + j - i) for i in range(layers)]) for j in range(layers)
    ]
    if two_sided:
        tables = (up, down)
    else:
        first = where_ref[0] == 0
        tables = ([jnp.where(first, u, d) for u, d in zip(up, down)],)
    for w in range(windows):
        copies[w].wait()
        for x in range(planes):
            parts = primitives([windows_ref[w, f, x] for f in range(5)])
            for f, value in enumerate(flux(parts, 0)):
                scratch[f, x] = value
            for f, value in enumerate(flux(parts, 1)):
                for ref, table in zip(wall_refs, tables):
                    total = None
                    for j in range(layers):
                        term = table[j] * value[j : j + 1, :]
                        total = term if total is None else total + term
                    ref[w, f, x] = total
        for f in range(5):
            for i in range(REACH):
                total = None
                for j in range(planes):
                    c = weight(j - planes - i)
                    if c:
                        term = c * scratch[f, j]
                        total = term if total is None else total + term
                left_ref[w, f, i] = total
                total = None
                for j in range(planes):
                    c = weight(j + REACH - i)
                    if c:
                        term = c * scratch[f, j]
                        total = term if total is None else total + term
                right_ref[w, f, i] = total


def wall_group(where_ref, windows_ref, group_ref, lows, base, keep_x):
    windows, _, planes, layers, cells = windows_ref.shape
    tile = (layers, cells)
    first = where_ref[0] == 0
    table = [
        jnp.where(
            first,
            row_weights(tile, [weight(j - layers - i) for i in range(layers)]),
            row_weights(tile, [weight(layers + j - i) for i in range(layers)]),
        )
        for j in range(layers)
    ]
    for w in range(windows):
        upper = [[] for _ in range(5)]
        lower = [[] for _ in range(5)]
        for x in range(planes // 2):
            parts = primitives([windows_ref[w, f, base + x] for f in range(5)])
            keep_x(w, base + x, parts)
            for f, value in enumerate(flux(parts, 1)):
                total = None
                for j in range(layers):
                    term = table[j] * value[j : j + 1, :]
                    total = term if total is None else total + term
                high = total.astype(jnp.bfloat16).astype(jnp.float32)
                rest = total - high
                upper[f].append(high)
                lower[f].append(jnp.where(first, rest[0:2], rest[2:4]))
        for f in range(5):
            group_ref[f, 16 * w : 16 * w + 16] = jnp.concatenate(upper[f], axis=0).astype(
                jnp.bfloat16
            )
            lows[f, 8 * w : 8 * w + 8] = jnp.concatenate(lower[f], axis=0)
    for f in range(5):
        group_ref[f, 32:48] = lows[f].astype(jnp.bfloat16)


def near_kernel(where_ref, source_ref, group_ref, kept_ref, lows, sem):
    copy = pltpu.make_async_copy(source_ref, kept_ref, sem)
    copy.start()
    base = source_ref.shape[2] // 2 * where_ref[0]
    wall_group(where_ref, source_ref, group_ref, lows, base, lambda w, x, parts: None)
    copy.wait()


def later_kernel(where_ref, _, windows_ref, group_ref, first_ref, second_ref, scratch, lows):
    windows, _, planes, layers, cells = windows_ref.shape
    half = planes // 2

    def keep_x(w, x, parts):
        for f, value in enumerate(flux(parts, 0)):
            scratch[w, f, x] = value

    base = half * (1 - where_ref[0])
    wall_group(where_ref, windows_ref, group_ref, lows, base, keep_x)
    for w in range(windows):
        for x in range(half):
            plane = half * where_ref[0] + x
            keep_x(w, plane, primitives([windows_ref[w, f, plane] for f in range(5)]))
        for f in range(5):
            for i in range(REACH):
                sides = []
                for offset in (-planes, REACH):
                    total = None
                    for j in range(planes):
                        c = weight(j + offset - i)
                        if c:
                            term = c * scratch[w, f, j]
                            total = term if total is None else total + term
                    sides.append(total)
                to_next, to_last = sides
                first_ref[w, f, i] = jnp.where(where_ref[0] == 0, to_last, to_next)
                second_ref[w, f, i] = jnp.where(where_ref[0] == 0, to_next, to_last)


def inner_part(windows_ref, part_ref, scratch):
    windows, _, planes, layers, cells = windows_ref.shape
    tile = (windows * layers, cells)
    walls = {
        k: row_weights(
            tile, [weight(k) if 0 <= i + k < layers else 0.0 for i in range(layers)] * windows
        )
        for k in range(-REACH, REACH + 1)
        if 0 < abs(k) < layers
    }
    for x in range(planes):
        fields = [
            jnp.concatenate([windows_ref[w, f, x] for w in range(windows)], axis=0)
            for f in range(5)
        ]
        parts = primitives(fields)
        for f, value in enumerate(flux(parts, 0)):
            scratch[f, x] = value
        flux_y, flux_z = flux(parts, 1), flux(parts, 2)
        for f in range(5):
            total = fields[f]
            for k, line in walls.items():
                total = total + line * pltpu.roll(flux_y[f], -k % tile[0], 0)
            for k in range(1, REACH + 1):
                total = total + weight(k) * (
                    pltpu.roll(flux_z[f], cells - k, 1) - pltpu.roll(flux_z[f], k, 1)
                )
            scratch[5 + f, x] = total
    for f in range(5):
        for x in range(planes):
            total = scratch[5 + f, x]
            for k in range(-REACH, REACH + 1):
                if k and 0 <= x + k < planes:
                    total = total + weight(k) * scratch[f, x + k]
            for w in range(windows):
                part_ref[w, f, x] = total[layers * w : layers * (w + 1)]


def gram_blocks(basis_ref, chunks, per_chunk, right, left):
    half = left.shape[0]
    for c in chunks:
        rows = jnp.concatenate(
            [modes_of(basis_ref, t) for t in range(c * per_chunk, (c + 1) * per_chunk)], axis=1
        )
        right = right + lax.dot_general(
            rows, rows[half:], NT, preferred_element_type=jnp.float32
        )
        left = left + lax.dot_general(
            rows[:half], rows[:half], NT, preferred_element_type=jnp.float32
        )
    return right, left


def inner_gram_kernel(
    early, windows_ref, basis_ref, part_ref, right_ref, left_ref, kept_ref, scratch, sems
):
    chunks = sems.shape[0]
    per_chunk = kept_ref.shape[1] // chunks
    copies = []
    for c in range(chunks):
        span = pl.ds(c * per_chunk, per_chunk)
        copies.append(
            pltpu.make_async_copy(basis_ref.at[:, span], kept_ref.at[:, span], sems.at[c])
        )
        copies[c].start()
    inner_part(windows_ref, part_ref, scratch)
    right, left = jnp.zeros(right_ref.shape, jnp.float32), jnp.zeros(left_ref.shape, jnp.float32)
    for c in range(chunks):
        copies[c].wait()
        if c < early:
            right, left = gram_blocks(kept_ref, [c], per_chunk, right, left)
    right_ref[...] = right
    left_ref[...] = left


def gram_kernel(early, chunks, _, right_ref, left_ref, basis_ref, gram_ref, total):
    modes, tiles = basis_ref.shape[:2]
    wide = modes * 8
    half = wide // 2
    right, left = gram_blocks(
        basis_ref, range(early, chunks), tiles // chunks, right_ref[...], left_ref[...]
    )
    tiles_left = half // LANES
    turned = right[0:half].T
    for tile in range(tiles_left):
        span = slice(tile * LANES, (tile + 1) * LANES)
        total[tile, 0:half] = left[:, span]
        total[tile, half:] = turned[:, span]
        total[tiles_left + tile] = right[:, span]
    rows = folded(total, modes)
    picks = (
        lax.broadcasted_iota(jnp.int32, (wide, modes), 0) // 8
        == lax.broadcasted_iota(jnp.int32, (wide, modes), 1)
    ).astype(jnp.float32)
    gram = jnp.dot(rows, picks, precision=HIGHEST, preferred_element_type=jnp.float32)
    gram_ref[:, 0:modes] = gram[0 : modes // 2]
    gram_ref[:, modes:] = gram[modes // 2 :]


def join_kernel(walls, part_ref, left_ref, right_ref, *rest):
    wall_refs, next_ref = rest[:walls], rest[walls]
    windows, _, planes, layers, cells = part_ref.shape
    for w in range(windows):
        for f in range(5):
            for x in range(planes):
                total = part_ref[w, f, x]
                for ref in wall_refs:
                    total = total + ref[w, f, x]
                if x < REACH:
                    total = total + left_ref[w, f, x]
                if x >= planes - REACH:
                    total = total + right_ref[w, f, x - planes + REACH]
                next_ref[w, f, x] = total


def wall_terms_of(first, group_ref, w, f):
    upper = group_ref[f, 16 * w : 16 * w + 16].astype(jnp.float32)
    lower = group_ref[f, 32:48].astype(jnp.float32)[8 * w : 8 * w + 8]
    zero = jnp.zeros((2, upper.shape[1]), jnp.float32)
    made = []
    for x in range(4):
        rest = lower[2 * x : 2 * x + 2]
        rest = jnp.where(
            first, jnp.concatenate([zero, rest], axis=0), jnp.concatenate([rest, zero], axis=0)
        )
        made.append(upper[4 * x : 4 * x + 4] + rest)
    return made


def wall_join_kernel(where_ref, part_ref, group_ref, given_ref):
    windows, _, planes = part_ref.shape[:3]
    base = planes // 2 * (1 - where_ref[0])
    for w in range(windows):
        for f in range(5):
            for x, term in enumerate(wall_terms_of(where_ref[0] == 0, group_ref, w, f)):
                given_ref[w, f, x] = part_ref[w, f, base + x] + term


def edge_join_kernel(part_ref, edge_ref, made, snaps_ref):
    windows, _, half = part_ref.shape[:3]
    for w in range(windows):
        for f in range(5):
            done = []
            for x in range(half):
                total = part_ref[w, f, x] + edge_ref[w, f, x]
                made[w, f, x] = total
                done.append(total)
            snaps_ref[w, f] = jnp.concatenate(done, axis=0).astype(jnp.bfloat16)


def own_join_kernel(where_ref, _, part_ref, edge_ref, group_ref, made, snaps_ref):
    windows, _, planes = part_ref.shape[:3]
    base = planes // 2 * where_ref[0]
    for w in range(windows):
        for f in range(5):
            done = []
            for x, term in enumerate(wall_terms_of(where_ref[0] == 0, group_ref, w, f)):
                total = part_ref[w, f, base + x] + term + edge_ref[w, f, x]
                made[w, f, x] = total
                done.append(total)
            snaps_ref[w, f] = jnp.concatenate(done, axis=0).astype(jnp.bfloat16)


def same_layer(shape):
    rows = lax.broadcasted_iota(jnp.int32, shape, 0)
    columns = lax.broadcasted_iota(jnp.int32, shape, 1)
    return lax.rem(rows, 8) == lax.rem(columns, 8)


def folded(total, modes):
    kept = lax.rem(lax.broadcasted_iota(jnp.int32, (modes, LANES), 1), 8)
    made = []
    for tile in range(total.shape[0]):
        rows = jnp.zeros((modes, LANES), jnp.float32)
        for y in range(8):
            rows = jnp.where(kept == y, total[tile, pl.ds(y, modes, 8), :], rows)
        made.append(rows)
    return made[0] if len(made) == 1 else jnp.concatenate(made, axis=1)


def modes_of(basis_ref, t):
    modes, _, layers, cells = basis_ref.shape
    return basis_ref[:, t].reshape(modes * layers, cells)


def project_kernel(paired, where_ref, *rest):
    if paired:
        (
            own_ref, got_ref, next_own_ref, next_given_ref, basis_ref,
            sums_ref, snaps_ref, next_ref, square, wide_sums, sems,
        ) = rest
        first = where_ref[0] == 0
        half = next_own_ref.shape[2]
        copies = []
        for i, (source, base) in enumerate(
            ((next_own_ref, half * where_ref[0]), (next_given_ref, half * (1 - where_ref[0])))
        ):
            copies.append(
                pltpu.make_async_copy(source, next_ref.at[:, :, pl.ds(base, half)], sems.at[i])
            )
            copies[i].start()
        for w in range(own_ref.shape[0]):
            for f in range(own_ref.shape[1]):
                own = own_ref[w, f].astype(jnp.float32)
                got = got_ref[w, f].astype(jnp.float32)
                low = jnp.where(first, own, got)
                high = jnp.where(first, got, own)
                for t in range(4):
                    snaps_ref[4 * f + t, pl.ds(8 * w, 8)] = jnp.concatenate(
                        [low[4 * t : 4 * t + 4], high[4 * t : 4 * t + 4]], axis=0
                    ).astype(jnp.bfloat16)
    else:
        snaps_ref, basis_ref, sums_ref, square, wide_sums = rest
        copies = []
    modes, tiles = basis_ref.shape[:2]
    columns = snaps_ref.shape[1]
    total = jnp.zeros((modes * 8, columns), jnp.float32)
    small = jnp.zeros((columns, columns), jnp.float32)
    for t in range(tiles):
        snaps = snaps_ref[t]
        total = total + lax.dot_general(
            modes_of(basis_ref, t), snaps, NT, preferred_element_type=jnp.float32
        )
        small = small + lax.dot_general(snaps, snaps, NT, preferred_element_type=jnp.float32)
    wide_sums[0, :, 0:columns] = total
    square[...] = jnp.zeros_like(square)
    square[0:modes, :] = folded(wide_sums, modes)
    kept = jnp.where(same_layer(small.shape), small, 0.0)
    square[modes : modes + 1, 0:columns] = jnp.sum(kept[0:8], axis=0, keepdims=True)
    square[modes + 1 : modes + 2, 0:columns] = jnp.sum(kept[8:16], axis=0, keepdims=True)
    lanes = lax.broadcasted_iota(jnp.int32, square.shape, 1)
    turned = jnp.where(lanes < columns, square[...], 0.0).T
    sums = jnp.concatenate(
        [
            jnp.sum(turned[0:8], axis=0, keepdims=True),
            jnp.sum(turned[8:16], axis=0, keepdims=True),
        ],
        axis=0,
    )
    sums_ref[...] = jnp.concatenate(
        [sums, jnp.zeros((6, sums.shape[1]), jnp.float32)], axis=0
    )
    for copy in copies:
        copy.wait()


def merge_kernel(gram_ref, far_ref, sums_ref, merged_ref):
    rows = gram_ref.shape[0]
    merged_ref[0:rows] = gram_ref[...] + far_ref[...]
    merged_ref[rows:] = sums_ref[...]


def unpacked(sums_ref, modes):
    half = modes // 2
    return jnp.concatenate([sums_ref[0:half, 0:modes], sums_ref[0:half, modes:]], axis=0)


def inverse_kernel(sums_ref, inverse_ref, spread_ref, plain, scaled):
    modes = inverse_ref.shape[0]
    rows = lax.broadcasted_iota(jnp.int32, (8, 2 * modes), 0)
    lanes = lax.broadcasted_iota(jnp.int32, (8, 2 * modes), 1)
    tiles = []
    gram = unpacked(sums_ref, modes)
    for tile in range(modes // 8):
        eye = (lanes == rows + (modes + 8 * tile)).astype(jnp.float32)
        start = 8 * tile % (modes // 2)
        line = sums_ref[start : start + 8, :]
        if 8 * tile >= modes // 2:
            line = pltpu.roll(line, modes, 1)
        tiles.append(jnp.where(lanes < modes, line, eye))
    count = modes // 8
    for home in range(count):
        columns = [
            [
                jnp.broadcast_to(
                    tiles[tile][:, 8 * home + j : 8 * home + j + 1], (8, 2 * modes)
                )
                for tile in range(home, count)
            ]
            for j in range(8)
        ]
        for j in range(8):
            k = 8 * home + j
            inverse = 1.0 / columns[j][0]
            inverse = inverse[j : j + 1, :]
            row = tiles[home][j : j + 1, :]
            ready = row * inverse
            plain[k : k + 1, :] = row
            scaled[k : k + 1, :] = ready
            factors = [jnp.where(rows > j, columns[j][0], 0.0)] + columns[j][1:]
            for later in range(j + 1, 8):
                share = columns[j][0][later : later + 1, :] * inverse
                columns[later] = [c - f * share for c, f in zip(columns[later], factors)]
            for tile in range(home, count):
                tiles[tile] = tiles[tile] - factors[tile - home] * ready
    exact = functools.partial(
        lax.dot_general, precision=HIGHEST, preferred_element_type=jnp.float32
    )
    plainly = (((1,), (0,)), ((), ()))
    inverse = exact(plain[:, modes:], scaled[:, modes:], (((0,), (0,)), ((), ())))
    square = (modes, modes)
    eye = lax.broadcasted_iota(jnp.int32, square, 0) == lax.broadcasted_iota(jnp.int32, square, 1)
    off = eye.astype(jnp.float32) - exact(gram, inverse, plainly)
    inverse = inverse + exact(inverse, off, plainly)
    inverse_ref[...] = inverse
    wide = spread_ref.shape[1]
    spread = (
        lax.broadcasted_iota(jnp.int32, (modes, wide), 1) // 8
        == lax.broadcasted_iota(jnp.int32, (modes, wide), 0)
    ).astype(jnp.float32)
    spread_ref[...] = exact(inverse, spread, plainly)


def finish_kernel(
    rows_total, projected_ref, sums_ref, inverse_ref, spread_ref, snaps_ref, basis_ref,
    modes_ref, solved_ref, factor_ref, made, sems,
):
    modes, tiles, _, cells = basis_ref.shape
    wide = modes * 8
    exact = functools.partial(jnp.dot, precision=HIGHEST, preferred_element_type=jnp.float32)
    base = modes // 2
    projected = projected_ref[base : base + 8, 0:modes]
    lines = exact(projected, spread_ref[...])
    full = jnp.concatenate(
        [jnp.broadcast_to(lines[0:1], (8, wide)), jnp.broadcast_to(lines[1:2], (8, wide))],
        axis=0,
    )
    full = jnp.where(same_layer(full.shape), full, 0.0)
    upper = full.astype(jnp.bfloat16)
    fit = jnp.concatenate([upper, (full - upper.astype(jnp.float32)).astype(jnp.bfloat16)], axis=0)
    solved = exact(projected, inverse_ref[...])
    left = projected - exact(solved, unpacked(sums_ref, modes))

    def inner(p, i, q, j):
        return jnp.sum(p[i : i + 1] * q[j : j + 1], axis=1, keepdims=True)

    def entry(i, j):
        square = projected_ref[base + i : base + i + 1, modes + j : modes + j + 1]
        return square - inner(projected, i, solved, j) - inner(solved, i, left, j)

    first = jnp.sqrt(entry(0, 0))
    below = entry(1, 0) / first
    second = jnp.sqrt(entry(1, 1) - below * below)
    scaling = jnp.sqrt(jnp.float32(rows_total))
    w00 = scaling / first
    w11 = scaling / second
    w01 = -(below / first) * w11
    solved_ref[...] = solved[0:2]
    factor_ref[0:1, 0:1] = first / scaling
    factor_ref[0:1, 1:2] = below / scaling
    factor_ref[1:2, 0:1] = jnp.zeros_like(first)
    factor_ref[1:2, 1:2] = second / scaling
    chunks = sems.shape[0]
    per_chunk = tiles // chunks
    copies = []
    for c in range(chunks):
        for t in range(c * per_chunk, (c + 1) * per_chunk):
            fitted = jnp.dot(fit, modes_of(basis_ref, t), preferred_element_type=jnp.float32)
            fitted = fitted[0:16] + fitted[16:32]
            snaps = snaps_ref[t].astype(jnp.float32)
            left_over = snaps - fitted
            made[0, t] = left_over[0:8] * w00
            made[1, t] = left_over[8:16] * w11 + left_over[0:8] * w01
        span = pl.ds(c * per_chunk, per_chunk)
        copies.append(
            pltpu.make_async_copy(made.at[:, span], modes_ref.at[:, span], sems.at[c])
        )
        copies[c].start()
    for copy in copies:
        copy.wait()


def params(mib):
    return pltpu.CompilerParams(vmem_limit_bytes=mib * 1024 * 1024)


def cost(flops, moved):
    return pl.CostEstimate(flops=flops, bytes_accessed=moved, transcendentals=0)


WHOLE = pl.BlockSpec(memory_space=pltpu.VMEM)
FAR = pl.BlockSpec(memory_space=pltpu.HBM)
LOOSE = pl.BlockSpec(memory_space=pl.ANY)
SCALAR = pl.BlockSpec(memory_space=pltpu.SMEM)


def swap_added(value, axis, bit):
    count = lax.axis_size(axis)
    return value + lax.ppermute(value, axis, [(i, i ^ bit) for i in range(count)])


def bits(count):
    made = [1 << k for k in range(count.bit_length() - 1)]
    if count != 1 << len(made):
        raise ValueError("axis size")
    return made


def body(windows, pod_basis):
    f32, bf16 = jnp.float32, jnp.bfloat16
    shape = jax.ShapeDtypeStruct
    count, fields, planes, layers, cells = windows.shape
    ring, walls = lax.axis_size("solver"), lax.axis_size("analysis")
    paired = walls == 2 and planes == 8 and layers == 4
    place = lax.axis_index("analysis").astype(jnp.int32).reshape(1)
    modes, _, pod_planes, pod_layers, _ = pod_basis.shape
    tiles = fields * pod_planes * (pod_layers // 8)
    basis = pod_basis.reshape(modes, tiles, 8, cells)
    wide = modes * 8
    basis_bytes = basis.size * 2

    to_right = [(i, (i + 1) % ring) for i in range(ring)]
    to_left = [((i + 1) % ring, i) for i in range(ring)]
    edge_shape = shape((count, fields, REACH, layers, cells), f32)
    face_scratch = [pltpu.VMEM((fields, planes, layers, cells), f32)]
    face_cost = cost(10_000_000, 10 * windows.size)
    if paired:
        swap = [(0, 1), (1, 0)]
        group_shape = shape((fields, 48, cells), bf16)
        lows = pltpu.VMEM((fields, 16, cells), f32)
        near_group, kept = pl.pallas_call(
            near_kernel,
            out_shape=[group_shape, shape(windows.shape, f32)],
            in_specs=[SCALAR, WHOLE],
            out_specs=[WHOLE] * 2,
            scratch_shapes=[lows, pltpu.SemaphoreType.DMA],
            compiler_params=params(16),
            cost_estimate=face_cost,
            name="near_faces",
        )(place, windows)
        later_group, first_edge, second_edge = pl.pallas_call(
            later_kernel,
            out_shape=[group_shape] + [edge_shape] * 2,
            in_specs=[SCALAR, LOOSE, WHOLE],
            out_specs=[WHOLE] * 3,
            scratch_shapes=[pltpu.VMEM((count, fields, planes, layers, cells), f32), lows],
            compiler_params=params(16),
            cost_estimate=face_cost,
            name="later_faces",
        )(place, near_group, kept)
        near_group = lax.ppermute(near_group, "analysis", swap)
        down = [(2 * ((i + 1) % ring), 2 * i) for i in range(ring)]
        up = [(2 * i, 2 * ((i + 1) % ring)) for i in range(ring)]
        odd = lambda pairs: [(a + 1, b + 1) for a, b in pairs]
        first_edge = lax.ppermute(first_edge, ("solver", "analysis"), down + odd(up))
        second_edge = lax.ppermute(second_edge, ("solver", "analysis"), up + odd(down))
        later_group = lax.ppermute(later_group, "analysis", swap)
    else:
        kept, to_next, to_last, up, down = pl.pallas_call(
            functools.partial(face_kernel, True),
            out_shape=[shape(windows.shape, f32)]
            + [edge_shape] * 2
            + [shape(windows.shape, f32)] * 2,
            in_specs=[SCALAR, FAR],
            out_specs=[WHOLE] * 5,
            scratch_shapes=face_scratch + [pltpu.SemaphoreType.DMA((count,))],
            compiler_params=params(16),
            cost_estimate=face_cost,
            name="faces",
        )(place, windows)
        wall_terms = [
            lax.ppermute(up, "analysis", [(i, i + 1) for i in range(walls - 1)]),
            lax.ppermute(down, "analysis", [(i + 1, i) for i in range(walls - 1)]),
        ]
        from_left = lax.ppermute(to_next, "solver", to_right)
        from_right = lax.ppermute(to_last, "solver", to_left)

    early = 2
    gram_flops = 2 * wide * wide * cells * tiles
    inner, right, left, basis = pl.pallas_call(
        functools.partial(inner_gram_kernel, early),
        out_shape=[
            shape(windows.shape, f32),
            shape((wide, wide // 2), f32),
            shape((wide // 2, wide // 2), f32),
            shape(basis.shape, bf16),
        ],
        in_specs=[WHOLE, FAR],
        out_specs=[WHOLE] * 4,
        scratch_shapes=[
            pltpu.VMEM((2 * fields, planes, count * layers, cells), f32),
            pltpu.SemaphoreType.DMA((fields,)),
        ],
        compiler_params=params(40),
        cost_estimate=cost(1_000_000, windows.size),
        name="inner_gram",
    )(kept, basis)

    def rest_of_gram(after):
        return pl.pallas_call(
            functools.partial(gram_kernel, early, fields),
            out_shape=shape((modes // 2, 2 * modes), f32),
            in_specs=[LOOSE] + [WHOLE] * 3,
            out_specs=WHOLE,
            scratch_shapes=[pltpu.VMEM((wide // LANES, wide, LANES), f32)],
            compiler_params=params(24),
            cost_estimate=cost(gram_flops // 2, basis_bytes),
            name="gram",
        )(after, right, left, basis)

    join_cost = cost(1_000_000, 16 * windows.size)
    if paired:
        half_shape = (count, fields, planes * layers // 2, cells)

        half_next = shape((count, fields, planes // 2, layers, cells), f32)

        inner_given = pl.pallas_call(
            wall_join_kernel,
            out_shape=half_next,
            in_specs=[SCALAR] + [WHOLE] * 2,
            out_specs=WHOLE,
            compiler_params=params(16),
            cost_estimate=cost(gram_flops // 2, basis_bytes),
            name="wall_join",
        )(place, inner, near_group)
        next_given, given = pl.pallas_call(
            edge_join_kernel,
            out_shape=[half_next, shape(half_shape, bf16)],
            in_specs=[WHOLE] * 2,
            out_specs=[WHOLE] * 2,
            compiler_params=params(16),
            cost_estimate=join_cost,
            name="edge_join",
        )(inner_given, first_edge)
        got = lax.ppermute(given, "analysis", swap)
        gram = rest_of_gram(given)
    else:
        next_windows = pl.pallas_call(
            functools.partial(join_kernel, 2),
            out_shape=shape(windows.shape, f32),
            in_specs=[WHOLE] * 5,
            out_specs=WHOLE,
            compiler_params=params(16),
            cost_estimate=join_cost,
            name="join",
        )(inner, from_left, from_right, *wall_terms)
        gram = rest_of_gram(place)
    ring_bits = bits(ring)
    lone = ring_bits.pop(1 if len(ring_bits) > 1 else 0)
    gram_far = lax.ppermute(gram, "solver", [(i, i ^ lone) for i in range(ring)])
    if paired:
        next_own, own = pl.pallas_call(
            own_join_kernel,
            out_shape=[half_next, shape(half_shape, bf16)],
            in_specs=[SCALAR, LOOSE] + [WHOLE] * 3,
            out_specs=[WHOLE] * 2,
            compiler_params=params(16),
            cost_estimate=join_cost,
            name="own_join",
        )(place, gram, inner, second_edge, later_group)

    sums_shape = shape((8, LANES), f32)
    snaps_shape = shape((tiles, 2 * 8, cells), bf16)
    scratch = [pltpu.VMEM((LANES, LANES), f32), pltpu.VMEM((1, wide, LANES), f32)]
    project_cost = cost(2 * wide * 16 * cells * tiles, basis_bytes)
    if paired:
        sums, snaps, next_windows = pl.pallas_call(
            functools.partial(project_kernel, True),
            out_shape=[sums_shape, snaps_shape, shape(windows.shape, f32)],
            in_specs=[SCALAR] + [WHOLE] * 5,
            out_specs=[WHOLE, WHOLE, FAR],
            scratch_shapes=scratch + [pltpu.SemaphoreType.DMA((2,))],
            compiler_params=params(16),
            cost_estimate=project_cost,
            name="project",
        )(place, own, got, next_own, next_given, basis)
    else:
        relaid = lax.all_to_all(
            next_windows.astype(bf16), "analysis", split_axis=2, concat_axis=3, tiled=True
        )
        snaps = relaid.reshape(count, tiles, 8, cells).transpose(1, 0, 2, 3)
        snaps = snaps.reshape(tiles, count * 8, cells)
        sums = pl.pallas_call(
            functools.partial(project_kernel, False),
            out_shape=sums_shape,
            in_specs=[SCALAR] + [WHOLE] * 2,
            out_specs=WHOLE,
            scratch_shapes=scratch,
            compiler_params=params(16),
            cost_estimate=project_cost,
            name="project",
        )(place, snaps, basis)
    sums = pl.pallas_call(
        merge_kernel,
        out_shape=shape((modes // 2 + 8, LANES), f32),
        in_specs=[WHOLE] * 3,
        out_specs=WHOLE,
        compiler_params=params(16),
        cost_estimate=cost(10_000, 8 * modes * LANES),
        name="merge",
    )(gram, gram_far, sums)
    for bit in bits(walls):
        sums = swap_added(sums, "analysis", bit)
    for bit in ring_bits:
        sums = swap_added(sums, "solver", bit)
    inverse, spread = pl.pallas_call(
        inverse_kernel,
        out_shape=[shape((modes, modes), f32), shape((modes, wide), f32)],
        in_specs=[WHOLE],
        out_specs=[WHOLE] * 2,
        scratch_shapes=[pltpu.VMEM((modes, 2 * modes), f32)] * 2,
        compiler_params=params(16),
        cost_estimate=cost(20_000_000, 8 * modes * modes),
        name="inverse",
    )(sums)
    projected = swap_added(sums, "solver", lone)

    rows_total = ring * walls * tiles * 8 * cells
    new_modes, solved, factor = pl.pallas_call(
        functools.partial(finish_kernel, rows_total),
        out_shape=[
            shape((count, tiles, 8, cells), f32),
            shape((count, modes), f32),
            shape((count, count), f32),
        ],
        in_specs=[WHOLE] * 6,
        out_specs=[FAR, WHOLE, WHOLE],
        scratch_shapes=[
            pltpu.VMEM((count, tiles, 8, cells), f32),
            pltpu.SemaphoreType.DMA((fields,)),
        ],
        compiler_params=params(16),
        cost_estimate=cost(2 * wide * 32 * cells * tiles, basis_bytes + 8 * windows.size),
        name="finish",
    )(projected, sums, inverse, spread, snaps, basis)
    new_modes = new_modes.reshape(count, fields, pod_planes, pod_layers, cells)
    return next_windows, solved, new_modes, factor


def solution(mesh):
    in_specs = (
        P(None, None, "solver", "analysis", None),
        P(None, None, ("solver", "analysis"), None, None),
    )
    out_specs = (
        P(None, None, "solver", "analysis", None),
        P(),
        P(None, None, ("solver", "analysis"), None, None),
        P(),
    )
    return jax.shard_map(body, mesh=mesh, in_specs=in_specs, out_specs=out_specs, check_vma=False)
```

```python
import functools

import jax
import jax.numpy as jnp
from jax import lax
from jax.experimental import pallas as pl
from jax.experimental.pallas import tpu as pltpu
from jax.sharding import PartitionSpec as P

PRESSURE_FACTOR = 1.4 - 1.0
SECTION_STEP = 0.25
CENTRAL_WEIGHTS = (0.8, -0.2, 4.0 / 105.0, -1.0 / 280.0)
REACH = 4
LANES = 128
HIGHEST = lax.Precision.HIGHEST
NT = (((1,), (1,)), ((), ()))


def weight(k):
    if k == 0 or abs(k) > REACH:
        return 0.0
    value = -SECTION_STEP * CENTRAL_WEIGHTS[abs(k) - 1]
    return value if k > 0 else -value


def row_weights(shape, values):
    rows = lax.broadcasted_iota(jnp.int32, shape, len(shape) - 2)
    made = jnp.full(shape, values[0], jnp.float32)
    for i, value in enumerate(values[1:], start=1):
        made = jnp.where(rows == i, jnp.float32(value), made)
    return made


def primitives(fields):
    density, mx, my, mz, energy = fields
    inverse = 1.0 / density
    ux, uy, uz = mx * inverse, my * inverse, mz * inverse
    pressure = PRESSURE_FACTOR * (energy - 0.5 * (mx * ux + my * uy + mz * uz))
    return (mx, my, mz), (ux, uy, uz), pressure, energy + pressure


def flux(parts, direction):
    moments, speeds, pressure, enthalpy = parts
    speed = speeds[direction]
    made = [moments[direction]]
    for axis in range(3):
        term = moments[axis] * speed
        made.append(term + pressure if axis == direction else term)
    made.append(enthalpy * speed)
    return made


def face_kernel(two_sided, where_ref, source_ref, windows_ref, left_ref, right_ref, *rest):
    windows, _, planes, layers, cells = windows_ref.shape
    wall_refs, scratch, sems = rest[:-2], rest[-2], rest[-1]
    copies = [
        pltpu.make_async_copy(source_ref.at[w], windows_ref.at[w], sems.at[w])
        for w in range(windows)
    ]
    for copy in copies:
        copy.start()
    tile = (layers, cells)
    up = [
        row_weights(tile, [weight(j - layers - i) for i in range(layers)]) for j in range(layers)
    ]
    down = [
        row_weights(tile, [weight(layers + j - i) for i in range(layers)]) for j in range(layers)
    ]
    if two_sided:
        tables = (up, down)
    else:
        first = where_ref[0] == 0
        tables = ([jnp.where(first, u, d) for u, d in zip(up, down)],)
    for w in range(windows):
        copies[w].wait()
        for x in range(planes):
            parts = primitives([windows_ref[w, f, x] for f in range(5)])
            for f, value in enumerate(flux(parts, 0)):
                scratch[f, x] = value
            for f, value in enumerate(flux(parts, 1)):
                for ref, table in zip(wall_refs, tables):
                    total = None
                    for j in range(layers):
                        term = table[j] * value[j : j + 1, :]
                        total = term if total is None else total + term
                    ref[w, f, x] = total
        for f in range(5):
            for i in range(REACH):
                total = None
                for j in range(planes):
                    c = weight(j - planes - i)
                    if c:
                        term = c * scratch[f, j]
                        total = term if total is None else total + term
                left_ref[w, f, i] = total
                total = None
                for j in range(planes):
                    c = weight(j + REACH - i)
                    if c:
                        term = c * scratch[f, j]
                        total = term if total is None else total + term
                right_ref[w, f, i] = total


def wall_group(where_ref, windows_ref, group_ref, lows, base, keep_x):
    windows, _, planes, layers, cells = windows_ref.shape
    tile = (layers, cells)
    first = where_ref[0] == 0
    table = [
        jnp.where(
            first,
            row_weights(tile, [weight(j - layers - i) for i in range(layers)]),
            row_weights(tile, [weight(layers + j - i) for i in range(layers)]),
        )
        for j in range(layers)
    ]
    for w in range(windows):
        upper = [[] for _ in range(5)]
        lower = [[] for _ in range(5)]
        for x in range(planes // 2):
            parts = primitives([windows_ref[w, f, base + x] for f in range(5)])
            keep_x(w, base + x, parts)
            for f, value in enumerate(flux(parts, 1)):
                total = None
                for j in range(layers):
                    term = table[j] * value[j : j + 1, :]
                    total = term if total is None else total + term
                high = total.astype(jnp.bfloat16).astype(jnp.float32)
                rest = total - high
                upper[f].append(high)
                lower[f].append(jnp.where(first, rest[0:2], rest[2:4]))
        for f in range(5):
            group_ref[f, 16 * w : 16 * w + 16] = jnp.concatenate(upper[f], axis=0).astype(
                jnp.bfloat16
            )
            lows[f, 8 * w : 8 * w + 8] = jnp.concatenate(lower[f], axis=0)
    for f in range(5):
        group_ref[f, 32:48] = lows[f].astype(jnp.bfloat16)


def near_kernel(where_ref, source_ref, group_ref, kept_ref, lows, sem):
    copy = pltpu.make_async_copy(source_ref, kept_ref, sem)
    copy.start()
    base = source_ref.shape[2] // 2 * where_ref[0]
    wall_group(where_ref, source_ref, group_ref, lows, base, lambda w, x, parts: None)
    copy.wait()


def later_kernel(where_ref, _, windows_ref, group_ref, first_ref, second_ref, scratch, lows):
    windows, _, planes, layers, cells = windows_ref.shape
    half = planes // 2

    def keep_x(w, x, parts):
        for f, value in enumerate(flux(parts, 0)):
            scratch[w, f, x] = value

    base = half * (1 - where_ref[0])
    wall_group(where_ref, windows_ref, group_ref, lows, base, keep_x)
    for w in range(windows):
        for x in range(half):
            plane = half * where_ref[0] + x
            keep_x(w, plane, primitives([windows_ref[w, f, plane] for f in range(5)]))
        for f in range(5):
            for i in range(REACH):
                sides = []
                for offset in (-planes, REACH):
                    total = None
                    for j in range(planes):
                        c = weight(j + offset - i)
                        if c:
                            term = c * scratch[w, f, j]
                            total = term if total is None else total + term
                    sides.append(total)
                to_next, to_last = sides
                first_ref[w, f, i] = jnp.where(where_ref[0] == 0, to_last, to_next)
                second_ref[w, f, i] = jnp.where(where_ref[0] == 0, to_next, to_last)


def inner_part(windows_ref, part_ref, scratch):
    windows, _, planes, layers, cells = windows_ref.shape
    tile = (windows * layers, cells)
    walls = {
        k: row_weights(
            tile, [weight(k) if 0 <= i + k < layers else 0.0 for i in range(layers)] * windows
        )
        for k in range(-REACH, REACH + 1)
        if 0 < abs(k) < layers
    }
    for x in range(planes):
        fields = [
            jnp.concatenate([windows_ref[w, f, x] for w in range(windows)], axis=0)
            for f in range(5)
        ]
        parts = primitives(fields)
        for f, value in enumerate(flux(parts, 0)):
            scratch[f, x] = value
        flux_y, flux_z = flux(parts, 1), flux(parts, 2)
        for f in range(5):
            total = fields[f]
            for k, line in walls.items():
                total = total + line * pltpu.roll(flux_y[f], -k % tile[0], 0)
            for k in range(1, REACH + 1):
                total = total + weight(k) * (
                    pltpu.roll(flux_z[f], cells - k, 1) - pltpu.roll(flux_z[f], k, 1)
                )
            scratch[5 + f, x] = total
    for f in range(5):
        for x in range(planes):
            total = scratch[5 + f, x]
            for k in range(-REACH, REACH + 1):
                if k and 0 <= x + k < planes:
                    total = total + weight(k) * scratch[f, x + k]
            for w in range(windows):
                part_ref[w, f, x] = total[layers * w : layers * (w + 1)]


def gram_blocks(basis_ref, chunks, per_chunk, right, left):
    half = left.shape[0]
    for c in chunks:
        rows = jnp.concatenate(
            [modes_of(basis_ref, t) for t in range(c * per_chunk, (c + 1) * per_chunk)], axis=1
        )
        right = right + lax.dot_general(
            rows, rows[half:], NT, preferred_element_type=jnp.float32
        )
        left = left + lax.dot_general(
            rows[:half], rows[:half], NT, preferred_element_type=jnp.float32
        )
    return right, left


def inner_gram_kernel(
    early, windows_ref, basis_ref, part_ref, right_ref, left_ref, kept_ref, scratch, sems
):
    chunks = sems.shape[0]
    per_chunk = kept_ref.shape[1] // chunks
    copies = []
    for c in range(chunks):
        span = pl.ds(c * per_chunk, per_chunk)
        copies.append(
            pltpu.make_async_copy(basis_ref.at[:, span], kept_ref.at[:, span], sems.at[c])
        )
        copies[c].start()
    inner_part(windows_ref, part_ref, scratch)
    right, left = jnp.zeros(right_ref.shape, jnp.float32), jnp.zeros(left_ref.shape, jnp.float32)
    for c in range(chunks):
        copies[c].wait()
        if c < early:
            right, left = gram_blocks(kept_ref, [c], per_chunk, right, left)
    right_ref[...] = right
    left_ref[...] = left


def gram_kernel(early, chunks, _, right_ref, left_ref, basis_ref, gram_ref, total):
    modes, tiles = basis_ref.shape[:2]
    wide = modes * 8
    half = wide // 2
    right, left = gram_blocks(
        basis_ref, range(early, chunks), tiles // chunks, right_ref[...], left_ref[...]
    )
    tiles_left = half // LANES
    turned = right[0:half].T
    for tile in range(tiles_left):
        span = slice(tile * LANES, (tile + 1) * LANES)
        total[tile, 0:half] = left[:, span]
        total[tile, half:] = turned[:, span]
        total[tiles_left + tile] = right[:, span]
    rows = folded(total, modes)
    picks = (
        lax.broadcasted_iota(jnp.int32, (wide, modes), 0) // 8
        == lax.broadcasted_iota(jnp.int32, (wide, modes), 1)
    ).astype(jnp.float32)
    gram = jnp.dot(rows, picks, precision=HIGHEST, preferred_element_type=jnp.float32)
    gram_ref[:, 0:modes] = gram[0 : modes // 2]
    gram_ref[:, modes:] = gram[modes // 2 :]


def join_kernel(walls, part_ref, left_ref, right_ref, *rest):
    wall_refs, next_ref = rest[:walls], rest[walls]
    windows, _, planes, layers, cells = part_ref.shape
    for w in range(windows):
        for f in range(5):
            for x in range(planes):
                total = part_ref[w, f, x]
                for ref in wall_refs:
                    total = total + ref[w, f, x]
                if x < REACH:
                    total = total + left_ref[w, f, x]
                if x >= planes - REACH:
                    total = total + right_ref[w, f, x - planes + REACH]
                next_ref[w, f, x] = total


def wall_terms_of(first, group_ref, w, f):
    upper = group_ref[f, 16 * w : 16 * w + 16].astype(jnp.float32)
    lower = group_ref[f, 32:48].astype(jnp.float32)[8 * w : 8 * w + 8]
    zero = jnp.zeros((2, upper.shape[1]), jnp.float32)
    made = []
    for x in range(4):
        rest = lower[2 * x : 2 * x + 2]
        rest = jnp.where(
            first, jnp.concatenate([zero, rest], axis=0), jnp.concatenate([rest, zero], axis=0)
        )
        made.append(upper[4 * x : 4 * x + 4] + rest)
    return made


def wall_join_kernel(where_ref, part_ref, group_ref, given_ref):
    windows, _, planes = part_ref.shape[:3]
    base = planes // 2 * (1 - where_ref[0])
    for w in range(windows):
        for f in range(5):
            for x, term in enumerate(wall_terms_of(where_ref[0] == 0, group_ref, w, f)):
                given_ref[w, f, x] = part_ref[w, f, base + x] + term


def edge_join_kernel(part_ref, edge_ref, made, snaps_ref):
    windows, _, half = part_ref.shape[:3]
    for w in range(windows):
        for f in range(5):
            done = []
            for x in range(half):
                total = part_ref[w, f, x] + edge_ref[w, f, x]
                made[w, f, x] = total
                done.append(total)
            snaps_ref[w, f] = jnp.concatenate(done, axis=0).astype(jnp.bfloat16)


def own_join_kernel(where_ref, _, part_ref, edge_ref, group_ref, made, snaps_ref):
    windows, _, planes = part_ref.shape[:3]
    base = planes // 2 * where_ref[0]
    for w in range(windows):
        for f in range(5):
            done = []
            for x, term in enumerate(wall_terms_of(where_ref[0] == 0, group_ref, w, f)):
                total = part_ref[w, f, base + x] + term + edge_ref[w, f, x]
                made[w, f, x] = total
                done.append(total)
            snaps_ref[w, f] = jnp.concatenate(done, axis=0).astype(jnp.bfloat16)


def same_layer(shape):
    rows = lax.broadcasted_iota(jnp.int32, shape, 0)
    columns = lax.broadcasted_iota(jnp.int32, shape, 1)
    return lax.rem(rows, 8) == lax.rem(columns, 8)


def folded(total, modes):
    kept = lax.rem(lax.broadcasted_iota(jnp.int32, (modes, LANES), 1), 8)
    made = []
    for tile in range(total.shape[0]):
        rows = jnp.zeros((modes, LANES), jnp.float32)
        for y in range(8):
            rows = jnp.where(kept == y, total[tile, pl.ds(y, modes, 8), :], rows)
        made.append(rows)
    return made[0] if len(made) == 1 else jnp.concatenate(made, axis=1)


def modes_of(basis_ref, t):
    modes, _, layers, cells = basis_ref.shape
    return basis_ref[:, t].reshape(modes * layers, cells)


def project_kernel(paired, where_ref, *rest):
    if paired:
        (
            own_ref, got_ref, next_own_ref, next_given_ref, basis_ref,
            sums_ref, snaps_ref, next_ref, square, wide_sums, sems,
        ) = rest
        first = where_ref[0] == 0
        half = next_own_ref.shape[2]
        copies = []
        for i, (source, base) in enumerate(
            ((next_own_ref, half * where_ref[0]), (next_given_ref, half * (1 - where_ref[0])))
        ):
            copies.append(
                pltpu.make_async_copy(source, next_ref.at[:, :, pl.ds(base, half)], sems.at[i])
            )
            copies[i].start()
        for w in range(own_ref.shape[0]):
            for f in range(own_ref.shape[1]):
                own = own_ref[w, f].astype(jnp.float32)
                got = got_ref[w, f].astype(jnp.float32)
                low = jnp.where(first, own, got)
                high = jnp.where(first, got, own)
                for t in range(4):
                    snaps_ref[4 * f + t, pl.ds(8 * w, 8)] = jnp.concatenate(
                        [low[4 * t : 4 * t + 4], high[4 * t : 4 * t + 4]], axis=0
                    ).astype(jnp.bfloat16)
    else:
        snaps_ref, basis_ref, sums_ref, square, wide_sums = rest
        copies = []
    modes, tiles = basis_ref.shape[:2]
    columns = snaps_ref.shape[1]
    total = jnp.zeros((modes * 8, columns), jnp.float32)
    small = jnp.zeros((columns, columns), jnp.float32)
    for t in range(tiles):
        snaps = snaps_ref[t]
        total = total + lax.dot_general(
            modes_of(basis_ref, t), snaps, NT, preferred_element_type=jnp.float32
        )
        small = small + lax.dot_general(snaps, snaps, NT, preferred_element_type=jnp.float32)
    wide_sums[0, :, 0:columns] = total
    square[...] = jnp.zeros_like(square)
    square[0:modes, :] = folded(wide_sums, modes)
    kept = jnp.where(same_layer(small.shape), small, 0.0)
    square[modes : modes + 1, 0:columns] = jnp.sum(kept[0:8], axis=0, keepdims=True)
    square[modes + 1 : modes + 2, 0:columns] = jnp.sum(kept[8:16], axis=0, keepdims=True)
    lanes = lax.broadcasted_iota(jnp.int32, square.shape, 1)
    turned = jnp.where(lanes < columns, square[...], 0.0).T
    sums = jnp.concatenate(
        [
            jnp.sum(turned[0:8], axis=0, keepdims=True),
            jnp.sum(turned[8:16], axis=0, keepdims=True),
        ],
        axis=0,
    )
    sums_ref[...] = jnp.concatenate(
        [sums, jnp.zeros((6, sums.shape[1]), jnp.float32)], axis=0
    )
    for copy in copies:
        copy.wait()


def merge_kernel(gram_ref, far_ref, sums_ref, merged_ref):
    rows = gram_ref.shape[0]
    merged_ref[0:rows] = gram_ref[...] + far_ref[...]
    merged_ref[rows:] = sums_ref[...]


def unpacked(sums_ref, modes):
    half = modes // 2
    return jnp.concatenate([sums_ref[0:half, 0:modes], sums_ref[0:half, modes:]], axis=0)


def inverse_kernel(sums_ref, inverse_ref, spread_ref, plain, scaled):
    modes = inverse_ref.shape[0]
    rows = lax.broadcasted_iota(jnp.int32, (8, 2 * modes), 0)
    lanes = lax.broadcasted_iota(jnp.int32, (8, 2 * modes), 1)
    tiles = []
    gram = unpacked(sums_ref, modes)
    for tile in range(modes // 8):
        eye = (lanes == rows + (modes + 8 * tile)).astype(jnp.float32)
        start = 8 * tile % (modes // 2)
        line = sums_ref[start : start + 8, :]
        if 8 * tile >= modes // 2:
            line = pltpu.roll(line, modes, 1)
        tiles.append(jnp.where(lanes < modes, line, eye))
    count = modes // 8
    for home in range(count):
        columns = [
            [
                jnp.broadcast_to(
                    tiles[tile][:, 8 * home + j : 8 * home + j + 1], (8, 2 * modes)
                )
                for tile in range(home, count)
            ]
            for j in range(8)
        ]
        for j in range(8):
            k = 8 * home + j
            inverse = 1.0 / columns[j][0]
            inverse = inverse[j : j + 1, :]
            row = tiles[home][j : j + 1, :]
            ready = row * inverse
            plain[k : k + 1, :] = row
            scaled[k : k + 1, :] = ready
            factors = [jnp.where(rows > j, columns[j][0], 0.0)] + columns[j][1:]
            for later in range(j + 1, 8):
                share = columns[j][0][later : later + 1, :] * inverse
                columns[later] = [c - f * share for c, f in zip(columns[later], factors)]
            for tile in range(home, count):
                tiles[tile] = tiles[tile] - factors[tile - home] * ready
    exact = functools.partial(
        lax.dot_general, precision=HIGHEST, preferred_element_type=jnp.float32
    )
    plainly = (((1,), (0,)), ((), ()))
    inverse = exact(plain[:, modes:], scaled[:, modes:], (((0,), (0,)), ((), ())))
    square = (modes, modes)
    eye = lax.broadcasted_iota(jnp.int32, square, 0) == lax.broadcasted_iota(jnp.int32, square, 1)
    off = eye.astype(jnp.float32) - exact(gram, inverse, plainly)
    inverse = inverse + exact(inverse, off, plainly)
    inverse_ref[...] = inverse
    wide = spread_ref.shape[1]
    spread = (
        lax.broadcasted_iota(jnp.int32, (modes, wide), 1) // 8
        == lax.broadcasted_iota(jnp.int32, (modes, wide), 0)
    ).astype(jnp.float32)
    spread_ref[...] = exact(inverse, spread, plainly)


def finish_kernel(
    rows_total, projected_ref, sums_ref, inverse_ref, spread_ref, snaps_ref, basis_ref,
    modes_ref, solved_ref, factor_ref, made, sems,
):
    modes, tiles, _, cells = basis_ref.shape
    wide = modes * 8
    exact = functools.partial(jnp.dot, precision=HIGHEST, preferred_element_type=jnp.float32)
    base = modes // 2
    projected = projected_ref[base : base + 8, 0:modes]
    lines = exact(projected, spread_ref[...])
    full = jnp.concatenate(
        [jnp.broadcast_to(lines[0:1], (8, wide)), jnp.broadcast_to(lines[1:2], (8, wide))],
        axis=0,
    )
    full = jnp.where(same_layer(full.shape), full, 0.0)
    upper = full.astype(jnp.bfloat16)
    fit = jnp.concatenate([upper, (full - upper.astype(jnp.float32)).astype(jnp.bfloat16)], axis=0)
    solved = exact(projected, inverse_ref[...])
    left = projected - exact(solved, unpacked(sums_ref, modes))

    def inner(p, i, q, j):
        return jnp.sum(p[i : i + 1] * q[j : j + 1], axis=1, keepdims=True)

    def entry(i, j):
        square = projected_ref[base + i : base + i + 1, modes + j : modes + j + 1]
        return square - inner(projected, i, solved, j) - inner(solved, i, left, j)

    first = jnp.sqrt(entry(0, 0))
    below = entry(1, 0) / first
    second = jnp.sqrt(entry(1, 1) - below * below)
    scaling = jnp.sqrt(jnp.float32(rows_total))
    w00 = scaling / first
    w11 = scaling / second
    w01 = -(below / first) * w11
    solved_ref[...] = solved[0:2]
    factor_ref[0:1, 0:1] = first / scaling
    factor_ref[0:1, 1:2] = below / scaling
    factor_ref[1:2, 0:1] = jnp.zeros_like(first)
    factor_ref[1:2, 1:2] = second / scaling
    chunks = sems.shape[0]
    per_chunk = tiles // chunks
    copies = []
    for c in range(chunks):
        for t in range(c * per_chunk, (c + 1) * per_chunk):
            fitted = jnp.dot(fit, modes_of(basis_ref, t), preferred_element_type=jnp.float32)
            fitted = fitted[0:16] + fitted[16:32]
            snaps = snaps_ref[t].astype(jnp.float32)
            left_over = snaps - fitted
            made[0, t] = left_over[0:8] * w00
            made[1, t] = left_over[8:16] * w11 + left_over[0:8] * w01
        span = pl.ds(c * per_chunk, per_chunk)
        copies.append(
            pltpu.make_async_copy(made.at[:, span], modes_ref.at[:, span], sems.at[c])
        )
        copies[c].start()
    for copy in copies:
        copy.wait()


def params(mib):
    return pltpu.CompilerParams(vmem_limit_bytes=mib * 1024 * 1024)


def cost(flops, moved):
    return pl.CostEstimate(flops=flops, bytes_accessed=moved, transcendentals=0)


WHOLE = pl.BlockSpec(memory_space=pltpu.VMEM)
FAR = pl.BlockSpec(memory_space=pltpu.HBM)
LOOSE = pl.BlockSpec(memory_space=pl.ANY)
SCALAR = pl.BlockSpec(memory_space=pltpu.SMEM)


def swap_added(value, axis, bit):
    count = lax.axis_size(axis)
    return value + lax.ppermute(value, axis, [(i, i ^ bit) for i in range(count)])


def bits(count):
    made = [1 << k for k in range(count.bit_length() - 1)]
    if count != 1 << len(made):
        raise ValueError("axis size")
    return made


def body(windows, pod_basis):
    f32, bf16 = jnp.float32, jnp.bfloat16
    shape = jax.ShapeDtypeStruct
    count, fields, planes, layers, cells = windows.shape
    ring, walls = lax.axis_size("solver"), lax.axis_size("analysis")
    paired = walls == 2 and planes == 8 and layers == 4
    place = lax.axis_index("analysis").astype(jnp.int32).reshape(1)
    modes, _, pod_planes, pod_layers, _ = pod_basis.shape
    tiles = fields * pod_planes * (pod_layers // 8)
    basis = pod_basis.reshape(modes, tiles, 8, cells)
    wide = modes * 8
    basis_bytes = basis.size * 2

    to_right = [(i, (i + 1) % ring) for i in range(ring)]
    to_left = [((i + 1) % ring, i) for i in range(ring)]
    edge_shape = shape((count, fields, REACH, layers, cells), f32)
    face_scratch = [pltpu.VMEM((fields, planes, layers, cells), f32)]
    face_cost = cost(10_000_000, 10 * windows.size)
    if paired:
        swap = [(0, 1), (1, 0)]
        group_shape = shape((fields, 48, cells), bf16)
        lows = pltpu.VMEM((fields, 16, cells), f32)
        near_group, kept = pl.pallas_call(
            near_kernel,
            out_shape=[group_shape, shape(windows.shape, f32)],
            in_specs=[SCALAR, WHOLE],
            out_specs=[WHOLE] * 2,
            scratch_shapes=[lows, pltpu.SemaphoreType.DMA],
            compiler_params=params(16),
            cost_estimate=face_cost,
            name="near_faces",
        )(place, windows)
        later_group, first_edge, second_edge = pl.pallas_call(
            later_kernel,
            out_shape=[group_shape] + [edge_shape] * 2,
            in_specs=[SCALAR, LOOSE, WHOLE],
            out_specs=[WHOLE] * 3,
            scratch_shapes=[pltpu.VMEM((count, fields, planes, layers, cells), f32), lows],
            compiler_params=params(16),
            cost_estimate=face_cost,
            name="later_faces",
        )(place, near_group, kept)
        near_group = lax.ppermute(near_group, "analysis", swap)
        down = [(2 * ((i + 1) % ring), 2 * i) for i in range(ring)]
        up = [(2 * i, 2 * ((i + 1) % ring)) for i in range(ring)]
        odd = lambda pairs: [(a + 1, b + 1) for a, b in pairs]
        first_edge = lax.ppermute(first_edge, ("solver", "analysis"), down + odd(up))
        second_edge = lax.ppermute(second_edge, ("solver", "analysis"), up + odd(down))
        later_group = lax.ppermute(later_group, "analysis", swap)
    else:
        kept, to_next, to_last, up, down = pl.pallas_call(
            functools.partial(face_kernel, True),
            out_shape=[shape(windows.shape, f32)]
            + [edge_shape] * 2
            + [shape(windows.shape, f32)] * 2,
            in_specs=[SCALAR, FAR],
            out_specs=[WHOLE] * 5,
            scratch_shapes=face_scratch + [pltpu.SemaphoreType.DMA((count,))],
            compiler_params=params(16),
            cost_estimate=face_cost,
            name="faces",
        )(place, windows)
        wall_terms = [
            lax.ppermute(up, "analysis", [(i, i + 1) for i in range(walls - 1)]),
            lax.ppermute(down, "analysis", [(i + 1, i) for i in range(walls - 1)]),
        ]
        from_left = lax.ppermute(to_next, "solver", to_right)
        from_right = lax.ppermute(to_last, "solver", to_left)

    early = 3
    gram_flops = 2 * wide * wide * cells * tiles
    inner, right, left, basis = pl.pallas_call(
        functools.partial(inner_gram_kernel, early),
        out_shape=[
            shape(windows.shape, f32),
            shape((wide, wide // 2), f32),
            shape((wide // 2, wide // 2), f32),
            shape(basis.shape, bf16),
        ],
        in_specs=[WHOLE, FAR],
        out_specs=[WHOLE] * 4,
        scratch_shapes=[
            pltpu.VMEM((2 * fields, planes, count * layers, cells), f32),
            pltpu.SemaphoreType.DMA((fields,)),
        ],
        compiler_params=params(40),
        cost_estimate=cost(1_000_000, windows.size),
        name="inner_gram",
    )(kept, basis)

    def rest_of_gram(after):
        return pl.pallas_call(
            functools.partial(gram_kernel, early, fields),
            out_shape=shape((modes // 2, 2 * modes), f32),
            in_specs=[LOOSE] + [WHOLE] * 3,
            out_specs=WHOLE,
            scratch_shapes=[pltpu.VMEM((wide // LANES, wide, LANES), f32)],
            compiler_params=params(24),
            cost_estimate=cost(gram_flops // 2, basis_bytes),
            name="gram",
        )(after, right, left, basis)

    join_cost = cost(1_000_000, 16 * windows.size)
    if paired:
        half_shape = (count, fields, planes * layers // 2, cells)

        half_next = shape((count, fields, planes // 2, layers, cells), f32)

        inner_given = pl.pallas_call(
            wall_join_kernel,
            out_shape=half_next,
            in_specs=[SCALAR] + [WHOLE] * 2,
            out_specs=WHOLE,
            compiler_params=params(16),
            cost_estimate=cost(gram_flops // 2, basis_bytes),
            name="wall_join",
        )(place, inner, near_group)
        next_given, given = pl.pallas_call(
            edge_join_kernel,
            out_shape=[half_next, shape(half_shape, bf16)],
            in_specs=[WHOLE] * 2,
            out_specs=[WHOLE] * 2,
            compiler_params=params(16),
            cost_estimate=join_cost,
            name="edge_join",
        )(inner_given, first_edge)
        got = lax.ppermute(given, "analysis", swap)
        gram = rest_of_gram(given)
    else:
        next_windows = pl.pallas_call(
            functools.partial(join_kernel, 2),
            out_shape=shape(windows.shape, f32),
            in_specs=[WHOLE] * 5,
            out_specs=WHOLE,
            compiler_params=params(16),
            cost_estimate=join_cost,
            name="join",
        )(inner, from_left, from_right, *wall_terms)
        gram = rest_of_gram(place)
    ring_bits = bits(ring)
    lone = ring_bits.pop(1 if len(ring_bits) > 1 else 0)
    gram_far = lax.ppermute(gram, "solver", [(i, i ^ lone) for i in range(ring)])
    if paired:
        next_own, own = pl.pallas_call(
            own_join_kernel,
            out_shape=[half_next, shape(half_shape, bf16)],
            in_specs=[SCALAR, LOOSE] + [WHOLE] * 3,
            out_specs=[WHOLE] * 2,
            compiler_params=params(16),
            cost_estimate=join_cost,
            name="own_join",
        )(place, gram, inner, second_edge, later_group)

    sums_shape = shape((8, LANES), f32)
    snaps_shape = shape((tiles, 2 * 8, cells), bf16)
    scratch = [pltpu.VMEM((LANES, LANES), f32), pltpu.VMEM((1, wide, LANES), f32)]
    project_cost = cost(2 * wide * 16 * cells * tiles, basis_bytes)
    if paired:
        sums, snaps, next_windows = pl.pallas_call(
            functools.partial(project_kernel, True),
            out_shape=[sums_shape, snaps_shape, shape(windows.shape, f32)],
            in_specs=[SCALAR] + [WHOLE] * 5,
            out_specs=[WHOLE, WHOLE, FAR],
            scratch_shapes=scratch + [pltpu.SemaphoreType.DMA((2,))],
            compiler_params=params(16),
            cost_estimate=project_cost,
            name="project",
        )(place, own, got, next_own, next_given, basis)
    else:
        relaid = lax.all_to_all(
            next_windows.astype(bf16), "analysis", split_axis=2, concat_axis=3, tiled=True
        )
        snaps = relaid.reshape(count, tiles, 8, cells).transpose(1, 0, 2, 3)
        snaps = snaps.reshape(tiles, count * 8, cells)
        sums = pl.pallas_call(
            functools.partial(project_kernel, False),
            out_shape=sums_shape,
            in_specs=[SCALAR] + [WHOLE] * 2,
            out_specs=WHOLE,
            scratch_shapes=scratch,
            compiler_params=params(16),
            cost_estimate=project_cost,
            name="project",
        )(place, snaps, basis)
    sums = pl.pallas_call(
        merge_kernel,
        out_shape=shape((modes // 2 + 8, LANES), f32),
        in_specs=[WHOLE] * 3,
        out_specs=WHOLE,
        compiler_params=params(16),
        cost_estimate=cost(10_000, 8 * modes * LANES),
        name="merge",
    )(gram, gram_far, sums)
    for bit in bits(walls):
        sums = swap_added(sums, "analysis", bit)
    for bit in ring_bits:
        sums = swap_added(sums, "solver", bit)
    inverse, spread = pl.pallas_call(
        inverse_kernel,
        out_shape=[shape((modes, modes), f32), shape((modes, wide), f32)],
        in_specs=[WHOLE],
        out_specs=[WHOLE] * 2,
        scratch_shapes=[pltpu.VMEM((modes, 2 * modes), f32)] * 2,
        compiler_params=params(16),
        cost_estimate=cost(20_000_000, 8 * modes * modes),
        name="inverse",
    )(sums)
    projected = swap_added(sums, "solver", lone)

    rows_total = ring * walls * tiles * 8 * cells
    new_modes, solved, factor = pl.pallas_call(
        functools.partial(finish_kernel, rows_total),
        out_shape=[
            shape((count, tiles, 8, cells), f32),
            shape((count, modes), f32),
            shape((count, count), f32),
        ],
        in_specs=[WHOLE] * 6,
        out_specs=[FAR, WHOLE, WHOLE],
        scratch_shapes=[
            pltpu.VMEM((count, tiles, 8, cells), f32),
            pltpu.SemaphoreType.DMA((fields,)),
        ],
        compiler_params=params(16),
        cost_estimate=cost(2 * wide * 32 * cells * tiles, basis_bytes + 8 * windows.size),
        name="finish",
    )(projected, sums, inverse, spread, snaps, basis)
    new_modes = new_modes.reshape(count, fields, pod_planes, pod_layers, cells)
    return next_windows, solved, new_modes, factor


def solution(mesh):
    in_specs = (
        P(None, None, "solver", "analysis", None),
        P(None, None, ("solver", "analysis"), None, None),
    )
    out_specs = (
        P(None, None, "solver", "analysis", None),
        P(),
        P(None, None, ("solver", "analysis"), None, None),
        P(),
    )
    return jax.shard_map(body, mesh=mesh, in_specs=in_specs, out_specs=out_specs, check_vma=False)
```

```python
import functools

import jax
import jax.numpy as jnp
from jax import lax
from jax.experimental import pallas as pl
from jax.experimental.pallas import tpu as pltpu
from jax.sharding import PartitionSpec as P

PRESSURE_FACTOR = 1.4 - 1.0
SECTION_STEP = 0.25
CENTRAL_WEIGHTS = (0.8, -0.2, 4.0 / 105.0, -1.0 / 280.0)
REACH = 4
LANES = 128
HIGHEST = lax.Precision.HIGHEST
NT = (((1,), (1,)), ((), ()))


def weight(k):
    if k == 0 or abs(k) > REACH:
        return 0.0
    value = -SECTION_STEP * CENTRAL_WEIGHTS[abs(k) - 1]
    return value if k > 0 else -value


def row_weights(shape, values):
    rows = lax.broadcasted_iota(jnp.int32, shape, len(shape) - 2)
    made = jnp.full(shape, values[0], jnp.float32)
    for i, value in enumerate(values[1:], start=1):
        made = jnp.where(rows == i, jnp.float32(value), made)
    return made


def primitives(fields):
    density, mx, my, mz, energy = fields
    inverse = 1.0 / density
    ux, uy, uz = mx * inverse, my * inverse, mz * inverse
    pressure = PRESSURE_FACTOR * (energy - 0.5 * (mx * ux + my * uy + mz * uz))
    return (mx, my, mz), (ux, uy, uz), pressure, energy + pressure


def flux(parts, direction):
    moments, speeds, pressure, enthalpy = parts
    speed = speeds[direction]
    made = [moments[direction]]
    for axis in range(3):
        term = moments[axis] * speed
        made.append(term + pressure if axis == direction else term)
    made.append(enthalpy * speed)
    return made


def face_kernel(two_sided, where_ref, source_ref, windows_ref, left_ref, right_ref, *rest):
    windows, _, planes, layers, cells = windows_ref.shape
    wall_refs, scratch, sems = rest[:-2], rest[-2], rest[-1]
    copies = [
        pltpu.make_async_copy(source_ref.at[w], windows_ref.at[w], sems.at[w])
        for w in range(windows)
    ]
    for copy in copies:
        copy.start()
    tile = (layers, cells)
    up = [
        row_weights(tile, [weight(j - layers - i) for i in range(layers)]) for j in range(layers)
    ]
    down = [
        row_weights(tile, [weight(layers + j - i) for i in range(layers)]) for j in range(layers)
    ]
    if two_sided:
        tables = (up, down)
    else:
        first = where_ref[0] == 0
        tables = ([jnp.where(first, u, d) for u, d in zip(up, down)],)
    for w in range(windows):
        copies[w].wait()
        for x in range(planes):
            parts = primitives([windows_ref[w, f, x] for f in range(5)])
            for f, value in enumerate(flux(parts, 0)):
                scratch[f, x] = value
            for f, value in enumerate(flux(parts, 1)):
                for ref, table in zip(wall_refs, tables):
                    total = None
                    for j in range(layers):
                        term = table[j] * value[j : j + 1, :]
                        total = term if total is None else total + term
                    ref[w, f, x] = total
        for f in range(5):
            for i in range(REACH):
                total = None
                for j in range(planes):
                    c = weight(j - planes - i)
                    if c:
                        term = c * scratch[f, j]
                        total = term if total is None else total + term
                left_ref[w, f, i] = total
                total = None
                for j in range(planes):
                    c = weight(j + REACH - i)
                    if c:
                        term = c * scratch[f, j]
                        total = term if total is None else total + term
                right_ref[w, f, i] = total


def wall_group(where_ref, windows_ref, group_ref, lows, base, keep_x):
    windows, _, planes, layers, cells = windows_ref.shape
    tile = (layers, cells)
    first = where_ref[0] == 0
    table = [
        jnp.where(
            first,
            row_weights(tile, [weight(j - layers - i) for i in range(layers)]),
            row_weights(tile, [weight(layers + j - i) for i in range(layers)]),
        )
        for j in range(layers)
    ]
    for w in range(windows):
        upper = [[] for _ in range(5)]
        lower = [[] for _ in range(5)]
        for x in range(planes // 2):
            parts = primitives([windows_ref[w, f, base + x] for f in range(5)])
            keep_x(w, base + x, parts)
            for f, value in enumerate(flux(parts, 1)):
                total = None
                for j in range(layers):
                    term = table[j] * value[j : j + 1, :]
                    total = term if total is None else total + term
                high = total.astype(jnp.bfloat16).astype(jnp.float32)
                rest = total - high
                upper[f].append(high)
                lower[f].append(jnp.where(first, rest[0:2], rest[2:4]))
        for f in range(5):
            group_ref[f, 16 * w : 16 * w + 16] = jnp.concatenate(upper[f], axis=0).astype(
                jnp.bfloat16
            )
            lows[f, 8 * w : 8 * w + 8] = jnp.concatenate(lower[f], axis=0)
    for f in range(5):
        group_ref[f, 32:48] = lows[f].astype(jnp.bfloat16)


def near_kernel(where_ref, source_ref, group_ref, kept_ref, lows, sem):
    copy = pltpu.make_async_copy(source_ref, kept_ref, sem)
    copy.start()
    base = source_ref.shape[2] // 2 * where_ref[0]
    wall_group(where_ref, source_ref, group_ref, lows, base, lambda w, x, parts: None)
    copy.wait()


def later_kernel(where_ref, _, windows_ref, group_ref, first_ref, second_ref, scratch, lows):
    windows, _, planes, layers, cells = windows_ref.shape
    half = planes // 2

    def keep_x(w, x, parts):
        for f, value in enumerate(flux(parts, 0)):
            scratch[w, f, x] = value

    base = half * (1 - where_ref[0])
    wall_group(where_ref, windows_ref, group_ref, lows, base, keep_x)
    for w in range(windows):
        for x in range(half):
            plane = half * where_ref[0] + x
            keep_x(w, plane, primitives([windows_ref[w, f, plane] for f in range(5)]))
        for f in range(5):
            for i in range(REACH):
                sides = []
                for offset in (-planes, REACH):
                    total = None
                    for j in range(planes):
                        c = weight(j + offset - i)
                        if c:
                            term = c * scratch[w, f, j]
                            total = term if total is None else total + term
                    sides.append(total)
                to_next, to_last = sides
                first_ref[w, f, i] = jnp.where(where_ref[0] == 0, to_last, to_next)
                second_ref[w, f, i] = jnp.where(where_ref[0] == 0, to_next, to_last)


def inner_part(windows_ref, part_ref, scratch):
    windows, _, planes, layers, cells = windows_ref.shape
    tile = (windows * layers, cells)
    walls = {
        k: row_weights(
            tile, [weight(k) if 0 <= i + k < layers else 0.0 for i in range(layers)] * windows
        )
        for k in range(-REACH, REACH + 1)
        if 0 < abs(k) < layers
    }
    for x in range(planes):
        fields = [
            jnp.concatenate([windows_ref[w, f, x] for w in range(windows)], axis=0)
            for f in range(5)
        ]
        parts = primitives(fields)
        for f, value in enumerate(flux(parts, 0)):
            scratch[f, x] = value
        flux_y, flux_z = flux(parts, 1), flux(parts, 2)
        for f in range(5):
            total = fields[f]
            for k, line in walls.items():
                total = total + line * pltpu.roll(flux_y[f], -k % tile[0], 0)
            for k in range(1, REACH + 1):
                total = total + weight(k) * (
                    pltpu.roll(flux_z[f], cells - k, 1) - pltpu.roll(flux_z[f], k, 1)
                )
            scratch[5 + f, x] = total
    for f in range(5):
        for x in range(planes):
            total = scratch[5 + f, x]
            for k in range(-REACH, REACH + 1):
                if k and 0 <= x + k < planes:
                    total = total + weight(k) * scratch[f, x + k]
            for w in range(windows):
                part_ref[w, f, x] = total[layers * w : layers * (w + 1)]


def gram_blocks(basis_ref, chunks, per_chunk, right, left):
    half = left.shape[0]
    for c in chunks:
        rows = jnp.concatenate(
            [modes_of(basis_ref, t) for t in range(c * per_chunk, (c + 1) * per_chunk)], axis=1
        )
        right = right + lax.dot_general(
            rows, rows[half:], NT, preferred_element_type=jnp.float32
        )
        left = left + lax.dot_general(
            rows[:half], rows[:half], NT, preferred_element_type=jnp.float32
        )
    return right, left


def inner_gram_kernel(
    early, windows_ref, basis_ref, part_ref, right_ref, left_ref, kept_ref, scratch, sems
):
    chunks = sems.shape[0]
    per_chunk = kept_ref.shape[1] // chunks
    copies = []
    for c in range(chunks):
        span = pl.ds(c * per_chunk, per_chunk)
        copies.append(
            pltpu.make_async_copy(basis_ref.at[:, span], kept_ref.at[:, span], sems.at[c])
        )
        copies[c].start()
    inner_part(windows_ref, part_ref, scratch)
    right, left = jnp.zeros(right_ref.shape, jnp.float32), jnp.zeros(left_ref.shape, jnp.float32)
    for c in range(chunks):
        copies[c].wait()
        if c < early:
            right, left = gram_blocks(kept_ref, [c], per_chunk, right, left)
    right_ref[...] = right
    left_ref[...] = left


def gram_kernel(early, chunks, _, right_ref, left_ref, basis_ref, gram_ref, total):
    modes, tiles = basis_ref.shape[:2]
    wide = modes * 8
    half = wide // 2
    right, left = gram_blocks(
        basis_ref, range(early, chunks), tiles // chunks, right_ref[...], left_ref[...]
    )
    tiles_left = half // LANES
    turned = right[0:half].T
    for tile in range(tiles_left):
        span = slice(tile * LANES, (tile + 1) * LANES)
        total[tile, 0:half] = left[:, span]
        total[tile, half:] = turned[:, span]
        total[tiles_left + tile] = right[:, span]
    rows = folded(total, modes)
    picks = (
        lax.broadcasted_iota(jnp.int32, (wide, modes), 0) // 8
        == lax.broadcasted_iota(jnp.int32, (wide, modes), 1)
    ).astype(jnp.float32)
    gram = jnp.dot(rows, picks, precision=HIGHEST, preferred_element_type=jnp.float32)
    gram_ref[:, 0:modes] = gram[0 : modes // 2]
    gram_ref[:, modes:] = gram[modes // 2 :]


def join_kernel(walls, part_ref, left_ref, right_ref, *rest):
    wall_refs, next_ref = rest[:walls], rest[walls]
    windows, _, planes, layers, cells = part_ref.shape
    for w in range(windows):
        for f in range(5):
            for x in range(planes):
                total = part_ref[w, f, x]
                for ref in wall_refs:
                    total = total + ref[w, f, x]
                if x < REACH:
                    total = total + left_ref[w, f, x]
                if x >= planes - REACH:
                    total = total + right_ref[w, f, x - planes + REACH]
                next_ref[w, f, x] = total


def wall_terms_of(first, group_ref, w, f):
    upper = group_ref[f, 16 * w : 16 * w + 16].astype(jnp.float32)
    lower = group_ref[f, 32:48].astype(jnp.float32)[8 * w : 8 * w + 8]
    zero = jnp.zeros((2, upper.shape[1]), jnp.float32)
    made = []
    for x in range(4):
        rest = lower[2 * x : 2 * x + 2]
        rest = jnp.where(
            first, jnp.concatenate([zero, rest], axis=0), jnp.concatenate([rest, zero], axis=0)
        )
        made.append(upper[4 * x : 4 * x + 4] + rest)
    return made


def wall_join_kernel(where_ref, part_ref, group_ref, given_ref):
    windows, _, planes = part_ref.shape[:3]
    base = planes // 2 * (1 - where_ref[0])
    for w in range(windows):
        for f in range(5):
            for x, term in enumerate(wall_terms_of(where_ref[0] == 0, group_ref, w, f)):
                given_ref[w, f, x] = part_ref[w, f, base + x] + term


def edge_join_kernel(part_ref, edge_ref, made, snaps_ref):
    windows, _, half = part_ref.shape[:3]
    for w in range(windows):
        for f in range(5):
            done = []
            for x in range(half):
                total = part_ref[w, f, x] + edge_ref[w, f, x]
                made[w, f, x] = total
                done.append(total)
            snaps_ref[w, f] = jnp.concatenate(done, axis=0).astype(jnp.bfloat16)


def own_join_kernel(where_ref, _, part_ref, edge_ref, group_ref, made, snaps_ref):
    windows, _, planes = part_ref.shape[:3]
    base = planes // 2 * where_ref[0]
    for w in range(windows):
        for f in range(5):
            done = []
            for x, term in enumerate(wall_terms_of(where_ref[0] == 0, group_ref, w, f)):
                total = part_ref[w, f, base + x] + term + edge_ref[w, f, x]
                made[w, f, x] = total
                done.append(total)
            snaps_ref[w, f] = jnp.concatenate(done, axis=0).astype(jnp.bfloat16)


def same_layer(shape):
    rows = lax.broadcasted_iota(jnp.int32, shape, 0)
    columns = lax.broadcasted_iota(jnp.int32, shape, 1)
    return lax.rem(rows, 8) == lax.rem(columns, 8)


def folded(total, modes):
    kept = lax.rem(lax.broadcasted_iota(jnp.int32, (modes, LANES), 1), 8)
    made = []
    for tile in range(total.shape[0]):
        rows = jnp.zeros((modes, LANES), jnp.float32)
        for y in range(8):
            rows = jnp.where(kept == y, total[tile, pl.ds(y, modes, 8), :], rows)
        made.append(rows)
    return made[0] if len(made) == 1 else jnp.concatenate(made, axis=1)


def modes_of(basis_ref, t):
    modes, _, layers, cells = basis_ref.shape
    return basis_ref[:, t].reshape(modes * layers, cells)


def project_kernel(paired, where_ref, *rest):
    if paired:
        (
            own_ref, got_ref, next_own_ref, next_given_ref, basis_ref,
            sums_ref, snaps_ref, next_ref, square, wide_sums, sems,
        ) = rest
        first = where_ref[0] == 0
        half = next_own_ref.shape[2]
        copies = []
        for i, (source, base) in enumerate(
            ((next_own_ref, half * where_ref[0]), (next_given_ref, half * (1 - where_ref[0])))
        ):
            copies.append(
                pltpu.make_async_copy(source, next_ref.at[:, :, pl.ds(base, half)], sems.at[i])
            )
            copies[i].start()
        for w in range(own_ref.shape[0]):
            for f in range(own_ref.shape[1]):
                own = own_ref[w, f].astype(jnp.float32)
                got = got_ref[w, f].astype(jnp.float32)
                low = jnp.where(first, own, got)
                high = jnp.where(first, got, own)
                for t in range(4):
                    snaps_ref[4 * f + t, pl.ds(8 * w, 8)] = jnp.concatenate(
                        [low[4 * t : 4 * t + 4], high[4 * t : 4 * t + 4]], axis=0
                    ).astype(jnp.bfloat16)
    else:
        snaps_ref, basis_ref, sums_ref, square, wide_sums = rest
        copies = []
    modes, tiles = basis_ref.shape[:2]
    columns = snaps_ref.shape[1]
    total = jnp.zeros((modes * 8 + columns, columns), jnp.float32)
    for start in range(0, tiles, 4):
        span = range(start, min(start + 4, tiles))
        snaps = jnp.concatenate([snaps_ref[t] for t in span], axis=1)
        rows = jnp.concatenate([modes_of(basis_ref, t) for t in span], axis=1)
        total = total + lax.dot_general(
            jnp.concatenate([rows, snaps], axis=0), snaps, NT, preferred_element_type=jnp.float32
        )
    small = total[modes * 8 :]
    total = total[: modes * 8]
    wide_sums[0, :, 0:columns] = total
    square[...] = jnp.zeros_like(square)
    square[0:modes, :] = folded(wide_sums, modes)
    kept = jnp.where(same_layer(small.shape), small, 0.0)
    square[modes : modes + 1, 0:columns] = jnp.sum(kept[0:8], axis=0, keepdims=True)
    square[modes + 1 : modes + 2, 0:columns] = jnp.sum(kept[8:16], axis=0, keepdims=True)
    lanes = lax.broadcasted_iota(jnp.int32, square.shape, 1)
    turned = jnp.where(lanes < columns, square[...], 0.0).T
    sums = jnp.concatenate(
        [
            jnp.sum(turned[0:8], axis=0, keepdims=True),
            jnp.sum(turned[8:16], axis=0, keepdims=True),
        ],
        axis=0,
    )
    sums_ref[...] = jnp.concatenate(
        [sums, jnp.zeros((6, sums.shape[1]), jnp.float32)], axis=0
    )
    for copy in copies:
        copy.wait()


def merge_kernel(gram_ref, far_ref, sums_ref, merged_ref):
    rows = gram_ref.shape[0]
    merged_ref[0:rows] = gram_ref[...] + far_ref[...]
    merged_ref[rows:] = sums_ref[...]


def unpacked(sums_ref, modes):
    half = modes // 2
    return jnp.concatenate([sums_ref[0:half, 0:modes], sums_ref[0:half, modes:]], axis=0)


def inverse_kernel(sums_ref, inverse_ref, spread_ref, plain, scaled):
    modes = inverse_ref.shape[0]
    rows = lax.broadcasted_iota(jnp.int32, (8, 2 * modes), 0)
    lanes = lax.broadcasted_iota(jnp.int32, (8, 2 * modes), 1)
    tiles = []
    gram = unpacked(sums_ref, modes)
    for tile in range(modes // 8):
        eye = (lanes == rows + (modes + 8 * tile)).astype(jnp.float32)
        start = 8 * tile % (modes // 2)
        line = sums_ref[start : start + 8, :]
        if 8 * tile >= modes // 2:
            line = pltpu.roll(line, modes, 1)
        tiles.append(jnp.where(lanes < modes, line, eye))
    count = modes // 8
    for home in range(count):
        columns = [
            [
                jnp.broadcast_to(
                    tiles[tile][:, 8 * home + j : 8 * home + j + 1], (8, 2 * modes)
                )
                for tile in range(home, count)
            ]
            for j in range(8)
        ]
        for j in range(8):
            k = 8 * home + j
            inverse = 1.0 / columns[j][0]
            inverse = inverse[j : j + 1, :]
            row = tiles[home][j : j + 1, :]
            ready = row * inverse
            plain[k : k + 1, :] = row
            scaled[k : k + 1, :] = ready
            factors = [jnp.where(rows > j, columns[j][0], 0.0)] + columns[j][1:]
            for later in range(j + 1, 8):
                share = columns[j][0][later : later + 1, :] * inverse
                columns[later] = [c - f * share for c, f in zip(columns[later], factors)]
            for tile in range(home, count):
                tiles[tile] = tiles[tile] - factors[tile - home] * ready
    exact = functools.partial(
        lax.dot_general, precision=HIGHEST, preferred_element_type=jnp.float32
    )
    plainly = (((1,), (0,)), ((), ()))
    inverse = exact(plain[:, modes:], scaled[:, modes:], (((0,), (0,)), ((), ())))
    square = (modes, modes)
    eye = lax.broadcasted_iota(jnp.int32, square, 0) == lax.broadcasted_iota(jnp.int32, square, 1)
    off = eye.astype(jnp.float32) - exact(gram, inverse, plainly)
    inverse = inverse + exact(inverse, off, plainly)
    inverse_ref[...] = inverse
    wide = spread_ref.shape[1]
    spread = (
        lax.broadcasted_iota(jnp.int32, (modes, wide), 1) // 8
        == lax.broadcasted_iota(jnp.int32, (modes, wide), 0)
    ).astype(jnp.bfloat16)
    parts = []
    rest = inverse
    for _ in range(3):
        parts.append(rest.astype(jnp.bfloat16))
        rest = rest - parts[-1].astype(jnp.float32)
    wide_parts = jnp.dot(
        jnp.concatenate(parts, axis=0), spread, preferred_element_type=jnp.float32
    )
    spread_ref[...] = (
        wide_parts[0:modes] + wide_parts[modes : 2 * modes] + wide_parts[2 * modes :]
    )


def finish_kernel(
    rows_total, projected_ref, sums_ref, inverse_ref, spread_ref, snaps_ref, basis_ref,
    modes_ref, solved_ref, factor_ref, made, sems,
):
    modes, tiles, _, cells = basis_ref.shape
    wide = modes * 8
    exact = functools.partial(jnp.dot, precision=HIGHEST, preferred_element_type=jnp.float32)
    base = modes // 2
    projected = projected_ref[base : base + 8, 0:modes]
    lines = exact(projected, spread_ref[...])
    full = jnp.concatenate(
        [jnp.broadcast_to(lines[0:1], (8, wide)), jnp.broadcast_to(lines[1:2], (8, wide))],
        axis=0,
    )
    full = jnp.where(same_layer(full.shape), full, 0.0)
    upper = full.astype(jnp.bfloat16)
    fit = jnp.concatenate([upper, (full - upper.astype(jnp.float32)).astype(jnp.bfloat16)], axis=0)
    solved = exact(projected, inverse_ref[...])
    left = projected - exact(solved, unpacked(sums_ref, modes))

    def inner(p, i, q, j):
        return jnp.sum(p[i : i + 1] * q[j : j + 1], axis=1, keepdims=True)

    def entry(i, j):
        square = projected_ref[base + i : base + i + 1, modes + j : modes + j + 1]
        return square - inner(projected, i, solved, j) - inner(solved, i, left, j)

    first = jnp.sqrt(entry(0, 0))
    below = entry(1, 0) / first
    second = jnp.sqrt(entry(1, 1) - below * below)
    scaling = jnp.sqrt(jnp.float32(rows_total))
    w00 = scaling / first
    w11 = scaling / second
    w01 = -(below / first) * w11
    solved_ref[...] = solved[0:2]
    factor_ref[0:1, 0:1] = first / scaling
    factor_ref[0:1, 1:2] = below / scaling
    factor_ref[1:2, 0:1] = jnp.zeros_like(first)
    factor_ref[1:2, 1:2] = second / scaling
    chunks = sems.shape[0]
    per_chunk = tiles // chunks
    copies = []
    for c in range(chunks):
        for t in range(c * per_chunk, (c + 1) * per_chunk):
            fitted = jnp.dot(fit, modes_of(basis_ref, t), preferred_element_type=jnp.float32)
            fitted = fitted[0:16] + fitted[16:32]
            snaps = snaps_ref[t].astype(jnp.float32)
            left_over = snaps - fitted
            made[0, t] = left_over[0:8] * w00
            made[1, t] = left_over[8:16] * w11 + left_over[0:8] * w01
        span = pl.ds(c * per_chunk, per_chunk)
        copies.append(
            pltpu.make_async_copy(made.at[:, span], modes_ref.at[:, span], sems.at[c])
        )
        copies[c].start()
    for copy in copies:
        copy.wait()


def params(mib):
    return pltpu.CompilerParams(vmem_limit_bytes=mib * 1024 * 1024)


def cost(flops, moved):
    return pl.CostEstimate(flops=flops, bytes_accessed=moved, transcendentals=0)


WHOLE = pl.BlockSpec(memory_space=pltpu.VMEM)
FAR = pl.BlockSpec(memory_space=pltpu.HBM)
LOOSE = pl.BlockSpec(memory_space=pl.ANY)
SCALAR = pl.BlockSpec(memory_space=pltpu.SMEM)


def swap_added(value, axis, bit):
    count = lax.axis_size(axis)
    return value + lax.ppermute(value, axis, [(i, i ^ bit) for i in range(count)])


def bits(count):
    made = [1 << k for k in range(count.bit_length() - 1)]
    if count != 1 << len(made):
        raise ValueError("axis size")
    return made


def body(windows, pod_basis):
    f32, bf16 = jnp.float32, jnp.bfloat16
    shape = jax.ShapeDtypeStruct
    count, fields, planes, layers, cells = windows.shape
    ring, walls = lax.axis_size("solver"), lax.axis_size("analysis")
    paired = walls == 2 and planes == 8 and layers == 4
    place = lax.axis_index("analysis").astype(jnp.int32).reshape(1)
    modes, _, pod_planes, pod_layers, _ = pod_basis.shape
    tiles = fields * pod_planes * (pod_layers // 8)
    basis = pod_basis.reshape(modes, tiles, 8, cells)
    wide = modes * 8
    basis_bytes = basis.size * 2

    to_right = [(i, (i + 1) % ring) for i in range(ring)]
    to_left = [((i + 1) % ring, i) for i in range(ring)]
    edge_shape = shape((count, fields, REACH, layers, cells), f32)
    face_scratch = [pltpu.VMEM((fields, planes, layers, cells), f32)]
    face_cost = cost(10_000_000, 10 * windows.size)
    if paired:
        swap = [(0, 1), (1, 0)]
        group_shape = shape((fields, 48, cells), bf16)
        lows = pltpu.VMEM((fields, 16, cells), f32)
        near_group, kept = pl.pallas_call(
            near_kernel,
            out_shape=[group_shape, shape(windows.shape, f32)],
            in_specs=[SCALAR, WHOLE],
            out_specs=[WHOLE] * 2,
            scratch_shapes=[lows, pltpu.SemaphoreType.DMA],
            compiler_params=params(16),
            cost_estimate=face_cost,
            name="near_faces",
        )(place, windows)
        later_group, first_edge, second_edge = pl.pallas_call(
            later_kernel,
            out_shape=[group_shape] + [edge_shape] * 2,
            in_specs=[SCALAR, LOOSE, WHOLE],
            out_specs=[WHOLE] * 3,
            scratch_shapes=[pltpu.VMEM((count, fields, planes, layers, cells), f32), lows],
            compiler_params=params(16),
            cost_estimate=face_cost,
            name="later_faces",
        )(place, near_group, kept)
        near_group = lax.ppermute(near_group, "analysis", swap)
        down = [(2 * ((i + 1) % ring), 2 * i) for i in range(ring)]
        up = [(2 * i, 2 * ((i + 1) % ring)) for i in range(ring)]
        odd = lambda pairs: [(a + 1, b + 1) for a, b in pairs]
        first_edge = lax.ppermute(first_edge, ("solver", "analysis"), down + odd(up))
        second_edge = lax.ppermute(second_edge, ("solver", "analysis"), up + odd(down))
        later_group = lax.ppermute(later_group, "analysis", swap)
    else:
        kept, to_next, to_last, up, down = pl.pallas_call(
            functools.partial(face_kernel, True),
            out_shape=[shape(windows.shape, f32)]
            + [edge_shape] * 2
            + [shape(windows.shape, f32)] * 2,
            in_specs=[SCALAR, FAR],
            out_specs=[WHOLE] * 5,
            scratch_shapes=face_scratch + [pltpu.SemaphoreType.DMA((count,))],
            compiler_params=params(16),
            cost_estimate=face_cost,
            name="faces",
        )(place, windows)
        wall_terms = [
            lax.ppermute(up, "analysis", [(i, i + 1) for i in range(walls - 1)]),
            lax.ppermute(down, "analysis", [(i + 1, i) for i in range(walls - 1)]),
        ]
        from_left = lax.ppermute(to_next, "solver", to_right)
        from_right = lax.ppermute(to_last, "solver", to_left)

    early = 2
    gram_flops = 2 * wide * wide * cells * tiles
    inner, right, left, basis = pl.pallas_call(
        functools.partial(inner_gram_kernel, early),
        out_shape=[
            shape(windows.shape, f32),
            shape((wide, wide // 2), f32),
            shape((wide // 2, wide // 2), f32),
            shape(basis.shape, bf16),
        ],
        in_specs=[WHOLE, FAR],
        out_specs=[WHOLE] * 4,
        scratch_shapes=[
            pltpu.VMEM((2 * fields, planes, count * layers, cells), f32),
            pltpu.SemaphoreType.DMA((fields,)),
        ],
        compiler_params=params(40),
        cost_estimate=cost(1_000_000, windows.size),
        name="inner_gram",
    )(kept, basis)

    def rest_of_gram(after):
        return pl.pallas_call(
            functools.partial(gram_kernel, early, fields),
            out_shape=shape((modes // 2, 2 * modes), f32),
            in_specs=[LOOSE] + [WHOLE] * 3,
            out_specs=WHOLE,
            scratch_shapes=[pltpu.VMEM((wide // LANES, wide, LANES), f32)],
            compiler_params=params(24),
            cost_estimate=cost(gram_flops // 2, basis_bytes),
            name="gram",
        )(after, right, left, basis)

    join_cost = cost(1_000_000, 16 * windows.size)
    if paired:
        half_shape = (count, fields, planes * layers // 2, cells)

        half_next = shape((count, fields, planes // 2, layers, cells), f32)

        inner_given = pl.pallas_call(
            wall_join_kernel,
            out_shape=half_next,
            in_specs=[SCALAR] + [WHOLE] * 2,
            out_specs=WHOLE,
            compiler_params=params(16),
            cost_estimate=cost(gram_flops // 2, basis_bytes),
            name="wall_join",
        )(place, inner, near_group)
        next_given, given = pl.pallas_call(
            edge_join_kernel,
            out_shape=[half_next, shape(half_shape, bf16)],
            in_specs=[WHOLE] * 2,
            out_specs=[WHOLE] * 2,
            compiler_params=params(16),
            cost_estimate=join_cost,
            name="edge_join",
        )(inner_given, first_edge)
        got = lax.ppermute(given, "analysis", swap)
        gram = rest_of_gram(given)
    else:
        next_windows = pl.pallas_call(
            functools.partial(join_kernel, 2),
            out_shape=shape(windows.shape, f32),
            in_specs=[WHOLE] * 5,
            out_specs=WHOLE,
            compiler_params=params(16),
            cost_estimate=join_cost,
            name="join",
        )(inner, from_left, from_right, *wall_terms)
        gram = rest_of_gram(place)
    ring_bits = bits(ring)
    lone = ring_bits.pop(1 if len(ring_bits) > 1 else 0)
    gram_far = lax.ppermute(gram, "solver", [(i, i ^ lone) for i in range(ring)])
    if paired:
        next_own, own = pl.pallas_call(
            own_join_kernel,
            out_shape=[half_next, shape(half_shape, bf16)],
            in_specs=[SCALAR, LOOSE] + [WHOLE] * 3,
            out_specs=[WHOLE] * 2,
            compiler_params=params(16),
            cost_estimate=join_cost,
            name="own_join",
        )(place, gram, inner, second_edge, later_group)

    sums_shape = shape((8, LANES), f32)
    snaps_shape = shape((tiles, 2 * 8, cells), bf16)
    scratch = [pltpu.VMEM((LANES, LANES), f32), pltpu.VMEM((1, wide, LANES), f32)]
    project_cost = cost(2 * wide * 16 * cells * tiles, basis_bytes)
    if paired:
        sums, snaps, next_windows = pl.pallas_call(
            functools.partial(project_kernel, True),
            out_shape=[sums_shape, snaps_shape, shape(windows.shape, f32)],
            in_specs=[SCALAR] + [WHOLE] * 5,
            out_specs=[WHOLE, WHOLE, FAR],
            scratch_shapes=scratch + [pltpu.SemaphoreType.DMA((2,))],
            compiler_params=params(16),
            cost_estimate=project_cost,
            name="project",
        )(place, own, got, next_own, next_given, basis)
    else:
        relaid = lax.all_to_all(
            next_windows.astype(bf16), "analysis", split_axis=2, concat_axis=3, tiled=True
        )
        snaps = relaid.reshape(count, tiles, 8, cells).transpose(1, 0, 2, 3)
        snaps = snaps.reshape(tiles, count * 8, cells)
        sums = pl.pallas_call(
            functools.partial(project_kernel, False),
            out_shape=sums_shape,
            in_specs=[SCALAR] + [WHOLE] * 2,
            out_specs=WHOLE,
            scratch_shapes=scratch,
            compiler_params=params(16),
            cost_estimate=project_cost,
            name="project",
        )(place, snaps, basis)
    sums = pl.pallas_call(
        merge_kernel,
        out_shape=shape((modes // 2 + 8, LANES), f32),
        in_specs=[WHOLE] * 3,
        out_specs=WHOLE,
        compiler_params=params(16),
        cost_estimate=cost(10_000, 8 * modes * LANES),
        name="merge",
    )(gram, gram_far, sums)
    for bit in bits(walls):
        sums = swap_added(sums, "analysis", bit)
    for bit in ring_bits:
        sums = swap_added(sums, "solver", bit)
    inverse, spread = pl.pallas_call(
        inverse_kernel,
        out_shape=[shape((modes, modes), f32), shape((modes, wide), f32)],
        in_specs=[WHOLE],
        out_specs=[WHOLE] * 2,
        scratch_shapes=[pltpu.VMEM((modes, 2 * modes), f32)] * 2,
        compiler_params=params(16),
        cost_estimate=cost(20_000_000, 8 * modes * modes),
        name="inverse",
    )(sums)
    projected = swap_added(sums, "solver", lone)

    rows_total = ring * walls * tiles * 8 * cells
    new_modes, solved, factor = pl.pallas_call(
        functools.partial(finish_kernel, rows_total),
        out_shape=[
            shape((count, tiles, 8, cells), f32),
            shape((count, modes), f32),
            shape((count, count), f32),
        ],
        in_specs=[WHOLE] * 6,
        out_specs=[FAR, WHOLE, WHOLE],
        scratch_shapes=[
            pltpu.VMEM((count, tiles, 8, cells), f32),
            pltpu.SemaphoreType.DMA((fields,)),
        ],
        compiler_params=params(16),
        cost_estimate=cost(2 * wide * 32 * cells * tiles, basis_bytes + 8 * windows.size),
        name="finish",
    )(projected, sums, inverse, spread, snaps, basis)
    new_modes = new_modes.reshape(count, fields, pod_planes, pod_layers, cells)
    return next_windows, solved, new_modes, factor


def solution(mesh):
    in_specs = (
        P(None, None, "solver", "analysis", None),
        P(None, None, ("solver", "analysis"), None, None),
    )
    out_specs = (
        P(None, None, "solver", "analysis", None),
        P(),
        P(None, None, ("solver", "analysis"), None, None),
        P(),
    )
    return jax.shard_map(body, mesh=mesh, in_specs=in_specs, out_specs=out_specs, check_vma=False)
```

```python
import functools

import jax
import jax.numpy as jnp
from jax import lax
from jax.experimental import pallas as pl
from jax.experimental.pallas import tpu as pltpu
from jax.sharding import PartitionSpec as P

PRESSURE_FACTOR = 1.4 - 1.0
SECTION_STEP = 0.25
CENTRAL_WEIGHTS = (0.8, -0.2, 4.0 / 105.0, -1.0 / 280.0)
REACH = 4
LANES = 128
HIGHEST = lax.Precision.HIGHEST
NT = (((1,), (1,)), ((), ()))


def weight(k):
    if k == 0 or abs(k) > REACH:
        return 0.0
    value = -SECTION_STEP * CENTRAL_WEIGHTS[abs(k) - 1]
    return value if k > 0 else -value


def row_weights(shape, values):
    rows = lax.broadcasted_iota(jnp.int32, shape, len(shape) - 2)
    made = jnp.full(shape, values[0], jnp.float32)
    for i, value in enumerate(values[1:], start=1):
        made = jnp.where(rows == i, jnp.float32(value), made)
    return made


def primitives(fields):
    density, mx, my, mz, energy = fields
    inverse = 1.0 / density
    ux, uy, uz = mx * inverse, my * inverse, mz * inverse
    pressure = PRESSURE_FACTOR * (energy - 0.5 * (mx * ux + my * uy + mz * uz))
    return (mx, my, mz), (ux, uy, uz), pressure, energy + pressure


def flux(parts, direction):
    moments, speeds, pressure, enthalpy = parts
    speed = speeds[direction]
    made = [moments[direction]]
    for axis in range(3):
        term = moments[axis] * speed
        made.append(term + pressure if axis == direction else term)
    made.append(enthalpy * speed)
    return made


def face_kernel(two_sided, where_ref, source_ref, windows_ref, left_ref, right_ref, *rest):
    windows, _, planes, layers, cells = windows_ref.shape
    wall_refs, scratch, sems = rest[:-2], rest[-2], rest[-1]
    copies = [
        pltpu.make_async_copy(source_ref.at[w], windows_ref.at[w], sems.at[w])
        for w in range(windows)
    ]
    for copy in copies:
        copy.start()
    tile = (layers, cells)
    up = [
        row_weights(tile, [weight(j - layers - i) for i in range(layers)]) for j in range(layers)
    ]
    down = [
        row_weights(tile, [weight(layers + j - i) for i in range(layers)]) for j in range(layers)
    ]
    if two_sided:
        tables = (up, down)
    else:
        first = where_ref[0] == 0
        tables = ([jnp.where(first, u, d) for u, d in zip(up, down)],)
    for w in range(windows):
        copies[w].wait()
        for x in range(planes):
            parts = primitives([windows_ref[w, f, x] for f in range(5)])
            for f, value in enumerate(flux(parts, 0)):
                scratch[f, x] = value
            for f, value in enumerate(flux(parts, 1)):
                for ref, table in zip(wall_refs, tables):
                    total = None
                    for j in range(layers):
                        term = table[j] * value[j : j + 1, :]
                        total = term if total is None else total + term
                    ref[w, f, x] = total
        for f in range(5):
            for i in range(REACH):
                total = None
                for j in range(planes):
                    c = weight(j - planes - i)
                    if c:
                        term = c * scratch[f, j]
                        total = term if total is None else total + term
                left_ref[w, f, i] = total
                total = None
                for j in range(planes):
                    c = weight(j + REACH - i)
                    if c:
                        term = c * scratch[f, j]
                        total = term if total is None else total + term
                right_ref[w, f, i] = total


def wall_group(where_ref, windows_ref, group_ref, lows, base, keep_x):
    windows, _, planes, layers, cells = windows_ref.shape
    tile = (layers, cells)
    first = where_ref[0] == 0
    table = [
        jnp.where(
            first,
            row_weights(tile, [weight(j - layers - i) for i in range(layers)]),
            row_weights(tile, [weight(layers + j - i) for i in range(layers)]),
        )
        for j in range(layers)
    ]
    for w in range(windows):
        upper = [[] for _ in range(5)]
        lower = [[] for _ in range(5)]
        for x in range(planes // 2):
            parts = primitives([windows_ref[w, f, base + x] for f in range(5)])
            keep_x(w, base + x, parts)
            for f, value in enumerate(flux(parts, 1)):
                total = None
                for j in range(layers):
                    term = table[j] * value[j : j + 1, :]
                    total = term if total is None else total + term
                high = total.astype(jnp.bfloat16).astype(jnp.float32)
                rest = total - high
                upper[f].append(high)
                lower[f].append(jnp.where(first, rest[0:2], rest[2:4]))
        for f in range(5):
            group_ref[f, 16 * w : 16 * w + 16] = jnp.concatenate(upper[f], axis=0).astype(
                jnp.bfloat16
            )
            lows[f, 8 * w : 8 * w + 8] = jnp.concatenate(lower[f], axis=0)
    for f in range(5):
        group_ref[f, 32:48] = lows[f].astype(jnp.bfloat16)


def near_kernel(where_ref, source_ref, group_ref, kept_ref, lows, sem):
    copy = pltpu.make_async_copy(source_ref, kept_ref, sem)
    copy.start()
    base = source_ref.shape[2] // 2 * where_ref[0]
    wall_group(where_ref, source_ref, group_ref, lows, base, lambda w, x, parts: None)
    copy.wait()


def later_kernel(where_ref, _, windows_ref, group_ref, first_ref, second_ref, scratch, lows):
    windows, _, planes, layers, cells = windows_ref.shape
    half = planes // 2

    def keep_x(w, x, parts):
        for f, value in enumerate(flux(parts, 0)):
            scratch[w, f, x] = value

    base = half * (1 - where_ref[0])
    wall_group(where_ref, windows_ref, group_ref, lows, base, keep_x)
    for w in range(windows):
        for x in range(half):
            plane = half * where_ref[0] + x
            keep_x(w, plane, primitives([windows_ref[w, f, plane] for f in range(5)]))
        for f in range(5):
            for i in range(REACH):
                sides = []
                for offset in (-planes, REACH):
                    total = None
                    for j in range(planes):
                        c = weight(j + offset - i)
                        if c:
                            term = c * scratch[w, f, j]
                            total = term if total is None else total + term
                    sides.append(total)
                to_next, to_last = sides
                first_ref[w, f, i] = jnp.where(where_ref[0] == 0, to_last, to_next)
                second_ref[w, f, i] = jnp.where(where_ref[0] == 0, to_next, to_last)


def inner_part(windows_ref, part_ref, scratch):
    windows, _, planes, layers, cells = windows_ref.shape
    tile = (windows * layers, cells)
    walls = {
        k: row_weights(
            tile, [weight(k) if 0 <= i + k < layers else 0.0 for i in range(layers)] * windows
        )
        for k in range(-REACH, REACH + 1)
        if 0 < abs(k) < layers
    }
    for x in range(planes):
        fields = [
            jnp.concatenate([windows_ref[w, f, x] for w in range(windows)], axis=0)
            for f in range(5)
        ]
        parts = primitives(fields)
        for f, value in enumerate(flux(parts, 0)):
            scratch[f, x] = value
        flux_y, flux_z = flux(parts, 1), flux(parts, 2)
        for f in range(5):
            total = fields[f]
            for k, line in walls.items():
                total = total + line * pltpu.roll(flux_y[f], -k % tile[0], 0)
            for k in range(1, REACH + 1):
                total = total + weight(k) * (
                    pltpu.roll(flux_z[f], cells - k, 1) - pltpu.roll(flux_z[f], k, 1)
                )
            scratch[5 + f, x] = total
    for f in range(5):
        for x in range(planes):
            total = scratch[5 + f, x]
            for k in range(-REACH, REACH + 1):
                if k and 0 <= x + k < planes:
                    total = total + weight(k) * scratch[f, x + k]
            for w in range(windows):
                part_ref[w, f, x] = total[layers * w : layers * (w + 1)]


def gram_blocks(basis_ref, chunks, per_chunk, right, left):
    half = left.shape[0]
    for c in chunks:
        rows = jnp.concatenate(
            [modes_of(basis_ref, t) for t in range(c * per_chunk, (c + 1) * per_chunk)], axis=1
        )
        right = right + lax.dot_general(
            rows, rows[half:], NT, preferred_element_type=jnp.float32
        )
        left = left + lax.dot_general(
            rows[:half], rows[:half], NT, preferred_element_type=jnp.float32
        )
    return right, left


def inner_gram_kernel(
    early, windows_ref, basis_ref, part_ref, right_ref, left_ref, kept_ref, scratch, sems
):
    chunks = sems.shape[0]
    per_chunk = kept_ref.shape[1] // chunks
    copies = []
    for c in range(chunks):
        span = pl.ds(c * per_chunk, per_chunk)
        copies.append(
            pltpu.make_async_copy(basis_ref.at[:, span], kept_ref.at[:, span], sems.at[c])
        )
        copies[c].start()
    inner_part(windows_ref, part_ref, scratch)
    right, left = jnp.zeros(right_ref.shape, jnp.float32), jnp.zeros(left_ref.shape, jnp.float32)
    for c in range(chunks):
        copies[c].wait()
        if c < early:
            right, left = gram_blocks(kept_ref, [c], per_chunk, right, left)
    right_ref[...] = right
    left_ref[...] = left


def gram_kernel(early, chunks, _, right_ref, left_ref, basis_ref, gram_ref, total):
    modes, tiles = basis_ref.shape[:2]
    wide = modes * 8
    half = wide // 2
    right, left = gram_blocks(
        basis_ref, range(early, chunks), tiles // chunks, right_ref[...], left_ref[...]
    )
    tiles_left = half // LANES
    turned = right[0:half].T
    for tile in range(tiles_left):
        span = slice(tile * LANES, (tile + 1) * LANES)
        total[tile, 0:half] = left[:, span]
        total[tile, half:] = turned[:, span]
        total[tiles_left + tile] = right[:, span]
    rows = folded(total, modes)
    picks = (
        lax.broadcasted_iota(jnp.int32, (wide, modes), 0) // 8
        == lax.broadcasted_iota(jnp.int32, (wide, modes), 1)
    ).astype(jnp.float32)
    gram = jnp.dot(rows, picks, precision=HIGHEST, preferred_element_type=jnp.float32)
    gram_ref[:, 0:modes] = gram[0 : modes // 2]
    gram_ref[:, modes:] = gram[modes // 2 :]


def join_kernel(walls, part_ref, left_ref, right_ref, *rest):
    wall_refs, next_ref = rest[:walls], rest[walls]
    windows, _, planes, layers, cells = part_ref.shape
    for w in range(windows):
        for f in range(5):
            for x in range(planes):
                total = part_ref[w, f, x]
                for ref in wall_refs:
                    total = total + ref[w, f, x]
                if x < REACH:
                    total = total + left_ref[w, f, x]
                if x >= planes - REACH:
                    total = total + right_ref[w, f, x - planes + REACH]
                next_ref[w, f, x] = total


def wall_terms_of(first, group_ref, w, f):
    upper = group_ref[f, 16 * w : 16 * w + 16].astype(jnp.float32)
    lower = group_ref[f, 32:48].astype(jnp.float32)[8 * w : 8 * w + 8]
    zero = jnp.zeros((2, upper.shape[1]), jnp.float32)
    made = []
    for x in range(4):
        rest = lower[2 * x : 2 * x + 2]
        rest = jnp.where(
            first, jnp.concatenate([zero, rest], axis=0), jnp.concatenate([rest, zero], axis=0)
        )
        made.append(upper[4 * x : 4 * x + 4] + rest)
    return made


def wall_join_kernel(where_ref, part_ref, group_ref, given_ref):
    windows, _, planes = part_ref.shape[:3]
    base = planes // 2 * (1 - where_ref[0])
    for w in range(windows):
        for f in range(5):
            for x, term in enumerate(wall_terms_of(where_ref[0] == 0, group_ref, w, f)):
                given_ref[w, f, x] = part_ref[w, f, base + x] + term


def edge_join_kernel(part_ref, edge_ref, made, snaps_ref):
    windows, _, half = part_ref.shape[:3]
    for w in range(windows):
        for f in range(5):
            done = []
            for x in range(half):
                total = part_ref[w, f, x] + edge_ref[w, f, x]
                made[w, f, x] = total
                done.append(total)
            snaps_ref[w, f] = jnp.concatenate(done, axis=0).astype(jnp.bfloat16)


def own_edge_kernel(where_ref, _, part_ref, edge_ref, own_ref):
    windows, _, planes = part_ref.shape[:3]
    base = planes // 2 * where_ref[0]
    for w in range(windows):
        for f in range(5):
            for x in range(planes // 2):
                own_ref[w, f, x] = part_ref[w, f, base + x] + edge_ref[w, f, x]


def own_join_kernel(where_ref, _, part_ref, group_ref, made, snaps_ref):
    for w in range(part_ref.shape[0]):
        for f in range(5):
            done = []
            for x, term in enumerate(wall_terms_of(where_ref[0] == 0, group_ref, w, f)):
                total = part_ref[w, f, x] + term
                made[w, f, x] = total
                done.append(total)
            snaps_ref[w, f] = jnp.concatenate(done, axis=0).astype(jnp.bfloat16)


def same_layer(shape):
    rows = lax.broadcasted_iota(jnp.int32, shape, 0)
    columns = lax.broadcasted_iota(jnp.int32, shape, 1)
    return lax.rem(rows, 8) == lax.rem(columns, 8)


def folded(total, modes):
    kept = lax.rem(lax.broadcasted_iota(jnp.int32, (modes, LANES), 1), 8)
    made = []
    for tile in range(total.shape[0]):
        rows = jnp.zeros((modes, LANES), jnp.float32)
        for y in range(8):
            rows = jnp.where(kept == y, total[tile, pl.ds(y, modes, 8), :], rows)
        made.append(rows)
    return made[0] if len(made) == 1 else jnp.concatenate(made, axis=1)


def modes_of(basis_ref, t):
    modes, _, layers, cells = basis_ref.shape
    return basis_ref[:, t].reshape(modes * layers, cells)


def project_kernel(paired, where_ref, *rest):
    if paired:
        (
            own_ref, got_ref, next_own_ref, next_given_ref, basis_ref,
            sums_ref, snaps_ref, next_ref, square, wide_sums, sems,
        ) = rest
        first = where_ref[0] == 0
        half = next_own_ref.shape[2]
        copies = []
        for i, (source, base) in enumerate(
            ((next_own_ref, half * where_ref[0]), (next_given_ref, half * (1 - where_ref[0])))
        ):
            copies.append(
                pltpu.make_async_copy(source, next_ref.at[:, :, pl.ds(base, half)], sems.at[i])
            )
            copies[i].start()
        for w in range(own_ref.shape[0]):
            for f in range(own_ref.shape[1]):
                own = own_ref[w, f].astype(jnp.float32)
                got = got_ref[w, f].astype(jnp.float32)
                low = jnp.where(first, own, got)
                high = jnp.where(first, got, own)
                for t in range(4):
                    snaps_ref[4 * f + t, pl.ds(8 * w, 8)] = jnp.concatenate(
                        [low[4 * t : 4 * t + 4], high[4 * t : 4 * t + 4]], axis=0
                    ).astype(jnp.bfloat16)
    else:
        snaps_ref, basis_ref, sums_ref, square, wide_sums = rest
        copies = []
    modes, tiles = basis_ref.shape[:2]
    columns = snaps_ref.shape[1]
    total = jnp.zeros((modes * 8 + columns, columns), jnp.float32)
    for start in range(0, tiles, 4):
        span = range(start, min(start + 4, tiles))
        snaps = jnp.concatenate([snaps_ref[t] for t in span], axis=1)
        rows = jnp.concatenate([modes_of(basis_ref, t) for t in span], axis=1)
        total = total + lax.dot_general(
            jnp.concatenate([rows, snaps], axis=0), snaps, NT, preferred_element_type=jnp.float32
        )
    small = total[modes * 8 :]
    total = total[: modes * 8]
    wide_sums[0, :, 0:columns] = total
    square[...] = jnp.zeros_like(square)
    square[0:modes, :] = folded(wide_sums, modes)
    kept = jnp.where(same_layer(small.shape), small, 0.0)
    square[modes : modes + 1, 0:columns] = jnp.sum(kept[0:8], axis=0, keepdims=True)
    square[modes + 1 : modes + 2, 0:columns] = jnp.sum(kept[8:16], axis=0, keepdims=True)
    lanes = lax.broadcasted_iota(jnp.int32, square.shape, 1)
    turned = jnp.where(lanes < columns, square[...], 0.0).T
    sums = jnp.concatenate(
        [
            jnp.sum(turned[0:8], axis=0, keepdims=True),
            jnp.sum(turned[8:16], axis=0, keepdims=True),
        ],
        axis=0,
    )
    sums_ref[...] = jnp.concatenate(
        [sums, jnp.zeros((6, sums.shape[1]), jnp.float32)], axis=0
    )
    for copy in copies:
        copy.wait()


def merge_kernel(gram_ref, far_ref, sums_ref, merged_ref):
    rows = gram_ref.shape[0]
    merged_ref[0:rows] = gram_ref[...] + far_ref[...]
    merged_ref[rows:] = sums_ref[...]


def unpacked(sums_ref, modes):
    half = modes // 2
    return jnp.concatenate([sums_ref[0:half, 0:modes], sums_ref[0:half, modes:]], axis=0)


def inverse_kernel(sums_ref, inverse_ref, spread_ref, plain, scaled):
    modes = inverse_ref.shape[0]
    rows = lax.broadcasted_iota(jnp.int32, (8, 2 * modes), 0)
    lanes = lax.broadcasted_iota(jnp.int32, (8, 2 * modes), 1)
    tiles = []
    gram = unpacked(sums_ref, modes)
    for tile in range(modes // 8):
        eye = (lanes == rows + (modes + 8 * tile)).astype(jnp.float32)
        start = 8 * tile % (modes // 2)
        line = sums_ref[start : start + 8, :]
        if 8 * tile >= modes // 2:
            line = pltpu.roll(line, modes, 1)
        tiles.append(jnp.where(lanes < modes, line, eye))
    count = modes // 8
    for home in range(count):
        columns = [
            [
                jnp.broadcast_to(
                    tiles[tile][:, 8 * home + j : 8 * home + j + 1], (8, 2 * modes)
                )
                for tile in range(home, count)
            ]
            for j in range(8)
        ]
        for j in range(8):
            k = 8 * home + j
            inverse = 1.0 / columns[j][0]
            inverse = inverse[j : j + 1, :]
            row = tiles[home][j : j + 1, :]
            ready = row * inverse
            plain[k : k + 1, :] = row
            scaled[k : k + 1, :] = ready
            factors = [jnp.where(rows > j, columns[j][0], 0.0)] + columns[j][1:]
            for later in range(j + 1, 8):
                share = columns[j][0][later : later + 1, :] * inverse
                columns[later] = [c - f * share for c, f in zip(columns[later], factors)]
            for tile in range(home, count):
                tiles[tile] = tiles[tile] - factors[tile - home] * ready
    exact = functools.partial(
        lax.dot_general, precision=HIGHEST, preferred_element_type=jnp.float32
    )
    plainly = (((1,), (0,)), ((), ()))
    inverse = exact(plain[:, modes:], scaled[:, modes:], (((0,), (0,)), ((), ())))
    square = (modes, modes)
    eye = lax.broadcasted_iota(jnp.int32, square, 0) == lax.broadcasted_iota(jnp.int32, square, 1)
    off = eye.astype(jnp.float32) - exact(gram, inverse, plainly)
    inverse = inverse + exact(inverse, off, plainly)
    inverse_ref[...] = inverse
    wide = spread_ref.shape[1]
    spread = (
        lax.broadcasted_iota(jnp.int32, (modes, wide), 1) // 8
        == lax.broadcasted_iota(jnp.int32, (modes, wide), 0)
    ).astype(jnp.bfloat16)
    parts = []
    rest = inverse
    for _ in range(3):
        parts.append(rest.astype(jnp.bfloat16))
        rest = rest - parts[-1].astype(jnp.float32)
    wide_parts = jnp.dot(
        jnp.concatenate(parts, axis=0), spread, preferred_element_type=jnp.float32
    )
    spread_ref[...] = (
        wide_parts[0:modes] + wide_parts[modes : 2 * modes] + wide_parts[2 * modes :]
    )


def finish_kernel(
    rows_total, projected_ref, sums_ref, inverse_ref, spread_ref, snaps_ref, basis_ref,
    modes_ref, solved_ref, factor_ref, made, sems,
):
    modes, tiles, _, cells = basis_ref.shape
    wide = modes * 8
    exact = functools.partial(jnp.dot, precision=HIGHEST, preferred_element_type=jnp.float32)
    base = modes // 2
    projected = projected_ref[base : base + 8, 0:modes]
    lines = exact(projected, spread_ref[...])
    full = jnp.concatenate(
        [jnp.broadcast_to(lines[0:1], (8, wide)), jnp.broadcast_to(lines[1:2], (8, wide))],
        axis=0,
    )
    full = jnp.where(same_layer(full.shape), full, 0.0)
    upper = full.astype(jnp.bfloat16)
    fit = jnp.concatenate([upper, (full - upper.astype(jnp.float32)).astype(jnp.bfloat16)], axis=0)
    solved = exact(projected, inverse_ref[...])
    left = projected - exact(solved, unpacked(sums_ref, modes))

    def inner(p, i, q, j):
        return jnp.sum(p[i : i + 1] * q[j : j + 1], axis=1, keepdims=True)

    def entry(i, j):
        square = projected_ref[base + i : base + i + 1, modes + j : modes + j + 1]
        return square - inner(projected, i, solved, j) - inner(solved, i, left, j)

    first = jnp.sqrt(entry(0, 0))
    below = entry(1, 0) / first
    second = jnp.sqrt(entry(1, 1) - below * below)
    scaling = jnp.sqrt(jnp.float32(rows_total))
    w00 = scaling / first
    w11 = scaling / second
    w01 = -(below / first) * w11
    solved_ref[...] = solved[0:2]
    factor_ref[0:1, 0:1] = first / scaling
    factor_ref[0:1, 1:2] = below / scaling
    factor_ref[1:2, 0:1] = jnp.zeros_like(first)
    factor_ref[1:2, 1:2] = second / scaling
    chunks = sems.shape[0]
    per_chunk = tiles // chunks
    copies = []
    for c in range(chunks):
        for t in range(c * per_chunk, (c + 1) * per_chunk):
            fitted = jnp.dot(fit, modes_of(basis_ref, t), preferred_element_type=jnp.float32)
            fitted = fitted[0:16] + fitted[16:32]
            snaps = snaps_ref[t].astype(jnp.float32)
            left_over = snaps - fitted
            made[0, t] = left_over[0:8] * w00
            made[1, t] = left_over[8:16] * w11 + left_over[0:8] * w01
        span = pl.ds(c * per_chunk, per_chunk)
        copies.append(
            pltpu.make_async_copy(made.at[:, span], modes_ref.at[:, span], sems.at[c])
        )
        copies[c].start()
    for copy in copies:
        copy.wait()


def params(mib):
    return pltpu.CompilerParams(vmem_limit_bytes=mib * 1024 * 1024)


def cost(flops, moved):
    return pl.CostEstimate(flops=flops, bytes_accessed=moved, transcendentals=0)


WHOLE = pl.BlockSpec(memory_space=pltpu.VMEM)
FAR = pl.BlockSpec(memory_space=pltpu.HBM)
LOOSE = pl.BlockSpec(memory_space=pl.ANY)
SCALAR = pl.BlockSpec(memory_space=pltpu.SMEM)


def swap_added(value, axis, bit):
    count = lax.axis_size(axis)
    return value + lax.ppermute(value, axis, [(i, i ^ bit) for i in range(count)])


def bits(count):
    made = [1 << k for k in range(count.bit_length() - 1)]
    if count != 1 << len(made):
        raise ValueError("axis size")
    return made


def body(windows, pod_basis):
    f32, bf16 = jnp.float32, jnp.bfloat16
    shape = jax.ShapeDtypeStruct
    count, fields, planes, layers, cells = windows.shape
    ring, walls = lax.axis_size("solver"), lax.axis_size("analysis")
    paired = walls == 2 and planes == 8 and layers == 4
    place = lax.axis_index("analysis").astype(jnp.int32).reshape(1)
    modes, _, pod_planes, pod_layers, _ = pod_basis.shape
    tiles = fields * pod_planes * (pod_layers // 8)
    basis = pod_basis.reshape(modes, tiles, 8, cells)
    wide = modes * 8
    basis_bytes = basis.size * 2

    to_right = [(i, (i + 1) % ring) for i in range(ring)]
    to_left = [((i + 1) % ring, i) for i in range(ring)]
    edge_shape = shape((count, fields, REACH, layers, cells), f32)
    face_scratch = [pltpu.VMEM((fields, planes, layers, cells), f32)]
    face_cost = cost(10_000_000, 10 * windows.size)
    if paired:
        swap = [(0, 1), (1, 0)]
        group_shape = shape((fields, 48, cells), bf16)
        lows = pltpu.VMEM((fields, 16, cells), f32)
        near_group, kept = pl.pallas_call(
            near_kernel,
            out_shape=[group_shape, shape(windows.shape, f32)],
            in_specs=[SCALAR, WHOLE],
            out_specs=[WHOLE] * 2,
            scratch_shapes=[lows, pltpu.SemaphoreType.DMA],
            compiler_params=params(16),
            cost_estimate=face_cost,
            name="near_faces",
        )(place, windows)
        later_group, first_edge, second_edge = pl.pallas_call(
            later_kernel,
            out_shape=[group_shape] + [edge_shape] * 2,
            in_specs=[SCALAR, LOOSE, WHOLE],
            out_specs=[WHOLE] * 3,
            scratch_shapes=[pltpu.VMEM((count, fields, planes, layers, cells), f32), lows],
            compiler_params=params(16),
            cost_estimate=face_cost,
            name="later_faces",
        )(place, near_group, kept)
        near_group = lax.ppermute(near_group, "analysis", swap)
        down = [(2 * ((i + 1) % ring), 2 * i) for i in range(ring)]
        up = [(2 * i, 2 * ((i + 1) % ring)) for i in range(ring)]
        odd = lambda pairs: [(a + 1, b + 1) for a, b in pairs]
        first_edge = lax.ppermute(first_edge, ("solver", "analysis"), down + odd(up))
        second_edge = lax.ppermute(second_edge, ("solver", "analysis"), up + odd(down))
        later_group = lax.ppermute(later_group, "analysis", swap)
    else:
        kept, to_next, to_last, up, down = pl.pallas_call(
            functools.partial(face_kernel, True),
            out_shape=[shape(windows.shape, f32)]
            + [edge_shape] * 2
            + [shape(windows.shape, f32)] * 2,
            in_specs=[SCALAR, FAR],
            out_specs=[WHOLE] * 5,
            scratch_shapes=face_scratch + [pltpu.SemaphoreType.DMA((count,))],
            compiler_params=params(16),
            cost_estimate=face_cost,
            name="faces",
        )(place, windows)
        wall_terms = [
            lax.ppermute(up, "analysis", [(i, i + 1) for i in range(walls - 1)]),
            lax.ppermute(down, "analysis", [(i + 1, i) for i in range(walls - 1)]),
        ]
        from_left = lax.ppermute(to_next, "solver", to_right)
        from_right = lax.ppermute(to_last, "solver", to_left)

    early = 2
    gram_flops = 2 * wide * wide * cells * tiles
    inner, right, left, basis = pl.pallas_call(
        functools.partial(inner_gram_kernel, early),
        out_shape=[
            shape(windows.shape, f32),
            shape((wide, wide // 2), f32),
            shape((wide // 2, wide // 2), f32),
            shape(basis.shape, bf16),
        ],
        in_specs=[WHOLE, FAR],
        out_specs=[WHOLE] * 4,
        scratch_shapes=[
            pltpu.VMEM((2 * fields, planes, count * layers, cells), f32),
            pltpu.SemaphoreType.DMA((fields,)),
        ],
        compiler_params=params(40),
        cost_estimate=cost(1_000_000, windows.size),
        name="inner_gram",
    )(kept, basis)

    def rest_of_gram(after):
        return pl.pallas_call(
            functools.partial(gram_kernel, early, fields),
            out_shape=shape((modes // 2, 2 * modes), f32),
            in_specs=[LOOSE] + [WHOLE] * 3,
            out_specs=WHOLE,
            scratch_shapes=[pltpu.VMEM((wide // LANES, wide, LANES), f32)],
            compiler_params=params(24),
            cost_estimate=cost(gram_flops // 2, basis_bytes),
            name="gram",
        )(after, right, left, basis)

    join_cost = cost(1_000_000, 16 * windows.size)
    if paired:
        half_shape = (count, fields, planes * layers // 2, cells)

        half_next = shape((count, fields, planes // 2, layers, cells), f32)

        inner_given = pl.pallas_call(
            wall_join_kernel,
            out_shape=half_next,
            in_specs=[SCALAR] + [WHOLE] * 2,
            out_specs=WHOLE,
            compiler_params=params(16),
            cost_estimate=cost(gram_flops // 2, basis_bytes),
            name="wall_join",
        )(place, inner, near_group)
        next_given, given = pl.pallas_call(
            edge_join_kernel,
            out_shape=[half_next, shape(half_shape, bf16)],
            in_specs=[WHOLE] * 2,
            out_specs=[WHOLE] * 2,
            compiler_params=params(16),
            cost_estimate=join_cost,
            name="edge_join",
        )(inner_given, first_edge)
        got = lax.ppermute(given, "analysis", swap)
        inner_own = pl.pallas_call(
            own_edge_kernel,
            out_shape=half_next,
            in_specs=[SCALAR, LOOSE] + [WHOLE] * 2,
            out_specs=WHOLE,
            compiler_params=params(16),
            cost_estimate=join_cost,
            name="own_edge",
        )(place, given, inner, second_edge)
        gram = rest_of_gram(inner_own)
    else:
        next_windows = pl.pallas_call(
            functools.partial(join_kernel, 2),
            out_shape=shape(windows.shape, f32),
            in_specs=[WHOLE] * 5,
            out_specs=WHOLE,
            compiler_params=params(16),
            cost_estimate=join_cost,
            name="join",
        )(inner, from_left, from_right, *wall_terms)
        gram = rest_of_gram(place)
    ring_bits = bits(ring)
    lone = ring_bits.pop(1 if len(ring_bits) > 1 else 0)
    gram_far = lax.ppermute(gram, "solver", [(i, i ^ lone) for i in range(ring)])
    if paired:
        next_own, own = pl.pallas_call(
            own_join_kernel,
            out_shape=[half_next, shape(half_shape, bf16)],
            in_specs=[SCALAR, LOOSE] + [WHOLE] * 2,
            out_specs=[WHOLE] * 2,
            compiler_params=params(16),
            cost_estimate=join_cost,
            name="own_join",
        )(place, gram, inner_own, later_group)

    sums_shape = shape((8, LANES), f32)
    snaps_shape = shape((tiles, 2 * 8, cells), bf16)
    scratch = [pltpu.VMEM((LANES, LANES), f32), pltpu.VMEM((1, wide, LANES), f32)]
    project_cost = cost(2 * wide * 16 * cells * tiles, basis_bytes)
    if paired:
        sums, snaps, next_windows = pl.pallas_call(
            functools.partial(project_kernel, True),
            out_shape=[sums_shape, snaps_shape, shape(windows.shape, f32)],
            in_specs=[SCALAR] + [WHOLE] * 5,
            out_specs=[WHOLE, WHOLE, FAR],
            scratch_shapes=scratch + [pltpu.SemaphoreType.DMA((2,))],
            compiler_params=params(16),
            cost_estimate=project_cost,
            name="project",
        )(place, own, got, next_own, next_given, basis)
    else:
        relaid = lax.all_to_all(
            next_windows.astype(bf16), "analysis", split_axis=2, concat_axis=3, tiled=True
        )
        snaps = relaid.reshape(count, tiles, 8, cells).transpose(1, 0, 2, 3)
        snaps = snaps.reshape(tiles, count * 8, cells)
        sums = pl.pallas_call(
            functools.partial(project_kernel, False),
            out_shape=sums_shape,
            in_specs=[SCALAR] + [WHOLE] * 2,
            out_specs=WHOLE,
            scratch_shapes=scratch,
            compiler_params=params(16),
            cost_estimate=project_cost,
            name="project",
        )(place, snaps, basis)
    sums = pl.pallas_call(
        merge_kernel,
        out_shape=shape((modes // 2 + 8, LANES), f32),
        in_specs=[WHOLE] * 3,
        out_specs=WHOLE,
        compiler_params=params(16),
        cost_estimate=cost(10_000, 8 * modes * LANES),
        name="merge",
    )(gram, gram_far, sums)
    for bit in bits(walls):
        sums = swap_added(sums, "analysis", bit)
    for bit in ring_bits:
        sums = swap_added(sums, "solver", bit)
    inverse, spread = pl.pallas_call(
        inverse_kernel,
        out_shape=[shape((modes, modes), f32), shape((modes, wide), f32)],
        in_specs=[WHOLE],
        out_specs=[WHOLE] * 2,
        scratch_shapes=[pltpu.VMEM((modes, 2 * modes), f32)] * 2,
        compiler_params=params(16),
        cost_estimate=cost(20_000_000, 8 * modes * modes),
        name="inverse",
    )(sums)
    projected = swap_added(sums, "solver", lone)

    rows_total = ring * walls * tiles * 8 * cells
    new_modes, solved, factor = pl.pallas_call(
        functools.partial(finish_kernel, rows_total),
        out_shape=[
            shape((count, tiles, 8, cells), f32),
            shape((count, modes), f32),
            shape((count, count), f32),
        ],
        in_specs=[WHOLE] * 6,
        out_specs=[FAR, WHOLE, WHOLE],
        scratch_shapes=[
            pltpu.VMEM((count, tiles, 8, cells), f32),
            pltpu.SemaphoreType.DMA((fields,)),
        ],
        compiler_params=params(16),
        cost_estimate=cost(2 * wide * 32 * cells * tiles, basis_bytes + 8 * windows.size),
        name="finish",
    )(projected, sums, inverse, spread, snaps, basis)
    new_modes = new_modes.reshape(count, fields, pod_planes, pod_layers, cells)
    return next_windows, solved, new_modes, factor


def solution(mesh):
    in_specs = (
        P(None, None, "solver", "analysis", None),
        P(None, None, ("solver", "analysis"), None, None),
    )
    out_specs = (
        P(None, None, "solver", "analysis", None),
        P(),
        P(None, None, ("solver", "analysis"), None, None),
        P(),
    )
    return jax.shard_map(body, mesh=mesh, in_specs=in_specs, out_specs=out_specs, check_vma=False)
```

```python
import functools

import jax
import jax.numpy as jnp
from jax import lax
from jax.experimental import pallas as pl
from jax.experimental.pallas import tpu as pltpu
from jax.sharding import PartitionSpec as P

PRESSURE_FACTOR = 1.4 - 1.0
SECTION_STEP = 0.25
CENTRAL_WEIGHTS = (0.8, -0.2, 4.0 / 105.0, -1.0 / 280.0)
REACH = 4
LANES = 128
HIGHEST = lax.Precision.HIGHEST
NT = (((1,), (1,)), ((), ()))


def weight(k):
    if k == 0 or abs(k) > REACH:
        return 0.0
    value = -SECTION_STEP * CENTRAL_WEIGHTS[abs(k) - 1]
    return value if k > 0 else -value


def row_weights(shape, values):
    rows = lax.broadcasted_iota(jnp.int32, shape, len(shape) - 2)
    made = jnp.full(shape, values[0], jnp.float32)
    for i, value in enumerate(values[1:], start=1):
        made = jnp.where(rows == i, jnp.float32(value), made)
    return made


def primitives(fields):
    density, mx, my, mz, energy = fields
    inverse = 1.0 / density
    ux, uy, uz = mx * inverse, my * inverse, mz * inverse
    pressure = PRESSURE_FACTOR * (energy - 0.5 * (mx * ux + my * uy + mz * uz))
    return (mx, my, mz), (ux, uy, uz), pressure, energy + pressure


def flux(parts, direction):
    moments, speeds, pressure, enthalpy = parts
    speed = speeds[direction]
    made = [moments[direction]]
    for axis in range(3):
        term = moments[axis] * speed
        made.append(term + pressure if axis == direction else term)
    made.append(enthalpy * speed)
    return made


def face_kernel(two_sided, where_ref, source_ref, windows_ref, left_ref, right_ref, *rest):
    windows, _, planes, layers, cells = windows_ref.shape
    wall_refs, scratch, sems = rest[:-2], rest[-2], rest[-1]
    copies = [
        pltpu.make_async_copy(source_ref.at[w], windows_ref.at[w], sems.at[w])
        for w in range(windows)
    ]
    for copy in copies:
        copy.start()
    tile = (layers, cells)
    up = [
        row_weights(tile, [weight(j - layers - i) for i in range(layers)]) for j in range(layers)
    ]
    down = [
        row_weights(tile, [weight(layers + j - i) for i in range(layers)]) for j in range(layers)
    ]
    if two_sided:
        tables = (up, down)
    else:
        first = where_ref[0] == 0
        tables = ([jnp.where(first, u, d) for u, d in zip(up, down)],)
    for w in range(windows):
        copies[w].wait()
        for x in range(planes):
            parts = primitives([windows_ref[w, f, x] for f in range(5)])
            for f, value in enumerate(flux(parts, 0)):
                scratch[f, x] = value
            for f, value in enumerate(flux(parts, 1)):
                for ref, table in zip(wall_refs, tables):
                    total = None
                    for j in range(layers):
                        term = table[j] * value[j : j + 1, :]
                        total = term if total is None else total + term
                    ref[w, f, x] = total
        for f in range(5):
            for i in range(REACH):
                total = None
                for j in range(planes):
                    c = weight(j - planes - i)
                    if c:
                        term = c * scratch[f, j]
                        total = term if total is None else total + term
                left_ref[w, f, i] = total
                total = None
                for j in range(planes):
                    c = weight(j + REACH - i)
                    if c:
                        term = c * scratch[f, j]
                        total = term if total is None else total + term
                right_ref[w, f, i] = total


def wall_group(where_ref, windows_ref, group_ref, lows, base, keep_x):
    windows, _, planes, layers, cells = windows_ref.shape
    tile = (layers, cells)
    first = where_ref[0] == 0
    table = [
        jnp.where(
            first,
            row_weights(tile, [weight(j - layers - i) for i in range(layers)]),
            row_weights(tile, [weight(layers + j - i) for i in range(layers)]),
        )
        for j in range(layers)
    ]
    for w in range(windows):
        upper = [[] for _ in range(5)]
        lower = [[] for _ in range(5)]
        for x in range(planes // 2):
            parts = primitives([windows_ref[w, f, base + x] for f in range(5)])
            keep_x(w, base + x, parts)
            for f, value in enumerate(flux(parts, 1)):
                total = None
                for j in range(layers):
                    term = table[j] * value[j : j + 1, :]
                    total = term if total is None else total + term
                high = total.astype(jnp.bfloat16).astype(jnp.float32)
                rest = total - high
                upper[f].append(high)
                lower[f].append(jnp.where(first, rest[0:2], rest[2:4]))
        for f in range(5):
            group_ref[f, 16 * w : 16 * w + 16] = jnp.concatenate(upper[f], axis=0).astype(
                jnp.bfloat16
            )
            lows[f, 8 * w : 8 * w + 8] = jnp.concatenate(lower[f], axis=0)
    for f in range(5):
        group_ref[f, 32:48] = lows[f].astype(jnp.bfloat16)


def near_kernel(where_ref, source_ref, group_ref, kept_ref, lows, sem):
    copy = pltpu.make_async_copy(source_ref, kept_ref, sem)
    copy.start()
    base = source_ref.shape[2] // 2 * where_ref[0]
    wall_group(where_ref, source_ref, group_ref, lows, base, lambda w, x, parts: None)
    copy.wait()


def later_kernel(
    where_ref, _, windows_ref, group_ref, first_ref, second_ref, scratch, lows,
    edge_lows,
):
    windows, _, planes, layers, cells = windows_ref.shape
    half = planes // 2

    def keep_x(w, x, parts):
        for f, value in enumerate(flux(parts, 0)):
            scratch[w, f, x] = value

    base = half * (1 - where_ref[0])
    wall_group(where_ref, windows_ref, group_ref, lows, base, keep_x)
    for w in range(windows):
        for x in range(half):
            plane = half * where_ref[0] + x
            keep_x(w, plane, primitives([windows_ref[w, f, plane] for f in range(5)]))
        for f in range(5):
            last, after = [], []
            for made, offset in ((after, -planes), (last, REACH)):
                for i in range(REACH):
                    total = None
                    for j in range(planes):
                        c = weight(j + offset - i)
                        if c:
                            term = c * scratch[w, f, j]
                            total = term if total is None else total + term
                    made.append(total)
            zeroth = where_ref[0] == 0
            for k, (ref, high) in enumerate(((first_ref, zeroth), (second_ref, where_ref[0] == 1))):
                both = [
                    jnp.where(high, x, y) for x, y in zip(last, after)
                ]
                upper = [x.astype(jnp.bfloat16).astype(jnp.float32) for x in both]
                rest = [x - y for x, y in zip(both, upper)]
                ref[f, 16 * w : 16 * w + 16] = jnp.concatenate(upper, axis=0).astype(jnp.bfloat16)
                edge_lows[k, f, 8 * w : 8 * w + 8] = jnp.concatenate(
                    [jnp.where(high, rest[2], rest[0]), jnp.where(high, rest[3], rest[1])], axis=0
                )
    for k, ref in enumerate((first_ref, second_ref)):
        for f in range(5):
            ref[f, 32:48] = edge_lows[k, f].astype(jnp.bfloat16)


def inner_part(windows_ref, part_ref, scratch):
    windows, _, planes, layers, cells = windows_ref.shape
    tile = (windows * layers, cells)
    walls = {
        k: row_weights(
            tile, [weight(k) if 0 <= i + k < layers else 0.0 for i in range(layers)] * windows
        )
        for k in range(-REACH, REACH + 1)
        if 0 < abs(k) < layers
    }
    for x in range(planes):
        fields = [
            jnp.concatenate([windows_ref[w, f, x] for w in range(windows)], axis=0)
            for f in range(5)
        ]
        parts = primitives(fields)
        for f, value in enumerate(flux(parts, 0)):
            scratch[f, x] = value
        flux_y, flux_z = flux(parts, 1), flux(parts, 2)
        for f in range(5):
            total = fields[f]
            for k, line in walls.items():
                total = total + line * pltpu.roll(flux_y[f], -k % tile[0], 0)
            for k in range(1, REACH + 1):
                total = total + weight(k) * (
                    pltpu.roll(flux_z[f], cells - k, 1) - pltpu.roll(flux_z[f], k, 1)
                )
            scratch[5 + f, x] = total
    for f in range(5):
        for x in range(planes):
            total = scratch[5 + f, x]
            for k in range(-REACH, REACH + 1):
                if k and 0 <= x + k < planes:
                    total = total + weight(k) * scratch[f, x + k]
            for w in range(windows):
                part_ref[w, f, x] = total[layers * w : layers * (w + 1)]


def gram_blocks(basis_ref, chunks, per_chunk, right, left):
    half = left.shape[0]
    for c in chunks:
        rows = jnp.concatenate(
            [modes_of(basis_ref, t) for t in range(c * per_chunk, (c + 1) * per_chunk)], axis=1
        )
        right = right + lax.dot_general(
            rows, rows[half:], NT, preferred_element_type=jnp.float32
        )
        left = left + lax.dot_general(
            rows[:half], rows[:half], NT, preferred_element_type=jnp.float32
        )
    return right, left


def inner_gram_kernel(
    early, windows_ref, basis_ref, part_ref, right_ref, left_ref, kept_ref, scratch, sems
):
    chunks = sems.shape[0]
    per_chunk = kept_ref.shape[1] // chunks
    copies = []
    for c in range(chunks):
        span = pl.ds(c * per_chunk, per_chunk)
        copies.append(
            pltpu.make_async_copy(basis_ref.at[:, span], kept_ref.at[:, span], sems.at[c])
        )
        copies[c].start()
    inner_part(windows_ref, part_ref, scratch)
    right, left = jnp.zeros(right_ref.shape, jnp.float32), jnp.zeros(left_ref.shape, jnp.float32)
    for c in range(chunks):
        copies[c].wait()
        if c < early:
            right, left = gram_blocks(kept_ref, [c], per_chunk, right, left)
    right_ref[...] = right
    left_ref[...] = left


def gram_kernel(early, chunks, _, right_ref, left_ref, basis_ref, gram_ref, total):
    modes, tiles = basis_ref.shape[:2]
    wide = modes * 8
    half = wide // 2
    right, left = gram_blocks(
        basis_ref, range(early, chunks), tiles // chunks, right_ref[...], left_ref[...]
    )
    tiles_left = half // LANES
    turned = right[0:half].T
    for tile in range(tiles_left):
        span = slice(tile * LANES, (tile + 1) * LANES)
        total[tile, 0:half] = left[:, span]
        total[tile, half:] = turned[:, span]
        total[tiles_left + tile] = right[:, span]
    rows = folded(total, modes)
    picks = (
        lax.broadcasted_iota(jnp.int32, (wide, modes), 0) // 8
        == lax.broadcasted_iota(jnp.int32, (wide, modes), 1)
    ).astype(jnp.float32)
    gram = jnp.dot(rows, picks, precision=HIGHEST, preferred_element_type=jnp.float32)
    gram_ref[:, 0:modes] = gram[0 : modes // 2]
    gram_ref[:, modes:] = gram[modes // 2 :]


def join_kernel(walls, part_ref, left_ref, right_ref, *rest):
    wall_refs, next_ref = rest[:walls], rest[walls]
    windows, _, planes, layers, cells = part_ref.shape
    for w in range(windows):
        for f in range(5):
            for x in range(planes):
                total = part_ref[w, f, x]
                for ref in wall_refs:
                    total = total + ref[w, f, x]
                if x < REACH:
                    total = total + left_ref[w, f, x]
                if x >= planes - REACH:
                    total = total + right_ref[w, f, x - planes + REACH]
                next_ref[w, f, x] = total


def wall_terms_of(first, group_ref, w, f):
    upper = group_ref[f, 16 * w : 16 * w + 16].astype(jnp.float32)
    lower = group_ref[f, 32:48].astype(jnp.float32)[8 * w : 8 * w + 8]
    zero = jnp.zeros((2, upper.shape[1]), jnp.float32)
    made = []
    for x in range(4):
        rest = lower[2 * x : 2 * x + 2]
        rest = jnp.where(
            first, jnp.concatenate([zero, rest], axis=0), jnp.concatenate([rest, zero], axis=0)
        )
        made.append(upper[4 * x : 4 * x + 4] + rest)
    return made


def wall_join_kernel(where_ref, part_ref, group_ref, given_ref):
    windows, _, planes = part_ref.shape[:3]
    base = planes // 2 * (1 - where_ref[0])
    for w in range(windows):
        for f in range(5):
            for x, term in enumerate(wall_terms_of(where_ref[0] == 0, group_ref, w, f)):
                given_ref[w, f, x] = part_ref[w, f, base + x] + term


def edge_terms_of(high, edge_ref, w, f):
    upper = edge_ref[f, 16 * w : 16 * w + 16].astype(jnp.float32)
    lower = edge_ref[f, 32:48].astype(jnp.float32)[8 * w : 8 * w + 8]
    made = []
    for x in range(4):
        rest = lower[4 * (x % 2) : 4 * (x % 2) + 4]
        rest = jnp.where(high, rest, 0.0) if x > 1 else jnp.where(high, 0.0, rest)
        made.append(upper[4 * x : 4 * x + 4] + rest)
    return made


def edge_join_kernel(where_ref, part_ref, edge_ref, made, snaps_ref):
    windows = part_ref.shape[0]
    for w in range(windows):
        for f in range(5):
            done = []
            for x, term in enumerate(edge_terms_of(where_ref[0] == 0, edge_ref, w, f)):
                total = part_ref[w, f, x] + term
                made[w, f, x] = total
                done.append(total)
            snaps_ref[w, f] = jnp.concatenate(done, axis=0).astype(jnp.bfloat16)


def own_join_kernel(where_ref, _, part_ref, edge_ref, group_ref, made, snaps_ref):
    windows, _, planes = part_ref.shape[:3]
    base = planes // 2 * where_ref[0]
    for w in range(windows):
        for f in range(5):
            done = []
            edges = edge_terms_of(where_ref[0] == 1, edge_ref, w, f)
            for x, term in enumerate(wall_terms_of(where_ref[0] == 0, group_ref, w, f)):
                total = part_ref[w, f, base + x] + term + edges[x]
                made[w, f, x] = total
                done.append(total)
            snaps_ref[w, f] = jnp.concatenate(done, axis=0).astype(jnp.bfloat16)


def same_layer(shape):
    rows = lax.broadcasted_iota(jnp.int32, shape, 0)
    columns = lax.broadcasted_iota(jnp.int32, shape, 1)
    return lax.rem(rows, 8) == lax.rem(columns, 8)


def folded(total, modes):
    kept = lax.rem(lax.broadcasted_iota(jnp.int32, (modes, LANES), 1), 8)
    made = []
    for tile in range(total.shape[0]):
        rows = jnp.zeros((modes, LANES), jnp.float32)
        for y in range(8):
            rows = jnp.where(kept == y, total[tile, pl.ds(y, modes, 8), :], rows)
        made.append(rows)
    return made[0] if len(made) == 1 else jnp.concatenate(made, axis=1)


def modes_of(basis_ref, t):
    modes, _, layers, cells = basis_ref.shape
    return basis_ref[:, t].reshape(modes * layers, cells)


def project_kernel(paired, where_ref, *rest):
    if paired:
        (
            own_ref, got_ref, next_own_ref, next_given_ref, basis_ref,
            sums_ref, snaps_ref, next_ref, square, wide_sums, sems,
        ) = rest
        first = where_ref[0] == 0
        half = next_own_ref.shape[2]
        copies = []
        for i, (source, base) in enumerate(
            ((next_own_ref, half * where_ref[0]), (next_given_ref, half * (1 - where_ref[0])))
        ):
            copies.append(
                pltpu.make_async_copy(source, next_ref.at[:, :, pl.ds(base, half)], sems.at[i])
            )
            copies[i].start()
        for w in range(own_ref.shape[0]):
            for f in range(own_ref.shape[1]):
                own = own_ref[w, f].astype(jnp.float32)
                got = got_ref[w, f].astype(jnp.float32)
                low = jnp.where(first, own, got)
                high = jnp.where(first, got, own)
                for t in range(4):
                    snaps_ref[4 * f + t, pl.ds(8 * w, 8)] = jnp.concatenate(
                        [low[4 * t : 4 * t + 4], high[4 * t : 4 * t + 4]], axis=0
                    ).astype(jnp.bfloat16)
    else:
        snaps_ref, basis_ref, sums_ref, square, wide_sums = rest
        copies = []
    modes, tiles = basis_ref.shape[:2]
    columns = snaps_ref.shape[1]
    total = jnp.zeros((modes * 8 + columns, columns), jnp.float32)
    for start in range(0, tiles, 4):
        span = range(start, min(start + 4, tiles))
        snaps = jnp.concatenate([snaps_ref[t] for t in span], axis=1)
        rows = jnp.concatenate([modes_of(basis_ref, t) for t in span], axis=1)
        total = total + lax.dot_general(
            jnp.concatenate([rows, snaps], axis=0), snaps, NT, preferred_element_type=jnp.float32
        )
    small = total[modes * 8 :]
    total = total[: modes * 8]
    wide_sums[0, :, 0:columns] = total
    square[...] = jnp.zeros_like(square)
    square[0:modes, :] = folded(wide_sums, modes)
    kept = jnp.where(same_layer(small.shape), small, 0.0)
    square[modes : modes + 1, 0:columns] = jnp.sum(kept[0:8], axis=0, keepdims=True)
    square[modes + 1 : modes + 2, 0:columns] = jnp.sum(kept[8:16], axis=0, keepdims=True)
    lanes = lax.broadcasted_iota(jnp.int32, square.shape, 1)
    turned = jnp.where(lanes < columns, square[...], 0.0).T
    sums = jnp.concatenate(
        [
            jnp.sum(turned[0:8], axis=0, keepdims=True),
            jnp.sum(turned[8:16], axis=0, keepdims=True),
        ],
        axis=0,
    )
    sums_ref[...] = jnp.concatenate(
        [sums, jnp.zeros((6, sums.shape[1]), jnp.float32)], axis=0
    )
    for copy in copies:
        copy.wait()


def merge_kernel(gram_ref, far_ref, sums_ref, merged_ref):
    rows = gram_ref.shape[0]
    merged_ref[0:rows] = gram_ref[...] + far_ref[...]
    merged_ref[rows:] = sums_ref[...]


def unpacked(sums_ref, modes):
    half = modes // 2
    return jnp.concatenate([sums_ref[0:half, 0:modes], sums_ref[0:half, modes:]], axis=0)


def inverse_kernel(sums_ref, inverse_ref, spread_ref, plain, scaled):
    modes = inverse_ref.shape[0]
    rows = lax.broadcasted_iota(jnp.int32, (8, 2 * modes), 0)
    lanes = lax.broadcasted_iota(jnp.int32, (8, 2 * modes), 1)
    tiles = []
    gram = unpacked(sums_ref, modes)
    for tile in range(modes // 8):
        eye = (lanes == rows + (modes + 8 * tile)).astype(jnp.float32)
        start = 8 * tile % (modes // 2)
        line = sums_ref[start : start + 8, :]
        if 8 * tile >= modes // 2:
            line = pltpu.roll(line, modes, 1)
        tiles.append(jnp.where(lanes < modes, line, eye))
    count = modes // 8
    for home in range(count):
        columns = [
            [
                jnp.broadcast_to(
                    tiles[tile][:, 8 * home + j : 8 * home + j + 1], (8, 2 * modes)
                )
                for tile in range(home, count)
            ]
            for j in range(8)
        ]
        for j in range(8):
            k = 8 * home + j
            inverse = 1.0 / columns[j][0]
            inverse = inverse[j : j + 1, :]
            row = tiles[home][j : j + 1, :]
            ready = row * inverse
            plain[k : k + 1, :] = row
            scaled[k : k + 1, :] = ready
            factors = [jnp.where(rows > j, columns[j][0], 0.0)] + columns[j][1:]
            for later in range(j + 1, 8):
                share = columns[j][0][later : later + 1, :] * inverse
                columns[later] = [c - f * share for c, f in zip(columns[later], factors)]
            for tile in range(home, count):
                tiles[tile] = tiles[tile] - factors[tile - home] * ready
    exact = functools.partial(
        lax.dot_general, precision=HIGHEST, preferred_element_type=jnp.float32
    )
    plainly = (((1,), (0,)), ((), ()))
    inverse = exact(plain[:, modes:], scaled[:, modes:], (((0,), (0,)), ((), ())))
    square = (modes, modes)
    eye = lax.broadcasted_iota(jnp.int32, square, 0) == lax.broadcasted_iota(jnp.int32, square, 1)
    off = eye.astype(jnp.float32) - exact(gram, inverse, plainly)
    inverse = inverse + exact(inverse, off, plainly)
    inverse_ref[...] = inverse
    wide = spread_ref.shape[1]
    spread = (
        lax.broadcasted_iota(jnp.int32, (modes, wide), 1) // 8
        == lax.broadcasted_iota(jnp.int32, (modes, wide), 0)
    ).astype(jnp.bfloat16)
    parts = []
    rest = inverse
    for _ in range(3):
        parts.append(rest.astype(jnp.bfloat16))
        rest = rest - parts[-1].astype(jnp.float32)
    wide_parts = jnp.dot(
        jnp.concatenate(parts, axis=0), spread, preferred_element_type=jnp.float32
    )
    spread_ref[...] = (
        wide_parts[0:modes] + wide_parts[modes : 2 * modes] + wide_parts[2 * modes :]
    )


def finish_kernel(
    rows_total, projected_ref, sums_ref, inverse_ref, spread_ref, snaps_ref, basis_ref,
    modes_ref, solved_ref, factor_ref, made, sems,
):
    modes, tiles, _, cells = basis_ref.shape
    wide = modes * 8
    exact = functools.partial(jnp.dot, precision=HIGHEST, preferred_element_type=jnp.float32)
    base = modes // 2
    projected = projected_ref[base : base + 8, 0:modes]
    lines = exact(projected, spread_ref[...])
    full = jnp.concatenate(
        [jnp.broadcast_to(lines[0:1], (8, wide)), jnp.broadcast_to(lines[1:2], (8, wide))],
        axis=0,
    )
    full = jnp.where(same_layer(full.shape), full, 0.0)
    upper = full.astype(jnp.bfloat16)
    fit = jnp.concatenate([upper, (full - upper.astype(jnp.float32)).astype(jnp.bfloat16)], axis=0)
    solved = exact(projected, inverse_ref[...])
    left = projected - exact(solved, unpacked(sums_ref, modes))

    def inner(p, i, q, j):
        return jnp.sum(p[i : i + 1] * q[j : j + 1], axis=1, keepdims=True)

    def entry(i, j):
        square = projected_ref[base + i : base + i + 1, modes + j : modes + j + 1]
        return square - inner(projected, i, solved, j) - inner(solved, i, left, j)

    first = jnp.sqrt(entry(0, 0))
    below = entry(1, 0) / first
    second = jnp.sqrt(entry(1, 1) - below * below)
    scaling = jnp.sqrt(jnp.float32(rows_total))
    w00 = scaling / first
    w11 = scaling / second
    w01 = -(below / first) * w11
    solved_ref[...] = solved[0:2]
    factor_ref[0:1, 0:1] = first / scaling
    factor_ref[0:1, 1:2] = below / scaling
    factor_ref[1:2, 0:1] = jnp.zeros_like(first)
    factor_ref[1:2, 1:2] = second / scaling
    chunks = sems.shape[0]
    per_chunk = tiles // chunks
    copies = []
    for c in range(chunks):
        for t in range(c * per_chunk, (c + 1) * per_chunk):
            fitted = jnp.dot(fit, modes_of(basis_ref, t), preferred_element_type=jnp.float32)
            fitted = fitted[0:16] + fitted[16:32]
            snaps = snaps_ref[t].astype(jnp.float32)
            left_over = snaps - fitted
            made[0, t] = left_over[0:8] * w00
            made[1, t] = left_over[8:16] * w11 + left_over[0:8] * w01
        span = pl.ds(c * per_chunk, per_chunk)
        copies.append(
            pltpu.make_async_copy(made.at[:, span], modes_ref.at[:, span], sems.at[c])
        )
        copies[c].start()
    for copy in copies:
        copy.wait()


def params(mib):
    return pltpu.CompilerParams(vmem_limit_bytes=mib * 1024 * 1024)


def cost(flops, moved):
    return pl.CostEstimate(flops=flops, bytes_accessed=moved, transcendentals=0)


WHOLE = pl.BlockSpec(memory_space=pltpu.VMEM)
FAR = pl.BlockSpec(memory_space=pltpu.HBM)
LOOSE = pl.BlockSpec(memory_space=pl.ANY)
SCALAR = pl.BlockSpec(memory_space=pltpu.SMEM)


def swap_added(value, axis, bit):
    count = lax.axis_size(axis)
    return value + lax.ppermute(value, axis, [(i, i ^ bit) for i in range(count)])


def bits(count):
    made = [1 << k for k in range(count.bit_length() - 1)]
    if count != 1 << len(made):
        raise ValueError("axis size")
    return made


def body(windows, pod_basis):
    f32, bf16 = jnp.float32, jnp.bfloat16
    shape = jax.ShapeDtypeStruct
    count, fields, planes, layers, cells = windows.shape
    ring, walls = lax.axis_size("solver"), lax.axis_size("analysis")
    paired = walls == 2 and planes == 8 and layers == 4
    place = lax.axis_index("analysis").astype(jnp.int32).reshape(1)
    modes, _, pod_planes, pod_layers, _ = pod_basis.shape
    tiles = fields * pod_planes * (pod_layers // 8)
    basis = pod_basis.reshape(modes, tiles, 8, cells)
    wide = modes * 8
    basis_bytes = basis.size * 2

    to_right = [(i, (i + 1) % ring) for i in range(ring)]
    to_left = [((i + 1) % ring, i) for i in range(ring)]
    edge_shape = shape((count, fields, REACH, layers, cells), f32)
    face_scratch = [pltpu.VMEM((fields, planes, layers, cells), f32)]
    face_cost = cost(10_000_000, 10 * windows.size)
    if paired:
        swap = [(0, 1), (1, 0)]
        group_shape = shape((fields, 48, cells), bf16)
        lows = pltpu.VMEM((fields, 16, cells), f32)
        near_group, kept = pl.pallas_call(
            near_kernel,
            out_shape=[group_shape, shape(windows.shape, f32)],
            in_specs=[SCALAR, WHOLE],
            out_specs=[WHOLE] * 2,
            scratch_shapes=[lows, pltpu.SemaphoreType.DMA],
            compiler_params=params(16),
            cost_estimate=face_cost,
            name="near_faces",
        )(place, windows)
        later_group, first_edge, second_edge = pl.pallas_call(
            later_kernel,
            out_shape=[group_shape] * 3,
            in_specs=[SCALAR, LOOSE, WHOLE],
            out_specs=[WHOLE] * 3,
            scratch_shapes=[
                pltpu.VMEM((count, fields, planes, layers, cells), f32),
                lows,
                pltpu.VMEM((2, fields, 16, cells), f32),
            ],
            compiler_params=params(16),
            cost_estimate=face_cost,
            name="later_faces",
        )(place, near_group, kept)
        near_group = lax.ppermute(near_group, "analysis", swap)
        down = [(2 * ((i + 1) % ring), 2 * i) for i in range(ring)]
        up = [(2 * i, 2 * ((i + 1) % ring)) for i in range(ring)]
        odd = lambda pairs: [(a + 1, b + 1) for a, b in pairs]
        first_edge = lax.ppermute(first_edge, ("solver", "analysis"), down + odd(up))
        second_edge = lax.ppermute(second_edge, ("solver", "analysis"), up + odd(down))
        later_group = lax.ppermute(later_group, "analysis", swap)
    else:
        kept, to_next, to_last, up, down = pl.pallas_call(
            functools.partial(face_kernel, True),
            out_shape=[shape(windows.shape, f32)]
            + [edge_shape] * 2
            + [shape(windows.shape, f32)] * 2,
            in_specs=[SCALAR, FAR],
            out_specs=[WHOLE] * 5,
            scratch_shapes=face_scratch + [pltpu.SemaphoreType.DMA((count,))],
            compiler_params=params(16),
            cost_estimate=face_cost,
            name="faces",
        )(place, windows)
        wall_terms = [
            lax.ppermute(up, "analysis", [(i, i + 1) for i in range(walls - 1)]),
            lax.ppermute(down, "analysis", [(i + 1, i) for i in range(walls - 1)]),
        ]
        from_left = lax.ppermute(to_next, "solver", to_right)
        from_right = lax.ppermute(to_last, "solver", to_left)

    early = 2
    gram_flops = 2 * wide * wide * cells * tiles
    inner, right, left, basis = pl.pallas_call(
        functools.partial(inner_gram_kernel, early),
        out_shape=[
            shape(windows.shape, f32),
            shape((wide, wide // 2), f32),
            shape((wide // 2, wide // 2), f32),
            shape(basis.shape, bf16),
        ],
        in_specs=[WHOLE, FAR],
        out_specs=[WHOLE] * 4,
        scratch_shapes=[
            pltpu.VMEM((2 * fields, planes, count * layers, cells), f32),
            pltpu.SemaphoreType.DMA((fields,)),
        ],
        compiler_params=params(40),
        cost_estimate=cost(1_000_000, windows.size),
        name="inner_gram",
    )(kept, basis)

    def rest_of_gram(after):
        return pl.pallas_call(
            functools.partial(gram_kernel, early, fields),
            out_shape=shape((modes // 2, 2 * modes), f32),
            in_specs=[LOOSE] + [WHOLE] * 3,
            out_specs=WHOLE,
            scratch_shapes=[pltpu.VMEM((wide // LANES, wide, LANES), f32)],
            compiler_params=params(24),
            cost_estimate=cost(gram_flops // 2, basis_bytes),
            name="gram",
        )(after, right, left, basis)

    join_cost = cost(1_000_000, 16 * windows.size)
    if paired:
        half_shape = (count, fields, planes * layers // 2, cells)

        half_next = shape((count, fields, planes // 2, layers, cells), f32)

        inner_given = pl.pallas_call(
            wall_join_kernel,
            out_shape=half_next,
            in_specs=[SCALAR] + [WHOLE] * 2,
            out_specs=WHOLE,
            compiler_params=params(16),
            cost_estimate=cost(gram_flops // 2, basis_bytes),
            name="wall_join",
        )(place, inner, near_group)
        next_given, given = pl.pallas_call(
            edge_join_kernel,
            out_shape=[half_next, shape(half_shape, bf16)],
            in_specs=[SCALAR] + [WHOLE] * 2,
            out_specs=[WHOLE] * 2,
            compiler_params=params(16),
            cost_estimate=join_cost,
            name="edge_join",
        )(place, inner_given, first_edge)
        got = lax.ppermute(given, "analysis", swap)
        gram = rest_of_gram(given)
    else:
        next_windows = pl.pallas_call(
            functools.partial(join_kernel, 2),
            out_shape=shape(windows.shape, f32),
            in_specs=[WHOLE] * 5,
            out_specs=WHOLE,
            compiler_params=params(16),
            cost_estimate=join_cost,
            name="join",
        )(inner, from_left, from_right, *wall_terms)
        gram = rest_of_gram(place)
    ring_bits = bits(ring)
    lone = ring_bits.pop(1 if len(ring_bits) > 1 else 0)
    gram_far = lax.ppermute(gram, "solver", [(i, i ^ lone) for i in range(ring)])
    if paired:
        next_own, own = pl.pallas_call(
            own_join_kernel,
            out_shape=[half_next, shape(half_shape, bf16)],
            in_specs=[SCALAR, LOOSE] + [WHOLE] * 3,
            out_specs=[WHOLE] * 2,
            compiler_params=params(16),
            cost_estimate=join_cost,
            name="own_join",
        )(place, gram, inner, second_edge, later_group)

    sums_shape = shape((8, LANES), f32)
    snaps_shape = shape((tiles, 2 * 8, cells), bf16)
    scratch = [pltpu.VMEM((LANES, LANES), f32), pltpu.VMEM((1, wide, LANES), f32)]
    project_cost = cost(2 * wide * 16 * cells * tiles, basis_bytes)
    if paired:
        sums, snaps, next_windows = pl.pallas_call(
            functools.partial(project_kernel, True),
            out_shape=[sums_shape, snaps_shape, shape(windows.shape, f32)],
            in_specs=[SCALAR] + [WHOLE] * 5,
            out_specs=[WHOLE, WHOLE, FAR],
            scratch_shapes=scratch + [pltpu.SemaphoreType.DMA((2,))],
            compiler_params=params(16),
            cost_estimate=project_cost,
            name="project",
        )(place, own, got, next_own, next_given, basis)
    else:
        relaid = lax.all_to_all(
            next_windows.astype(bf16), "analysis", split_axis=2, concat_axis=3, tiled=True
        )
        snaps = relaid.reshape(count, tiles, 8, cells).transpose(1, 0, 2, 3)
        snaps = snaps.reshape(tiles, count * 8, cells)
        sums = pl.pallas_call(
            functools.partial(project_kernel, False),
            out_shape=sums_shape,
            in_specs=[SCALAR] + [WHOLE] * 2,
            out_specs=WHOLE,
            scratch_shapes=scratch,
            compiler_params=params(16),
            cost_estimate=project_cost,
            name="project",
        )(place, snaps, basis)
    sums = pl.pallas_call(
        merge_kernel,
        out_shape=shape((modes // 2 + 8, LANES), f32),
        in_specs=[WHOLE] * 3,
        out_specs=WHOLE,
        compiler_params=params(16),
        cost_estimate=cost(10_000, 8 * modes * LANES),
        name="merge",
    )(gram, gram_far, sums)
    for bit in bits(walls):
        sums = swap_added(sums, "analysis", bit)
    for bit in ring_bits:
        sums = swap_added(sums, "solver", bit)
    inverse, spread = pl.pallas_call(
        inverse_kernel,
        out_shape=[shape((modes, modes), f32), shape((modes, wide), f32)],
        in_specs=[WHOLE],
        out_specs=[WHOLE] * 2,
        scratch_shapes=[pltpu.VMEM((modes, 2 * modes), f32)] * 2,
        compiler_params=params(16),
        cost_estimate=cost(20_000_000, 8 * modes * modes),
        name="inverse",
    )(sums)
    projected = swap_added(sums, "solver", lone)

    rows_total = ring * walls * tiles * 8 * cells
    new_modes, solved, factor = pl.pallas_call(
        functools.partial(finish_kernel, rows_total),
        out_shape=[
            shape((count, tiles, 8, cells), f32),
            shape((count, modes), f32),
            shape((count, count), f32),
        ],
        in_specs=[WHOLE] * 6,
        out_specs=[FAR, WHOLE, WHOLE],
        scratch_shapes=[
            pltpu.VMEM((count, tiles, 8, cells), f32),
            pltpu.SemaphoreType.DMA((fields,)),
        ],
        compiler_params=params(16),
        cost_estimate=cost(2 * wide * 32 * cells * tiles, basis_bytes + 8 * windows.size),
        name="finish",
    )(projected, sums, inverse, spread, snaps, basis)
    new_modes = new_modes.reshape(count, fields, pod_planes, pod_layers, cells)
    return next_windows, solved, new_modes, factor


def solution(mesh):
    in_specs = (
        P(None, None, "solver", "analysis", None),
        P(None, None, ("solver", "analysis"), None, None),
    )
    out_specs = (
        P(None, None, "solver", "analysis", None),
        P(),
        P(None, None, ("solver", "analysis"), None, None),
        P(),
    )
    return jax.shard_map(body, mesh=mesh, in_specs=in_specs, out_specs=out_specs, check_vma=False)
```

```python
import functools

import jax
import jax.numpy as jnp
from jax import lax
from jax.experimental import pallas as pl
from jax.experimental.pallas import tpu as pltpu
from jax.sharding import PartitionSpec as P

PRESSURE_FACTOR = 1.4 - 1.0
SECTION_STEP = 0.25
CENTRAL_WEIGHTS = (0.8, -0.2, 4.0 / 105.0, -1.0 / 280.0)
REACH = 4
LANES = 128
HIGHEST = lax.Precision.HIGHEST
NT = (((1,), (1,)), ((), ()))


def weight(k):
    if k == 0 or abs(k) > REACH:
        return 0.0
    value = -SECTION_STEP * CENTRAL_WEIGHTS[abs(k) - 1]
    return value if k > 0 else -value


def row_weights(shape, values):
    rows = lax.broadcasted_iota(jnp.int32, shape, len(shape) - 2)
    made = jnp.full(shape, values[0], jnp.float32)
    for i, value in enumerate(values[1:], start=1):
        made = jnp.where(rows == i, jnp.float32(value), made)
    return made


def primitives(fields):
    density, mx, my, mz, energy = fields
    inverse = 1.0 / density
    ux, uy, uz = mx * inverse, my * inverse, mz * inverse
    pressure = PRESSURE_FACTOR * (energy - 0.5 * (mx * ux + my * uy + mz * uz))
    return (mx, my, mz), (ux, uy, uz), pressure, energy + pressure


def flux(parts, direction):
    moments, speeds, pressure, enthalpy = parts
    speed = speeds[direction]
    made = [moments[direction]]
    for axis in range(3):
        term = moments[axis] * speed
        made.append(term + pressure if axis == direction else term)
    made.append(enthalpy * speed)
    return made


def face_kernel(two_sided, where_ref, source_ref, windows_ref, left_ref, right_ref, *rest):
    windows, _, planes, layers, cells = windows_ref.shape
    wall_refs, scratch, sems = rest[:-2], rest[-2], rest[-1]
    copies = [
        pltpu.make_async_copy(source_ref.at[w], windows_ref.at[w], sems.at[w])
        for w in range(windows)
    ]
    for copy in copies:
        copy.start()
    tile = (layers, cells)
    up = [
        row_weights(tile, [weight(j - layers - i) for i in range(layers)]) for j in range(layers)
    ]
    down = [
        row_weights(tile, [weight(layers + j - i) for i in range(layers)]) for j in range(layers)
    ]
    if two_sided:
        tables = (up, down)
    else:
        first = where_ref[0] == 0
        tables = ([jnp.where(first, u, d) for u, d in zip(up, down)],)
    for w in range(windows):
        copies[w].wait()
        for x in range(planes):
            parts = primitives([windows_ref[w, f, x] for f in range(5)])
            for f, value in enumerate(flux(parts, 0)):
                scratch[f, x] = value
            for f, value in enumerate(flux(parts, 1)):
                for ref, table in zip(wall_refs, tables):
                    total = None
                    for j in range(layers):
                        term = table[j] * value[j : j + 1, :]
                        total = term if total is None else total + term
                    ref[w, f, x] = total
        for f in range(5):
            for i in range(REACH):
                total = None
                for j in range(planes):
                    c = weight(j - planes - i)
                    if c:
                        term = c * scratch[f, j]
                        total = term if total is None else total + term
                left_ref[w, f, i] = total
                total = None
                for j in range(planes):
                    c = weight(j + REACH - i)
                    if c:
                        term = c * scratch[f, j]
                        total = term if total is None else total + term
                right_ref[w, f, i] = total


def wall_group(where_ref, windows_ref, group_ref, lows, base, keep_x):
    windows, _, planes, layers, cells = windows_ref.shape
    tile = (layers, cells)
    first = where_ref[0] == 0
    table = [
        jnp.where(
            first,
            row_weights(tile, [weight(j - layers - i) for i in range(layers)]),
            row_weights(tile, [weight(layers + j - i) for i in range(layers)]),
        )
        for j in range(layers)
    ]
    for w in range(windows):
        upper = [[] for _ in range(5)]
        lower = [[] for _ in range(5)]
        for x in range(planes // 2):
            parts = primitives([windows_ref[w, f, base + x] for f in range(5)])
            keep_x(w, base + x, parts)
            for f, value in enumerate(flux(parts, 1)):
                total = None
                for j in range(layers):
                    term = table[j] * value[j : j + 1, :]
                    total = term if total is None else total + term
                high = total.astype(jnp.bfloat16).astype(jnp.float32)
                rest = total - high
                upper[f].append(high)
                lower[f].append(jnp.where(first, rest[0:2], rest[2:4]))
        for f in range(5):
            group_ref[f, 16 * w : 16 * w + 16] = jnp.concatenate(upper[f], axis=0).astype(
                jnp.bfloat16
            )
            lows[f, 8 * w : 8 * w + 8] = jnp.concatenate(lower[f], axis=0)
    for f in range(5):
        group_ref[f, 32:48] = lows[f].astype(jnp.bfloat16)


def near_kernel(where_ref, source_ref, group_ref, kept_ref, lows, sem):
    copy = pltpu.make_async_copy(source_ref, kept_ref, sem)
    copy.start()
    base = source_ref.shape[2] // 2 * where_ref[0]
    wall_group(where_ref, source_ref, group_ref, lows, base, lambda w, x, parts: None)
    copy.wait()


def later_kernel(
    where_ref, _, windows_ref, group_ref, first_ref, second_ref, scratch, lows,
    edge_lows,
):
    windows, _, planes, layers, cells = windows_ref.shape
    half = planes // 2

    def keep_x(w, x, parts):
        for f, value in enumerate(flux(parts, 0)):
            scratch[w, f, x] = value

    base = half * (1 - where_ref[0])
    wall_group(where_ref, windows_ref, group_ref, lows, base, keep_x)
    for w in range(windows):
        for x in range(half):
            plane = half * where_ref[0] + x
            keep_x(w, plane, primitives([windows_ref[w, f, plane] for f in range(5)]))
        for f in range(5):
            last, after = [], []
            for made, offset in ((after, -planes), (last, REACH)):
                for i in range(REACH):
                    total = None
                    for j in range(planes):
                        c = weight(j + offset - i)
                        if c:
                            term = c * scratch[w, f, j]
                            total = term if total is None else total + term
                    made.append(total)
            zeroth = where_ref[0] == 0
            for k, (ref, high) in enumerate(((first_ref, zeroth), (second_ref, where_ref[0] == 1))):
                both = [
                    jnp.where(high, x, y) for x, y in zip(last, after)
                ]
                upper = [x.astype(jnp.bfloat16).astype(jnp.float32) for x in both]
                rest = [x - y for x, y in zip(both, upper)]
                ref[f, 16 * w : 16 * w + 16] = jnp.concatenate(upper, axis=0).astype(jnp.bfloat16)
                edge_lows[k, f, 8 * w : 8 * w + 8] = jnp.concatenate(
                    [jnp.where(high, rest[2], rest[0]), jnp.where(high, rest[3], rest[1])], axis=0
                )
    for k, ref in enumerate((first_ref, second_ref)):
        for f in range(5):
            ref[f, 32:48] = edge_lows[k, f].astype(jnp.bfloat16)


def inner_part(windows_ref, part_ref, scratch):
    windows, _, planes, layers, cells = windows_ref.shape
    tile = (windows * layers, cells)
    walls = {
        k: row_weights(
            tile, [weight(k) if 0 <= i + k < layers else 0.0 for i in range(layers)] * windows
        )
        for k in range(-REACH, REACH + 1)
        if 0 < abs(k) < layers
    }
    for x in range(planes):
        fields = [
            jnp.concatenate([windows_ref[w, f, x] for w in range(windows)], axis=0)
            for f in range(5)
        ]
        parts = primitives(fields)
        for f, value in enumerate(flux(parts, 0)):
            scratch[f, x] = value
        flux_y, flux_z = flux(parts, 1), flux(parts, 2)
        for f in range(5):
            total = fields[f]
            for k, line in walls.items():
                total = total + line * pltpu.roll(flux_y[f], -k % tile[0], 0)
            for k in range(1, REACH + 1):
                total = total + weight(k) * (
                    pltpu.roll(flux_z[f], cells - k, 1) - pltpu.roll(flux_z[f], k, 1)
                )
            scratch[5 + f, x] = total
    for f in range(5):
        for x in range(planes):
            total = scratch[5 + f, x]
            for k in range(-REACH, REACH + 1):
                if k and 0 <= x + k < planes:
                    total = total + weight(k) * scratch[f, x + k]
            for w in range(windows):
                part_ref[w, f, x] = total[layers * w : layers * (w + 1)]


def gram_blocks(basis_ref, chunks, per_chunk, right, left):
    half = left.shape[0]
    for c in chunks:
        rows = jnp.concatenate(
            [modes_of(basis_ref, t) for t in range(c * per_chunk, (c + 1) * per_chunk)], axis=1
        )
        right = right + lax.dot_general(
            rows, rows[half:], NT, preferred_element_type=jnp.float32
        )
        left = left + lax.dot_general(
            rows[:half], rows[:half], NT, preferred_element_type=jnp.float32
        )
    return right, left


def inner_gram_kernel(
    early, windows_ref, basis_ref, part_ref, right_ref, left_ref, kept_ref, scratch, sems
):
    chunks = sems.shape[0]
    per_chunk = kept_ref.shape[1] // chunks
    copies = []
    for c in range(chunks):
        span = pl.ds(c * per_chunk, per_chunk)
        copies.append(
            pltpu.make_async_copy(basis_ref.at[:, span], kept_ref.at[:, span], sems.at[c])
        )
        copies[c].start()
    inner_part(windows_ref, part_ref, scratch)
    right, left = jnp.zeros(right_ref.shape, jnp.float32), jnp.zeros(left_ref.shape, jnp.float32)
    for c in range(chunks):
        copies[c].wait()
        if c < early:
            right, left = gram_blocks(kept_ref, [c], per_chunk, right, left)
    right_ref[...] = right
    left_ref[...] = left


def gram_kernel(early, chunks, _, right_ref, left_ref, basis_ref, gram_ref, total):
    modes, tiles = basis_ref.shape[:2]
    wide = modes * 8
    half = wide // 2
    right, left = gram_blocks(
        basis_ref, range(early, chunks), tiles // chunks, right_ref[...], left_ref[...]
    )
    tiles_left = half // LANES
    turned = right[0:half].T
    for tile in range(tiles_left):
        span = slice(tile * LANES, (tile + 1) * LANES)
        total[tile, 0:half] = left[:, span]
        total[tile, half:] = turned[:, span]
        total[tiles_left + tile] = right[:, span]
    rows = folded(total, modes)
    picks = (
        lax.broadcasted_iota(jnp.int32, (wide, modes), 0) // 8
        == lax.broadcasted_iota(jnp.int32, (wide, modes), 1)
    ).astype(jnp.float32)
    gram = jnp.dot(rows, picks, precision=HIGHEST, preferred_element_type=jnp.float32)
    gram_ref[:, 0:modes] = gram[0 : modes // 2]
    gram_ref[:, modes:] = gram[modes // 2 :]


def join_kernel(walls, part_ref, left_ref, right_ref, *rest):
    wall_refs, next_ref = rest[:walls], rest[walls]
    windows, _, planes, layers, cells = part_ref.shape
    for w in range(windows):
        for f in range(5):
            for x in range(planes):
                total = part_ref[w, f, x]
                for ref in wall_refs:
                    total = total + ref[w, f, x]
                if x < REACH:
                    total = total + left_ref[w, f, x]
                if x >= planes - REACH:
                    total = total + right_ref[w, f, x - planes + REACH]
                next_ref[w, f, x] = total


def wall_terms_of(first, group_ref, w, f):
    upper = group_ref[f, 16 * w : 16 * w + 16].astype(jnp.float32)
    lower = group_ref[f, 32:48].astype(jnp.float32)[8 * w : 8 * w + 8]
    zero = jnp.zeros((2, upper.shape[1]), jnp.float32)
    made = []
    for x in range(4):
        rest = lower[2 * x : 2 * x + 2]
        rest = jnp.where(
            first, jnp.concatenate([zero, rest], axis=0), jnp.concatenate([rest, zero], axis=0)
        )
        made.append(upper[4 * x : 4 * x + 4] + rest)
    return made


def wall_join_kernel(where_ref, part_ref, group_ref, given_ref):
    windows, _, planes = part_ref.shape[:3]
    base = planes // 2 * (1 - where_ref[0])
    for w in range(windows):
        for f in range(5):
            for x, term in enumerate(wall_terms_of(where_ref[0] == 0, group_ref, w, f)):
                given_ref[w, f, x] = part_ref[w, f, base + x] + term


def edge_terms_of(high, edge_ref, w, f):
    upper = edge_ref[f, 16 * w : 16 * w + 16].astype(jnp.float32)
    lower = edge_ref[f, 32:48].astype(jnp.float32)[8 * w : 8 * w + 8]
    made = []
    for x in range(4):
        rest = lower[4 * (x % 2) : 4 * (x % 2) + 4]
        rest = jnp.where(high, rest, 0.0) if x > 1 else jnp.where(high, 0.0, rest)
        made.append(upper[4 * x : 4 * x + 4] + rest)
    return made


def edge_join_kernel(where_ref, part_ref, edge_ref, made, snaps_ref):
    windows = part_ref.shape[0]
    for w in range(windows):
        for f in range(5):
            done = []
            for x, term in enumerate(edge_terms_of(where_ref[0] == 0, edge_ref, w, f)):
                total = part_ref[w, f, x] + term
                made[w, f, x] = total
                done.append(total)
            snaps_ref[w, f] = jnp.concatenate(done, axis=0).astype(jnp.bfloat16)


def own_join_kernel(where_ref, _, part_ref, edge_ref, group_ref, made, snaps_ref):
    windows, _, planes = part_ref.shape[:3]
    base = planes // 2 * where_ref[0]
    for w in range(windows):
        for f in range(5):
            done = []
            edges = edge_terms_of(where_ref[0] == 1, edge_ref, w, f)
            for x, term in enumerate(wall_terms_of(where_ref[0] == 0, group_ref, w, f)):
                total = part_ref[w, f, base + x] + term + edges[x]
                made[w, f, x] = total
                done.append(total)
            snaps_ref[w, f] = jnp.concatenate(done, axis=0).astype(jnp.bfloat16)


def same_layer(shape):
    rows = lax.broadcasted_iota(jnp.int32, shape, 0)
    columns = lax.broadcasted_iota(jnp.int32, shape, 1)
    return lax.rem(rows, 8) == lax.rem(columns, 8)


def folded(total, modes):
    kept = lax.rem(lax.broadcasted_iota(jnp.int32, (modes, LANES), 1), 8)
    made = []
    for tile in range(total.shape[0]):
        rows = jnp.zeros((modes, LANES), jnp.float32)
        for y in range(8):
            rows = jnp.where(kept == y, total[tile, pl.ds(y, modes, 8), :], rows)
        made.append(rows)
    return made[0] if len(made) == 1 else jnp.concatenate(made, axis=1)


def modes_of(basis_ref, t):
    modes, _, layers, cells = basis_ref.shape
    return basis_ref[:, t].reshape(modes * layers, cells)


def project_kernel(paired, where_ref, *rest):
    if paired:
        (
            own_ref, got_ref, next_own_ref, next_given_ref, basis_ref,
            sums_ref, snaps_ref, next_ref, square, wide_sums, sems,
        ) = rest
        first = where_ref[0] == 0
        half = next_own_ref.shape[2]
        copies = []
        for i, (source, base) in enumerate(
            ((next_own_ref, half * where_ref[0]), (next_given_ref, half * (1 - where_ref[0])))
        ):
            copies.append(
                pltpu.make_async_copy(source, next_ref.at[:, :, pl.ds(base, half)], sems.at[i])
            )
            copies[i].start()
        for w in range(own_ref.shape[0]):
            for f in range(own_ref.shape[1]):
                own = own_ref[w, f].astype(jnp.float32)
                got = got_ref[w, f].astype(jnp.float32)
                low = jnp.where(first, own, got)
                high = jnp.where(first, got, own)
                for t in range(4):
                    snaps_ref[4 * f + t, pl.ds(8 * w, 8)] = jnp.concatenate(
                        [low[4 * t : 4 * t + 4], high[4 * t : 4 * t + 4]], axis=0
                    ).astype(jnp.bfloat16)
    else:
        snaps_ref, basis_ref, sums_ref, square, wide_sums = rest
        copies = []
    modes, tiles = basis_ref.shape[:2]
    columns = snaps_ref.shape[1]
    total = jnp.zeros((modes * 8 + columns, columns), jnp.float32)
    for start in range(0, tiles, 4):
        span = range(start, min(start + 4, tiles))
        snaps = jnp.concatenate([snaps_ref[t] for t in span], axis=1)
        rows = jnp.concatenate([modes_of(basis_ref, t) for t in span], axis=1)
        total = total + lax.dot_general(
            jnp.concatenate([rows, snaps], axis=0), snaps, NT, preferred_element_type=jnp.float32
        )
    small = total[modes * 8 :]
    total = total[: modes * 8]
    wide_sums[0, :, 0:columns] = total
    square[...] = jnp.zeros_like(square)
    square[0:modes, :] = folded(wide_sums, modes)
    kept = jnp.where(same_layer(small.shape), small, 0.0)
    square[modes : modes + 1, 0:columns] = jnp.sum(kept[0:8], axis=0, keepdims=True)
    square[modes + 1 : modes + 2, 0:columns] = jnp.sum(kept[8:16], axis=0, keepdims=True)
    lanes = lax.broadcasted_iota(jnp.int32, square.shape, 1)
    turned = jnp.where(lanes < columns, square[...], 0.0).T
    sums = jnp.concatenate(
        [
            jnp.sum(turned[0:8], axis=0, keepdims=True),
            jnp.sum(turned[8:16], axis=0, keepdims=True),
        ],
        axis=0,
    )
    sums_ref[...] = jnp.concatenate(
        [sums, jnp.zeros((6, sums.shape[1]), jnp.float32)], axis=0
    )
    for copy in copies:
        copy.wait()


def merge_kernel(gram_ref, far_ref, sums_ref, merged_ref):
    rows = gram_ref.shape[0]
    merged_ref[0:rows] = gram_ref[...] + far_ref[...]
    merged_ref[rows:] = sums_ref[...]


def unpacked(sums_ref, modes):
    half = modes // 2
    return jnp.concatenate([sums_ref[0:half, 0:modes], sums_ref[0:half, modes:]], axis=0)


def inverse_kernel(sums_ref, inverse_ref, spread_ref, plain, scaled):
    modes = inverse_ref.shape[0]
    rows = lax.broadcasted_iota(jnp.int32, (8, 2 * modes), 0)
    lanes = lax.broadcasted_iota(jnp.int32, (8, 2 * modes), 1)
    tiles = []
    gram = unpacked(sums_ref, modes)
    for tile in range(modes // 8):
        eye = (lanes == rows + (modes + 8 * tile)).astype(jnp.float32)
        start = 8 * tile % (modes // 2)
        line = sums_ref[start : start + 8, :]
        if 8 * tile >= modes // 2:
            line = pltpu.roll(line, modes, 1)
        tiles.append(jnp.where(lanes < modes, line, eye))
    count = modes // 8
    for home in range(count):
        columns = [
            [
                jnp.broadcast_to(
                    tiles[tile][:, 8 * home + j : 8 * home + j + 1], (8, 2 * modes)
                )
                for tile in range(home, count)
            ]
            for j in range(8)
        ]
        for j in range(8):
            k = 8 * home + j
            inverse = 1.0 / columns[j][0]
            inverse = inverse[j : j + 1, :]
            row = tiles[home][j : j + 1, :]
            ready = row * inverse
            plain[k : k + 1, :] = row
            scaled[k : k + 1, :] = ready
            factors = [jnp.where(rows > j, columns[j][0], 0.0)] + columns[j][1:]
            for later in range(j + 1, 8):
                share = columns[j][0][later : later + 1, :] * inverse
                columns[later] = [c - f * share for c, f in zip(columns[later], factors)]
            for tile in range(home, count):
                tiles[tile] = tiles[tile] - factors[tile - home] * ready
    exact = functools.partial(
        lax.dot_general, precision=HIGHEST, preferred_element_type=jnp.float32
    )
    plainly = (((1,), (0,)), ((), ()))
    inverse = exact(plain[:, modes:], scaled[:, modes:], (((0,), (0,)), ((), ())))
    square = (modes, modes)
    eye = lax.broadcasted_iota(jnp.int32, square, 0) == lax.broadcasted_iota(jnp.int32, square, 1)
    off = eye.astype(jnp.float32) - exact(gram, inverse, plainly)
    inverse = inverse + exact(inverse, off, plainly)
    inverse_ref[...] = inverse
    wide = spread_ref.shape[1]
    spread = (
        lax.broadcasted_iota(jnp.int32, (modes, wide), 1) // 8
        == lax.broadcasted_iota(jnp.int32, (modes, wide), 0)
    ).astype(jnp.bfloat16)
    parts = []
    rest = inverse
    for _ in range(3):
        parts.append(rest.astype(jnp.bfloat16))
        rest = rest - parts[-1].astype(jnp.float32)
    wide_parts = jnp.dot(
        jnp.concatenate(parts, axis=0), spread, preferred_element_type=jnp.float32
    )
    spread_ref[...] = (
        wide_parts[0:modes] + wide_parts[modes : 2 * modes] + wide_parts[2 * modes :]
    )


def finish_kernel(
    rows_total, projected_ref, sums_ref, inverse_ref, spread_ref, snaps_ref, basis_ref,
    modes_ref, solved_ref, factor_ref, made, sems,
):
    modes, tiles, _, cells = basis_ref.shape
    wide = modes * 8
    exact = functools.partial(jnp.dot, precision=HIGHEST, preferred_element_type=jnp.float32)
    base = modes // 2
    projected = projected_ref[base : base + 8, 0:modes]
    lines = exact(projected, spread_ref[...])
    full = jnp.concatenate(
        [jnp.broadcast_to(lines[0:1], (8, wide)), jnp.broadcast_to(lines[1:2], (8, wide))],
        axis=0,
    )
    full = jnp.where(same_layer(full.shape), full, 0.0)
    upper = full.astype(jnp.bfloat16)
    fit = jnp.concatenate([upper, (full - upper.astype(jnp.float32)).astype(jnp.bfloat16)], axis=0)
    solved = exact(projected, inverse_ref[...])
    left = projected - exact(solved, unpacked(sums_ref, modes))

    def inner(p, i, q, j):
        return jnp.sum(p[i : i + 1] * q[j : j + 1], axis=1, keepdims=True)

    def entry(i, j):
        square = projected_ref[base + i : base + i + 1, modes + j : modes + j + 1]
        return square - inner(projected, i, solved, j) - inner(solved, i, left, j)

    first = jnp.sqrt(entry(0, 0))
    below = entry(1, 0) / first
    second = jnp.sqrt(entry(1, 1) - below * below)
    scaling = jnp.sqrt(jnp.float32(rows_total))
    w00 = scaling / first
    w11 = scaling / second
    w01 = -(below / first) * w11
    solved_ref[...] = solved[0:2]
    factor_ref[0:1, 0:1] = first / scaling
    factor_ref[0:1, 1:2] = below / scaling
    factor_ref[1:2, 0:1] = jnp.zeros_like(first)
    factor_ref[1:2, 1:2] = second / scaling
    chunks = sems.shape[0]
    per_chunk = tiles // chunks
    copies = []
    for c in range(chunks):
        for t in range(c * per_chunk, (c + 1) * per_chunk):
            fitted = jnp.dot(fit, modes_of(basis_ref, t), preferred_element_type=jnp.float32)
            fitted = fitted[0:16] + fitted[16:32]
            snaps = snaps_ref[t].astype(jnp.float32)
            left_over = snaps - fitted
            made[0, t] = left_over[0:8] * w00
            made[1, t] = left_over[8:16] * w11 + left_over[0:8] * w01
        span = pl.ds(c * per_chunk, per_chunk)
        copies.append(
            pltpu.make_async_copy(made.at[:, span], modes_ref.at[:, span], sems.at[c])
        )
        copies[c].start()
    for copy in copies:
        copy.wait()


def params(mib):
    return pltpu.CompilerParams(vmem_limit_bytes=mib * 1024 * 1024)


def cost(flops, moved):
    return pl.CostEstimate(flops=flops, bytes_accessed=moved, transcendentals=0)


WHOLE = pl.BlockSpec(memory_space=pltpu.VMEM)
FAR = pl.BlockSpec(memory_space=pltpu.HBM)
LOOSE = pl.BlockSpec(memory_space=pl.ANY)
SCALAR = pl.BlockSpec(memory_space=pltpu.SMEM)


def swap_added(value, axis, bit):
    count = lax.axis_size(axis)
    return value + lax.ppermute(value, axis, [(i, i ^ bit) for i in range(count)])


def bits(count):
    made = [1 << k for k in range(count.bit_length() - 1)]
    if count != 1 << len(made):
        raise ValueError("axis size")
    return made


def body(windows, pod_basis):
    f32, bf16 = jnp.float32, jnp.bfloat16
    shape = jax.ShapeDtypeStruct
    count, fields, planes, layers, cells = windows.shape
    ring, walls = lax.axis_size("solver"), lax.axis_size("analysis")
    paired = walls == 2 and planes == 8 and layers == 4
    place = lax.axis_index("analysis").astype(jnp.int32).reshape(1)
    modes, _, pod_planes, pod_layers, _ = pod_basis.shape
    tiles = fields * pod_planes * (pod_layers // 8)
    basis = pod_basis.reshape(modes, tiles, 8, cells)
    wide = modes * 8
    basis_bytes = basis.size * 2

    to_right = [(i, (i + 1) % ring) for i in range(ring)]
    to_left = [((i + 1) % ring, i) for i in range(ring)]
    edge_shape = shape((count, fields, REACH, layers, cells), f32)
    face_scratch = [pltpu.VMEM((fields, planes, layers, cells), f32)]
    face_cost = cost(10_000_000, 10 * windows.size)
    if paired:
        swap = [(0, 1), (1, 0)]
        group_shape = shape((fields, 48, cells), bf16)
        lows = pltpu.VMEM((fields, 16, cells), f32)
        near_group, kept = pl.pallas_call(
            near_kernel,
            out_shape=[group_shape, shape(windows.shape, f32)],
            in_specs=[SCALAR, WHOLE],
            out_specs=[WHOLE] * 2,
            scratch_shapes=[lows, pltpu.SemaphoreType.DMA],
            compiler_params=params(16),
            cost_estimate=face_cost,
            name="near_faces",
        )(place, windows)
        later_group, first_edge, second_edge = pl.pallas_call(
            later_kernel,
            out_shape=[group_shape] * 3,
            in_specs=[SCALAR, LOOSE, WHOLE],
            out_specs=[WHOLE] * 3,
            scratch_shapes=[
                pltpu.VMEM((count, fields, planes, layers, cells), f32),
                lows,
                pltpu.VMEM((2, fields, 16, cells), f32),
            ],
            compiler_params=params(16),
            cost_estimate=face_cost,
            name="later_faces",
        )(place, near_group, kept)
        near_group = lax.ppermute(near_group, "analysis", swap)
        down = [(2 * ((i + 1) % ring), 2 * i) for i in range(ring)]
        up = [(2 * i, 2 * ((i + 1) % ring)) for i in range(ring)]
        odd = lambda pairs: [(a + 1, b + 1) for a, b in pairs]
        first_edge = lax.ppermute(first_edge, ("solver", "analysis"), down + odd(up))
        second_edge = lax.ppermute(second_edge, ("solver", "analysis"), up + odd(down))
        later_group = lax.ppermute(later_group, "analysis", swap)
    else:
        kept, to_next, to_last, up, down = pl.pallas_call(
            functools.partial(face_kernel, True),
            out_shape=[shape(windows.shape, f32)]
            + [edge_shape] * 2
            + [shape(windows.shape, f32)] * 2,
            in_specs=[SCALAR, FAR],
            out_specs=[WHOLE] * 5,
            scratch_shapes=face_scratch + [pltpu.SemaphoreType.DMA((count,))],
            compiler_params=params(16),
            cost_estimate=face_cost,
            name="faces",
        )(place, windows)
        wall_terms = [
            lax.ppermute(up, "analysis", [(i, i + 1) for i in range(walls - 1)]),
            lax.ppermute(down, "analysis", [(i + 1, i) for i in range(walls - 1)]),
        ]
        from_left = lax.ppermute(to_next, "solver", to_right)
        from_right = lax.ppermute(to_last, "solver", to_left)

    early = 2
    gram_flops = 2 * wide * wide * cells * tiles
    inner, right, left, basis = pl.pallas_call(
        functools.partial(inner_gram_kernel, early),
        out_shape=[
            shape(windows.shape, f32),
            shape((wide, wide // 2), f32),
            shape((wide // 2, wide // 2), f32),
            shape(basis.shape, bf16),
        ],
        in_specs=[WHOLE, FAR],
        out_specs=[WHOLE] * 4,
        scratch_shapes=[
            pltpu.VMEM((2 * fields, planes, count * layers, cells), f32),
            pltpu.SemaphoreType.DMA((fields,)),
        ],
        compiler_params=params(40),
        cost_estimate=cost(1_000_000, windows.size),
        name="inner_gram",
    )(kept, basis)

    def rest_of_gram(after):
        return pl.pallas_call(
            functools.partial(gram_kernel, early, fields),
            out_shape=shape((modes // 2, 2 * modes), f32),
            in_specs=[LOOSE] + [WHOLE] * 3,
            out_specs=WHOLE,
            scratch_shapes=[pltpu.VMEM((wide // LANES, wide, LANES), f32)],
            compiler_params=params(24),
            cost_estimate=cost(gram_flops // 2, basis_bytes),
            name="gram",
        )(after, right, left, basis)

    join_cost = cost(1_000_000, 16 * windows.size)
    if paired:
        half_shape = (count, fields, planes * layers // 2, cells)

        half_next = shape((count, fields, planes // 2, layers, cells), f32)

        inner_given = pl.pallas_call(
            wall_join_kernel,
            out_shape=half_next,
            in_specs=[SCALAR] + [WHOLE] * 2,
            out_specs=WHOLE,
            compiler_params=params(16),
            cost_estimate=cost(gram_flops // 2, basis_bytes),
            name="wall_join",
        )(place, inner, near_group)
        next_given, given = pl.pallas_call(
            edge_join_kernel,
            out_shape=[half_next, shape(half_shape, bf16)],
            in_specs=[SCALAR] + [WHOLE] * 2,
            out_specs=[WHOLE] * 2,
            compiler_params=params(16),
            cost_estimate=join_cost,
            name="edge_join",
        )(place, inner_given, first_edge)
        got = lax.ppermute(given, "analysis", swap)
        gram = rest_of_gram(given)
    else:
        next_windows = pl.pallas_call(
            functools.partial(join_kernel, 2),
            out_shape=shape(windows.shape, f32),
            in_specs=[WHOLE] * 5,
            out_specs=WHOLE,
            compiler_params=params(16),
            cost_estimate=join_cost,
            name="join",
        )(inner, from_left, from_right, *wall_terms)
        gram = rest_of_gram(place)
    ring_bits = bits(ring)
    lone = ring_bits.pop(1 if len(ring_bits) > 1 else 0)
    gram_far = lax.ppermute(gram, "solver", [(i, i ^ lone) for i in range(ring)])
    if paired:
        next_own, own = pl.pallas_call(
            own_join_kernel,
            out_shape=[half_next, shape(half_shape, bf16)],
            in_specs=[SCALAR, LOOSE] + [WHOLE] * 3,
            out_specs=[WHOLE] * 2,
            compiler_params=params(16),
            cost_estimate=join_cost,
            name="own_join",
        )(place, gram, inner, second_edge, later_group)

    sums_shape = shape((8, LANES), f32)
    snaps_shape = shape((tiles, 2 * 8, cells), bf16)
    scratch = [pltpu.VMEM((LANES, LANES), f32), pltpu.VMEM((1, wide, LANES), f32)]
    project_cost = cost(2 * wide * 16 * cells * tiles, basis_bytes)
    if paired:
        sums, snaps, next_windows = pl.pallas_call(
            functools.partial(project_kernel, True),
            out_shape=[sums_shape, snaps_shape, shape(windows.shape, f32)],
            in_specs=[SCALAR] + [WHOLE] * 5,
            out_specs=[WHOLE, WHOLE, FAR],
            scratch_shapes=scratch + [pltpu.SemaphoreType.DMA((2,))],
            compiler_params=params(16),
            cost_estimate=project_cost,
            name="project",
        )(place, own, got, next_own, next_given, basis)
    else:
        relaid = lax.all_to_all(
            next_windows.astype(bf16), "analysis", split_axis=2, concat_axis=3, tiled=True
        )
        snaps = relaid.reshape(count, tiles, 8, cells).transpose(1, 0, 2, 3)
        snaps = snaps.reshape(tiles, count * 8, cells)
        sums = pl.pallas_call(
            functools.partial(project_kernel, False),
            out_shape=sums_shape,
            in_specs=[SCALAR] + [WHOLE] * 2,
            out_specs=WHOLE,
            scratch_shapes=scratch,
            compiler_params=params(16),
            cost_estimate=project_cost,
            name="project",
        )(place, snaps, basis)
    sums = pl.pallas_call(
        merge_kernel,
        out_shape=shape((modes // 2 + 8, LANES), f32),
        in_specs=[WHOLE] * 3,
        out_specs=WHOLE,
        compiler_params=params(16),
        cost_estimate=cost(10_000, 8 * modes * LANES),
        name="merge",
    )(gram, gram_far, sums)
    for bit in bits(walls):
        sums = swap_added(sums, "analysis", bit)
    for bit in ring_bits:
        sums = swap_added(sums, "solver", bit)
    inverse, spread = pl.pallas_call(
        inverse_kernel,
        out_shape=[shape((modes, modes), f32), shape((modes, wide), f32)],
        in_specs=[WHOLE],
        out_specs=[WHOLE] * 2,
        scratch_shapes=[pltpu.VMEM((modes, 2 * modes), f32)] * 2,
        compiler_params=params(16),
        cost_estimate=cost(20_000_000, 8 * modes * modes),
        name="inverse",
    )(sums)
    projected = swap_added(sums, "solver", lone)

    rows_total = ring * walls * tiles * 8 * cells
    new_modes, solved, factor = pl.pallas_call(
        functools.partial(finish_kernel, rows_total),
        out_shape=[
            shape((count, tiles, 8, cells), f32),
            shape((count, modes), f32),
            shape((count, count), f32),
        ],
        in_specs=[WHOLE] * 6,
        out_specs=[FAR, WHOLE, WHOLE],
        scratch_shapes=[
            pltpu.VMEM((count, tiles, 8, cells), f32),
            pltpu.SemaphoreType.DMA((2 * fields,)),
        ],
        compiler_params=params(16),
        cost_estimate=cost(2 * wide * 32 * cells * tiles, basis_bytes + 8 * windows.size),
        name="finish",
    )(projected, sums, inverse, spread, snaps, basis)
    new_modes = new_modes.reshape(count, fields, pod_planes, pod_layers, cells)
    return next_windows, solved, new_modes, factor


def solution(mesh):
    in_specs = (
        P(None, None, "solver", "analysis", None),
        P(None, None, ("solver", "analysis"), None, None),
    )
    out_specs = (
        P(None, None, "solver", "analysis", None),
        P(),
        P(None, None, ("solver", "analysis"), None, None),
        P(),
    )
    return jax.shard_map(body, mesh=mesh, in_specs=in_specs, out_specs=out_specs, check_vma=False)
```
